32 devices in a mesh: dp: 16 (over z, x, core), tensor: 2 (over y).
Axes of the slice: x: 2, y: 2, z: 4, core: 2. Of those that a mesh axis runs over, the one named last changes fastest.
Arguments:
- block_input: bfloat16 [2, 16, 1024, 768], P(None, 'dp', 'tensor'), may hold values from -6 to 6
- cotangent: bfloat16 [2, 16, 1024, 768], P(None, 'dp', 'tensor'), may hold values from -6 to 6
- lengths: int32 [2, 16], P(None, 'dp'), may hold values from 128 to 1024, as said below
- ln1_gain: float32 [768], replicated, may hold values from 0.5 to 1.5
- ln1_bias: float32 [768], replicated, may hold values from -1.5 to 1.5
- ln2_gain: float32 [768], replicated, may hold values from 0.5 to 1.5
- ln2_bias: float32 [768], replicated, may hold values from -1.5 to 1.5
- w_query: bfloat16 [768, 768], P('dp', 'tensor'), may hold values from -0.21875 to 0.21875
- b_query: float32 [768], P('tensor'), may hold values from -3 to 3
- w_shared: bfloat16 [768, 128], P('dp'), may hold values from -0.21875 to 0.21875
- b_shared: float32 [128], replicated, may hold values from -3 to 3
- w_out: bfloat16 [768, 768], P('tensor', 'dp'), may hold values from -1.75 to 1.75
- b_out: float32 [768], replicated, may hold values from -3 to 3
- w_up: bfloat16 [768, 3072], P('dp', 'tensor'), may hold values from -0.21875 to 0.21875
- b_up: float32 [3072], P('tensor'), may hold values from -3 to 3
- w_down: bfloat16 [3072, 768], P('tensor', 'dp'), may hold values from -0.109375 to 0.109375
- b_down: float32 [768], replicated, may hold values from -3 to 3
Outputs:
- output: bfloat16 [2, 16, 1024, 768], P(None, 'dp', 'tensor')
- grad_input: bfloat16 [2, 16, 1024, 768], P(None, 'dp', 'tensor')
- grad_ln1_gain: float32 [768], replicated
- grad_ln1_bias: float32 [768], replicated
- grad_ln2_gain: float32 [768], replicated
- grad_ln2_bias: float32 [768], replicated
- grad_w_query: float32 [768, 768], P('dp', 'tensor')
- grad_b_query: float32 [768], P('tensor')
- grad_w_shared: float32 [768, 128], P('dp')
- grad_b_shared: float32 [128], replicated
- grad_w_out: float32 [768, 768], P('tensor', 'dp')
- grad_b_out: float32 [768], replicated
- grad_w_up: float32 [768, 3072], P('dp', 'tensor')
- grad_b_up: float32 [3072], P('tensor')
- grad_w_down: float32 [3072, 768], P('tensor', 'dp')
- grad_b_down: float32 [768], replicated
The draws below stay inside these ranges and needn't reach their ends.
Inputs may be any that keep to these rules, and one draw needn't show every extreme that they name: `lengths`: each entry is the number of real tokens at the start of its padded sequence, the rest padding. For every sequence index s one of its 2 micro-batches has a length over 512, and one sequence of the whole batch has length exactly 1024.
All inputs are finite; a program needn't handle non-finite values.
Results may differ from the reference program's by a relative error of at most 0.011.
Values may be sent and summed in bfloat16 or wider, within the bound.
A program may use at most 192 MiB of HBM per device.

```python
import jax
import jax.numpy as jnp
from jax import lax

D = 768
HEADS = 12
HEAD_DIM = 64
FF = 3072
ROT = 16
LEN = 1024
MB = 2
QBLK = 512
SEQS = 16


def draw_lengths(key, part):
    key = jax.random.fold_in(key, 11)
    keys = jax.random.split(key, 6)
    shape = (MB, SEQS)
    least = LEN // 8
    expo = jnp.minimum(jax.random.randint(keys[0], shape, 0, 4), jax.random.randint(keys[1], shape, 0, 4))
    base = least * jnp.left_shift(jnp.ones(shape, jnp.int32), expo)
    extra = jax.random.randint(keys[2], shape, 0, 1024) * base // 1024
    length = jnp.minimum(base + extra, LEN)
    picked = jax.random.randint(keys[3], (SEQS,), 0, MB)
    longer = LEN // 2 + 1 + jax.random.randint(keys[4], (SEQS,), 0, LEN // 2)
    chosen = jnp.arange(MB)[:, None] == picked[None, :]
    length = jnp.where(chosen, jnp.maximum(length, longer[None, :]), length)
    full_at = jax.random.randint(keys[5], (), 0, MB * SEQS)
    flat_pos = jnp.arange(MB * SEQS).reshape(shape)
    length = jnp.where(flat_pos == full_at, LEN, length)
    return length.astype(jnp.int32)


def raised(entries, key, source, target, blocks, factor):
    owner, partner = [(jnp.arange(entries.shape[axis_at]) // (entries.shape[axis_at] // blocks)).reshape([-1 if axis == axis_at else 1 for axis in range(entries.ndim)]) for axis_at in (source, target)]
    chosen = jax.random.permutation(key, blocks)[partner]
    strong = (owner == chosen) | (owner == (partner + blocks // 2) % blocks)
    return jnp.where(strong, factor * entries, entries)


def steps_of(key, shape, cuts, low, top_value):
    factor_of, own = 1.0, jax.random.fold_in(key, 6)
    for dim, shards_of in cuts:
        steps = jnp.exp(jax.random.uniform(jax.random.fold_in(own, dim), (shards_of,), jnp.float32, low / len(cuts), top_value / len(cuts)))
        factor_of = factor_of * jnp.repeat(steps, shape[dim] // shards_of).reshape([-1 if axis == dim else 1 for axis in range(len(shape))])
    return factor_of


def scatter_about(stream_key, extent, deviation, bound, shards=(), dtype=jnp.bfloat16):
    drawn = deviation * jax.random.normal(stream_key, extent, jnp.float32)
    if shards:
        drawn = drawn * steps_of(stream_key, extent, shards, -0.22, 0.18)
    return jnp.clip(drawn, -bound, bound).astype(dtype)


def gaussian_with(own_key, dims, width, bound, pieces, heavy, held_as=jnp.bfloat16):
    array = width * jax.random.normal(own_key, dims, jnp.float32)
    if pieces:
        array = array * steps_of(own_key, dims, pieces, -0.22, 0.18)
    return jnp.clip(raised(array, jax.random.fold_in(own_key, 3), *heavy), -bound, bound).astype(held_as)


def setup_inputs(seed: int = 0) -> dict:
    arg_keys = jax.random.split(jax.random.key(seed), 18)
    return {
        "block_input": gaussian_with(arg_keys[0], (MB, SEQS, LEN, D), 1.0, 6.0, ((1, 16), (2, 2)), (1, 3, 16, 2.0)),
        "cotangent": gaussian_with(arg_keys[1], (MB, SEQS, LEN, D), 1.0, 6.0, ((1, 16), (2, 2)), (1, 3, 16, 2.0)),
        "lengths": draw_lengths(jax.random.fold_in(arg_keys[17], 71), 0),
        "ln1_gain": jnp.clip(1.0 + 0.1 * jax.random.normal(arg_keys[3], (D,), jnp.float32), 0.5, 1.5),
        "ln1_bias": scatter_about(arg_keys[4], (D,), 0.3, 1.5, (), jnp.float32),
        "ln2_gain": jnp.clip(1.0 + 0.1 * jax.random.normal(arg_keys[5], (D,), jnp.float32), 0.5, 1.5),
        "ln2_bias": scatter_about(arg_keys[6], (D,), 0.3, 1.5, (), jnp.float32),
        "w_query": scatter_about(arg_keys[7], (D, D), D ** -0.5, 0.21875, ((0, 16), (1, 2))),
        "b_query": scatter_about(arg_keys[8], (D,), 0.5, 3.0, ((0, 2),), jnp.float32),
        "w_shared": scatter_about(arg_keys[9], (D, 2 * HEAD_DIM), D ** -0.5, 0.21875, ((0, 16),)),
        "b_shared": scatter_about(arg_keys[10], (2 * HEAD_DIM,), 0.5, 3.0, (), jnp.float32),
        "w_out": scatter_about(arg_keys[11], (D, D), (D // 64) ** -0.5, 1.75, ((0, 2), (1, 16))),
        "b_out": scatter_about(arg_keys[12], (D,), 0.5, 3.0, (), jnp.float32),
        "w_up": scatter_about(arg_keys[13], (D, FF), D ** -0.5, 0.21875, ((0, 16), (1, 2))),
        "b_up": scatter_about(arg_keys[14], (FF,), 0.5, 3.0, ((0, 2),), jnp.float32),
        "w_down": scatter_about(arg_keys[15], (FF, D), FF ** -0.5, 0.109375, ((0, 2), (1, 16))),
        "b_down": scatter_about(arg_keys[16], (D,), 0.5, 3.0, (), jnp.float32),
    }


EPS = 1e-05
HIGH = lax.Precision.HIGHEST

@jax.custom_vjp
def low(v):
    return lax.optimization_barrier(v.astype(jnp.bfloat16)).astype(jnp.float32)

@jax.custom_vjp
def low_back(v):
    return v

def low_keep(v):
    return (low(v), None)

def low_pass(kept, grad):
    return (grad,)

def back_keep(v):
    return (v, None)

def back_low(kept, grad):
    return (low(grad),)
low.defvjp(low_keep, low_pass)
low_back.defvjp(back_keep, back_low)

def tables(count):
    places = jnp.arange(count).astype(jnp.float32)
    freqs = jnp.power(10000.0, -jnp.arange(ROT // 2).astype(jnp.float32) * 2.0 / ROT)
    angles = places[:, None] * freqs[None, :]
    return (jnp.cos(angles)[:, None, :], jnp.sin(angles)[:, None, :])

def rotate(vector, cosine, sine):
    first = vector[..., :ROT // 2]
    second = vector[..., ROT // 2:ROT]
    return jnp.concatenate([first * cosine - second * sine, second * cosine + first * sine, vector[..., ROT:]], axis=-1)

def normalize(vector, gain, shift):
    centre = vector - lax.optimization_barrier(jnp.mean(vector, axis=-1, keepdims=True))
    spread = lax.optimization_barrier(jnp.mean(centre * centre, axis=-1, keepdims=True))
    return centre * lax.rsqrt(spread + EPS) * gain + shift

def matmul(left, right):
    return jnp.dot(left, right, precision=HIGH, preferred_element_type=jnp.float32)

def sequence_forward(inputs, params, length):
    g1, b1, g2, b2, w_query, b_query, w_shared, b_shared, w_out, b_out, wup, bup, wdown, bdown = params
    cosine, sine = tables(LEN)
    normed_one = low(normalize(inputs, g1, b1))
    normed_two = low(normalize(inputs, g2, b2))
    queries = low_back(matmul(normed_one, w_query) + b_query).reshape(LEN, HEADS, HEAD_DIM)
    queries = low(rotate(queries, cosine, sine) * 0.125)
    shared = low_back(matmul(normed_one, w_shared) + b_shared)
    keys = low(rotate(shared[:, None, :HEAD_DIM], cosine, sine)[:, 0])
    values = low(shared[:, HEAD_DIM:])
    key_pos = jnp.arange(LEN)

    def block(start):
        rows = lax.dynamic_slice_in_dim(queries, start, QBLK, 0)
        row_pos = start + jnp.arange(QBLK)
        scores = low_back(jnp.einsum('qhd,kd->hqk', rows, keys, precision=HIGH))
        allowed = (key_pos[None, :] <= row_pos[:, None]) & (key_pos[None, :] < length)
        scores = jnp.where(allowed[None], scores, jnp.float32(-1e+30))
        top = lax.optimization_barrier(jnp.max(scores, axis=-1, keepdims=True))
        expo = jnp.exp(scores - top)
        probs = low(expo / lax.optimization_barrier(jnp.sum(expo, axis=-1, keepdims=True)))
        return jnp.einsum('hqk,kd->qhd', probs, values, precision=HIGH)
    starts = (jnp.arange(LEN // QBLK) * QBLK).astype(jnp.int32)
    attended = lax.map(jax.checkpoint(block), starts)
    attended = low(low_back(attended.reshape(LEN, D)))
    hidden = low_back(matmul(normed_two, wup) + bup)
    active = low(jax.nn.gelu(hidden, approximate=False))
    return inputs + (matmul(attended, w_out) + b_out) + (matmul(active, wdown) + bdown)

def reference(block_input, cotangent, lengths, ln1_gain, ln1_bias, ln2_gain, ln2_bias, w_query, b_query, w_shared, b_shared, w_out, b_out, w_up, b_up, w_down, b_down):
    params = tuple((w.astype(jnp.float32) for w in (ln1_gain, ln1_bias, ln2_gain, ln2_bias, w_query, b_query, w_shared, b_shared, w_out, b_out, w_up, b_up, w_down, b_down)))
    flat_x = block_input.reshape(MB * SEQS, LEN, D).astype(jnp.float32)
    flat_cot = cotangent.reshape(MB * SEQS, LEN, D).astype(jnp.float32)
    flat_len = lengths.reshape(MB * SEQS).astype(jnp.int32)

    def step(total, item):
        inputs, upstream, length = item
        result, pull = jax.vjp(lambda a, b: sequence_forward(a, b, length), inputs, params)
        valid = (jnp.arange(LEN) < length).astype(jnp.float32)[:, None]
        grad_in, grad_params = pull(upstream * valid)
        total = jax.tree.map(jnp.add, total, grad_params)
        return (total, (result.astype(jnp.bfloat16), grad_in.astype(jnp.bfloat16)))
    zeros = jax.tree.map(jnp.zeros_like, params)
    total, (results, grads) = lax.scan(step, zeros, (flat_x, flat_cot, flat_len))
    return (results.reshape(block_input.shape), grads.reshape(block_input.shape), total[0], total[1], total[2], total[3], total[4], total[5], total[6], total[7], total[8], total[9], total[10], total[11], total[12], total[13])
```

```python
from functools import partial

import jax
import jax.numpy as jnp
import numpy as np
from jax import lax
from jax.experimental import pallas as pl
from jax.experimental.pallas import tpu as pltpu
from jax.sharding import PartitionSpec as P

HEAD_DIM = 64
ROT = 16
MB = 2
QBLK = 512


EPS = 1e-05


def tables(count):
    places = jnp.arange(count).astype(jnp.float32)
    freqs = jnp.power(10000.0, -jnp.arange(ROT // 2).astype(jnp.float32) * 2.0 / ROT)
    angles = places[:, None] * freqs[None, :]
    return (jnp.cos(angles)[:, None, :], jnp.sin(angles)[:, None, :])


def rotate(vector, cosine, sine):
    first = vector[..., : ROT // 2]
    second = vector[..., ROT // 2 : ROT]
    return jnp.concatenate(
        [first * cosine - second * sine, second * cosine + first * sine, vector[..., ROT:]], axis=-1
    )


def unrotate(grad, cosine, sine):
    first = grad[..., : ROT // 2]
    second = grad[..., ROT // 2 : ROT]
    return jnp.concatenate(
        [first * cosine + second * sine, second * cosine - first * sine, grad[..., ROT:]], axis=-1
    )


def normalize(vector):
    centre = vector - jnp.mean(vector, axis=-1, keepdims=True)
    spread = jnp.mean(centre * centre, axis=-1, keepdims=True)
    scale = lax.rsqrt(spread + EPS)
    return (centre * scale, scale)


def norm_back(grad, normed, scale, gain):
    weighted = grad * gain
    return scale * (
        weighted
        - jnp.mean(weighted, axis=-1, keepdims=True)
        - normed * jnp.mean(weighted * normed, axis=-1, keepdims=True)
    )


def block_scores(rows, keys, start, limit, count):
    scores = jnp.einsum("qhd,kd->hqk", rows, keys, preferred_element_type=jnp.float32)
    row_pos = start + jnp.arange(QBLK)
    key_pos = jnp.arange(count)
    allowed = (key_pos[None, :] <= row_pos[:, None]) & (key_pos[None, :] < limit)
    return (scores, allowed[None])


def attend(queries, keys, values, limit):
    count = queries.shape[0]

    def block(start):
        rows = lax.dynamic_slice_in_dim(queries, start, QBLK, 0)
        scores, allowed = block_scores(rows, keys, start, limit, count)
        scores = jnp.where(allowed, scores, jnp.float32(-1e30))
        top = jnp.max(scores, axis=-1, keepdims=True)
        expo = jnp.exp(scores - top)
        total = jnp.sum(expo, axis=-1, keepdims=True)
        weights = (expo / total).astype(jnp.bfloat16)
        result = jnp.einsum("hqk,kd->qhd", weights, values, preferred_element_type=jnp.float32)
        return (result, (top + jnp.log(total))[..., 0])

    starts = jnp.arange(count // QBLK) * QBLK
    results, logsum = lax.map(block, starts)
    return (results.reshape(count, -1, HEAD_DIM), logsum)


def attend_back(queries, keys, values, limit, logsum, grad_out):
    count = queries.shape[0]

    def block(carry, item):
        start, block_logsum = item
        rows = lax.dynamic_slice_in_dim(queries, start, QBLK, 0)
        grads = lax.dynamic_slice_in_dim(grad_out, start, QBLK, 0)
        scores, allowed = block_scores(rows, keys, start, limit, count)
        probs = jnp.where(allowed, jnp.exp(scores - block_logsum[:, :, None]), 0.0)
        weights = probs.astype(jnp.bfloat16)
        dprobs = jnp.einsum("qhd,kd->hqk", grads, values, preferred_element_type=jnp.float32)
        delta = jnp.sum(probs * dprobs, axis=-1, keepdims=True)
        dscores = (probs * (dprobs - delta)).astype(jnp.bfloat16)
        drows = jnp.einsum("hqk,kd->qhd", dscores, keys, preferred_element_type=jnp.float32)
        dkeys = carry[0] + jnp.einsum(
            "hqk,qhd->kd", dscores, rows, preferred_element_type=jnp.float32
        )
        dvalues = carry[1] + jnp.einsum(
            "hqk,qhd->kd", weights, grads, preferred_element_type=jnp.float32
        )
        return ((dkeys, dvalues), drows)

    starts = jnp.arange(count // QBLK) * QBLK
    empty = jnp.zeros((count, HEAD_DIM), jnp.float32)
    (dkeys, dvalues), drows = lax.scan(block, (empty, empty), (starts, logsum))
    return (drows.reshape(count, -1, HEAD_DIM), dkeys, dvalues)


def fetch_each(w_query, w_shared, w_out, w_up, w_down):
    return (
        lax.all_gather(w_query, "dp", axis=0, tiled=True),
        lax.all_gather(w_shared, "dp", axis=0, tiled=True),
        lax.all_gather(w_out, "dp", axis=1, tiled=True),
        lax.all_gather(w_up, "dp", axis=0, tiled=True),
        lax.all_gather(w_down, "dp", axis=1, tiled=True),
    )


def reduce_each(step_grads):
    return (
        lax.psum_scatter(step_grads[0], "dp", scatter_dimension=0, tiled=True),
        lax.psum_scatter(step_grads[1], "dp", scatter_dimension=0, tiled=True),
        lax.psum_scatter(step_grads[2], "dp", scatter_dimension=1, tiled=True),
        lax.psum_scatter(step_grads[3], "dp", scatter_dimension=0, tiled=True),
        lax.psum_scatter(step_grads[4], "dp", scatter_dimension=1, tiled=True),
    )


def per_device(
    block_input,
    cotangent,
    lengths,
    ln1_gain,
    ln1_bias,
    ln2_gain,
    ln2_bias,
    w_query,
    b_query,
    w_shared,
    b_shared,
    w_out,
    b_out,
    w_up,
    b_up,
    w_down,
    b_down,
):
    shard_rows = block_input.shape[2]
    groups = lax.axis_size("tensor")
    rank = lax.axis_index("tensor")
    seq_len = shard_rows * groups
    tail_bias = b_out + b_down
    weight_sums = None
    cos_all, sin_all = tables(seq_len)
    own_pos = rank * shard_rows + jnp.arange(shard_rows)
    outputs = []
    input_grads = []
    sum_bq = jnp.zeros(b_query.shape, jnp.float32)
    sum_bkv = jnp.zeros(b_shared.shape, jnp.float32)
    sum_bup = jnp.zeros(b_up.shape, jnp.float32)
    sum_gain1 = jnp.zeros(ln1_gain.shape, jnp.float32)
    sum_shift1 = jnp.zeros(ln1_gain.shape, jnp.float32)
    sum_gain2 = jnp.zeros(ln1_gain.shape, jnp.float32)
    sum_shift2 = jnp.zeros(ln1_gain.shape, jnp.float32)
    sum_out = jnp.zeros(ln1_gain.shape, jnp.float32)
    for micro in range(MB):
        fetched = fetch_each(w_query, w_shared, w_out, w_up, w_down)
        wq_all, wkv_all, wo_all, wup_all, wdown_all = fetched
        limit = lengths[micro, 0]
        inputs = block_input[micro, 0].astype(jnp.float32)
        normed_one, scale_one = normalize(inputs)
        normed_two, scale_two = normalize(inputs)
        low_one = (normed_one * ln1_gain + ln1_bias).astype(jnp.bfloat16)
        low_two = (normed_two * ln2_gain + ln2_bias).astype(jnp.bfloat16)
        whole_one, whole_two = (
            lax.all_gather(low_one, "tensor", axis=0, tiled=True),
            lax.all_gather(low_two, "tensor", axis=0, tiled=True),
        )
        query_lin = jnp.dot(whole_one, wq_all, preferred_element_type=jnp.float32) + b_query
        query_lin = query_lin.reshape(seq_len, -1, HEAD_DIM)
        queries = (rotate(query_lin, cos_all, sin_all) * 0.125).astype(jnp.bfloat16)
        shared = jnp.dot(whole_one, wkv_all, preferred_element_type=jnp.float32) + b_shared
        keys = rotate(shared[:, None, :HEAD_DIM], cos_all, sin_all)[:, 0].astype(jnp.bfloat16)
        values = shared[:, HEAD_DIM:].astype(jnp.bfloat16)
        attended, logsum = attend(queries, keys, values, limit)
        attended_low = attended.reshape(seq_len, -1).astype(jnp.bfloat16)
        hidden = jnp.dot(whole_two, wup_all, preferred_element_type=jnp.float32) + b_up
        active = jax.nn.gelu(hidden, approximate=False).astype(jnp.bfloat16)
        partial_out = jnp.dot(attended_low, wo_all, preferred_element_type=jnp.float32) + jnp.dot(
            active, wdown_all, preferred_element_type=jnp.float32
        )
        branch = lax.psum_scatter(partial_out, "tensor", scatter_dimension=0, tiled=True)
        outputs.append((inputs + branch + tail_bias).astype(jnp.bfloat16))
        valid = (own_pos < limit).astype(jnp.float32)[:, None]
        upstream = cotangent[micro, 0].astype(jnp.float32) * valid
        whole_up = lax.all_gather(upstream.astype(jnp.bfloat16), "tensor", axis=0, tiled=True)
        sum_out = sum_out + jnp.sum(upstream, axis=0)
        grad_down = jnp.einsum("lf,ld->fd", active, whole_up, preferred_element_type=jnp.float32)
        dactive = jnp.einsum("ld,fd->lf", whole_up, wdown_all, preferred_element_type=jnp.float32)
        gelu_pull = jax.vjp(partial(jax.nn.gelu, approximate=False), hidden)[1]
        dhidden = gelu_pull(dactive)[0].astype(jnp.bfloat16)
        sum_bup = sum_bup + jnp.sum(dhidden.astype(jnp.float32), axis=0)
        grad_up = jnp.einsum("ld,lf->df", whole_two, dhidden, preferred_element_type=jnp.float32)
        dnormed_two = jnp.einsum("lf,df->ld", dhidden, wup_all, preferred_element_type=jnp.float32)
        dattended = jnp.einsum("ld,ed->le", whole_up, wo_all, preferred_element_type=jnp.float32)
        dattended = dattended.astype(jnp.bfloat16).reshape(seq_len, -1, HEAD_DIM)
        grad_out = jnp.einsum(
            "le,ld->ed", attended_low, whole_up, preferred_element_type=jnp.float32
        )
        dqueries, dkeys, dvalues = attend_back(queries, keys, values, limit, logsum, dattended)
        dquery_lin = (
            unrotate(dqueries * 0.125, cos_all, sin_all).reshape(seq_len, -1).astype(jnp.bfloat16)
        )
        dkey_lin = unrotate(dkeys[:, None, :], cos_all, sin_all)[:, 0]
        dshared = lax.psum(jnp.concatenate([dkey_lin, dvalues], axis=1), "tensor")
        dshared = dshared.astype(jnp.bfloat16)
        sum_bq = sum_bq + jnp.sum(dquery_lin.astype(jnp.float32), axis=0)
        sum_bkv = sum_bkv + jnp.sum(dshared.astype(jnp.float32), axis=0)
        grad_q = jnp.einsum("ld,le->de", whole_one, dquery_lin, preferred_element_type=jnp.float32)
        grad_kv = jnp.einsum("ld,lc->dc", whole_one, dshared, preferred_element_type=jnp.float32)
        dnormed_one = jnp.einsum(
            "le,de->ld", dquery_lin, wq_all, preferred_element_type=jnp.float32
        )
        dnormed_one, dnormed_two = (
            lax.psum_scatter(dnormed_one, "tensor", scatter_dimension=0, tiled=True),
            lax.psum_scatter(dnormed_two, "tensor", scatter_dimension=0, tiled=True),
        )
        own_shared = lax.dynamic_slice_in_dim(dshared, rank * shard_rows, shard_rows, 0)
        dnormed_one = dnormed_one + jnp.einsum(
            "lc,dc->ld", own_shared, wkv_all, preferred_element_type=jnp.float32
        )
        sum_gain1 = sum_gain1 + jnp.sum(dnormed_one * normed_one, axis=0)
        sum_shift1 = sum_shift1 + jnp.sum(dnormed_one, axis=0)
        sum_gain2 = sum_gain2 + jnp.sum(dnormed_two * normed_two, axis=0)
        sum_shift2 = sum_shift2 + jnp.sum(dnormed_two, axis=0)
        dinputs = (
            upstream
            + norm_back(dnormed_one, normed_one, scale_one, ln1_gain)
            + norm_back(dnormed_two, normed_two, scale_two, ln2_gain)
        )
        input_grads.append(dinputs.astype(jnp.bfloat16))
        step_grads = (grad_q, grad_kv, grad_out, grad_up, grad_down)
        step_grads = reduce_each(step_grads)
        if weight_sums is None:
            weight_sums = step_grads
        else:
            weight_sums = jax.tree.map(jnp.add, weight_sums, step_grads)
    output = jnp.stack(outputs, axis=0)[:, None]
    grad_input = jnp.stack(input_grads, axis=0)[:, None]
    sum_bq, sum_bkv, sum_bup = lax.psum((sum_bq, sum_bkv, sum_bup), "dp")
    sum_gain1, sum_shift1, sum_gain2, sum_shift2, sum_out = lax.psum(
        (sum_gain1, sum_shift1, sum_gain2, sum_shift2, sum_out), ("dp", "tensor")
    )
    grad_q, grad_kv, grad_o, grad_up, grad_down = weight_sums
    return (
        output,
        grad_input,
        sum_gain1,
        sum_shift1,
        sum_gain2,
        sum_shift2,
        grad_q,
        sum_bq,
        grad_kv,
        sum_bkv,
        grad_o,
        sum_out,
        grad_up,
        sum_bup,
        grad_down,
        sum_out,
    )


MESH = pl.DeviceIdType.MESH
BF = jnp.bfloat16
F32 = jnp.float32
LOG2E = 1.4426950408889634
LN2 = 0.6931471805599453
NEG = -1e30
ZC, XC, CC = 4, 2, 2
DMA = pltpu.SemaphoreType.DMA
VMEM = pltpu.VMEM
MIB = 1 << 20


def nn(a, b):
    return lax.dot_general(a, b, (((1,), (0,)), ((), ())), preferred_element_type=F32)


def nt(a, b):
    return lax.dot_general(a, b, (((1,), (1,)), ((), ())), preferred_element_type=F32)


def eye(n):
    return (
        lax.broadcasted_iota(jnp.int32, (n, n), 0) == lax.broadcasted_iota(jnp.int32, (n, n), 1)
    ).astype(BF)


def flat(block):
    return block.reshape(-1, block.shape[-1])


class Place:
    def __init__(self):
        self.dp = lax.axis_index("dp")
        self.t = lax.axis_index("tensor")
        self.core = lax.rem(self.dp, CC)
        self.x = lax.rem(lax.div(self.dp, CC), XC)
        self.z = lax.div(self.dp, CC * XC)

    def at(self, z, x, core):
        return (z * XC + x) * CC + core

    def z_peer(self, d):
        return {"dp": self.at(lax.rem(self.z + d, ZC), self.x, self.core)}

    def x_peer(self):
        return {"dp": self.at(self.z, 1 - self.x, self.core)}

    def core_peer(self):
        return {"dp": self.at(self.z, self.x, 1 - self.core)}

    def y_peer(self):
        return {"tensor": 1 - self.t}

    def greet(self):
        bar = pltpu.get_barrier_semaphore()
        peers = [self.z_peer(d) for d in (1, 2, 3)]
        peers += [self.x_peer(), self.core_peer(), self.y_peer()]
        for p in peers:
            pl.semaphore_signal(bar, inc=1, device_id=p, device_id_type=MESH)
        return bar, len(peers)


def remote(src, dst, ss, rs, peer):
    return pltpu.make_async_remote_copy(
        src_ref=src, dst_ref=dst, send_sem=ss, recv_sem=rs, device_id=peer, device_id_type=MESH
    )


def split_cols(width):
    a = (width // 128 + 1) // 2 * 128
    return ((0, a), (a, width - a))


class Gather:
    N_SEMS = 12

    def __init__(self, place, pieces, sems):
        self.p = place
        self.pieces = pieces
        self.sems = sems

    def z(self, c, h, d):
        p = self.p
        src, out, width = self.pieces[c]
        o, w = split_cols(width)[h]
        cols = pl.ds(o, w)
        return remote(
            src.at[:, cols],
            out.at[p.t, p.z, p.x, p.core, :, cols],
            self.sems.at[c, h, d - 1],
            self.sems.at[c, h, 3 + d - 1],
            p.z_peer(d),
        )

    def second(self, c, h):
        p = self.p
        _, out, width = self.pieces[c]
        o, w = split_cols(width)[h]
        view = out.at[p.t, :, p.x, p.core, :, pl.ds(o, w)]
        peer = p.x_peer() if h == 0 else p.y_peer()
        return remote(view, view, self.sems.at[c, h, 6], self.sems.at[c, h, 7], peer)

    def third(self, c, h):
        p = self.p
        _, out, width = self.pieces[c]
        o, w = split_cols(width)[h]
        cols = pl.ds(o, w)
        if h == 0:
            view, peer = out.at[p.t, :, :, p.core, :, cols], p.y_peer()
        else:
            view, peer = out.at[:, :, p.x, p.core, :, cols], p.x_peer()
        return remote(view, view, self.sems.at[c, h, 8], self.sems.at[c, h, 9], peer)

    def cores(self, c, h):
        p = self.p
        _, out, width = self.pieces[c]
        o, w = split_cols(width)[h]
        view = out.at[:, :, :, p.core, :, pl.ds(o, w)]
        return remote(view, view, self.sems.at[c, h, 10], self.sems.at[c, h, 11], p.core_peer())

    def begin(self, c):
        for h in (0, 1):
            for d in (1, 2, 3):
                self.z(c, h, d).start()

    def step(self, i):
        n = len(self.pieces)
        for h in (0, 1):
            if 0 <= i < n:
                for d in (1, 2, 3):
                    self.z(i, h, d).wait()
                self.second(i, h).start()
            if 0 <= i - 1 < n:
                self.second(i - 1, h).wait()
                self.third(i - 1, h).start()
            if 0 <= i - 2 < n:
                self.third(i - 2, h).wait()
                self.cores(i - 2, h).start()
            if 0 <= i - 3 < n:
                self.cores(i - 3, h).wait()

    def n_steps(self):
        return len(self.pieces) + 3


def normal_rows(rows):
    mean = jnp.mean(rows, axis=-1, keepdims=True)
    centre = rows - mean
    var = jnp.mean(centre * centre, axis=-1, keepdims=True)
    scale = lax.rsqrt(var + EPS)
    return centre * scale, scale


def rotate_t(v, cosine, sine):
    a, b = v[0:8], v[8:16]
    return jnp.concatenate([a * cosine - b * sine, b * cosine + a * sine, v[16:]], axis=0)


def unrotate_t(v, cosine, sine):
    a, b = v[0:8], v[8:16]
    return jnp.concatenate([a * cosine + b * sine, b * cosine - a * sine, v[16:]], axis=0)


def fill_bias(place, lens_ref, bias_ref, S):
    t = place.t
    for m in range(MB):
        limit = lens_ref[m]
        key = lax.broadcasted_iota(jnp.int32, (S, S), 0)
        row = lax.broadcasted_iota(jnp.int32, (S, S), 1)
        limit_other = jnp.where(t == 1, limit, 0)
        bias_ref[m, 0:S] = jnp.where(key < limit_other, 0.0, NEG).astype(F32)
        own = (key <= row) & (key + t * S < limit)
        bias_ref[m, S : 2 * S] = jnp.where(own, 0.0, NEG).astype(F32)


def front_kernel(
    dims,
    x_ref,
    lens_ref,
    tab_ref,
    ln_ref,
    bpack_ref,
    bsh_ref,
    wq_ref,
    wsh_ref,
    wout_ref,
    wup_ref,
    wdown_ref,
    wa,
    wb,
    wf,
    ball,
    h1_ref,
    h2_ref,
    qt_ref,
    att_ref,
    lse_ref,
    kc_ref,
    vc_ref,
    kt_ref,
    sa,
    sb,
    sf,
    kvt,
    kvo,
    vte,
    bias,
    bcol,
    gsem,
    lsem,
    ysem,
):
    S, HT, NH, NF, T = dims["S"], dims["HT"], dims["NH"], dims["NF"], dims["T"]
    D = x_ref.shape[1]
    R = sa.shape[0]
    p = Place()
    bar, npeers = p.greet()

    sa[:, 0:HT] = wq_ref[...]
    sa[:, HT:] = wsh_ref[...]
    ident = eye(R)
    sb[...] = nt(ident, wout_ref[...]).astype(BF)
    for f in range(NF):
        sf[f, :, 0:256] = wup_ref[:, 256 * f : 256 * f + 256]
        sf[f, :, 256:512] = nt(ident, wdown_ref[256 * f : 256 * f + 256, :]).astype(BF)
    ball[p.t] = bpack_ref[...]

    pieces = [(sa, wa, sa.shape[1]), (sb, wb, sb.shape[1])]
    pieces += [(sf.at[f], wf.at[f], sf.shape[2]) for f in range(NF)]
    g = Gather(p, pieces, gsem)

    locals_ = [
        pltpu.make_async_copy(pieces[c][0], pieces[c][1].at[p.t, p.z, p.x, p.core], lsem.at[c])
        for c in range(len(pieces))
    ]
    for cp in locals_:
        cp.start()
    pl.semaphore_wait(bar, npeers)
    bias_copy = remote(ball.at[p.t], ball.at[p.t], ysem.at[0], ysem.at[1], p.y_peer())
    bias_copy.start()
    for c in range(len(pieces)):
        g.begin(c)

    @pl.loop(0, T // 128)
    def _(i):
        rows = pl.ds(pl.multiple_of(i * 128, 128), 128)
        z, _ = normal_rows(x_ref[rows, :].astype(F32))
        h1_ref[rows, :] = (z * ln_ref[0:1, :] + ln_ref[1:2, :]).astype(BF)
        h2_ref[rows, :] = (z * ln_ref[2:3, :] + ln_ref[3:4, :]).astype(BF)

    for cp in locals_:
        cp.wait()
    g.step(0)
    fill_bias(p, lens_ref, bias, S)
    bias_copy.wait()
    nq = HT // 128
    for t in range(2):
        for j in range(nq):
            row = jnp.broadcast_to(ball[t, j : j + 1, :], (128, 128))
            bcol[(t * nq + j) * 128 : (t * nq + j + 1) * 128, :] = row.T
    bcol[2 * HT : 2 * HT + 128, :] = jnp.broadcast_to(bsh_ref[...], (128, 128)).T
    for i in (1, 2, 3):
        g.step(i)

    cosine, sine = tab_ref[p.t, 0:8, :], tab_ref[p.t, 8:16, :]
    wsh_t = nt(eye(128), flat(wa[0, :, :, :, :, HT:])).astype(BF)
    for m in range(MB):
        cols = slice(m * S, m * S + S)
        kv = nt(wsh_t, h1_ref[cols, :]) + bcol[2 * HT : 2 * HT + 128, 0:1]
        kvt[0:HEAD_DIM, cols] = rotate_t(kv[0:HEAD_DIM], cosine, sine).astype(BF)
        kvt[HEAD_DIM:, cols] = kv[HEAD_DIM:].astype(BF)
    kv_copy = remote(kvt, kvo, ysem.at[2], ysem.at[3], p.y_peer())
    kv_copy.start()

    for t in range(2):
        wq_t = nt(eye(HT), flat(wa[t, :, :, :, :, 0:HT])).astype(BF)
        for m in range(MB):
            cols = slice(m * S, m * S + S)
            q = nt(wq_t, h1_ref[cols, :])
            for h in range(HT // HEAD_DIM):
                base = t * HT + h * HEAD_DIM
                qh = q[h * HEAD_DIM : (h + 1) * HEAD_DIM] + bcol[base : base + HEAD_DIM, 0:1]
                qh = rotate_t(qh, cosine, sine) * (0.125 * LOG2E)
                qt_ref[base : base + HEAD_DIM, cols] = qh.astype(BF)

    id256 = eye(256)
    kv_copy.wait()
    for m in range(MB):
        for half, src in ((0, kvo), (1, kvt)):
            cols = slice(m * S, m * S + S)
            keys = slice(half * S, half * S + S)
            kt_ref[m, :, keys] = src[0:HEAD_DIM, cols]
            vte[m, 0:HEAD_DIM, keys] = src[HEAD_DIM:, cols]
        ones = (lax.broadcasted_iota(jnp.int32, (16, 2 * S), 0) == 0).astype(BF)
        vte[m, HEAD_DIM:, :] = ones
        for b in range(2 * S // 256):
            blk = slice(b * 256, b * 256 + 256)
            kc_ref[m, blk, :] = nt(id256, kt_ref[m, :, blk]).astype(BF)
            vc_ref[m, blk, :] = nt(id256, vte[m, 0:HEAD_DIM, blk]).astype(BF)

    first = 4

    @pl.loop(0, MB * NH)
    def _(i):
        m = lax.div(i, NH)
        h = lax.rem(i, NH)
        head = pl.ds(pl.multiple_of(h * HEAD_DIM, HEAD_DIM), HEAD_DIM)
        for r in range(S // 256):
            nk = S + 256 * (r + 1)
            cols = pl.ds(pl.multiple_of(m * S + r * 256, 256), 256)
            q = qt_ref[head, cols]
            s = nn(kc_ref[m, 0:nk, :], q) + bias[m, 0:nk, r * 256 : r * 256 + 256]
            top = jnp.max(s, axis=0, keepdims=True)
            e = jnp.exp2(s - top).astype(BF)
            o = nn(vte[m, :, 0:nk], e)
            total = o[HEAD_DIM : HEAD_DIM + 1]
            att_ref[head, cols] = (o[0:HEAD_DIM] * (1.0 / total)).astype(BF)
            lse_ref[i, :, r * 256 : r * 256 + 256] = top + jnp.log2(total)
        for k in range(first, g.n_steps()):
            pl.when(i == 3 * (k - first) + 1)(partial(g.step, k))

    for k in range(g.n_steps()):
        if k >= first and 3 * (k - first) + 1 >= MB * NH:
            g.step(k)


def masked_rows(place_t, lens_ref, dy_ref, rows, start, S):
    m, off = divmod(start, S)
    n = rows.stop - rows.start
    pos = place_t * S + off + lax.broadcasted_iota(jnp.int32, (n, 1), 0)
    return jnp.where(pos < lens_ref[m], dy_ref[rows, :].astype(F32), 0.0)


def gelu_parts(u):
    dens = jnp.exp(-0.5 * u * u)
    v = jnp.abs(u) * 0.7071067811865476
    k = 1.0 / (1.0 + 0.3275911 * v)
    poly = k * (
        0.254829592
        + k * (-0.284496736 + k * (1.421413741 + k * (-1.453152027 + k * 1.061405429)))
    )
    tail = 0.5 * poly * dens
    return jnp.where(u < 0, tail, 1.0 - tail), dens * 0.3989422804014327


def ffn_kernel(
    dims,
    x_ref,
    dy_ref,
    lens_ref,
    h2_ref,
    att_ref,
    wb_ref,
    wf_ref,
    ball_ref,
    bo_ref,
    out_ref,
    gb_ref,
    gf_ref,
    dh2_ref,
    bup_ref,
    acc,
    dh2,
    dym,
    h2t,
    dyt,
):
    S, HT, NF, T = dims["S"], dims["HT"], dims["NF"], dims["T"]
    D = x_ref.shape[1]
    f = pl.program_id(0)
    t_ = lax.axis_index("tensor")

    @pl.when(f == 0)
    def _():
        id256 = eye(256)
        for b in range(T // 256):
            rows = slice(b * 256, b * 256 + 256)
            dym[rows, :] = masked_rows(t_, lens_ref, dy_ref, rows, b * 256, S).astype(BF)
            a = nt(id256, att_ref[:, rows]).astype(BF)
            acc[rows, :] = (
                x_ref[rows, :].astype(F32)
                + bo_ref[...]
                + nt(a[:, 0:HT], wb_ref[0])
                + nt(a[:, HT:], wb_ref[1])
            )
            for c in range(D // 256):
                cols = slice(c * 256, c * 256 + 256)
                dyt[cols, rows] = nt(id256, dym[rows, cols]).astype(BF)
                h2t[cols, rows] = nt(id256, h2_ref[rows, cols]).astype(BF)
        for t in range(2):
            gb_ref[t] = nt(dyt[...], att_ref[t * HT : (t + 1) * HT, :]).astype(BF)
        dh2[...] = jnp.zeros_like(dh2)

    first = ball_ref.shape[1] - 1 - 2 * NF
    for t in range(2):
        wu = wf_ref[0, t, :, 0:256]
        wd = wf_ref[0, t, :, 256:512]
        bias = jnp.concatenate(
            [ball_ref[t, pl.ds(first + 2 * f, 1), :], ball_ref[t, pl.ds(first + 2 * f + 1, 1), :]],
            axis=1,
        )
        u = nn(h2_ref[...], wu) + bias
        cdf, dens = gelu_parts(u)
        act = (u * cdf).astype(BF)
        slope = cdf + u * dens
        acc[...] += nt(act, wd)
        gf_ref[0, t, :, 256:512] = nn(dyt[...], act).astype(BF)
        du = (nn(dym[...], wd) * slope).astype(BF)
        sums = jnp.sum(du.astype(F32), axis=0, keepdims=True)
        bup_ref[0, 2 * t : 2 * t + 1, :] = sums[:, 0:128]
        bup_ref[0, 2 * t + 1 : 2 * t + 2, :] = sums[:, 128:256]
        gf_ref[0, t, :, 0:256] = nn(h2t[...], du).astype(BF)
        dh2[...] += nt(du, wu)

    @pl.when(f == NF - 1)
    def _():
        out_ref[...] = acc[...].astype(BF)
        dh2_ref[...] = dh2[...]


class Reduce:
    def __init__(self, place, pieces, own, rc, r2a, r2b, r3, r4, sems):
        self.p = place
        self.pieces = pieces
        self.own, self.rc, self.r2a, self.r2b, self.r3, self.r4 = own, rc, r2a, r2b, r3, r4
        self.sems = sems

    def cores(self, c):
        g, _, w, _ = self.pieces[c]
        return remote(
            g.at[:, :, :, 1 - self.p.core],
            self.rc.at[c, :, :, :, :, pl.ds(0, w)],
            self.sems.at[c, 0],
            self.sems.at[c, 1],
            self.p.core_peer(),
        )

    def local(self, c):
        g, _, w, _ = self.pieces[c]
        return pltpu.make_async_copy(
            g.at[:, :, :, self.p.core], self.own.at[c, :, :, :, :, pl.ds(0, w)], self.sems.at[c, 2]
        )

    def second(self, c, h):
        p = self.p
        o, w = split_cols(self.pieces[c][2])[h]
        if h == 0:
            src, dst, peer = self.rc.at[c, 1 - p.t, :, :, :, pl.ds(o, w)], self.r2a, p.y_peer()
        else:
            src, dst, peer = self.rc.at[c, :, :, 1 - p.x, :, pl.ds(o, w)], self.r2b, p.x_peer()
        dst = dst.at[c, :, :, :, pl.ds(0, w)]
        return remote(src, dst, self.sems.at[c, 3 + 2 * h], self.sems.at[c, 4 + 2 * h], peer)

    def third(self, c, h):
        p = self.p
        o, w = split_cols(self.pieces[c][2])[h]
        if h == 0:
            src, peer = self.r2a.at[c, :, 1 - p.x, :, pl.ds(0, w)], p.x_peer()
        else:
            src, peer = self.r2b.at[c, 1 - p.t, :, :, pl.ds(0, w)], p.y_peer()
        dst = self.r3.at[c, h, :, :, pl.ds(0, w)]
        return remote(src, dst, self.sems.at[c, 7 + 2 * h], self.sems.at[c, 8 + 2 * h], peer)

    def last(self, c, h, d):
        p = self.p
        o, w = split_cols(self.pieces[c][2])[h]
        src = self.r3.at[c, h, lax.rem(p.z + d, ZC), :, pl.ds(0, w)]
        dst = self.r4.at[c, h, d - 1, :, pl.ds(0, w)]
        k = 11 + (h * 3 + d - 1) * 2
        return remote(src, dst, self.sems.at[c, k], self.sems.at[c, k + 1], p.z_peer(d))

    N_SEMS = 23

    def begin(self, c):
        self.cores(c).start()
        if self.pieces[c][1]:
            self.local(c).start()

    def step1(self, c):
        p = self.p
        g, copied, width, _ = self.pieces[c]
        self.cores(c).wait()
        if copied:
            self.local(c).wait()
            own = self.own[c, :, :, :, :, 0:width]
        else:
            own = g[:, :, :, p.core]
        mine = self.rc[c, :, :, :, :, 0:width].astype(F32) + own.astype(F32)
        self.rc[c, :, :, :, :, 0:width] = mine.astype(BF)
        for h in (0, 1):
            self.second(c, h).start()

    def step2(self, c):
        p = self.p
        for h in (0, 1):
            self.second(c, h).wait()
            o, w = split_cols(self.pieces[c][2])[h]
            if h == 0:
                ref, mine = self.r2a, self.rc[c, p.t, :, :, :, o : o + w]
            else:
                ref, mine = self.r2b, self.rc[c, :, :, p.x, :, o : o + w]
            mine = mine.astype(F32) + ref[c, :, :, :, 0:w].astype(F32)
            ref[c, :, :, :, 0:w] = mine.astype(BF)
            self.third(c, h).start()

    def step3(self, c):
        p = self.p
        for h in (0, 1):
            self.third(c, h).wait()
            o, w = split_cols(self.pieces[c][2])[h]
            mine = self.r2a[c, :, p.x, :, 0:w] if h == 0 else self.r2b[c, p.t, :, :, 0:w]
            mine = mine.astype(F32) + self.r3[c, h, :, :, 0:w].astype(F32)
            self.r3[c, h, :, :, 0:w] = mine.astype(BF)
            for d in (1, 2, 3):
                self.last(c, h, d).start()

    def step4(self, c):
        p = self.p
        parts = []
        for h in (0, 1):
            o, w = split_cols(self.pieces[c][2])[h]
            for d in (1, 2, 3):
                self.last(c, h, d).wait()
            total = self.r3[c, h, p.z, :, 0:w].astype(F32)
            for d in range(3):
                total = total + self.r4[c, h, d, :, 0:w].astype(F32)
            parts.append(total)
        self.pieces[c][3](parts)

    def step(self, i, lo, hi):
        for k, act in enumerate((self.step4, self.step3, self.step2, self.step1)):
            c = lo + i - (3 - k)
            if lo <= c < hi:
                act(c)


def back_kernel(
    dims,
    x_ref,
    dy_ref,
    lens_ref,
    tab_ref,
    ln_ref,
    h1_ref,
    qt_ref,
    att_ref,
    lse_ref,
    kc_ref,
    vc_ref,
    kt_ref,
    wa_ref,
    wb_ref,
    dh2_ref,
    bup_ref,
    gb_in,
    gf_in,
    gx_ref,
    gq_ref,
    gkv_ref,
    go_ref,
    gup_ref,
    gdn_ref,
    sm,
    bias,
    da_ref,
    dq_ref,
    dkv,
    dkvr,
    dkvt,
    h1t,
    ga,
    sums,
    smr,
    own,
    rc,
    r2a,
    r2b,
    r3,
    r4,
    rsem,
    ysem,
):
    S, HT, NH, NF, T = dims["S"], dims["HT"], dims["NH"], dims["NF"], dims["T"]
    D = x_ref.shape[1]
    p = Place()
    bar, npeers = p.greet()

    def put_ffn(f):
        def put(parts):
            gup_ref[:, f * 256 : f * 256 + 256] = parts[0]
            gdn_ref[:, f * 256 : f * 256 + 256] = parts[1]

        return put

    def put_out(parts):
        a = parts[0].shape[1]
        go_ref[:, 0:a] = parts[0]
        go_ref[:, a:] = parts[1]

    def put_a(parts):
        a = parts[0].shape[1]
        gq_ref[:, 0:a] = parts[0]
        gq_ref[:, a:HT] = parts[1][:, 0 : HT - a]
        gkv_ref[...] = parts[1][:, HT - a :]

    pieces = [(gf_in.at[f], True, 512, put_ffn(f)) for f in range(NF)]
    pieces += [(gb_in, True, HT, put_out), (ga, False, HT + 128, put_a)]
    red = Reduce(p, pieces, own, rc, r2a, r2b, r3, r4, rsem)

    id256 = eye(256)
    fill_bias(p, lens_ref, bias, S)
    pl.semaphore_wait(bar, npeers)
    for c in range(NF + 1):
        red.begin(c)

    for t in range(2):
        wo = nt(eye(HT), wb_ref[t]).astype(BF)
        for b in range(T // 256):
            rows = slice(b * 256, b * 256 + 256)
            dyb = masked_rows(p.t, lens_ref, dy_ref, rows, b * 256, S).astype(BF)
            da_ref[t * HT : (t + 1) * HT, rows] = nt(wo, dyb).astype(BF)
    for b in range(T // 256):
        rows = slice(b * 256, b * 256 + 256)
        for c in range(D // 256):
            cols = slice(c * 256, c * 256 + 256)
            h1t[cols, rows] = nt(id256, h1_ref[rows, cols]).astype(BF)
    dkv[...] = jnp.zeros_like(dkv)

    n_first = NF + 1

    @pl.loop(0, MB * NH)
    def _(i):
        m = lax.div(i, NH)
        h = lax.rem(i, NH)
        head = pl.ds(pl.multiple_of(h * HEAD_DIM, HEAD_DIM), HEAD_DIM)
        for r in range(S // 256):
            nk = S + 256 * (r + 1)
            cols = pl.ds(pl.multiple_of(m * S + r * 256, 256), 256)
            cosine = tab_ref[p.t, 0:8, r * 256 : r * 256 + 256]
            sine = tab_ref[p.t, 8:16, r * 256 : r * 256 + 256]
            q = qt_ref[head, cols]
            da = da_ref[head, cols]
            delta = jnp.sum(
                da.astype(F32) * att_ref[head, cols].astype(F32), axis=0, keepdims=True
            )
            lse = lse_ref[i, :, r * 256 : r * 256 + 256]
            zero = jnp.zeros_like(q)
            both = jnp.concatenate(
                [jnp.concatenate([q, zero], axis=1), jnp.concatenate([zero, da], axis=1)], axis=0
            )
            dq = jnp.zeros((HEAD_DIM, 256), F32)
            for b in range(nk // 256):
                keys = slice(b * 256, b * 256 + 256)
                s = nn(kc_ref[m, keys, :], q) + bias[m, keys, r * 256 : r * 256 + 256]
                pr = jnp.exp2(s - lse)
                dp = nn(vc_ref[m, keys, :], da)
                ds = (pr * (dp - delta)).astype(BF)
                dq = dq + nn(kt_ref[m, :, keys], ds)
                dkv[m, keys, :] += nt(jnp.concatenate([ds, pr.astype(BF)], axis=1), both)
            dq_ref[head, cols] = (unrotate_t(dq, cosine, sine) * 0.125).astype(BF)
        for k in range(n_first + 3):
            pl.when(i == 2 * k + 1)(partial(red.step, k, 0, n_first))

    kv_copy = remote(dkv.at[:, 0:S, :], dkvr, ysem.at[0], ysem.at[1], p.y_peer())
    kv_copy.start()
    for t in range(2):
        gq = nt(h1t[...], dq_ref[t * HT : (t + 1) * HT, :]).astype(BF)
        ga[t, :, :, :, :, 0:HT] = gq.reshape(ZC, XC, CC, -1, HT)
    kv_copy.wait()
    cosine, sine = tab_ref[p.t, 0:8, :], tab_ref[p.t, 8:16, :]
    for m in range(MB):
        mine = (dkv[m, S : 2 * S, :] + dkvr[m]).T
        cols = slice(m * S, m * S + S)
        dkvt[0:HEAD_DIM, cols] = (unrotate_t(mine[0:HEAD_DIM], cosine, sine) * LN2).astype(BF)
        dkvt[HEAD_DIM:, cols] = mine[HEAD_DIM:].astype(BF)
    gkv = nt(h1t[...], dkvt[...]).astype(BF).reshape(ZC, XC, CC, -1, 128)
    for t in range(2):
        ga[t, :, :, :, :, HT:] = gkv
    red.begin(n_first)

    sums[...] = jnp.zeros_like(sums)
    wq = [flat(wa_ref[t, :, :, :, :, 0:HT]) for t in range(2)]
    wsh = flat(wa_ref[0, :, :, :, :, HT:])
    for b in range(T // 256):
        rows = slice(b * 256, b * 256 + 256)
        dq = nt(id256, dq_ref[:, rows])
        dkvn = nt(id256, dkvt[:, rows])
        dql = dq.astype(BF)
        dh1 = nt(dql[:, 0:HT], wq[0]) + nt(dql[:, HT:], wq[1]) + nt(dkvn.astype(BF), wsh)
        dh2 = dh2_ref[rows, :]
        z, scale = normal_rows(x_ref[rows, :].astype(F32))
        dy = masked_rows(p.t, lens_ref, dy_ref, rows, b * 256, S)
        e = dh1 * ln_ref[0:1, :] + dh2 * ln_ref[2:3, :]
        back = scale * (
            e - jnp.mean(e, axis=-1, keepdims=True) - z * jnp.mean(e * z, axis=-1, keepdims=True)
        )
        gx_ref[rows, :] = (dy + back).astype(BF)
        for k, v in enumerate((dh1 * z, dh1, dh2 * z, dh2, dy, dq)):
            sums[k : k + 1, :] += jnp.sum(v, axis=0, keepdims=True)
        sums[6:7, 0:128] += jnp.sum(dkvn, axis=0, keepdims=True)
        if b < 2:
            red.step(b, n_first, n_first + 1)
    n = D // 128
    for k in range(6):
        for j in range(n):
            sm[k * n + j : k * n + j + 1, :] = sums[k : k + 1, j * 128 : j * 128 + 128]
    sm[6 * n : 6 * n + 4, :] = jnp.zeros((4, 128), F32)
    sm[6 * n : 6 * n + 1, :] = sums[6:7, 0:128]
    for f in range(NF):
        sm[6 * n + 4 + 4 * f : 6 * n + 8 + 4 * f, :] = bup_ref[f]

    for k, peer in enumerate((p.core_peer(), p.y_peer(), p.x_peer())):
        cp = remote(sm, smr.at[k], ysem.at[2 + 2 * k], ysem.at[3 + 2 * k], peer)
        cp.start()
        if k < 2:
            red.step(k + 2, n_first, n_first + 1)
        cp.wait()
        sm[...] += smr[k]
    cps = [remote(sm, smr.at[2 + d], ysem.at[6 + 2 * d], ysem.at[7 + 2 * d], p.z_peer(d)) for d in (1, 2, 3)]
    for cp in cps:
        cp.start()
    for cp in cps:
        cp.wait()
    sm[...] += smr[3] + smr[4] + smr[5]


def angle_table(S):
    places = np.arange(2 * S, dtype=np.float64)
    freqs = 10000.0 ** (-np.arange(ROT // 2) * 2.0 / ROT)
    angles = (places[:, None] * freqs[None, :]).astype(np.float32).astype(np.float64)
    tab = np.concatenate([np.cos(angles).T, np.sin(angles).T], axis=0).astype(np.float32)
    return tab.reshape(ROT, 2, S).transpose(1, 0, 2)


def params(limit, collective_id=None):
    if collective_id is None:
        return pltpu.CompilerParams(vmem_limit_bytes=limit * MIB)
    return pltpu.CompilerParams(
        vmem_limit_bytes=limit * MIB, collective_id=collective_id, has_side_effects=True
    )


def token_plan(
    block_input,
    cotangent,
    lengths,
    ln1_gain,
    ln1_bias,
    ln2_gain,
    ln2_bias,
    w_query,
    b_query,
    w_shared,
    b_shared,
    w_out,
    b_out,
    w_up,
    b_up,
    w_down,
    b_down,
):
    S, D = block_input.shape[2:]
    R, HT = w_query.shape
    FT = w_up.shape[1]
    NF, T, NH = FT // 256, MB * S, 2 * HT // HEAD_DIM
    dims = dict(S=S, HT=HT, NF=NF, T=T, NH=NH)
    full = (2, ZC, XC, CC, R)
    t = lax.axis_index("tensor")

    def s(shape, dtype):
        return jax.ShapeDtypeStruct(shape, dtype)

    vm = pl.BlockSpec(memory_space=VMEM)
    hbm = pl.BlockSpec(memory_space=pl.ANY)
    smem = pl.BlockSpec(memory_space=pltpu.SMEM)

    x = block_input.reshape(T, D)
    dy = cotangent.reshape(T, D)
    lens = lengths.reshape(MB)
    tab = jnp.asarray(angle_table(S))
    ln = jnp.stack([ln1_gain, ln1_bias, ln2_gain, ln2_bias])
    bpack = jnp.concatenate([b_query, b_up, jnp.zeros((128,), F32)]).reshape(-1, 128)
    nb = bpack.shape[0]
    np_ = NF + 2

    outs = pl.pallas_call(
        partial(front_kernel, dims),
        out_shape=[
            s(full + (HT + 128,), BF),
            s(full + (HT,), BF),
            s((NF,) + full + (512,), BF),
            s((2, nb, 128), F32),
            s((T, D), BF),
            s((T, D), BF),
            s((D, T), BF),
            s((D, T), BF),
            s((MB * NH, 1, S), F32),
            s((MB, 2 * S, HEAD_DIM), BF),
            s((MB, 2 * S, HEAD_DIM), BF),
            s((MB, HEAD_DIM, 2 * S), BF),
        ],
        in_specs=[vm, smem] + [vm] * 9,
        out_specs=[vm, hbm, hbm] + [vm] * 9,
        scratch_shapes=[
            VMEM((R, HT + 128), BF),
            VMEM((R, HT), BF),
            VMEM((NF, R, 512), BF),
            VMEM((128, T), BF),
            VMEM((128, T), BF),
            VMEM((MB, HEAD_DIM + 16, 2 * S), BF),
            VMEM((MB, 2 * S, S), F32),
            VMEM((2 * HT + 128, 128), F32),
            DMA((np_, 2, Gather.N_SEMS)),
            DMA((np_,)),
            DMA((4,)),
        ],
        compiler_params=params(56, 0),
        name="front",
    )(x, lens, tab, ln, bpack, b_shared.reshape(1, 128), w_query, w_shared, w_out, w_up, w_down)
    wa, wb, wf, ball, h1, h2, qt, att, lse, kc, vc, kt = outs

    def whole(shape):
        return pl.BlockSpec(shape, lambda f: (0,) * len(shape))

    out, gb, gf, dh2, bup = pl.pallas_call(
        partial(ffn_kernel, dims),
        grid=(NF,),
        out_shape=[
            s((T, D), BF),
            s((2, D, HT), BF),
            s((NF, 2, D, 512), BF),
            s((T, D), F32),
            s((NF, 4, 128), F32),
        ],
        in_specs=[
            whole((T, D)),
            whole((T, D)),
            smem,
            whole((T, D)),
            whole((D, T)),
            whole((2, D, HT)),
            pl.BlockSpec((1, 2, D, 512), lambda f: (f, 0, 0, 0)),
            whole((2, nb, 128)),
            whole((1, D)),
        ],
        out_specs=[
            whole((T, D)),
            whole((2, D, HT)),
            pl.BlockSpec((1, 2, D, 512), lambda f: (f, 0, 0, 0)),
            whole((T, D)),
            pl.BlockSpec((1, 4, 128), lambda f: (f, 0, 0)),
        ],
        scratch_shapes=[
            VMEM((T, D), F32),
            VMEM((T, D), F32),
            VMEM((T, D), BF),
            VMEM((D, T), BF),
            VMEM((D, T), BF),
        ],
        compiler_params=params(60),
        name="ffn",
    )(
        x,
        dy,
        lens,
        h2,
        att,
        wb.reshape(2, D, HT),
        wf.reshape(NF, 2, D, 512),
        ball,
        (b_out + b_down).reshape(1, D),
    )

    outs = pl.pallas_call(
        partial(back_kernel, dims),
        out_shape=[
            s((T, D), BF),
            s((R, HT), F32),
            s((R, 128), F32),
            s((R, HT), F32),
            s((R, FT), F32),
            s((R, FT), F32),
            s((6 * (D // 128) + 4 + 4 * NF, 128), F32),
        ],
        in_specs=[vm, vm, smem] + [vm] * 13 + [hbm, hbm],
        out_specs=[vm] * 7,
        scratch_shapes=[
            VMEM((MB, 2 * S, S), F32),
            VMEM((D, T), BF),
            VMEM((D, T), BF),
            VMEM((MB, 2 * S, 128), F32),
            VMEM((MB, S, 128), F32),
            VMEM((128, T), BF),
            VMEM((D, T), BF),
            VMEM(full + (HT + 128,), BF),
            VMEM((8, D), F32),
            VMEM((6, 6 * (D // 128) + 4 + 4 * NF, 128), F32),
            VMEM((NF + 1, 2, ZC, XC, R, 512), BF),
            VMEM((np_, 2, ZC, XC, R, 512), BF),
            VMEM((np_, ZC, XC, R, 256), BF),
            VMEM((np_, 2, ZC, R, 256), BF),
            VMEM((np_, 2, ZC, R, 256), BF),
            VMEM((np_, 2, 3, R, 256), BF),
            DMA((np_, Reduce.N_SEMS)),
            DMA((14,)),
        ],
        compiler_params=params(62, 1),
        name="back",
    )(
        x,
        dy,
        lens,
        tab,
        ln,
        h1,
        qt,
        att,
        lse,
        kc,
        vc,
        kt,
        wa,
        wb.reshape(2, D, HT),
        dh2,
        bup,
        gb.reshape(full + (HT,)),
        gf.reshape((NF,) + full + (512,)),
    )
    gx, gq, gkv, go, gup, gdn, sm = outs
    n = D // 128
    five = sm[0 : 5 * n].reshape(5, D)
    bq = lax.dynamic_index_in_dim(sm[5 * n : 6 * n].reshape(2, HT), t, 0, False)
    bkv = sm[6 * n]
    bup = lax.dynamic_index_in_dim(sm[6 * n + 4 :].reshape(NF, 2, 256), t, 1, False).reshape(FT)
    return (
        out.reshape(block_input.shape),
        gx.reshape(block_input.shape),
        five[0],
        five[1],
        five[2],
        five[3],
        gq,
        bq,
        gkv,
        bkv,
        go.T,
        five[4],
        gup,
        bup,
        gdn.T,
        five[4],
    )


def fits_token_plan(mesh):
    return dict(mesh.shape) == {"dp": ZC * XC * CC, "tensor": 2}


def solution(mesh):
    in_specs = (
        P(None, "dp", "tensor", None),
        P(None, "dp", "tensor", None),
        P(None, "dp"),
        P(),
        P(),
        P(),
        P(),
        P("dp", "tensor"),
        P("tensor"),
        P("dp", None),
        P(),
        P("tensor", "dp"),
        P(),
        P("dp", "tensor"),
        P("tensor"),
        P("tensor", "dp"),
        P(),
    )
    out_specs = (
        P(None, "dp", "tensor", None),
        P(None, "dp", "tensor", None),
        P(),
        P(),
        P(),
        P(),
        P("dp", "tensor"),
        P("tensor"),
        P("dp", None),
        P(),
        P("tensor", "dp"),
        P(),
        P("dp", "tensor"),
        P("tensor"),
        P("tensor", "dp"),
        P(),
    )
    step = token_plan if fits_token_plan(mesh) else per_device
    return jax.shard_map(
        step, mesh=mesh, in_specs=in_specs, out_specs=out_specs, check_vma=False
    )
```

```python
from functools import partial

import jax
import jax.numpy as jnp
import numpy as np
from jax import lax
from jax.experimental import pallas as pl
from jax.experimental.pallas import tpu as pltpu
from jax.sharding import PartitionSpec as P

HEAD_DIM = 64
ROT = 16
MB = 2
QBLK = 512


EPS = 1e-05


def tables(count):
    places = jnp.arange(count).astype(jnp.float32)
    freqs = jnp.power(10000.0, -jnp.arange(ROT // 2).astype(jnp.float32) * 2.0 / ROT)
    angles = places[:, None] * freqs[None, :]
    return (jnp.cos(angles)[:, None, :], jnp.sin(angles)[:, None, :])


def rotate(vector, cosine, sine):
    first = vector[..., : ROT // 2]
    second = vector[..., ROT // 2 : ROT]
    return jnp.concatenate(
        [first * cosine - second * sine, second * cosine + first * sine, vector[..., ROT:]], axis=-1
    )


def unrotate(grad, cosine, sine):
    first = grad[..., : ROT // 2]
    second = grad[..., ROT // 2 : ROT]
    return jnp.concatenate(
        [first * cosine + second * sine, second * cosine - first * sine, grad[..., ROT:]], axis=-1
    )


def normalize(vector):
    centre = vector - jnp.mean(vector, axis=-1, keepdims=True)
    spread = jnp.mean(centre * centre, axis=-1, keepdims=True)
    scale = lax.rsqrt(spread + EPS)
    return (centre * scale, scale)


def norm_back(grad, normed, scale, gain):
    weighted = grad * gain
    return scale * (
        weighted
        - jnp.mean(weighted, axis=-1, keepdims=True)
        - normed * jnp.mean(weighted * normed, axis=-1, keepdims=True)
    )


def block_scores(rows, keys, start, limit, count):
    scores = jnp.einsum("qhd,kd->hqk", rows, keys, preferred_element_type=jnp.float32)
    row_pos = start + jnp.arange(QBLK)
    key_pos = jnp.arange(count)
    allowed = (key_pos[None, :] <= row_pos[:, None]) & (key_pos[None, :] < limit)
    return (scores, allowed[None])


def attend(queries, keys, values, limit):
    count = queries.shape[0]

    def block(start):
        rows = lax.dynamic_slice_in_dim(queries, start, QBLK, 0)
        scores, allowed = block_scores(rows, keys, start, limit, count)
        scores = jnp.where(allowed, scores, jnp.float32(-1e30))
        top = jnp.max(scores, axis=-1, keepdims=True)
        expo = jnp.exp(scores - top)
        total = jnp.sum(expo, axis=-1, keepdims=True)
        weights = (expo / total).astype(jnp.bfloat16)
        result = jnp.einsum("hqk,kd->qhd", weights, values, preferred_element_type=jnp.float32)
        return (result, (top + jnp.log(total))[..., 0])

    starts = jnp.arange(count // QBLK) * QBLK
    results, logsum = lax.map(block, starts)
    return (results.reshape(count, -1, HEAD_DIM), logsum)


def attend_back(queries, keys, values, limit, logsum, grad_out):
    count = queries.shape[0]

    def block(carry, item):
        start, block_logsum = item
        rows = lax.dynamic_slice_in_dim(queries, start, QBLK, 0)
        grads = lax.dynamic_slice_in_dim(grad_out, start, QBLK, 0)
        scores, allowed = block_scores(rows, keys, start, limit, count)
        probs = jnp.where(allowed, jnp.exp(scores - block_logsum[:, :, None]), 0.0)
        weights = probs.astype(jnp.bfloat16)
        dprobs = jnp.einsum("qhd,kd->hqk", grads, values, preferred_element_type=jnp.float32)
        delta = jnp.sum(probs * dprobs, axis=-1, keepdims=True)
        dscores = (probs * (dprobs - delta)).astype(jnp.bfloat16)
        drows = jnp.einsum("hqk,kd->qhd", dscores, keys, preferred_element_type=jnp.float32)
        dkeys = carry[0] + jnp.einsum(
            "hqk,qhd->kd", dscores, rows, preferred_element_type=jnp.float32
        )
        dvalues = carry[1] + jnp.einsum(
            "hqk,qhd->kd", weights, grads, preferred_element_type=jnp.float32
        )
        return ((dkeys, dvalues), drows)

    starts = jnp.arange(count // QBLK) * QBLK
    empty = jnp.zeros((count, HEAD_DIM), jnp.float32)
    (dkeys, dvalues), drows = lax.scan(block, (empty, empty), (starts, logsum))
    return (drows.reshape(count, -1, HEAD_DIM), dkeys, dvalues)


def fetch_each(w_query, w_shared, w_out, w_up, w_down):
    return (
        lax.all_gather(w_query, "dp", axis=0, tiled=True),
        lax.all_gather(w_shared, "dp", axis=0, tiled=True),
        lax.all_gather(w_out, "dp", axis=1, tiled=True),
        lax.all_gather(w_up, "dp", axis=0, tiled=True),
        lax.all_gather(w_down, "dp", axis=1, tiled=True),
    )


def reduce_each(step_grads):
    return (
        lax.psum_scatter(step_grads[0], "dp", scatter_dimension=0, tiled=True),
        lax.psum_scatter(step_grads[1], "dp", scatter_dimension=0, tiled=True),
        lax.psum_scatter(step_grads[2], "dp", scatter_dimension=1, tiled=True),
        lax.psum_scatter(step_grads[3], "dp", scatter_dimension=0, tiled=True),
        lax.psum_scatter(step_grads[4], "dp", scatter_dimension=1, tiled=True),
    )


def per_device(
    block_input,
    cotangent,
    lengths,
    ln1_gain,
    ln1_bias,
    ln2_gain,
    ln2_bias,
    w_query,
    b_query,
    w_shared,
    b_shared,
    w_out,
    b_out,
    w_up,
    b_up,
    w_down,
    b_down,
):
    shard_rows = block_input.shape[2]
    groups = lax.axis_size("tensor")
    rank = lax.axis_index("tensor")
    seq_len = shard_rows * groups
    tail_bias = b_out + b_down
    weight_sums = None
    cos_all, sin_all = tables(seq_len)
    own_pos = rank * shard_rows + jnp.arange(shard_rows)
    outputs = []
    input_grads = []
    sum_bq = jnp.zeros(b_query.shape, jnp.float32)
    sum_bkv = jnp.zeros(b_shared.shape, jnp.float32)
    sum_bup = jnp.zeros(b_up.shape, jnp.float32)
    sum_gain1 = jnp.zeros(ln1_gain.shape, jnp.float32)
    sum_shift1 = jnp.zeros(ln1_gain.shape, jnp.float32)
    sum_gain2 = jnp.zeros(ln1_gain.shape, jnp.float32)
    sum_shift2 = jnp.zeros(ln1_gain.shape, jnp.float32)
    sum_out = jnp.zeros(ln1_gain.shape, jnp.float32)
    for micro in range(MB):
        fetched = fetch_each(w_query, w_shared, w_out, w_up, w_down)
        wq_all, wkv_all, wo_all, wup_all, wdown_all = fetched
        limit = lengths[micro, 0]
        inputs = block_input[micro, 0].astype(jnp.float32)
        normed_one, scale_one = normalize(inputs)
        normed_two, scale_two = normalize(inputs)
        low_one = (normed_one * ln1_gain + ln1_bias).astype(jnp.bfloat16)
        low_two = (normed_two * ln2_gain + ln2_bias).astype(jnp.bfloat16)
        whole_one, whole_two = (
            lax.all_gather(low_one, "tensor", axis=0, tiled=True),
            lax.all_gather(low_two, "tensor", axis=0, tiled=True),
        )
        query_lin = jnp.dot(whole_one, wq_all, preferred_element_type=jnp.float32) + b_query
        query_lin = query_lin.reshape(seq_len, -1, HEAD_DIM)
        queries = (rotate(query_lin, cos_all, sin_all) * 0.125).astype(jnp.bfloat16)
        shared = jnp.dot(whole_one, wkv_all, preferred_element_type=jnp.float32) + b_shared
        keys = rotate(shared[:, None, :HEAD_DIM], cos_all, sin_all)[:, 0].astype(jnp.bfloat16)
        values = shared[:, HEAD_DIM:].astype(jnp.bfloat16)
        attended, logsum = attend(queries, keys, values, limit)
        attended_low = attended.reshape(seq_len, -1).astype(jnp.bfloat16)
        hidden = jnp.dot(whole_two, wup_all, preferred_element_type=jnp.float32) + b_up
        active = jax.nn.gelu(hidden, approximate=False).astype(jnp.bfloat16)
        partial_out = jnp.dot(attended_low, wo_all, preferred_element_type=jnp.float32) + jnp.dot(
            active, wdown_all, preferred_element_type=jnp.float32
        )
        branch = lax.psum_scatter(partial_out, "tensor", scatter_dimension=0, tiled=True)
        outputs.append((inputs + branch + tail_bias).astype(jnp.bfloat16))
        valid = (own_pos < limit).astype(jnp.float32)[:, None]
        upstream = cotangent[micro, 0].astype(jnp.float32) * valid
        whole_up = lax.all_gather(upstream.astype(jnp.bfloat16), "tensor", axis=0, tiled=True)
        sum_out = sum_out + jnp.sum(upstream, axis=0)
        grad_down = jnp.einsum("lf,ld->fd", active, whole_up, preferred_element_type=jnp.float32)
        dactive = jnp.einsum("ld,fd->lf", whole_up, wdown_all, preferred_element_type=jnp.float32)
        gelu_pull = jax.vjp(partial(jax.nn.gelu, approximate=False), hidden)[1]
        dhidden = gelu_pull(dactive)[0].astype(jnp.bfloat16)
        sum_bup = sum_bup + jnp.sum(dhidden.astype(jnp.float32), axis=0)
        grad_up = jnp.einsum("ld,lf->df", whole_two, dhidden, preferred_element_type=jnp.float32)
        dnormed_two = jnp.einsum("lf,df->ld", dhidden, wup_all, preferred_element_type=jnp.float32)
        dattended = jnp.einsum("ld,ed->le", whole_up, wo_all, preferred_element_type=jnp.float32)
        dattended = dattended.astype(jnp.bfloat16).reshape(seq_len, -1, HEAD_DIM)
        grad_out = jnp.einsum(
            "le,ld->ed", attended_low, whole_up, preferred_element_type=jnp.float32
        )
        dqueries, dkeys, dvalues = attend_back(queries, keys, values, limit, logsum, dattended)
        dquery_lin = (
            unrotate(dqueries * 0.125, cos_all, sin_all).reshape(seq_len, -1).astype(jnp.bfloat16)
        )
        dkey_lin = unrotate(dkeys[:, None, :], cos_all, sin_all)[:, 0]
        dshared = lax.psum(jnp.concatenate([dkey_lin, dvalues], axis=1), "tensor")
        dshared = dshared.astype(jnp.bfloat16)
        sum_bq = sum_bq + jnp.sum(dquery_lin.astype(jnp.float32), axis=0)
        sum_bkv = sum_bkv + jnp.sum(dshared.astype(jnp.float32), axis=0)
        grad_q = jnp.einsum("ld,le->de", whole_one, dquery_lin, preferred_element_type=jnp.float32)
        grad_kv = jnp.einsum("ld,lc->dc", whole_one, dshared, preferred_element_type=jnp.float32)
        dnormed_one = jnp.einsum(
            "le,de->ld", dquery_lin, wq_all, preferred_element_type=jnp.float32
        )
        dnormed_one, dnormed_two = (
            lax.psum_scatter(dnormed_one, "tensor", scatter_dimension=0, tiled=True),
            lax.psum_scatter(dnormed_two, "tensor", scatter_dimension=0, tiled=True),
        )
        own_shared = lax.dynamic_slice_in_dim(dshared, rank * shard_rows, shard_rows, 0)
        dnormed_one = dnormed_one + jnp.einsum(
            "lc,dc->ld", own_shared, wkv_all, preferred_element_type=jnp.float32
        )
        sum_gain1 = sum_gain1 + jnp.sum(dnormed_one * normed_one, axis=0)
        sum_shift1 = sum_shift1 + jnp.sum(dnormed_one, axis=0)
        sum_gain2 = sum_gain2 + jnp.sum(dnormed_two * normed_two, axis=0)
        sum_shift2 = sum_shift2 + jnp.sum(dnormed_two, axis=0)
        dinputs = (
            upstream
            + norm_back(dnormed_one, normed_one, scale_one, ln1_gain)
            + norm_back(dnormed_two, normed_two, scale_two, ln2_gain)
        )
        input_grads.append(dinputs.astype(jnp.bfloat16))
        step_grads = (grad_q, grad_kv, grad_out, grad_up, grad_down)
        step_grads = reduce_each(step_grads)
        if weight_sums is None:
            weight_sums = step_grads
        else:
            weight_sums = jax.tree.map(jnp.add, weight_sums, step_grads)
    output = jnp.stack(outputs, axis=0)[:, None]
    grad_input = jnp.stack(input_grads, axis=0)[:, None]
    sum_bq, sum_bkv, sum_bup = lax.psum((sum_bq, sum_bkv, sum_bup), "dp")
    sum_gain1, sum_shift1, sum_gain2, sum_shift2, sum_out = lax.psum(
        (sum_gain1, sum_shift1, sum_gain2, sum_shift2, sum_out), ("dp", "tensor")
    )
    grad_q, grad_kv, grad_o, grad_up, grad_down = weight_sums
    return (
        output,
        grad_input,
        sum_gain1,
        sum_shift1,
        sum_gain2,
        sum_shift2,
        grad_q,
        sum_bq,
        grad_kv,
        sum_bkv,
        grad_o,
        sum_out,
        grad_up,
        sum_bup,
        grad_down,
        sum_out,
    )


MESH = pl.DeviceIdType.MESH
BF = jnp.bfloat16
F32 = jnp.float32
LOG2E = 1.4426950408889634
LN2 = 0.6931471805599453
NEG = -1e30
ZC, XC, CC = 4, 2, 2
DMA = pltpu.SemaphoreType.DMA
VMEM = pltpu.VMEM
MIB = 1 << 20


def nn(a, b):
    return lax.dot_general(a, b, (((1,), (0,)), ((), ())), preferred_element_type=F32)


def nt(a, b):
    return lax.dot_general(a, b, (((1,), (1,)), ((), ())), preferred_element_type=F32)


def tn(a, b):
    return lax.dot_general(a, b, (((0,), (0,)), ((), ())), preferred_element_type=F32)


def eye(n):
    return (
        lax.broadcasted_iota(jnp.int32, (n, n), 0) == lax.broadcasted_iota(jnp.int32, (n, n), 1)
    ).astype(BF)


def flat(block):
    return block.reshape(-1, block.shape[-1])


class Place:
    def __init__(self):
        self.dp = lax.axis_index("dp")
        self.t = lax.axis_index("tensor")
        self.core = lax.rem(self.dp, CC)
        self.x = lax.rem(lax.div(self.dp, CC), XC)
        self.z = lax.div(self.dp, CC * XC)

    def at(self, z, x, core):
        return (z * XC + x) * CC + core

    def z_peer(self, d):
        return {"dp": self.at(lax.rem(self.z + d, ZC), self.x, self.core)}

    def x_peer(self):
        return {"dp": self.at(self.z, 1 - self.x, self.core)}

    def core_peer(self):
        return {"dp": self.at(self.z, self.x, 1 - self.core)}

    def y_peer(self):
        return {"tensor": 1 - self.t}

    def greet(self):
        bar = pltpu.get_barrier_semaphore()
        peers = [self.z_peer(d) for d in (1, 2, 3)]
        peers += [self.x_peer(), self.core_peer(), self.y_peer()]
        for p in peers:
            pl.semaphore_signal(bar, inc=1, device_id=p, device_id_type=MESH)
        return bar, len(peers)


def remote(src, dst, ss, rs, peer):
    return pltpu.make_async_remote_copy(
        src_ref=src, dst_ref=dst, send_sem=ss, recv_sem=rs, device_id=peer, device_id_type=MESH
    )


def split_cols(width):
    a = (width // 128 + 1) // 2 * 128
    return ((0, a), (a, width - a))


class Gather:
    N_SEMS = 12
    LAG = 2

    def __init__(self, place, pieces, sems):
        self.p = place
        self.pieces = pieces
        self.sems = sems

    def halves(self, c):
        if c == 0:
            return ((0, self.pieces[c][2], "zx"),)
        (o0, w0), (o1, w1) = split_cols(self.pieces[c][2])
        return ((o0, w0, "zxy"), (o1, w1, "zyx"))

    def copies(self, c, h, k):
        p = self.p
        src, out, _ = self.pieces[c]
        o, w, order = self.halves(c)[h]
        cols = pl.ds(o, w)
        sem = self.sems.at[c, h]
        if k == 0:
            dst = out.at[(p.z, p.x, p.core) + (slice(None), cols)] if c == 0 else out.at[
                p.t, p.z, p.x, p.core, :, cols
            ]
            return [
                remote(src.at[:, cols], dst, sem.at[d - 1], sem.at[2 + d], p.z_peer(d))
                for d in (1, 2, 3)
            ]
        done = order[:k]
        every = slice(None)
        index = (every, every if "x" in done else p.x, p.core, every, cols)
        if c:
            index = (every if "y" in done else p.t,) + index
        view = out.at[index]
        if k == len(order):
            peer = p.core_peer()
        else:
            peer = p.x_peer() if order[k] == "x" else p.y_peer()
        return [remote(view, view, sem.at[4 + 2 * k], sem.at[5 + 2 * k], peer)]

    def start(self, c, k):
        for h, (_, _, order) in enumerate(self.halves(c)):
            if k <= len(order):
                for cp in self.copies(c, h, k):
                    cp.start()

    def wait(self, c, k):
        for h, (_, _, order) in enumerate(self.halves(c)):
            if k <= len(order):
                for cp in self.copies(c, h, k):
                    cp.wait()

    def begin(self):
        for c in range(self.LAG):
            self.start(c, 0)

    def step(self, i):
        n = len(self.pieces)
        for k in (3, 2, 1, 0):
            c = i - k
            if 0 <= c < n:
                self.wait(c, k)
                if k < 3:
                    self.start(c, k + 1)
        if i + self.LAG < n:
            self.start(i + self.LAG, 0)


def normal_rows(rows):
    mean = jnp.mean(rows, axis=-1, keepdims=True)
    centre = rows - mean
    var = jnp.mean(centre * centre, axis=-1, keepdims=True)
    scale = lax.rsqrt(var + EPS)
    return centre * scale, scale


def rotate_t(v, cosine, sine):
    a, b = v[0:8], v[8:16]
    return jnp.concatenate([a * cosine - b * sine, b * cosine + a * sine, v[16:]], axis=0)


def unrotate_t(v, cosine, sine):
    a, b = v[0:8], v[8:16]
    return jnp.concatenate([a * cosine + b * sine, b * cosine - a * sine, v[16:]], axis=0)


def fill_bias(place, lens_ref, other_ref, own_ref, S):
    t = place.t
    for m in range(MB):
        limit = lens_ref[m]
        key = lax.broadcasted_iota(jnp.int32, (S, 128), 0)
        limit_other = jnp.where(t == 1, limit, 0)
        other_ref[m] = jnp.where(key < limit_other, 0.0, NEG).astype(F32)
        key = lax.broadcasted_iota(jnp.int32, (S, S), 0)
        row = lax.broadcasted_iota(jnp.int32, (S, S), 1)
        own = (key <= row) & (key + t * S < limit)
        own_ref[m] = jnp.where(own, 0.0, NEG).astype(F32)


def masked_rows(place_t, lens_ref, dy, start, S):
    m, off = divmod(start, S)
    pos = place_t * S + off + lax.broadcasted_iota(jnp.int32, (dy.shape[0], 1), 0)
    return jnp.where(pos < lens_ref[m], dy.astype(F32), 0.0)


class Reduce:
    def __init__(self, place, pieces, rc, r2a, r2b, r3, r4, sems):
        self.p = place
        self.pieces = pieces
        self.rc, self.r2a, self.r2b, self.r3, self.r4 = rc, r2a, r2b, r3, r4
        self.sems = sems

    def cores(self, c):
        g, w, _ = self.pieces[c]
        return remote(
            g.at[:, :, :, 1 - self.p.core],
            self.rc.at[c, :, :, :, :, pl.ds(0, w)],
            self.sems.at[c, 0],
            self.sems.at[c, 1],
            self.p.core_peer(),
        )

    def second(self, c, h):
        p = self.p
        o, w = split_cols(self.pieces[c][1])[h]
        if h == 0:
            src, dst, peer = self.rc.at[c, 1 - p.t, :, :, :, pl.ds(o, w)], self.r2a, p.y_peer()
        else:
            src, dst, peer = self.rc.at[c, :, :, 1 - p.x, :, pl.ds(o, w)], self.r2b, p.x_peer()
        dst = dst.at[c, :, :, :, pl.ds(0, w)]
        return remote(src, dst, self.sems.at[c, 2 + 2 * h], self.sems.at[c, 3 + 2 * h], peer)

    def third(self, c, h):
        p = self.p
        o, w = split_cols(self.pieces[c][1])[h]
        if h == 0:
            src, peer = self.r2a.at[c, :, 1 - p.x, :, pl.ds(0, w)], p.x_peer()
        else:
            src, peer = self.r2b.at[c, 1 - p.t, :, :, pl.ds(0, w)], p.y_peer()
        dst = self.r3.at[c, h, :, :, pl.ds(0, w)]
        return remote(src, dst, self.sems.at[c, 6 + 2 * h], self.sems.at[c, 7 + 2 * h], peer)

    def last(self, c, h, d):
        p = self.p
        o, w = split_cols(self.pieces[c][1])[h]
        src = self.r3.at[c, h, lax.rem(p.z + d, ZC), :, pl.ds(0, w)]
        dst = self.r4.at[c, h, d - 1, :, pl.ds(0, w)]
        k = 10 + (h * 3 + d - 1) * 2
        return remote(src, dst, self.sems.at[c, k], self.sems.at[c, k + 1], p.z_peer(d))

    N_SEMS = 22

    def begin(self, c):
        self.cores(c).start()

    def step1(self, c):
        p = self.p
        g, width, _ = self.pieces[c]
        self.cores(c).wait()
        own = g[:, :, :, p.core]
        mine = self.rc[c, :, :, :, :, 0:width].astype(F32) + own.astype(F32)
        self.rc[c, :, :, :, :, 0:width] = mine.astype(BF)
        for h in (0, 1):
            self.second(c, h).start()

    def step2(self, c):
        p = self.p
        for h in (0, 1):
            self.second(c, h).wait()
            o, w = split_cols(self.pieces[c][1])[h]
            if h == 0:
                ref, mine = self.r2a, self.rc[c, p.t, :, :, :, o : o + w]
            else:
                ref, mine = self.r2b, self.rc[c, :, :, p.x, :, o : o + w]
            mine = mine.astype(F32) + ref[c, :, :, :, 0:w].astype(F32)
            ref[c, :, :, :, 0:w] = mine.astype(BF)
            self.third(c, h).start()

    def step3(self, c):
        p = self.p
        for h in (0, 1):
            self.third(c, h).wait()
            o, w = split_cols(self.pieces[c][1])[h]
            mine = self.r2a[c, :, p.x, :, 0:w] if h == 0 else self.r2b[c, p.t, :, :, 0:w]
            mine = mine.astype(F32) + self.r3[c, h, :, :, 0:w].astype(F32)
            self.r3[c, h, :, :, 0:w] = mine.astype(BF)
            for d in (1, 2, 3):
                self.last(c, h, d).start()

    def step4(self, c):
        p = self.p
        parts = []
        for h in (0, 1):
            o, w = split_cols(self.pieces[c][1])[h]
            for d in (1, 2, 3):
                self.last(c, h, d).wait()
            total = self.r3[c, h, p.z, :, 0:w].astype(F32)
            for d in range(3):
                total = total + self.r4[c, h, d, :, 0:w].astype(F32)
            parts.append(total)
        self.pieces[c][2](parts)

    def step(self, i, lo, hi):
        for k, act in enumerate((self.step4, self.step3, self.step2, self.step1)):
            c = lo + i - (3 - k)
            if lo <= c < hi:
                act(c)


def block_kernel(
    dims,
    x_ref,
    dy_hbm,
    lens_ref,
    tab_ref,
    ln_ref,
    bpack_ref,
    bsh_ref,
    bo_ref,
    wq_in,
    wsh_in,
    wout_in,
    wup_in,
    wdown_in,
    out_hbm,
    gx_hbm,
    wf,
    gq_ref,
    gkv_ref,
    go_ref,
    gup_ref,
    gdn_ref,
    sm,
    sb,
    sf,
    wsh,
    wq,
    wb,
    won,
    wv,
    ball,
    bcol,
    dym,
    h1,
    h2,
    qt,
    att,
    da,
    tmp,
    acc,
    dh2,
    lse_ref,
    kvt,
    kvo,
    kc,
    vc,
    kt,
    vte,
    bias_o,
    bias_s,
    dkv,
    dkvr,
    dkvn,
    gring,
    gb,
    ga,
    bup,
    sums,
    smr,
    rc,
    r2a,
    r2b,
    r3,
    r4,
    gsem,
    rsem,
    lsem,
    wsem,
    ysem,
):
    S, HT, NH, NF, T = dims["S"], dims["HT"], dims["NH"], dims["NF"], dims["T"]
    D = x_ref.shape[1]
    R = sb.shape[0]
    NB = S // 256
    p = Place()
    bar, npeers = p.greet()

    dy_copy = pltpu.make_async_copy(dy_hbm, dym, lsem.at[0])
    dy_copy.start()
    ident = eye(R)
    sb[...] = nt(ident, wout_in[...]).astype(BF)
    for f in range(NF):
        sf[f, :, 0:256] = wup_in[:, 256 * f : 256 * f + 256]
        sf[f, :, 256:512] = nt(ident, wdown_in[256 * f : 256 * f + 256, :]).astype(BF)
    ball[p.t] = bpack_ref[...]

    pieces = [(wsh_in, wsh, 128), (wq_in, wq, HT), (sb, wb, HT)]
    pieces += [(sf.at[f], wf.at[f], 512) for f in range(NF)]
    g = Gather(p, pieces, gsem)
    mine = (p.z, p.x, p.core)
    locals_ = [
        pltpu.make_async_copy(src, out.at[mine if c == 0 else (p.t,) + mine], lsem.at[1 + c])
        for c, (src, out, _) in enumerate(pieces)
    ]
    for cp in locals_:
        cp.start()
    pl.semaphore_wait(bar, npeers)
    g.begin()
    bias_copy = remote(ball.at[p.t], ball.at[p.t], ysem.at[0], ysem.at[1], p.y_peer())
    bias_copy.start()

    def norm_block(i):
        rows = pl.ds(pl.multiple_of(i * 128, 128), 128)
        z, _ = normal_rows(x_ref[rows, :].astype(F32))
        h1[rows, :] = (z * ln_ref[0:1, :] + ln_ref[1:2, :]).astype(BF)
        h2[rows, :] = (z * ln_ref[2:3, :] + ln_ref[3:4, :]).astype(BF)

    half = T // 256
    pl.loop(0, half)(norm_block)
    for cp in locals_:
        cp.wait()
    g.step(0)
    pl.loop(half, 2 * half)(norm_block)
    g.step(1)
    fill_bias(p, lens_ref, bias_o, bias_s, S)
    bias_copy.wait()
    nq = HT // 128
    for t in range(2):
        for j in range(nq):
            row = jnp.broadcast_to(ball[t, j : j + 1, :], (128, 128))
            bcol[(t * nq + j) * 128 : (t * nq + j + 1) * 128, :] = row.T
    bcol[2 * HT : 2 * HT + 128, :] = jnp.broadcast_to(bsh_ref[...], (128, 128)).T
    g.step(2)

    id256 = eye(256)
    cosine, sine = tab_ref[p.t, 0:8, :], tab_ref[p.t, 8:16, :]
    wsh_t = nt(eye(128), flat(wsh[...])).astype(BF)
    for m in range(MB):
        cols = slice(m * S, m * S + S)
        kv = nt(wsh_t, h1[cols, :]) + bcol[2 * HT : 2 * HT + 128, 0:1]
        kvt[0:HEAD_DIM, cols] = rotate_t(kv[0:HEAD_DIM], cosine, sine).astype(BF)
        kvt[HEAD_DIM:, cols] = kv[HEAD_DIM:].astype(BF)
    kv_copy = remote(kvt, kvo, ysem.at[2], ysem.at[3], p.y_peer())
    kv_copy.start()
    g.step(3)
    dy_copy.wait()
    for b in range(T // 256):
        rows = slice(b * 256, b * 256 + 256)
        dym[rows, :] = masked_rows(p.t, lens_ref, dym[rows, :], b * 256, S).astype(BF)
    g.step(4)

    for t in range(2):
        wq_t = nt(eye(HT), flat(wq[t])).astype(BF)
        for m in range(MB):
            cols = slice(m * S, m * S + S)
            q = nt(wq_t, h1[cols, :])
            for h in range(HT // HEAD_DIM):
                base = t * HT + h * HEAD_DIM
                qh = q[h * HEAD_DIM : (h + 1) * HEAD_DIM] + bcol[base : base + HEAD_DIM, 0:1]
                qh = rotate_t(qh, cosine, sine) * (0.125 * LOG2E)
                qt[base : base + HEAD_DIM, cols] = qh.astype(BF)

    kv_copy.wait()
    for m in range(MB):
        cols = slice(m * S, m * S + S)
        for part, src in ((0, kvo), (1, kvt)):
            keys = slice(part * S, part * S + S)
            kt[m, :, keys] = src[0:HEAD_DIM, cols]
            vte[m, 0:HEAD_DIM, keys] = src[HEAD_DIM:, cols]
        ones = (lax.broadcasted_iota(jnp.int32, (16, 2 * S), 0) == 0).astype(BF)
        vte[m, HEAD_DIM:, :] = ones
        for b in range(2 * NB):
            blk = slice(b * 256, b * 256 + 256)
            kc[m, blk, :] = nt(id256, kt[m, :, blk]).astype(BF)
            vc[m, blk, :] = nt(id256, vte[m, 0:HEAD_DIM, blk]).astype(BF)

    def spots(i, group):
        res = []
        for u in range(group):
            j = i * group + u
            m, h = lax.div(j, NH), lax.rem(j, NH)
            head = pl.ds(pl.multiple_of(h * HEAD_DIM, HEAD_DIM), HEAD_DIM)
            for r in range(NB):
                cols = pl.ds(pl.multiple_of(m * S + r * 256, 256), 256)
                res.append((j, m, head, cols, S + 256 * (r + 1), r))
        return res

    def scores(m, q, nk, r):
        s = nn(kc[m, 0:nk, :], q)
        wide = slice(r * 256, r * 256 + 256)
        other = bias_o[m]
        other = jnp.concatenate([other, other], axis=1)
        return jnp.concatenate([s[0:S] + other, s[S:nk] + bias_s[m, 0 : nk - S, wide]], axis=0)

    group = 3

    @pl.loop(0, MB * NH // group)
    def _(i):
        todo = spots(i, group)
        sc = [scores(m, qt[head, cols], nk, r) for _, m, head, cols, nk, r in todo]
        tops = [jnp.max(s, axis=0, keepdims=True) for s in sc]
        ex = [jnp.exp2(s - top).astype(BF) for s, top in zip(sc, tops)]
        for (j, m, head, cols, nk, r), e, top in zip(todo, ex, tops):
            o = nn(vte[m, :, 0:nk], e)
            total = o[HEAD_DIM : HEAD_DIM + 1]
            att[head, cols] = (o[0:HEAD_DIM] * (1.0 / total)).astype(BF)
            lse_ref[j, :, r * 256 : r * 256 + 256] = top + jnp.log2(total)
        for at, k in ((0, 5), (3, 6), (6, 7)):
            pl.when(i == at)(partial(g.step, k))

    for t in range(2):
        won[t * HT : (t + 1) * HT, :] = nt(eye(HT), flat(wb[t])).astype(BF)

    def load(f, slot):
        return pltpu.make_async_copy(wf.at[f], wv.at[slot], wsem.at[slot])

    load(0, 0).start()
    for b in range(T // 256):
        rows = slice(b * 256, b * 256 + 256)
        tmp[rows, :] = nt(id256, att[:, rows]).astype(BF)
    acc[...] = x_ref[...].astype(F32) + bo_ref[...] + nn(tmp[...], won[...])
    for t in range(2):
        cols = slice(t * HT, (t + 1) * HT)
        gb[t] = tn(dym[...], tmp[:, cols]).astype(BF).reshape(ZC, XC, CC, R, HT)

    def put_out(parts):
        a = parts[0].shape[1]
        go_ref[:, 0:a] = parts[0]
        go_ref[:, a:] = parts[1]

    def put_ffn(f):
        def put(parts):
            gup_ref[:, f * 256 : f * 256 + 256] = parts[0]
            gdn_ref[:, f * 256 : f * 256 + 256] = parts[1]

        return put

    def put_a(parts):
        a = parts[0].shape[1]
        gq_ref[:, 0:a] = parts[0]
        gq_ref[:, a:HT] = parts[1][:, 0 : HT - a]
        gkv_ref[...] = parts[1][:, HT - a :]

    sums_of = [(gb, HT, put_out)]
    sums_of += [(gring.at[f % 3], 512, put_ffn(f)) for f in range(NF)]
    sums_of += [(ga, HT + 128, put_a)]
    red = Reduce(p, sums_of, rc, r2a, r2b, r3, r4, rsem)
    last = NF + 1
    red.begin(0)
    dh2[...] = jnp.zeros_like(dh2)
    first = ball.shape[1] - 1 - 2 * NF

    @pl.loop(0, NF)
    def _(f):
        slot = lax.rem(f, 2)
        load(f, slot).wait()
        for k in range(NF - 1):

            @pl.when(f == k)
            def _():
                g.step(8 + k)
                load(k + 1, (k + 1) % 2).start()

        for k in range(2, NF):
            pl.when(f == k)(partial(red.step, k - 2, 0, last))
        wu = [flat(wv[slot, t, :, :, :, :, 0:256]) for t in range(2)]
        wd = [flat(wv[slot, t, :, :, :, :, 256:512]) for t in range(2)]
        gslot = lax.rem(f, 3)
        hid = [nn(h2[...], wu[t]) for t in range(2)]
        dact = [nn(dym[...], wd[t]) for t in range(2)]
        act, dhid = [], []
        for t in range(2):
            row = jnp.concatenate(
                [ball[t, pl.ds(first + 2 * f, 1), :], ball[t, pl.ds(first + 2 * f + 1, 1), :]],
                axis=1,
            )
            u = hid[t] + row
            cdf = 0.5 + 0.5 * lax.erf(u * 0.7071067811865476)
            dens = jnp.exp(-0.5 * u * u) * 0.3989422804014327
            act.append((u * cdf).astype(BF))
            d = (dact[t] * (cdf + u * dens)).astype(BF)
            dhid.append(d)
            total = jnp.sum(d.astype(F32), axis=0, keepdims=True)
            bup[f, 2 * t : 2 * t + 1, :] = total[:, 0:128]
            bup[f, 2 * t + 1 : 2 * t + 2, :] = total[:, 128:256]
        acc[...] += nt(act[0], wd[0]) + nt(act[1], wd[1])
        dh2[...] += nt(dhid[0], wu[0]) + nt(dhid[1], wu[1])
        for t in range(2):
            gd = tn(dym[...], act[t]).astype(BF)
            gring[gslot, t, :, :, :, :, 256:512] = gd.reshape(ZC, XC, CC, R, 256)
            gu = tn(h2[...], dhid[t]).astype(BF)
            gring[gslot, t, :, :, :, :, 0:256] = gu.reshape(ZC, XC, CC, R, 256)
        for k in range(NF):
            pl.when(f == k)(partial(red.begin, 1 + k))

    h2[...] = acc[...].astype(BF)
    out_copy = pltpu.make_async_copy(h2, out_hbm, lsem.at[0])
    out_copy.start()

    da[...] = nt(won[...], dym[...]).astype(BF)
    dkv[...] = jnp.zeros_like(dkv)
    back = 2

    @pl.loop(0, MB * NH // back)
    def _(i):
        todo = spots(i, back)
        qs = [qt[head, cols] for _, m, head, cols, nk, r in todo]
        das = [da[head, cols] for _, m, head, cols, nk, r in todo]
        sc = [scores(m, q, nk, r) for (_, m, head, cols, nk, r), q in zip(todo, qs)]
        dp = [nn(vc[m, 0:nk, :], d) for (_, m, head, cols, nk, r), d in zip(todo, das)]
        pr, ds = [], []
        for (j, m, head, cols, nk, r), d, s, dpj in zip(todo, das, sc, dp):
            delta = jnp.sum(d.astype(F32) * att[head, cols].astype(F32), axis=0, keepdims=True)
            w = jnp.exp2(s - lse_ref[j, :, r * 256 : r * 256 + 256])
            pr.append(w.astype(BF))
            ds.append((w * (dpj - delta)).astype(BF))
        for (j, m, head, cols, nk, r), d in zip(todo, ds):
            wide = slice(r * 256, r * 256 + 256)
            dq = nn(kt[m, :, 0:nk], d)
            dq = unrotate_t(dq, tab_ref[p.t, 0:8, wide], tab_ref[p.t, 8:16, wide])
            qt[head, cols] = (dq * 0.125).astype(BF)
        m = todo[0][1]
        for blk in range(NB):
            lo = 0 if blk == 0 else S + 256 * blk
            hi = S + 256 * (blk + 1)
            left, right = [], []
            for u, (_, _, _, _, nk, r) in enumerate(todo):
                if nk >= hi:
                    zero = jnp.zeros_like(qs[u])
                    left += [ds[u][lo:hi], pr[u][lo:hi]]
                    right += [
                        jnp.concatenate([qs[u], zero], axis=0),
                        jnp.concatenate([zero, das[u]], axis=0),
                    ]
            dkv[m, lo:hi, :] += nt(
                jnp.concatenate(left, axis=1), jnp.concatenate(right, axis=1)
            )
        for k in range(NF - 2, last + 3):
            pl.when(i == 2 * (k - (NF - 2)) + 1)(partial(red.step, k, 0, last))

    kv_back = remote(dkv.at[:, 0:S, :], dkvr, ysem.at[4], ysem.at[5], p.y_peer())
    kv_back.start()
    for b in range(T // 256):
        rows = slice(b * 256, b * 256 + 256)
        tmp[rows, :] = nt(id256, qt[:, rows]).astype(BF)
    for t in range(2):
        gq = tn(h1[...], tmp[:, t * HT : (t + 1) * HT]).astype(BF)
        ga[t, :, :, :, :, 0:HT] = gq.reshape(ZC, XC, CC, R, HT)
    kv_back.wait()
    for m in range(MB):
        both = (dkv[m, S : 2 * S, :] + dkvr[m]).T
        dk = unrotate_t(both[0:HEAD_DIM], cosine, sine) * LN2
        both = jnp.concatenate([dk, both[HEAD_DIM:]], axis=0).astype(BF)
        for b in range(NB):
            rows = slice(m * S + b * 256, m * S + b * 256 + 256)
            dkvn[rows, :] = nt(id256, both[:, b * 256 : b * 256 + 256]).astype(BF)
    gkv = tn(h1[...], dkvn[...]).astype(BF).reshape(ZC, XC, CC, R, 128)
    for t in range(2):
        ga[t, :, :, :, :, HT:] = gkv
    red.begin(last)

    sums[...] = jnp.zeros_like(sums)
    wqf = [flat(wq[t]) for t in range(2)]
    wshf = flat(wsh[...])
    for b in range(T // 256):
        rows = slice(b * 256, b * 256 + 256)
        dq, dkvb = tmp[rows, :], dkvn[rows, :]
        dh1 = nt(dq[:, 0:HT], wqf[0]) + nt(dq[:, HT:], wqf[1]) + nt(dkvb, wshf)
        dh2b = dh2[rows, :]
        z, scale = normal_rows(x_ref[rows, :].astype(F32))
        dy = dym[rows, :].astype(F32)
        e = dh1 * ln_ref[0:1, :] + dh2b * ln_ref[2:3, :]
        back_in = scale * (
            e - jnp.mean(e, axis=-1, keepdims=True) - z * jnp.mean(e * z, axis=-1, keepdims=True)
        )
        h1[rows, :] = (dy + back_in).astype(BF)
        for k, v in enumerate((dh1 * z, dh1, dh2b * z, dh2b, dy, dq.astype(F32))):
            sums[k : k + 1, :] += jnp.sum(v, axis=0, keepdims=True)
        sums[6:7, 0:128] += jnp.sum(dkvb.astype(F32), axis=0, keepdims=True)
        if b < 2:
            red.step(b, last, last + 1)
    gx_copy = pltpu.make_async_copy(h1, gx_hbm, lsem.at[1])
    gx_copy.start()
    n = D // 128
    for k in range(6):
        for j in range(n):
            sm[k * n + j : k * n + j + 1, :] = sums[k : k + 1, j * 128 : j * 128 + 128]
    sm[6 * n : 6 * n + 4, :] = jnp.zeros((4, 128), F32)
    sm[6 * n : 6 * n + 1, :] = sums[6:7, 0:128]
    for f in range(NF):
        sm[6 * n + 4 + 4 * f : 6 * n + 8 + 4 * f, :] = bup[f]

    for k, peer in enumerate((p.core_peer(), p.y_peer(), p.x_peer())):
        cp = remote(sm, smr.at[k], ysem.at[6 + 2 * k], ysem.at[7 + 2 * k], peer)
        cp.start()
        if k < 2:
            red.step(k + 2, last, last + 1)
        cp.wait()
        sm[...] += smr[k]
    cps = [
        remote(sm, smr.at[2 + d], ysem.at[10 + 2 * d], ysem.at[11 + 2 * d], p.z_peer(d))
        for d in (1, 2, 3)
    ]
    for cp in cps:
        cp.start()
    for cp in cps:
        cp.wait()
    sm[...] += smr[3] + smr[4] + smr[5]
    out_copy.wait()
    gx_copy.wait()


def angle_table(S):
    places = np.arange(2 * S, dtype=np.float64)
    freqs = 10000.0 ** (-np.arange(ROT // 2) * 2.0 / ROT)
    angles = (places[:, None] * freqs[None, :]).astype(np.float32).astype(np.float64)
    tab = np.concatenate([np.cos(angles).T, np.sin(angles).T], axis=0).astype(np.float32)
    return tab.reshape(ROT, 2, S).transpose(1, 0, 2)


def token_plan(
    block_input,
    cotangent,
    lengths,
    ln1_gain,
    ln1_bias,
    ln2_gain,
    ln2_bias,
    w_query,
    b_query,
    w_shared,
    b_shared,
    w_out,
    b_out,
    w_up,
    b_up,
    w_down,
    b_down,
):
    S, D = block_input.shape[2:]
    R, HT = w_query.shape
    FT = w_up.shape[1]
    NF, T, NH = FT // 256, MB * S, 2 * HT // HEAD_DIM
    dims = dict(S=S, HT=HT, NF=NF, T=T, NH=NH)
    plane = (ZC, XC, CC, R)
    full = (2,) + plane
    t = lax.axis_index("tensor")

    def s(shape, dtype):
        return jax.ShapeDtypeStruct(shape, dtype)

    vm = pl.BlockSpec(memory_space=VMEM)
    hbm = pl.BlockSpec(memory_space=pl.ANY)
    smem = pl.BlockSpec(memory_space=pltpu.SMEM)

    ln = jnp.stack([ln1_gain, ln1_bias, ln2_gain, ln2_bias])
    bpack = jnp.concatenate([b_query, b_up, jnp.zeros((128,), F32)]).reshape(-1, 128)
    nb = bpack.shape[0]
    np_ = NF + 2
    n_small = 6 * (D // 128) + 4 + 4 * NF

    outs = pl.pallas_call(
        partial(block_kernel, dims),
        out_shape=[
            s((T, D), BF),
            s((T, D), BF),
            s((NF,) + full + (512,), BF),
            s((R, HT), F32),
            s((R, 128), F32),
            s((R, HT), F32),
            s((R, FT), F32),
            s((R, FT), F32),
            s((n_small, 128), F32),
        ],
        in_specs=[vm, hbm, smem] + [vm] * 10,
        out_specs=[hbm] * 3 + [vm] * 6,
        scratch_shapes=[
            VMEM((R, HT), BF),
            VMEM((NF, R, 512), BF),
            VMEM(plane + (128,), BF),
            VMEM(full + (HT,), BF),
            VMEM(full + (HT,), BF),
            VMEM((2 * HT, D), BF),
            VMEM((2,) + full + (512,), BF),
            VMEM((2, nb, 128), F32),
            VMEM((2 * HT + 128, 128), F32),
            VMEM((T, D), BF),
            VMEM((T, D), BF),
            VMEM((T, D), BF),
            VMEM((D, T), BF),
            VMEM((D, T), BF),
            VMEM((D, T), BF),
            VMEM((T, D), BF),
            VMEM((T, D), F32),
            VMEM((T, D), F32),
            VMEM((MB * NH, 1, S), F32),
            VMEM((128, T), BF),
            VMEM((128, T), BF),
            VMEM((MB, 2 * S, HEAD_DIM), BF),
            VMEM((MB, 2 * S, HEAD_DIM), BF),
            VMEM((MB, HEAD_DIM, 2 * S), BF),
            VMEM((MB, HEAD_DIM + 16, 2 * S), BF),
            VMEM((MB, S, 128), F32),
            VMEM((MB, S, S), F32),
            VMEM((MB, 2 * S, 128), F32),
            VMEM((MB, S, 128), F32),
            VMEM((T, 128), BF),
            VMEM((3,) + full + (512,), BF),
            VMEM(full + (HT,), BF),
            VMEM(full + (HT + 128,), BF),
            VMEM((NF, 4, 128), F32),
            VMEM((8, D), F32),
            VMEM((6, n_small, 128), F32),
            VMEM((np_, 2, ZC, XC, R, 512), BF),
            VMEM((np_, ZC, XC, R, 256), BF),
            VMEM((np_, 2, ZC, R, 256), BF),
            VMEM((np_, 2, ZC, R, 256), BF),
            VMEM((np_, 2, 3, R, 256), BF),
            DMA((np_ + 1, 2, Gather.N_SEMS)),
            DMA((np_, Reduce.N_SEMS)),
            DMA((np_ + 2,)),
            DMA((2,)),
            DMA((18,)),
        ],
        compiler_params=pltpu.CompilerParams(
            vmem_limit_bytes=64 * MIB - 65536, collective_id=0, has_side_effects=True
        ),
        name="block",
    )(
        block_input.reshape(T, D),
        cotangent.reshape(T, D),
        lengths.reshape(MB),
        jnp.asarray(angle_table(S)),
        ln,
        bpack,
        b_shared.reshape(1, 128),
        (b_out + b_down).reshape(1, D),
        w_query,
        w_shared,
        w_out,
        w_up,
        w_down,
    )
    out, gx, _, gq, gkv, go, gup, gdn, sm = outs
    n = D // 128
    five = sm[0 : 5 * n].reshape(5, D)
    bq = lax.dynamic_index_in_dim(sm[5 * n : 6 * n].reshape(2, HT), t, 0, False)
    bkv = sm[6 * n]
    bup = lax.dynamic_index_in_dim(sm[6 * n + 4 :].reshape(NF, 2, 256), t, 1, False).reshape(FT)
    return (
        out.reshape(block_input.shape),
        gx.reshape(block_input.shape),
        five[0],
        five[1],
        five[2],
        five[3],
        gq,
        bq,
        gkv,
        bkv,
        go.T,
        five[4],
        gup,
        bup,
        gdn.T,
        five[4],
    )


def fits_token_plan(mesh):
    return dict(mesh.shape) == {"dp": ZC * XC * CC, "tensor": 2}


def solution(mesh):
    in_specs = (
        P(None, "dp", "tensor", None),
        P(None, "dp", "tensor", None),
        P(None, "dp"),
        P(),
        P(),
        P(),
        P(),
        P("dp", "tensor"),
        P("tensor"),
        P("dp", None),
        P(),
        P("tensor", "dp"),
        P(),
        P("dp", "tensor"),
        P("tensor"),
        P("tensor", "dp"),
        P(),
    )
    out_specs = (
        P(None, "dp", "tensor", None),
        P(None, "dp", "tensor", None),
        P(),
        P(),
        P(),
        P(),
        P("dp", "tensor"),
        P("tensor"),
        P("dp", None),
        P(),
        P("tensor", "dp"),
        P(),
        P("dp", "tensor"),
        P("tensor"),
        P("tensor", "dp"),
        P(),
    )
    step = token_plan if fits_token_plan(mesh) else per_device
    return jax.shard_map(
        step, mesh=mesh, in_specs=in_specs, out_specs=out_specs, check_vma=False
    )
```

```python
from functools import partial

import jax
import jax.numpy as jnp
import numpy as np
from jax import lax
from jax.experimental import pallas as pl
from jax.experimental.pallas import tpu as pltpu
from jax.sharding import PartitionSpec as P

HEAD_DIM = 64
ROT = 16
MB = 2
QBLK = 512


EPS = 1e-05


def tables(count):
    places = jnp.arange(count).astype(jnp.float32)
    freqs = jnp.power(10000.0, -jnp.arange(ROT // 2).astype(jnp.float32) * 2.0 / ROT)
    angles = places[:, None] * freqs[None, :]
    return (jnp.cos(angles)[:, None, :], jnp.sin(angles)[:, None, :])


def rotate(vector, cosine, sine):
    first = vector[..., : ROT // 2]
    second = vector[..., ROT // 2 : ROT]
    return jnp.concatenate(
        [first * cosine - second * sine, second * cosine + first * sine, vector[..., ROT:]], axis=-1
    )


def unrotate(grad, cosine, sine):
    first = grad[..., : ROT // 2]
    second = grad[..., ROT // 2 : ROT]
    return jnp.concatenate(
        [first * cosine + second * sine, second * cosine - first * sine, grad[..., ROT:]], axis=-1
    )


def normalize(vector):
    centre = vector - jnp.mean(vector, axis=-1, keepdims=True)
    spread = jnp.mean(centre * centre, axis=-1, keepdims=True)
    scale = lax.rsqrt(spread + EPS)
    return (centre * scale, scale)


def norm_back(grad, normed, scale, gain):
    weighted = grad * gain
    return scale * (
        weighted
        - jnp.mean(weighted, axis=-1, keepdims=True)
        - normed * jnp.mean(weighted * normed, axis=-1, keepdims=True)
    )


def block_scores(rows, keys, start, limit, count):
    scores = jnp.einsum("qhd,kd->hqk", rows, keys, preferred_element_type=jnp.float32)
    row_pos = start + jnp.arange(QBLK)
    key_pos = jnp.arange(count)
    allowed = (key_pos[None, :] <= row_pos[:, None]) & (key_pos[None, :] < limit)
    return (scores, allowed[None])


def attend(queries, keys, values, limit):
    count = queries.shape[0]

    def block(start):
        rows = lax.dynamic_slice_in_dim(queries, start, QBLK, 0)
        scores, allowed = block_scores(rows, keys, start, limit, count)
        scores = jnp.where(allowed, scores, jnp.float32(-1e30))
        top = jnp.max(scores, axis=-1, keepdims=True)
        expo = jnp.exp(scores - top)
        total = jnp.sum(expo, axis=-1, keepdims=True)
        weights = (expo / total).astype(jnp.bfloat16)
        result = jnp.einsum("hqk,kd->qhd", weights, values, preferred_element_type=jnp.float32)
        return (result, (top + jnp.log(total))[..., 0])

    starts = jnp.arange(count // QBLK) * QBLK
    results, logsum = lax.map(block, starts)
    return (results.reshape(count, -1, HEAD_DIM), logsum)


def attend_back(queries, keys, values, limit, logsum, grad_out):
    count = queries.shape[0]

    def block(carry, item):
        start, block_logsum = item
        rows = lax.dynamic_slice_in_dim(queries, start, QBLK, 0)
        grads = lax.dynamic_slice_in_dim(grad_out, start, QBLK, 0)
        scores, allowed = block_scores(rows, keys, start, limit, count)
        probs = jnp.where(allowed, jnp.exp(scores - block_logsum[:, :, None]), 0.0)
        weights = probs.astype(jnp.bfloat16)
        dprobs = jnp.einsum("qhd,kd->hqk", grads, values, preferred_element_type=jnp.float32)
        delta = jnp.sum(probs * dprobs, axis=-1, keepdims=True)
        dscores = (probs * (dprobs - delta)).astype(jnp.bfloat16)
        drows = jnp.einsum("hqk,kd->qhd", dscores, keys, preferred_element_type=jnp.float32)
        dkeys = carry[0] + jnp.einsum(
            "hqk,qhd->kd", dscores, rows, preferred_element_type=jnp.float32
        )
        dvalues = carry[1] + jnp.einsum(
            "hqk,qhd->kd", weights, grads, preferred_element_type=jnp.float32
        )
        return ((dkeys, dvalues), drows)

    starts = jnp.arange(count // QBLK) * QBLK
    empty = jnp.zeros((count, HEAD_DIM), jnp.float32)
    (dkeys, dvalues), drows = lax.scan(block, (empty, empty), (starts, logsum))
    return (drows.reshape(count, -1, HEAD_DIM), dkeys, dvalues)


def fetch_each(w_query, w_shared, w_out, w_up, w_down):
    return (
        lax.all_gather(w_query, "dp", axis=0, tiled=True),
        lax.all_gather(w_shared, "dp", axis=0, tiled=True),
        lax.all_gather(w_out, "dp", axis=1, tiled=True),
        lax.all_gather(w_up, "dp", axis=0, tiled=True),
        lax.all_gather(w_down, "dp", axis=1, tiled=True),
    )


def reduce_each(step_grads):
    return (
        lax.psum_scatter(step_grads[0], "dp", scatter_dimension=0, tiled=True),
        lax.psum_scatter(step_grads[1], "dp", scatter_dimension=0, tiled=True),
        lax.psum_scatter(step_grads[2], "dp", scatter_dimension=1, tiled=True),
        lax.psum_scatter(step_grads[3], "dp", scatter_dimension=0, tiled=True),
        lax.psum_scatter(step_grads[4], "dp", scatter_dimension=1, tiled=True),
    )


def per_device(
    block_input,
    cotangent,
    lengths,
    ln1_gain,
    ln1_bias,
    ln2_gain,
    ln2_bias,
    w_query,
    b_query,
    w_shared,
    b_shared,
    w_out,
    b_out,
    w_up,
    b_up,
    w_down,
    b_down,
):
    shard_rows = block_input.shape[2]
    groups = lax.axis_size("tensor")
    rank = lax.axis_index("tensor")
    seq_len = shard_rows * groups
    tail_bias = b_out + b_down
    weight_sums = None
    cos_all, sin_all = tables(seq_len)
    own_pos = rank * shard_rows + jnp.arange(shard_rows)
    outputs = []
    input_grads = []
    sum_bq = jnp.zeros(b_query.shape, jnp.float32)
    sum_bkv = jnp.zeros(b_shared.shape, jnp.float32)
    sum_bup = jnp.zeros(b_up.shape, jnp.float32)
    sum_gain1 = jnp.zeros(ln1_gain.shape, jnp.float32)
    sum_shift1 = jnp.zeros(ln1_gain.shape, jnp.float32)
    sum_gain2 = jnp.zeros(ln1_gain.shape, jnp.float32)
    sum_shift2 = jnp.zeros(ln1_gain.shape, jnp.float32)
    sum_out = jnp.zeros(ln1_gain.shape, jnp.float32)
    for micro in range(MB):
        fetched = fetch_each(w_query, w_shared, w_out, w_up, w_down)
        wq_all, wkv_all, wo_all, wup_all, wdown_all = fetched
        limit = lengths[micro, 0]
        inputs = block_input[micro, 0].astype(jnp.float32)
        normed_one, scale_one = normalize(inputs)
        normed_two, scale_two = normalize(inputs)
        low_one = (normed_one * ln1_gain + ln1_bias).astype(jnp.bfloat16)
        low_two = (normed_two * ln2_gain + ln2_bias).astype(jnp.bfloat16)
        whole_one, whole_two = (
            lax.all_gather(low_one, "tensor", axis=0, tiled=True),
            lax.all_gather(low_two, "tensor", axis=0, tiled=True),
        )
        query_lin = jnp.dot(whole_one, wq_all, preferred_element_type=jnp.float32) + b_query
        query_lin = query_lin.reshape(seq_len, -1, HEAD_DIM)
        queries = (rotate(query_lin, cos_all, sin_all) * 0.125).astype(jnp.bfloat16)
        shared = jnp.dot(whole_one, wkv_all, preferred_element_type=jnp.float32) + b_shared
        keys = rotate(shared[:, None, :HEAD_DIM], cos_all, sin_all)[:, 0].astype(jnp.bfloat16)
        values = shared[:, HEAD_DIM:].astype(jnp.bfloat16)
        attended, logsum = attend(queries, keys, values, limit)
        attended_low = attended.reshape(seq_len, -1).astype(jnp.bfloat16)
        hidden = jnp.dot(whole_two, wup_all, preferred_element_type=jnp.float32) + b_up
        active = jax.nn.gelu(hidden, approximate=False).astype(jnp.bfloat16)
        partial_out = jnp.dot(attended_low, wo_all, preferred_element_type=jnp.float32) + jnp.dot(
            active, wdown_all, preferred_element_type=jnp.float32
        )
        branch = lax.psum_scatter(partial_out, "tensor", scatter_dimension=0, tiled=True)
        outputs.append((inputs + branch + tail_bias).astype(jnp.bfloat16))
        valid = (own_pos < limit).astype(jnp.float32)[:, None]
        upstream = cotangent[micro, 0].astype(jnp.float32) * valid
        whole_up = lax.all_gather(upstream.astype(jnp.bfloat16), "tensor", axis=0, tiled=True)
        sum_out = sum_out + jnp.sum(upstream, axis=0)
        grad_down = jnp.einsum("lf,ld->fd", active, whole_up, preferred_element_type=jnp.float32)
        dactive = jnp.einsum("ld,fd->lf", whole_up, wdown_all, preferred_element_type=jnp.float32)
        gelu_pull = jax.vjp(partial(jax.nn.gelu, approximate=False), hidden)[1]
        dhidden = gelu_pull(dactive)[0].astype(jnp.bfloat16)
        sum_bup = sum_bup + jnp.sum(dhidden.astype(jnp.float32), axis=0)
        grad_up = jnp.einsum("ld,lf->df", whole_two, dhidden, preferred_element_type=jnp.float32)
        dnormed_two = jnp.einsum("lf,df->ld", dhidden, wup_all, preferred_element_type=jnp.float32)
        dattended = jnp.einsum("ld,ed->le", whole_up, wo_all, preferred_element_type=jnp.float32)
        dattended = dattended.astype(jnp.bfloat16).reshape(seq_len, -1, HEAD_DIM)
        grad_out = jnp.einsum(
            "le,ld->ed", attended_low, whole_up, preferred_element_type=jnp.float32
        )
        dqueries, dkeys, dvalues = attend_back(queries, keys, values, limit, logsum, dattended)
        dquery_lin = (
            unrotate(dqueries * 0.125, cos_all, sin_all).reshape(seq_len, -1).astype(jnp.bfloat16)
        )
        dkey_lin = unrotate(dkeys[:, None, :], cos_all, sin_all)[:, 0]
        dshared = lax.psum(jnp.concatenate([dkey_lin, dvalues], axis=1), "tensor")
        dshared = dshared.astype(jnp.bfloat16)
        sum_bq = sum_bq + jnp.sum(dquery_lin.astype(jnp.float32), axis=0)
        sum_bkv = sum_bkv + jnp.sum(dshared.astype(jnp.float32), axis=0)
        grad_q = jnp.einsum("ld,le->de", whole_one, dquery_lin, preferred_element_type=jnp.float32)
        grad_kv = jnp.einsum("ld,lc->dc", whole_one, dshared, preferred_element_type=jnp.float32)
        dnormed_one = jnp.einsum(
            "le,de->ld", dquery_lin, wq_all, preferred_element_type=jnp.float32
        )
        dnormed_one, dnormed_two = (
            lax.psum_scatter(dnormed_one, "tensor", scatter_dimension=0, tiled=True),
            lax.psum_scatter(dnormed_two, "tensor", scatter_dimension=0, tiled=True),
        )
        own_shared = lax.dynamic_slice_in_dim(dshared, rank * shard_rows, shard_rows, 0)
        dnormed_one = dnormed_one + jnp.einsum(
            "lc,dc->ld", own_shared, wkv_all, preferred_element_type=jnp.float32
        )
        sum_gain1 = sum_gain1 + jnp.sum(dnormed_one * normed_one, axis=0)
        sum_shift1 = sum_shift1 + jnp.sum(dnormed_one, axis=0)
        sum_gain2 = sum_gain2 + jnp.sum(dnormed_two * normed_two, axis=0)
        sum_shift2 = sum_shift2 + jnp.sum(dnormed_two, axis=0)
        dinputs = (
            upstream
            + norm_back(dnormed_one, normed_one, scale_one, ln1_gain)
            + norm_back(dnormed_two, normed_two, scale_two, ln2_gain)
        )
        input_grads.append(dinputs.astype(jnp.bfloat16))
        step_grads = (grad_q, grad_kv, grad_out, grad_up, grad_down)
        step_grads = reduce_each(step_grads)
        if weight_sums is None:
            weight_sums = step_grads
        else:
            weight_sums = jax.tree.map(jnp.add, weight_sums, step_grads)
    output = jnp.stack(outputs, axis=0)[:, None]
    grad_input = jnp.stack(input_grads, axis=0)[:, None]
    sum_bq, sum_bkv, sum_bup = lax.psum((sum_bq, sum_bkv, sum_bup), "dp")
    sum_gain1, sum_shift1, sum_gain2, sum_shift2, sum_out = lax.psum(
        (sum_gain1, sum_shift1, sum_gain2, sum_shift2, sum_out), ("dp", "tensor")
    )
    grad_q, grad_kv, grad_o, grad_up, grad_down = weight_sums
    return (
        output,
        grad_input,
        sum_gain1,
        sum_shift1,
        sum_gain2,
        sum_shift2,
        grad_q,
        sum_bq,
        grad_kv,
        sum_bkv,
        grad_o,
        sum_out,
        grad_up,
        sum_bup,
        grad_down,
        sum_out,
    )


MESH = pl.DeviceIdType.MESH
BF = jnp.bfloat16
F32 = jnp.float32
LOG2E = 1.4426950408889634
LN2 = 0.6931471805599453
NEG = -1e30
ZC, XC, CC = 4, 2, 2
DMA = pltpu.SemaphoreType.DMA
VMEM = pltpu.VMEM
MIB = 1 << 20


def nn(a, b):
    return lax.dot_general(a, b, (((1,), (0,)), ((), ())), preferred_element_type=F32)


def nt(a, b):
    return lax.dot_general(a, b, (((1,), (1,)), ((), ())), preferred_element_type=F32)


def tn(a, b):
    return lax.dot_general(a, b, (((0,), (0,)), ((), ())), preferred_element_type=F32)


def eye(n):
    return (
        lax.broadcasted_iota(jnp.int32, (n, n), 0) == lax.broadcasted_iota(jnp.int32, (n, n), 1)
    ).astype(BF)


def flat(block):
    return block.reshape(-1, block.shape[-1])


class Place:
    def __init__(self):
        self.dp = lax.axis_index("dp")
        self.t = lax.axis_index("tensor")
        self.core = lax.rem(self.dp, CC)
        self.x = lax.rem(lax.div(self.dp, CC), XC)
        self.z = lax.div(self.dp, CC * XC)

    def at(self, z, x, core):
        return (z * XC + x) * CC + core

    def z_peer(self, d):
        return {"dp": self.at(lax.rem(self.z + d, ZC), self.x, self.core)}

    def x_peer(self):
        return {"dp": self.at(self.z, 1 - self.x, self.core)}

    def core_peer(self):
        return {"dp": self.at(self.z, self.x, 1 - self.core)}

    def y_peer(self):
        return {"tensor": 1 - self.t}

    def layer_peers(self):
        res = []
        for k in range(1, 8):
            x = 1 - self.x if k & 1 else self.x
            t = 1 - self.t if k & 2 else self.t
            core = 1 - self.core if k & 4 else self.core
            res.append({"dp": self.at(self.z, x, core), "tensor": t})
        return res

    def greet(self):
        bar = pltpu.get_barrier_semaphore()
        peers = [self.z_peer(d) for d in (1, 2, 3)] + self.layer_peers()
        for p in peers:
            pl.semaphore_signal(bar, inc=1, device_id=p, device_id_type=MESH)
        return bar, len(peers)


def remote(src, dst, ss, rs, peer):
    return pltpu.make_async_remote_copy(
        src_ref=src, dst_ref=dst, send_sem=ss, recv_sem=rs, device_id=peer, device_id_type=MESH
    )


def split_cols(width):
    a = (width // 128 + 1) // 2 * 128
    return ((0, a), (a, width - a))


class Gather:
    N_SEMS = 12

    def __init__(self, place, pieces, sems):
        self.p = place
        self.pieces = pieces
        self.sems = sems

    def own(self, c, h):
        p = self.p
        _, o, w, order = self.pieces[c][0][h]
        index = (p.z, p.x, p.core, slice(None), pl.ds(o, w))
        return self.pieces[c][1].at[(p.t,) + index if "y" in order else index]

    def copies(self, c, h, k):
        p = self.p
        src, o, w, order = self.pieces[c][0][h]
        sem = self.sems.at[c, h]
        if k == 0:
            dst = self.own(c, h)
            return [
                remote(src, dst, sem.at[d - 1], sem.at[2 + d], p.z_peer(d)) for d in (1, 2, 3)
            ]
        done = order[:k]
        every = slice(None)
        index = (every, every if "x" in done else p.x, p.core, every, pl.ds(o, w))
        if "y" in order:
            index = (every if "y" in done else p.t,) + index
        view = self.pieces[c][1].at[index]
        if k == len(order):
            peer = p.core_peer()
        else:
            peer = p.x_peer() if order[k] == "x" else p.y_peer()
        return [remote(view, view, sem.at[4 + 2 * k], sem.at[5 + 2 * k], peer)]

    def each(self, c, k):
        res = []
        for h, (_, _, _, order) in enumerate(self.pieces[c][0]):
            if k <= len(order):
                res += self.copies(c, h, k)
        return res

    def start(self, c, k):
        for cp in self.each(c, k):
            cp.start()

    def run(self, ops):
        for op in ops:
            if isinstance(op, int):
                self.start(op, 0)
                continue
            c, k = op
            for cp in self.each(c, k):
                cp.wait()
            self.start(c, k + 1)


class AllSum:
    N_SEMS = 20

    def __init__(self, place, buf, got, sems):
        self.p = place
        self.buf, self.got, self.sems = buf, got, sems

    def copies(self, k):
        peers = [self.p.z_peer(d) for d in (1, 2, 3)] if k else self.p.layer_peers()
        base = 7 if k else 0
        return [
            remote(
                self.buf,
                self.got.at[base + i],
                self.sems.at[2 * (base + i)],
                self.sems.at[2 * (base + i) + 1],
                peer,
            )
            for i, peer in enumerate(peers)
        ]

    def start(self, k):
        for cp in self.copies(k):
            cp.start()

    def end(self, k):
        for cp in self.copies(k):
            cp.wait()
        total = self.buf[...]
        for i in range(7, 10) if k else range(7):
            total = total + self.got[i]
        self.buf[...] = total


def normal_rows(rows):
    mean = jnp.mean(rows, axis=-1, keepdims=True)
    centre = rows - mean
    var = jnp.mean(centre * centre, axis=-1, keepdims=True)
    scale = lax.rsqrt(var + EPS)
    return centre * scale, scale


def rotate_t(v, cosine, sine):
    a, b = v[0:8], v[8:16]
    return jnp.concatenate([a * cosine - b * sine, b * cosine + a * sine, v[16:]], axis=0)


def unrotate_t(v, cosine, sine):
    a, b = v[0:8], v[8:16]
    return jnp.concatenate([a * cosine + b * sine, b * cosine - a * sine, v[16:]], axis=0)


def fill_bias(place, lens_ref, other_ref, own_ref, S):
    t = place.t
    for m in range(MB):
        limit = lens_ref[m]
        key = lax.broadcasted_iota(jnp.int32, (S, 128), 0)
        limit_other = jnp.where(t == 1, limit, 0)
        other_ref[m] = jnp.where(key < limit_other, 0.0, NEG).astype(F32)
        key = lax.broadcasted_iota(jnp.int32, (S, S), 0)
        row = lax.broadcasted_iota(jnp.int32, (S, S), 1)
        own = (key <= row) & (key + t * S < limit)
        own_ref[m] = jnp.where(own, 0.0, NEG).astype(F32)


def masked_rows(place_t, lens_ref, dy, start, S):
    m, off = divmod(start, S)
    pos = place_t * S + off + lax.broadcasted_iota(jnp.int32, (dy.shape[0], 1), 0)
    return jnp.where(pos < lens_ref[m], dy.astype(F32), 0.0)


class Reduce:
    def __init__(self, place, pieces, rc, r2a, r2b, r3, r4, sems):
        self.p = place
        self.pieces = pieces
        self.rc, self.r2a, self.r2b, self.r3, self.r4 = rc, r2a, r2b, r3, r4
        self.sems = sems

    def cols(self, c, h):
        widths = self.pieces[c][1]
        return sum(widths[:h]), widths[h]

    def halves(self, c):
        return range(len(self.pieces[c][1]))

    def cores(self, c):
        g, w = self.pieces[c][0], sum(self.pieces[c][1])
        return remote(
            g.at[:, :, :, 1 - self.p.core],
            self.rc.at[c, :, :, :, :, pl.ds(0, w)],
            self.sems.at[c, 0],
            self.sems.at[c, 1],
            self.p.core_peer(),
        )

    def second(self, c, h):
        p = self.p
        o, w = self.cols(c, h)
        if h == 0:
            src, dst, peer = self.rc.at[c, 1 - p.t, :, :, :, pl.ds(o, w)], self.r2a, p.y_peer()
        else:
            src, dst, peer = self.rc.at[c, :, :, 1 - p.x, :, pl.ds(o, w)], self.r2b, p.x_peer()
        dst = dst.at[c, :, :, :, pl.ds(0, w)]
        return remote(src, dst, self.sems.at[c, 2 + 2 * h], self.sems.at[c, 3 + 2 * h], peer)

    def third(self, c, h):
        p = self.p
        o, w = self.cols(c, h)
        if h == 0:
            src, peer = self.r2a.at[c, :, 1 - p.x, :, pl.ds(0, w)], p.x_peer()
        else:
            src, peer = self.r2b.at[c, 1 - p.t, :, :, pl.ds(0, w)], p.y_peer()
        dst = self.r3.at[c, h, :, :, pl.ds(0, w)]
        return remote(src, dst, self.sems.at[c, 6 + 2 * h], self.sems.at[c, 7 + 2 * h], peer)

    def last(self, c, h, d):
        p = self.p
        o, w = self.cols(c, h)
        src = self.r3.at[c, h, lax.rem(p.z + d, ZC), :, pl.ds(0, w)]
        dst = self.r4.at[c, h, d - 1, :, pl.ds(0, w)]
        k = 10 + (h * 3 + d - 1) * 2
        return remote(src, dst, self.sems.at[c, k], self.sems.at[c, k + 1], p.z_peer(d))

    N_SEMS = 22

    def begin(self, c):
        self.cores(c).start()

    def step1(self, c):
        p = self.p
        g, width = self.pieces[c][0], sum(self.pieces[c][1])
        self.cores(c).wait()
        own = g[:, :, :, p.core]
        mine = self.rc[c, :, :, :, :, 0:width].astype(F32) + own.astype(F32)
        self.rc[c, :, :, :, :, 0:width] = mine.astype(BF)
        for h in self.halves(c):
            self.second(c, h).start()

    def step2(self, c):
        p = self.p
        for h in self.halves(c):
            self.second(c, h).wait()
            o, w = self.cols(c, h)
            if h == 0:
                ref, mine = self.r2a, self.rc[c, p.t, :, :, :, o : o + w]
            else:
                ref, mine = self.r2b, self.rc[c, :, :, p.x, :, o : o + w]
            mine = mine.astype(F32) + ref[c, :, :, :, 0:w].astype(F32)
            ref[c, :, :, :, 0:w] = mine.astype(BF)
            self.third(c, h).start()

    def step3(self, c):
        p = self.p
        for h in self.halves(c):
            self.third(c, h).wait()
            o, w = self.cols(c, h)
            mine = self.r2a[c, :, p.x, :, 0:w] if h == 0 else self.r2b[c, p.t, :, :, 0:w]
            mine = mine.astype(F32) + self.r3[c, h, :, :, 0:w].astype(F32)
            self.r3[c, h, :, :, 0:w] = mine.astype(BF)
            for d in (1, 2, 3):
                self.last(c, h, d).start()

    def step4(self, c):
        p = self.p
        parts = []
        for h in self.halves(c):
            o, w = self.cols(c, h)
            for d in (1, 2, 3):
                self.last(c, h, d).wait()
            total = self.r3[c, h, p.z, :, 0:w].astype(F32)
            for d in range(3):
                total = total + self.r4[c, h, d, :, 0:w].astype(F32)
            parts.append(total)
        self.pieces[c][2](parts)

    def step(self, i, lo, hi):
        for late, act in ((4, self.step4), (3, self.step3), (2, self.step2), (0, self.step1)):
            c = lo + i - late
            if lo <= c < hi:
                act(c)


HEAD_OPS = (
    (0, 1, 2),
    ((0, 0), (1, 0), 3),
    ((0, 1), (2, 0), 4),
    ((1, 1), (0, 2), (3, 0), 5),
    ((1, 2), (2, 1)),
    ((1, 3), (4, 0), 6),
)
ATTENTION_OPS = {
    0: ((2, 2), (3, 1), (5, 0), 7),
    3: ((2, 3), (3, 2), (4, 1), (6, 0), 8),
    6: ((3, 3), (4, 2), (5, 1), (7, 0)),
}
MIDDLE_OPS = ((4, 3), (5, 2), (6, 1), (8, 0))
FFN_OPS = {
    1: ((5, 3), (6, 2), (7, 1)),
    2: ((6, 3), (7, 2), (8, 1)),
    3: ((7, 3), (8, 2)),
    4: ((8, 3),),
}
FFN_LAG = 2
BACK_FIRST, BACK_EVERY = 0, 2
LAST_STEP = 4


def block_kernel(
    dims,
    x_ref,
    dy_hbm,
    lens_ref,
    tab_ref,
    g1_ref,
    b1_ref,
    g2_ref,
    b2_ref,
    wq_in,
    bq_ref,
    wsh_in,
    bsh_ref,
    wout_in,
    bout_ref,
    wup_in,
    bup_ref,
    wdown_in,
    bdown_ref,
    out_hbm,
    gx_hbm,
    wf,
    grads,
    early,
    late,
    wsh,
    wq,
    wb,
    won,
    wv,
    ball,
    bcol,
    dym,
    h1,
    h2,
    qt,
    att,
    da,
    tmp,
    acc,
    dh2,
    lse_ref,
    kvt,
    kvo,
    kc,
    vc,
    kt,
    vte,
    bias_o,
    bias_s,
    dkv,
    dkvs,
    dkvr,
    dkvn,
    gring,
    gb,
    gq,
    gkv,
    sums,
    early_in,
    late_in,
    rc,
    r2a,
    r2b,
    r3,
    r4,
    gsem,
    rsem,
    lsem,
    wsem,
    ysem,
    esem,
    asem,
):
    S, HT, NH, NF, T = dims["S"], dims["HT"], dims["NH"], dims["NF"], dims["T"]
    D = x_ref.shape[1]
    R = wq_in.shape[0]
    NB = S // 256
    p = Place()
    bar, npeers = p.greet()
    dy_copy = pltpu.make_async_copy(dy_hbm, dym, lsem.at[0])
    dy_copy.start()

    def halves(ref):
        return [
            (ref.at[:, pl.ds(o, w)], o, w, order)
            for (o, w), order in zip(split_cols(HT), ("zxy", "zyx"))
        ]

    pieces = [([(wsh_in, 0, 128, "zx")], wsh), (halves(wq_in), wq), (halves(wout_in), wb)]
    for f in range(NF):
        cols = pl.ds(256 * f, 256)
        parts = [(wup_in.at[:, cols], 0, 256, "zxy"), (wdown_in.at[:, cols], 256, 256, "zyx")]
        pieces.append((parts, wf.at[f]))
    g = Gather(p, pieces, gsem)
    pl.semaphore_wait(bar, npeers)
    g.run(HEAD_OPS[0])
    locals_ = []
    for c in range(len(pieces)):
        for h in range(len(pieces[c][0])):
            own = pltpu.make_async_copy(pieces[c][0][h][0], g.own(c, h), lsem.at[1 + 2 * c + h])
            own.start()
            locals_.append(own)
    first = HT // 128
    rows_b = ball.shape[1]
    ball[p.t, 0:first, :] = bq_ref[...].reshape(first, 128)
    ball[p.t, first : first + 2 * NF, :] = bup_ref[...].reshape(2 * NF, 128)
    ball[p.t, first + 2 * NF :, :] = jnp.zeros((rows_b - first - 2 * NF, 128), F32)
    bias_copy = remote(ball.at[p.t], ball.at[p.t], ysem.at[0], ysem.at[1], p.y_peer())
    bias_copy.start()

    gain1, shift1, gain2, shift2 = (
        ref[...].reshape(1, D) for ref in (g1_ref, b1_ref, g2_ref, b2_ref)
    )

    def norm_block(i):
        rows = pl.ds(pl.multiple_of(i * 128, 128), 128)
        z, _ = normal_rows(x_ref[rows, :].astype(F32))
        h1[rows, :] = (z * gain1 + shift1).astype(BF)
        h2[rows, :] = (z * gain2 + shift2).astype(BF)

    half = T // 256
    pl.loop(0, half)(norm_block)
    for cp in locals_:
        cp.wait()
    g.run(HEAD_OPS[1])
    pl.loop(half, 2 * half)(norm_block)
    g.run(HEAD_OPS[2])
    fill_bias(p, lens_ref, bias_o, bias_s, S)
    bias_copy.wait()
    nq = HT // 128
    for t in range(2):
        for j in range(nq):
            row = jnp.broadcast_to(ball[t, j : j + 1, :], (128, 128))
            bcol[(t * nq + j) * 128 : (t * nq + j + 1) * 128, :] = row.T
    bcol[2 * HT : 2 * HT + 128, :] = jnp.broadcast_to(bsh_ref[...].reshape(1, 128), (128, 128)).T
    g.run(HEAD_OPS[3])

    id256 = eye(256)
    cosine, sine = tab_ref[p.t, 0:8, :], tab_ref[p.t, 8:16, :]
    wsh_t = nt(eye(128), flat(wsh[...])).astype(BF)
    kv_copies = [
        remote(kvt.at[m], kvo.at[m], ysem.at[2 + 2 * m], ysem.at[3 + 2 * m], p.y_peer())
        for m in range(MB)
    ]
    for m in range(MB):
        kv = nt(wsh_t, h1[m * S : m * S + S, :]) + bcol[2 * HT : 2 * HT + 128, 0:1]
        kvt[m, 0:HEAD_DIM, :] = rotate_t(kv[0:HEAD_DIM], cosine, sine).astype(BF)
        kvt[m, HEAD_DIM:, :] = kv[HEAD_DIM:].astype(BF)
        kv_copies[m].start()
    g.run(HEAD_OPS[4])
    dy_copy.wait()
    sums[...] = jnp.zeros_like(sums)
    for b in range(T // 256):
        rows = slice(b * 256, b * 256 + 256)
        dy = masked_rows(p.t, lens_ref, dym[rows, :], b * 256, S)
        dym[rows, :] = dy.astype(BF)
        sums[6:7, :] += jnp.sum(dy, axis=0, keepdims=True)
    g.run(HEAD_OPS[5])

    for t in range(2):
        wq_t = nt(eye(HT), flat(wq[t])).astype(BF)
        for m in range(MB):
            cols = slice(m * S, m * S + S)
            q = nt(wq_t, h1[cols, :])
            for h in range(HT // HEAD_DIM):
                base = t * HT + h * HEAD_DIM
                qh = q[h * HEAD_DIM : (h + 1) * HEAD_DIM] + bcol[base : base + HEAD_DIM, 0:1]
                qh = rotate_t(qh, cosine, sine) * (0.125 * LOG2E)
                qt[base : base + HEAD_DIM, cols] = qh.astype(BF)

    def both_halves(m):
        kv_copies[m].wait()
        for part, src in ((0, kvo), (1, kvt)):
            keys = slice(part * S, part * S + S)
            kt[m, :, keys] = src[m, 0:HEAD_DIM, :]
            vte[m, 0:HEAD_DIM, keys] = src[m, HEAD_DIM:, :]
        vte[m, HEAD_DIM:, :] = (
            lax.broadcasted_iota(jnp.int32, (16, 2 * S), 0) == 0
        ).astype(BF)
        for b in range(2 * NB):
            blk = slice(b * 256, b * 256 + 256)
            kc[m, blk, :] = nt(id256, kt[m, :, blk]).astype(BF)
            vc[m, blk, :] = nt(id256, vte[m, 0:HEAD_DIM, blk]).astype(BF)

    both_halves(0)

    def spots(i, group):
        res = []
        for u in range(group):
            j = i * group + u
            m, h = lax.div(j, NH), lax.rem(j, NH)
            head = pl.ds(pl.multiple_of(h * HEAD_DIM, HEAD_DIM), HEAD_DIM)
            for r in range(NB):
                cols = pl.ds(pl.multiple_of(m * S + r * 256, 256), 256)
                res.append((j, m, head, cols, S + 256 * (r + 1), r))
        return res

    def scores(m, q, nk, r):
        s = nn(kc[m, 0:nk, :], q)
        wide = slice(r * 256, r * 256 + 256)
        other = bias_o[m]
        other = jnp.concatenate([other, other], axis=1)
        return jnp.concatenate([s[0:S] + other, s[S:nk] + bias_s[m, 0 : nk - S, wide]], axis=0)

    group = 3

    @pl.loop(0, MB * NH // group)
    def _(i):
        for m in range(1, MB):
            pl.when(i == m * NH // group)(partial(both_halves, m))
        for at, ops in ATTENTION_OPS.items():
            pl.when(i == at)(partial(g.run, ops))
        todo = spots(i, group)
        sc = [scores(m, qt[head, cols], nk, r) for _, m, head, cols, nk, r in todo]
        tops = [jnp.max(s, axis=0, keepdims=True) for s in sc]
        ex = [jnp.exp2(s - top).astype(BF) for s, top in zip(sc, tops)]
        for (j, m, head, cols, nk, r), e, top in zip(todo, ex, tops):
            o = nn(vte[m, :, 0:nk], e)
            total = o[HEAD_DIM : HEAD_DIM + 1]
            att[head, cols] = (o[0:HEAD_DIM] * (1.0 / total)).astype(BF)
            lse_ref[j, :, r * 256 : r * 256 + 256] = top + jnp.log2(total)

    g.run(MIDDLE_OPS)
    for t in range(2):
        won[t * HT : (t + 1) * HT, :] = nt(eye(HT), flat(wb[t])).astype(BF)

    def load(f, slot):
        return pltpu.make_async_copy(wf.at[f], wv.at[slot], wsem.at[slot])

    load(0, 0).start()
    for b in range(T // 256):
        rows = slice(b * 256, b * 256 + 256)
        tmp[rows, :] = nt(id256, att[:, rows]).astype(BF)
    tail_bias = (bout_ref[...] + bdown_ref[...]).reshape(1, D)
    acc[...] = x_ref[...].astype(F32) + tail_bias + nn(tmp[...], won[...])
    for t in range(2):
        cols = slice(t * HT, (t + 1) * HT)
        gb[t] = tn(dym[...], tmp[:, cols]).astype(BF).reshape(ZC, XC, CC, R, HT)

    def put(*firsts):
        def store(parts):
            for o, v in zip(firsts, parts):
                grads[:, o : o + v.shape[1]] = v

        return store

    wide = [w for _, w in split_cols(HT)]
    at_out, at_up, at_down = HT + 128, 2 * HT + 128, 2 * HT + 128 + 256 * NF
    sums_of = [(gb, wide, put(at_out, at_out + wide[0]))]
    for f in range(NF):
        sums_of.append((gring.at[f % 3], [256, 256], put(at_up + 256 * f, at_down + 256 * f)))
    sums_of += [(gq, wide, put(0, wide[0])), (gkv, [128], put(HT))]
    red = Reduce(p, sums_of, rc, r2a, r2b, r3, r4, rsem)
    last = NF + 1
    red.begin(0)
    dh2[...] = jnp.zeros_like(dh2)

    @pl.loop(0, NF)
    def _(f):
        slot = lax.rem(f, 2)
        load(f, slot).wait()
        for k in range(NF - 1):

            @pl.when(f == k)
            def _():
                g.run(FFN_OPS.get(k, ()))
                load(k + 1, (k + 1) % 2).start()

        for k in range(FFN_LAG, NF):
            pl.when(f == k)(partial(red.step, k - FFN_LAG, 0, last))
        wu = [flat(wv[slot, t, :, :, :, :, 0:256]) for t in range(2)]
        wd = [flat(wv[slot, t, :, :, :, :, 256:512]) for t in range(2)]
        gslot = lax.rem(f, 3)
        hid = [nn(h2[...], wu[t]) for t in range(2)]
        dact = [nn(dym[...], wd[t]) for t in range(2)]
        act, dhid = [], []
        for t in range(2):
            row = jnp.concatenate(
                [ball[t, pl.ds(first + 2 * f, 1), :], ball[t, pl.ds(first + 2 * f + 1, 1), :]],
                axis=1,
            )
            u = hid[t] + row
            cdf = 0.5 + 0.5 * lax.erf(u * 0.7071067811865476)
            dens = jnp.exp(-0.5 * u * u) * 0.3989422804014327
            act.append((u * cdf).astype(BF))
            d = (dact[t] * (cdf + u * dens)).astype(BF)
            dhid.append(d)
            total = jnp.sum(d.astype(F32), axis=0, keepdims=True)
            for j in (0, 1):
                at = D // 128 + 4 * f + 2 * t + j
                early[pl.ds(at, 1), :] = total[:, 128 * j : 128 * j + 128]
        acc[...] += nt(act[0], wd[0]) + nt(act[1], wd[1])
        dh2[...] += nt(dhid[0], wu[0]) + nt(dhid[1], wu[1])
        for t in range(2):
            gd = tn(dym[...], act[t]).astype(BF)
            gring[gslot, t, :, :, :, :, 256:512] = gd.reshape(ZC, XC, CC, R, 256)
            gu = tn(h2[...], dhid[t]).astype(BF)
            gring[gslot, t, :, :, :, :, 0:256] = gu.reshape(ZC, XC, CC, R, 256)
        for k in range(NF):
            pl.when(f == k)(partial(red.begin, 1 + k))

    h2[...] = acc[...].astype(BF)
    out_copy = pltpu.make_async_copy(h2, out_hbm, lsem.at[0])
    out_copy.start()

    n = D // 128
    early[0:n, :] = sums[6:7, :].reshape(n, 128)
    early[n + 4 * NF :, :] = jnp.zeros((early.shape[0] - n - 4 * NF, 128), F32)
    early_sum = AllSum(p, early, early_in, esem)
    early_sum.start(0)

    da[...] = nt(won[...], dym[...]).astype(BF)
    dkv[...] = jnp.zeros_like(dkv)
    back = 2
    dkv_copies = [
        remote(dkvs.at[m], dkvr.at[m], ysem.at[6 + 2 * m], ysem.at[7 + 2 * m], p.y_peer())
        for m in range(MB)
    ]

    def send_dkv(m):
        dkvs[m] = dkv[m, 0:S, :].astype(BF)
        dkv_copies[m].start()

    def early_next():
        early_sum.end(0)
        early_sum.start(1)

    @pl.loop(0, MB * NH // back)
    def _(i):
        for m in range(1, MB):
            pl.when(i == m * NH // back)(partial(send_dkv, m - 1))
        pl.when(i == 2)(early_next)
        for k in range(NF - FFN_LAG, last + LAST_STEP):
            at = BACK_FIRST + BACK_EVERY * (k - (NF - FFN_LAG))
            pl.when(i == at)(partial(red.step, k, 0, last))
        todo = spots(i, back)
        qs = [qt[head, cols] for _, m, head, cols, nk, r in todo]
        das = [da[head, cols] for _, m, head, cols, nk, r in todo]
        sc = [scores(m, q, nk, r) for (_, m, head, cols, nk, r), q in zip(todo, qs)]
        dp = [nn(vc[m, 0:nk, :], d) for (_, m, head, cols, nk, r), d in zip(todo, das)]
        pr, ds = [], []
        for (j, m, head, cols, nk, r), d, s, dpj in zip(todo, das, sc, dp):
            delta = jnp.sum(d.astype(F32) * att[head, cols].astype(F32), axis=0, keepdims=True)
            w = jnp.exp2(s - lse_ref[j, :, r * 256 : r * 256 + 256])
            pr.append(w.astype(BF))
            ds.append((w * (dpj - delta)).astype(BF))
        for (j, m, head, cols, nk, r), d in zip(todo, ds):
            wide = slice(r * 256, r * 256 + 256)
            dq = nn(kt[m, :, 0:nk], d)
            dq = unrotate_t(dq, tab_ref[p.t, 0:8, wide], tab_ref[p.t, 8:16, wide])
            qt[head, cols] = (dq * 0.125).astype(BF)
        m = todo[0][1]
        for blk in range(NB):
            lo = 0 if blk == 0 else S + 256 * blk
            hi = S + 256 * (blk + 1)
            left, right = [], []
            for u, (_, _, _, _, nk, r) in enumerate(todo):
                if nk >= hi:
                    zero = jnp.zeros_like(qs[u])
                    left += [ds[u][lo:hi], pr[u][lo:hi]]
                    right += [
                        jnp.concatenate([qs[u], zero], axis=0),
                        jnp.concatenate([zero, das[u]], axis=0),
                    ]
            dkv[m, lo:hi, :] += nt(
                jnp.concatenate(left, axis=1), jnp.concatenate(right, axis=1)
            )

    send_dkv(MB - 1)
    for k in range(NF - FFN_LAG, last + LAST_STEP):
        if BACK_FIRST + BACK_EVERY * (k - (NF - FFN_LAG)) >= MB * NH // back:
            red.step(k, 0, last)
    for b in range(T // 256):
        rows = slice(b * 256, b * 256 + 256)
        tmp[rows, :] = nt(id256, qt[:, rows]).astype(BF)
    for t in range(2):
        v = tn(h1[...], tmp[:, t * HT : (t + 1) * HT]).astype(BF)
        gq[t] = v.reshape(ZC, XC, CC, R, HT)
    red.begin(last)

    def own_dkv(m):
        dkv_copies[m].wait()
        both = (dkv[m, S : 2 * S, :] + dkvr[m].astype(F32)).T
        dk = unrotate_t(both[0:HEAD_DIM], cosine, sine) * LN2
        both = jnp.concatenate([dk, both[HEAD_DIM:]], axis=0).astype(BF)
        for b in range(NB):
            rows = slice(m * S + b * 256, m * S + b * 256 + 256)
            dkvn[rows, :] = nt(id256, both[:, b * 256 : b * 256 + 256]).astype(BF)

    wqf = [flat(wq[t]) for t in range(2)]
    wshf = flat(wsh[...])

    def input_grad(b):
        rows = slice(b * 256, b * 256 + 256)
        dq, dkvb = tmp[rows, :], dkvn[rows, :]
        dh1 = nt(dq[:, 0:HT], wqf[0]) + nt(dq[:, HT:], wqf[1]) + nt(dkvb, wshf)
        dh2b = dh2[rows, :]
        z, scale = normal_rows(x_ref[rows, :].astype(F32))
        dy = dym[rows, :].astype(F32)
        e = dh1 * gain1 + dh2b * gain2
        back_in = scale * (
            e - jnp.mean(e, axis=-1, keepdims=True) - z * jnp.mean(e * z, axis=-1, keepdims=True)
        )
        tmp[rows, :] = (dy + back_in).astype(BF)
        for k, v in enumerate((dh1 * z, dh1, dh2b * z, dh2b, dq.astype(F32))):
            sums[k : k + 1, :] += jnp.sum(v, axis=0, keepdims=True)
        sums[5:6, 0:128] += jnp.sum(dkvb.astype(F32), axis=0, keepdims=True)

    own_dkv(0)
    input_grad(0)
    red.step1(last)
    input_grad(1)
    own_dkv(1)
    gkvs = tn(h1[...], dkvn[...]).astype(BF).reshape(ZC, XC, CC, R, 128)
    for t in range(2):
        gkv[t] = gkvs
    red.begin(last + 1)
    input_grad(2)
    red.step2(last)
    input_grad(3)
    red.step1(last + 1)
    gx_copy = pltpu.make_async_copy(tmp, gx_hbm, lsem.at[1])
    gx_copy.start()
    for k in range(5):
        late[k * n : k * n + n, :] = sums[k : k + 1, :].reshape(n, 128)
    late[5 * n : 5 * n + 1, :] = sums[5:6, 0:128]
    late[5 * n + 1 :, :] = jnp.zeros((late.shape[0] - 5 * n - 1, 128), F32)
    late_sum = AllSum(p, late, late_in, asem)
    late_sum.start(0)
    early_sum.end(1)
    red.step3(last)
    red.step2(last + 1)
    late_sum.end(0)
    late_sum.start(1)
    red.step4(last)
    red.step3(last + 1)
    red.step4(last + 1)
    late_sum.end(1)
    out_copy.wait()
    gx_copy.wait()


def finish_kernel(dims, out_in, gx_in, grads, early, late, *refs):
    (out, gx, g1, b1, g2, b2, gq, bq, gkv, bkv, go, bo, gup, bup, gdn, bd, held, sem) = refs
    HT, NF = dims["HT"], dims["NF"]
    there, back = [], []
    for k, (src, dst) in enumerate(((out_in, out), (gx_in, gx))):
        there.append(pltpu.make_async_copy(src, held.at[k], sem.at[2 * k]))
        back.append(pltpu.make_async_copy(held.at[k], dst, sem.at[2 * k + 1]))
    for cp in there:
        cp.start()
    t = lax.axis_index("tensor")
    n = g1.shape[0] // 128
    for cp, then in zip(there, back):
        cp.wait()
        then.start()
    for k, ref in enumerate((g1, b1, g2, b2)):
        ref[...] = late[k * n : k * n + n, :].reshape(n * 128)
    half = HT // 128
    bq[...] = late[pl.ds(4 * n + half * t, half), :].reshape(HT)
    bkv[...] = late[5 * n : 5 * n + 1, :].reshape(128)
    total = early[0:n, :].reshape(n * 128)
    bo[...] = total
    bd[...] = total
    for f in range(NF):
        for j in (0, 1):
            at = 256 * f + 128 * j
            bup[at : at + 128] = early[pl.ds(n + 4 * f + 2 * t + j, 1), :].reshape(128)
    at = 0
    for ref in (gq, gkv, go, gup, gdn):
        width = ref.shape[1]
        ref[...] = grads[:, at : at + width]
        at += width
    for cp in back:
        cp.wait()


def angle_table(S):
    places = np.arange(2 * S, dtype=np.float64)
    freqs = 10000.0 ** (-np.arange(ROT // 2) * 2.0 / ROT)
    angles = (places[:, None] * freqs[None, :]).astype(np.float32).astype(np.float64)
    tab = np.concatenate([np.cos(angles).T, np.sin(angles).T], axis=0).astype(np.float32)
    return tab.reshape(ROT, 2, S).transpose(1, 0, 2)


def token_plan(
    block_input,
    cotangent,
    lengths,
    ln1_gain,
    ln1_bias,
    ln2_gain,
    ln2_bias,
    w_query,
    b_query,
    w_shared,
    b_shared,
    w_out,
    b_out,
    w_up,
    b_up,
    w_down,
    b_down,
):
    S, D = block_input.shape[2:]
    R, HT = w_query.shape
    FT = w_up.shape[1]
    NF, T, NH = FT // 256, MB * S, 2 * HT // HEAD_DIM
    dims = dict(S=S, HT=HT, NF=NF, T=T, NH=NH)
    plane = (ZC, XC, CC, R)
    full = (2,) + plane
    t = lax.axis_index("tensor")

    def s(shape, dtype):
        return jax.ShapeDtypeStruct(shape, dtype)

    vm = pl.BlockSpec(memory_space=VMEM)
    hbm = pl.BlockSpec(memory_space=pl.ANY)
    smem = pl.BlockSpec(memory_space=pltpu.SMEM)

    nb = HT // 128 + 2 * NF + 1
    np_ = NF + 3
    n_early, n_late = 8 * ((D // 128 + 4 * NF + 7) // 8), 8 * ((5 * (D // 128) + 8) // 8)
    n_grads = 2 * HT + 128 + 2 * FT

    outs = pl.pallas_call(
        partial(block_kernel, dims),
        out_shape=[
            s((T, D), BF),
            s((T, D), BF),
            s((NF,) + full + (512,), BF),
            s((R, n_grads), F32),
            s((n_early, 128), F32),
            s((n_late, 128), F32),
        ],
        in_specs=[vm, hbm, smem] + [vm] * 15,
        out_specs=[hbm] * 3 + [vm] * 3,
        scratch_shapes=[
            VMEM(plane + (128,), BF),
            VMEM(full + (HT,), BF),
            VMEM(full + (HT,), BF),
            VMEM((2 * HT, D), BF),
            VMEM((2,) + full + (512,), BF),
            VMEM((2, nb, 128), F32),
            VMEM((2 * HT + 128, 128), F32),
            VMEM((T, D), BF),
            VMEM((T, D), BF),
            VMEM((T, D), BF),
            VMEM((D, T), BF),
            VMEM((D, T), BF),
            VMEM((D, T), BF),
            VMEM((T, D), BF),
            VMEM((T, D), F32),
            VMEM((T, D), F32),
            VMEM((MB * NH, 1, S), F32),
            VMEM((MB, 128, S), BF),
            VMEM((MB, 128, S), BF),
            VMEM((MB, 2 * S, HEAD_DIM), BF),
            VMEM((MB, 2 * S, HEAD_DIM), BF),
            VMEM((MB, HEAD_DIM, 2 * S), BF),
            VMEM((MB, HEAD_DIM + 16, 2 * S), BF),
            VMEM((MB, S, 128), F32),
            VMEM((MB, S, S), F32),
            VMEM((MB, 2 * S, 128), F32),
            VMEM((MB, S, 128), BF),
            VMEM((MB, S, 128), BF),
            VMEM((T, 128), BF),
            VMEM((3,) + full + (512,), BF),
            VMEM(full + (HT,), BF),
            VMEM(full + (HT,), BF),
            VMEM(full + (128,), BF),
            VMEM((8, D), F32),
            VMEM((10, n_early, 128), F32),
            VMEM((10, n_late, 128), F32),
            VMEM((np_, 2, ZC, XC, R, 512), BF),
            VMEM((np_, ZC, XC, R, 256), BF),
            VMEM((np_, 2, ZC, R, 256), BF),
            VMEM((np_, 2, ZC, R, 256), BF),
            VMEM((np_, 2, 3, R, 256), BF),
            DMA((np_, 2, Gather.N_SEMS)),
            DMA((np_, Reduce.N_SEMS)),
            DMA((1 + 2 * np_,)),
            DMA((2,)),
            DMA((6 + 2 * MB,)),
            DMA((AllSum.N_SEMS,)),
            DMA((AllSum.N_SEMS,)),
        ],
        compiler_params=pltpu.CompilerParams(
            vmem_limit_bytes=64 * MIB - 65536, collective_id=0, has_side_effects=True
        ),
        name="block",
    )(
        block_input.reshape(T, D),
        cotangent.reshape(T, D),
        lengths.reshape(MB),
        jnp.asarray(angle_table(S)),
        ln1_gain,
        ln1_bias,
        ln2_gain,
        ln2_bias,
        w_query,
        b_query,
        w_shared,
        b_shared,
        w_out.T,
        b_out,
        w_up,
        b_up,
        w_down.T,
        b_down,
    )
    out, gx, _, grads, early, late = outs
    vec = s((D,), F32)
    shapes = [s((T, D), BF), s((T, D), BF), vec, vec, vec, vec, s((R, HT), F32), s((HT,), F32)]
    shapes += [s((R, 128), F32), s((128,), F32), s((R, HT), F32), vec, s((R, FT), F32)]
    shapes += [s((FT,), F32), s((R, FT), F32), vec]
    outs = pl.pallas_call(
        partial(finish_kernel, dims),
        out_shape=shapes,
        in_specs=[hbm, hbm, vm, vm, vm],
        out_specs=[hbm, hbm] + [vm] * 14,
        scratch_shapes=[VMEM((2, T, D), BF), DMA((4,))],
        compiler_params=pltpu.CompilerParams(vmem_limit_bytes=16 * MIB),
        name="finish",
    )(out, gx, grads, early, late)
    res = list(outs)
    res[0] = res[0].reshape(block_input.shape)
    res[1] = res[1].reshape(block_input.shape)
    res[10] = res[10].T
    res[14] = res[14].T
    return tuple(res)


def fits_token_plan(mesh):
    return dict(mesh.shape) == {"dp": ZC * XC * CC, "tensor": 2}


def solution(mesh):
    in_specs = (
        P(None, "dp", "tensor", None),
        P(None, "dp", "tensor", None),
        P(None, "dp"),
        P(),
        P(),
        P(),
        P(),
        P("dp", "tensor"),
        P("tensor"),
        P("dp", None),
        P(),
        P("tensor", "dp"),
        P(),
        P("dp", "tensor"),
        P("tensor"),
        P("tensor", "dp"),
        P(),
    )
    out_specs = (
        P(None, "dp", "tensor", None),
        P(None, "dp", "tensor", None),
        P(),
        P(),
        P(),
        P(),
        P("dp", "tensor"),
        P("tensor"),
        P("dp", None),
        P(),
        P("tensor", "dp"),
        P(),
        P("dp", "tensor"),
        P("tensor"),
        P("tensor", "dp"),
        P(),
    )
    step = token_plan if fits_token_plan(mesh) else per_device
    return jax.shard_map(
        step, mesh=mesh, in_specs=in_specs, out_specs=out_specs, check_vma=False
    )
```

```python
from functools import partial

import jax
import jax.numpy as jnp
import numpy as np
from jax import lax
from jax.experimental import pallas as pl
from jax.experimental.pallas import tpu as pltpu
from jax.sharding import PartitionSpec as P

HEAD_DIM = 64
ROT = 16
MB = 2
QBLK = 512


EPS = 1e-05


def tables(count):
    places = jnp.arange(count).astype(jnp.float32)
    freqs = jnp.power(10000.0, -jnp.arange(ROT // 2).astype(jnp.float32) * 2.0 / ROT)
    angles = places[:, None] * freqs[None, :]
    return (jnp.cos(angles)[:, None, :], jnp.sin(angles)[:, None, :])


def rotate(vector, cosine, sine):
    first = vector[..., : ROT // 2]
    second = vector[..., ROT // 2 : ROT]
    return jnp.concatenate(
        [first * cosine - second * sine, second * cosine + first * sine, vector[..., ROT:]], axis=-1
    )


def unrotate(grad, cosine, sine):
    first = grad[..., : ROT // 2]
    second = grad[..., ROT // 2 : ROT]
    return jnp.concatenate(
        [first * cosine + second * sine, second * cosine - first * sine, grad[..., ROT:]], axis=-1
    )


def normalize(vector):
    centre = vector - jnp.mean(vector, axis=-1, keepdims=True)
    spread = jnp.mean(centre * centre, axis=-1, keepdims=True)
    scale = lax.rsqrt(spread + EPS)
    return (centre * scale, scale)


def norm_back(grad, normed, scale, gain):
    weighted = grad * gain
    return scale * (
        weighted
        - jnp.mean(weighted, axis=-1, keepdims=True)
        - normed * jnp.mean(weighted * normed, axis=-1, keepdims=True)
    )


def block_scores(rows, keys, start, limit, count):
    scores = jnp.einsum("qhd,kd->hqk", rows, keys, preferred_element_type=jnp.float32)
    row_pos = start + jnp.arange(QBLK)
    key_pos = jnp.arange(count)
    allowed = (key_pos[None, :] <= row_pos[:, None]) & (key_pos[None, :] < limit)
    return (scores, allowed[None])


def attend(queries, keys, values, limit):
    count = queries.shape[0]

    def block(start):
        rows = lax.dynamic_slice_in_dim(queries, start, QBLK, 0)
        scores, allowed = block_scores(rows, keys, start, limit, count)
        scores = jnp.where(allowed, scores, jnp.float32(-1e30))
        top = jnp.max(scores, axis=-1, keepdims=True)
        expo = jnp.exp(scores - top)
        total = jnp.sum(expo, axis=-1, keepdims=True)
        weights = (expo / total).astype(jnp.bfloat16)
        result = jnp.einsum("hqk,kd->qhd", weights, values, preferred_element_type=jnp.float32)
        return (result, (top + jnp.log(total))[..., 0])

    starts = jnp.arange(count // QBLK) * QBLK
    results, logsum = lax.map(block, starts)
    return (results.reshape(count, -1, HEAD_DIM), logsum)


def attend_back(queries, keys, values, limit, logsum, grad_out):
    count = queries.shape[0]

    def block(carry, item):
        start, block_logsum = item
        rows = lax.dynamic_slice_in_dim(queries, start, QBLK, 0)
        grads = lax.dynamic_slice_in_dim(grad_out, start, QBLK, 0)
        scores, allowed = block_scores(rows, keys, start, limit, count)
        probs = jnp.where(allowed, jnp.exp(scores - block_logsum[:, :, None]), 0.0)
        weights = probs.astype(jnp.bfloat16)
        dprobs = jnp.einsum("qhd,kd->hqk", grads, values, preferred_element_type=jnp.float32)
        delta = jnp.sum(probs * dprobs, axis=-1, keepdims=True)
        dscores = (probs * (dprobs - delta)).astype(jnp.bfloat16)
        drows = jnp.einsum("hqk,kd->qhd", dscores, keys, preferred_element_type=jnp.float32)
        dkeys = carry[0] + jnp.einsum(
            "hqk,qhd->kd", dscores, rows, preferred_element_type=jnp.float32
        )
        dvalues = carry[1] + jnp.einsum(
            "hqk,qhd->kd", weights, grads, preferred_element_type=jnp.float32
        )
        return ((dkeys, dvalues), drows)

    starts = jnp.arange(count // QBLK) * QBLK
    empty = jnp.zeros((count, HEAD_DIM), jnp.float32)
    (dkeys, dvalues), drows = lax.scan(block, (empty, empty), (starts, logsum))
    return (drows.reshape(count, -1, HEAD_DIM), dkeys, dvalues)


def fetch_each(w_query, w_shared, w_out, w_up, w_down):
    return (
        lax.all_gather(w_query, "dp", axis=0, tiled=True),
        lax.all_gather(w_shared, "dp", axis=0, tiled=True),
        lax.all_gather(w_out, "dp", axis=1, tiled=True),
        lax.all_gather(w_up, "dp", axis=0, tiled=True),
        lax.all_gather(w_down, "dp", axis=1, tiled=True),
    )


def reduce_each(step_grads):
    return (
        lax.psum_scatter(step_grads[0], "dp", scatter_dimension=0, tiled=True),
        lax.psum_scatter(step_grads[1], "dp", scatter_dimension=0, tiled=True),
        lax.psum_scatter(step_grads[2], "dp", scatter_dimension=1, tiled=True),
        lax.psum_scatter(step_grads[3], "dp", scatter_dimension=0, tiled=True),
        lax.psum_scatter(step_grads[4], "dp", scatter_dimension=1, tiled=True),
    )


def per_device(
    block_input,
    cotangent,
    lengths,
    ln1_gain,
    ln1_bias,
    ln2_gain,
    ln2_bias,
    w_query,
    b_query,
    w_shared,
    b_shared,
    w_out,
    b_out,
    w_up,
    b_up,
    w_down,
    b_down,
):
    shard_rows = block_input.shape[2]
    groups = lax.axis_size("tensor")
    rank = lax.axis_index("tensor")
    seq_len = shard_rows * groups
    tail_bias = b_out + b_down
    weight_sums = None
    cos_all, sin_all = tables(seq_len)
    own_pos = rank * shard_rows + jnp.arange(shard_rows)
    outputs = []
    input_grads = []
    sum_bq = jnp.zeros(b_query.shape, jnp.float32)
    sum_bkv = jnp.zeros(b_shared.shape, jnp.float32)
    sum_bup = jnp.zeros(b_up.shape, jnp.float32)
    sum_gain1 = jnp.zeros(ln1_gain.shape, jnp.float32)
    sum_shift1 = jnp.zeros(ln1_gain.shape, jnp.float32)
    sum_gain2 = jnp.zeros(ln1_gain.shape, jnp.float32)
    sum_shift2 = jnp.zeros(ln1_gain.shape, jnp.float32)
    sum_out = jnp.zeros(ln1_gain.shape, jnp.float32)
    for micro in range(MB):
        fetched = fetch_each(w_query, w_shared, w_out, w_up, w_down)
        wq_all, wkv_all, wo_all, wup_all, wdown_all = fetched
        limit = lengths[micro, 0]
        inputs = block_input[micro, 0].astype(jnp.float32)
        normed_one, scale_one = normalize(inputs)
        normed_two, scale_two = normalize(inputs)
        low_one = (normed_one * ln1_gain + ln1_bias).astype(jnp.bfloat16)
        low_two = (normed_two * ln2_gain + ln2_bias).astype(jnp.bfloat16)
        whole_one, whole_two = (
            lax.all_gather(low_one, "tensor", axis=0, tiled=True),
            lax.all_gather(low_two, "tensor", axis=0, tiled=True),
        )
        query_lin = jnp.dot(whole_one, wq_all, preferred_element_type=jnp.float32) + b_query
        query_lin = query_lin.reshape(seq_len, -1, HEAD_DIM)
        queries = (rotate(query_lin, cos_all, sin_all) * 0.125).astype(jnp.bfloat16)
        shared = jnp.dot(whole_one, wkv_all, preferred_element_type=jnp.float32) + b_shared
        keys = rotate(shared[:, None, :HEAD_DIM], cos_all, sin_all)[:, 0].astype(jnp.bfloat16)
        values = shared[:, HEAD_DIM:].astype(jnp.bfloat16)
        attended, logsum = attend(queries, keys, values, limit)
        attended_low = attended.reshape(seq_len, -1).astype(jnp.bfloat16)
        hidden = jnp.dot(whole_two, wup_all, preferred_element_type=jnp.float32) + b_up
        active = jax.nn.gelu(hidden, approximate=False).astype(jnp.bfloat16)
        partial_out = jnp.dot(attended_low, wo_all, preferred_element_type=jnp.float32) + jnp.dot(
            active, wdown_all, preferred_element_type=jnp.float32
        )
        branch = lax.psum_scatter(partial_out, "tensor", scatter_dimension=0, tiled=True)
        outputs.append((inputs + branch + tail_bias).astype(jnp.bfloat16))
        valid = (own_pos < limit).astype(jnp.float32)[:, None]
        upstream = cotangent[micro, 0].astype(jnp.float32) * valid
        whole_up = lax.all_gather(upstream.astype(jnp.bfloat16), "tensor", axis=0, tiled=True)
        sum_out = sum_out + jnp.sum(upstream, axis=0)
        grad_down = jnp.einsum("lf,ld->fd", active, whole_up, preferred_element_type=jnp.float32)
        dactive = jnp.einsum("ld,fd->lf", whole_up, wdown_all, preferred_element_type=jnp.float32)
        gelu_pull = jax.vjp(partial(jax.nn.gelu, approximate=False), hidden)[1]
        dhidden = gelu_pull(dactive)[0].astype(jnp.bfloat16)
        sum_bup = sum_bup + jnp.sum(dhidden.astype(jnp.float32), axis=0)
        grad_up = jnp.einsum("ld,lf->df", whole_two, dhidden, preferred_element_type=jnp.float32)
        dnormed_two = jnp.einsum("lf,df->ld", dhidden, wup_all, preferred_element_type=jnp.float32)
        dattended = jnp.einsum("ld,ed->le", whole_up, wo_all, preferred_element_type=jnp.float32)
        dattended = dattended.astype(jnp.bfloat16).reshape(seq_len, -1, HEAD_DIM)
        grad_out = jnp.einsum(
            "le,ld->ed", attended_low, whole_up, preferred_element_type=jnp.float32
        )
        dqueries, dkeys, dvalues = attend_back(queries, keys, values, limit, logsum, dattended)
        dquery_lin = (
            unrotate(dqueries * 0.125, cos_all, sin_all).reshape(seq_len, -1).astype(jnp.bfloat16)
        )
        dkey_lin = unrotate(dkeys[:, None, :], cos_all, sin_all)[:, 0]
        dshared = lax.psum(jnp.concatenate([dkey_lin, dvalues], axis=1), "tensor")
        dshared = dshared.astype(jnp.bfloat16)
        sum_bq = sum_bq + jnp.sum(dquery_lin.astype(jnp.float32), axis=0)
        sum_bkv = sum_bkv + jnp.sum(dshared.astype(jnp.float32), axis=0)
        grad_q = jnp.einsum("ld,le->de", whole_one, dquery_lin, preferred_element_type=jnp.float32)
        grad_kv = jnp.einsum("ld,lc->dc", whole_one, dshared, preferred_element_type=jnp.float32)
        dnormed_one = jnp.einsum(
            "le,de->ld", dquery_lin, wq_all, preferred_element_type=jnp.float32
        )
        dnormed_one, dnormed_two = (
            lax.psum_scatter(dnormed_one, "tensor", scatter_dimension=0, tiled=True),
            lax.psum_scatter(dnormed_two, "tensor", scatter_dimension=0, tiled=True),
        )
        own_shared = lax.dynamic_slice_in_dim(dshared, rank * shard_rows, shard_rows, 0)
        dnormed_one = dnormed_one + jnp.einsum(
            "lc,dc->ld", own_shared, wkv_all, preferred_element_type=jnp.float32
        )
        sum_gain1 = sum_gain1 + jnp.sum(dnormed_one * normed_one, axis=0)
        sum_shift1 = sum_shift1 + jnp.sum(dnormed_one, axis=0)
        sum_gain2 = sum_gain2 + jnp.sum(dnormed_two * normed_two, axis=0)
        sum_shift2 = sum_shift2 + jnp.sum(dnormed_two, axis=0)
        dinputs = (
            upstream
            + norm_back(dnormed_one, normed_one, scale_one, ln1_gain)
            + norm_back(dnormed_two, normed_two, scale_two, ln2_gain)
        )
        input_grads.append(dinputs.astype(jnp.bfloat16))
        step_grads = (grad_q, grad_kv, grad_out, grad_up, grad_down)
        step_grads = reduce_each(step_grads)
        if weight_sums is None:
            weight_sums = step_grads
        else:
            weight_sums = jax.tree.map(jnp.add, weight_sums, step_grads)
    output = jnp.stack(outputs, axis=0)[:, None]
    grad_input = jnp.stack(input_grads, axis=0)[:, None]
    sum_bq, sum_bkv, sum_bup = lax.psum((sum_bq, sum_bkv, sum_bup), "dp")
    sum_gain1, sum_shift1, sum_gain2, sum_shift2, sum_out = lax.psum(
        (sum_gain1, sum_shift1, sum_gain2, sum_shift2, sum_out), ("dp", "tensor")
    )
    grad_q, grad_kv, grad_o, grad_up, grad_down = weight_sums
    return (
        output,
        grad_input,
        sum_gain1,
        sum_shift1,
        sum_gain2,
        sum_shift2,
        grad_q,
        sum_bq,
        grad_kv,
        sum_bkv,
        grad_o,
        sum_out,
        grad_up,
        sum_bup,
        grad_down,
        sum_out,
    )


MESH = pl.DeviceIdType.MESH
BF = jnp.bfloat16
F32 = jnp.float32
LOG2E = 1.4426950408889634
LN2 = 0.6931471805599453
NEG = -1e30
ZC, XC, CC = 4, 2, 2
DMA = pltpu.SemaphoreType.DMA
VMEM = pltpu.VMEM
VMEM_LIMIT = (64 << 20) - 65536


def nn(a, b):
    return lax.dot_general(a, b, (((1,), (0,)), ((), ())), preferred_element_type=F32)


def nt(a, b):
    return lax.dot_general(a, b, (((1,), (1,)), ((), ())), preferred_element_type=F32)


def tn(a, b):
    return lax.dot_general(a, b, (((0,), (0,)), ((), ())), preferred_element_type=F32)


def eye(n):
    return (
        lax.broadcasted_iota(jnp.int32, (n, n), 0) == lax.broadcasted_iota(jnp.int32, (n, n), 1)
    ).astype(BF)


def flat(block):
    return block.reshape(-1, block.shape[-1])


class Place:
    def __init__(self):
        self.dp = lax.axis_index("dp")
        self.t = lax.axis_index("tensor")
        self.core = lax.rem(self.dp, CC)
        self.x = lax.rem(lax.div(self.dp, CC), XC)
        self.z = lax.div(self.dp, CC * XC)

    def at(self, z, x, core):
        return (z * XC + x) * CC + core

    def z_peer(self, d):
        return {"dp": self.at(lax.rem(self.z + d, ZC), self.x, self.core)}

    def x_peer(self):
        return {"dp": self.at(self.z, 1 - self.x, self.core)}

    def core_peer(self):
        return {"dp": self.at(self.z, self.x, 1 - self.core)}

    def y_peer(self):
        return {"tensor": 1 - self.t}

    def layer_peers(self):
        res = []
        for k in range(1, 8):
            x = 1 - self.x if k & 1 else self.x
            t = 1 - self.t if k & 2 else self.t
            core = 1 - self.core if k & 4 else self.core
            res.append({"dp": self.at(self.z, x, core), "tensor": t})
        return res

    def greet(self):
        bar = pltpu.get_barrier_semaphore()
        peers = [self.z_peer(d) for d in (1, 2, 3)] + self.layer_peers()
        for p in peers:
            pl.semaphore_signal(bar, inc=1, device_id=p, device_id_type=MESH)
        return bar, len(peers)


def remote(src, dst, ss, rs, peer):
    return pltpu.make_async_remote_copy(
        src_ref=src, dst_ref=dst, send_sem=ss, recv_sem=rs, device_id=peer, device_id_type=MESH
    )


def split_cols(width):
    a = (width // 128 + 1) // 2 * 128
    return ((0, a), (a, width - a))


class Gather:
    SLOTS = 3

    def __init__(self, place, pieces, sends, gots):
        self.p = place
        self.pieces = pieces
        self.sends, self.gots = sends, gots

    def own(self, c, h):
        p = self.p
        _, o, w, order = self.pieces[c][0][h]
        index = (p.z, p.x, p.core, slice(None), pl.ds(o, w))
        return self.pieces[c][1].at[(p.t,) + index if "y" in order else index]

    def copies(self, c, k):
        p = self.p
        every = slice(None)
        res = []
        for h, (src, o, w, order) in enumerate(self.pieces[c][0]):
            if k == 0:
                pairs = [(src, self.own(c, h), p.z_peer(d)) for d in (1, 2, 3)]
            elif k <= len(order):
                done = order[:k]
                index = (every, every if "x" in done else p.x, p.core, every, pl.ds(o, w))
                if "y" in order:
                    index = (every if "y" in done else p.t,) + index
                view = self.pieces[c][1].at[index]
                axis = order[k] if k < len(order) else "core"
                peers = {"x": p.x_peer(), "y": p.y_peer(), "core": p.core_peer()}
                pairs = [(view, view, peers[axis])]
            else:
                pairs = []
            for a, b, peer in pairs:
                res.append(remote(a, b, self.sends.at[c % self.SLOTS, k], self.gots.at[c, k], peer))
        return res

    def total(self, c, k):
        parts, out = self.pieces[c]
        z = pl.ds(0, 3) if k == 0 else slice(None)
        x = slice(None) if k > 1 else 0
        index = (z, x, 0)
        if "y" in parts[0][3]:
            index = (slice(None) if k > 2 else 0,) + index
        view = out.at[index]
        return remote(
            view, view, self.sends.at[c % self.SLOTS, k], self.gots.at[c, k], self.p.core_peer()
        )

    def run(self, ops):
        for op in ops:
            c, k = (op, -1) if isinstance(op, int) else op
            if k >= 0:
                self.total(c, k).wait()
            for cp in self.copies(c, k + 1):
                cp.start()


class AllSum:
    def __init__(self, place, buf, got, sems):
        self.p = place
        self.buf, self.got, self.sems = buf, got, sems

    def part(self, k):
        return (7, 3) if k else (0, 7)

    def start(self, k):
        peers = [self.p.z_peer(d) for d in (1, 2, 3)] if k else self.p.layer_peers()
        at, _ = self.part(k)
        for i, peer in enumerate(peers):
            got = self.got.at[at + i]
            remote(self.buf, got, self.sems.at[2 * k], self.sems.at[2 * k + 1], peer).start()

    def end(self, k):
        at, n = self.part(k)
        view = self.got.at[pl.ds(at, n)]
        whole = remote(
            view, view, self.sems.at[2 * k], self.sems.at[2 * k + 1], self.p.core_peer()
        )
        whole.wait()
        total = self.buf[...]
        for i in range(at, at + n):
            total = total + self.got[i]
        self.buf[...] = total


def normal_rows(rows):
    mean = jnp.mean(rows, axis=-1, keepdims=True)
    centre = rows - mean
    var = jnp.mean(centre * centre, axis=-1, keepdims=True)
    scale = lax.rsqrt(var + EPS)
    return centre * scale, scale


def rotate_t(v, cosine, sine):
    a, b = v[0:8], v[8:16]
    return jnp.concatenate([a * cosine - b * sine, b * cosine + a * sine, v[16:]], axis=0)


def unrotate_t(v, cosine, sine):
    a, b = v[0:8], v[8:16]
    return jnp.concatenate([a * cosine + b * sine, b * cosine - a * sine, v[16:]], axis=0)


def fill_bias(place, lens_ref, other_ref, own_ref, S):
    t = place.t
    for m in range(MB):
        limit = lens_ref[m]
        key = lax.broadcasted_iota(jnp.int32, (S, 128), 0)
        limit_other = jnp.where(t == 1, limit, 0)
        other_ref[m] = jnp.where(key < limit_other, 0.0, NEG).astype(F32)
        key = lax.broadcasted_iota(jnp.int32, (S, S), 0)
        row = lax.broadcasted_iota(jnp.int32, (S, S), 1)
        own = (key <= row) & (key + t * S < limit)
        own_ref[m] = jnp.where(own, 0.0, NEG).astype(F32)


def masked_rows(place_t, lens_ref, dy, start, S):
    m, off = divmod(start, S)
    pos = place_t * S + off + lax.broadcasted_iota(jnp.int32, (dy.shape[0], 1), 0)
    return jnp.where(pos < lens_ref[m], dy.astype(F32), 0.0)


class Reduce:
    SLOTS = 3

    def __init__(self, place, pieces, rc, r2a, r2b, r3, r4, sends, gots):
        self.p = place
        self.pieces = pieces
        self.rc, self.r2a, self.r2b, self.r3, self.r4 = rc, r2a, r2b, r3, r4
        self.sends, self.gots = sends, gots

    def part(self, c, h):
        r, n, o, w = self.pieces[c][1][h]
        _, first, _, second = self.pieces[c][3]
        o += first
        return (slice(r, r + n), slice(o, o + w)), (slice(0, n), slice(second, second + w))

    def wide(self, c):
        first = self.pieces[c][3][1]
        return slice(first, first + self.pieces[c][0].shape[-1])

    def sems(self, c, k):
        return self.sends.at[c % self.SLOTS, k], self.gots.at[c, k]

    def copies(self, c, k):
        p = self.p
        if k == 0:
            src = self.pieces[c][0].at[:, :, :, 1 - p.core]
            dst = self.rc.at[self.pieces[c][3][0], :, :, :, :, self.wide(c)]
            return [remote(src, dst, *self.sems(c, k), p.core_peer())]
        res = []
        a, _, b, _ = self.pieces[c][3]
        for h in (0, 1):
            here, there = self.part(c, h)
            if k == 1 and h == 0:
                src, dst = self.rc.at[(a, 1 - p.t, slice(None), slice(None)) + here], self.r2a
                todo = [(src, dst.at[(b, slice(None), slice(None)) + there], p.y_peer())]
            elif k == 1:
                src, dst = self.rc.at[(a, slice(None), slice(None), 1 - p.x) + here], self.r2b
                todo = [(src, dst.at[(b, slice(None), slice(None)) + there], p.x_peer())]
            elif k == 2:
                if h == 0:
                    src, peer = self.r2a.at[(b, slice(None), 1 - p.x) + there], p.x_peer()
                else:
                    src, peer = self.r2b.at[(b, 1 - p.t, slice(None)) + there], p.y_peer()
                todo = [(src, self.r3.at[(b, h, slice(None)) + there], peer)]
            else:
                todo = [
                    (
                        self.r3.at[(b, h, lax.rem(p.z + d, ZC)) + there],
                        self.r4.at[(b, h, d - 1) + there],
                        p.z_peer(d),
                    )
                    for d in (1, 2, 3)
                ]
            res += [remote(src, dst, *self.sems(c, k), peer) for src, dst, peer in todo]
        return res

    def total(self, c, k):
        cols = self.wide(c)
        every = slice(None)
        index = {
            0: (every, every, every, every, cols),
            1: (0, every, every, every, cols),
            2: (0, every, 0, every, cols),
            3: (0, pl.ds(0, 3), 0, every, cols),
        }[k]
        view = self.rc.at[(self.pieces[c][3][0],) + index]
        return remote(view, view, *self.sems(c, k), self.p.core_peer())

    def start(self, c, k):
        for cp in self.copies(c, k):
            cp.start()

    def add(self, c, k):
        p = self.p
        a, _, b, _ = self.pieces[c][3]
        if k == 1:
            cols = self.wide(c)
            mine = self.pieces[c][0][:, :, :, p.core].astype(F32)
            mine = mine + self.rc[a, :, :, :, :, cols].astype(F32)
            self.rc[a, :, :, :, :, cols] = mine.astype(BF)
            return
        sums = []
        for h in (0, 1):
            here, there = self.part(c, h)
            every = slice(None)
            if k == 2:
                if h == 0:
                    ref, mine = self.r2a, self.rc[(a, p.t, every, every) + here]
                else:
                    ref, mine = self.r2b, self.rc[(a, every, every, p.x) + here]
                at = (b, every, every) + there
                ref[at] = (mine.astype(F32) + ref[at].astype(F32)).astype(BF)
            elif k == 3:
                if h == 0:
                    mine = self.r2a[(b, every, p.x) + there]
                else:
                    mine = self.r2b[(b, p.t, every) + there]
                at = (b, h, every) + there
                self.r3[at] = (mine.astype(F32) + self.r3[at].astype(F32)).astype(BF)
            else:
                total = self.r3[(b, h, p.z) + there].astype(F32)
                for d in range(3):
                    total = total + self.r4[(b, h, d) + there].astype(F32)
                sums.append(total)
        if k == 4:
            self.pieces[c][2](sums)

    def run(self, ops):
        for c, k in ops:
            if k:
                self.total(c, k - 1).wait()
                self.add(c, k)
            if k < 4:
                self.start(c, k)


HEAD_OPS = (
    (0, 1),
    ((0, 0), (1, 0), 2),
    ((0, 1), (1, 1), (2, 0), 3),
    ((0, 2), (1, 2), (3, 0), 4, 5),
    ((2, 1),),
    ((1, 3), (4, 0), 6),
)
ATTENTION_OPS = {
    0: ((2, 2), (3, 1), (5, 0), 7),
    3: ((2, 3), (3, 2), (4, 1), (6, 0), 8),
    6: ((3, 3), (4, 2), (5, 1), (7, 0)),
}
MIDDLE_OPS = ((4, 3), (5, 2), (6, 1), (8, 0))
FFN_OPS = {
    1: ((5, 3), (6, 2), (7, 1)),
    2: ((6, 3), (7, 2), (8, 1)),
    3: ((7, 3), (8, 2)),
    4: ((8, 3),),
}
FFN_SUMS = {
    2: ((0, 1),),
    3: ((1, 1),),
    4: ((0, 2), (2, 1)),
    5: ((0, 3), (1, 2), (3, 1)),
}
BACK_SUMS = {
    0: ((0, 4), (1, 3), (2, 2), (4, 1)),
    2: ((1, 4), (2, 3), (3, 2), (5, 1)),
    4: ((2, 4), (3, 3), (4, 2), (6, 1)),
    6: ((3, 4), (4, 3), (5, 2)),
    8: ((4, 4), (5, 3), (6, 2)),
    9: ((7, 1),),
    10: ((5, 4), (6, 3)),
    11: ((7, 2), (8, 1)),
}
LAST_SUMS = (
    ((6, 4), (7, 3), (8, 2)),
    ((9, 1), (7, 4), (8, 3)),
    ((9, 2),),
    ((10, 1), (9, 3)),
    ((10, 2), (8, 4), (9, 4)),
    ((10, 3), (10, 4)),
)


def block_kernel(
    dims,
    x_hbm,
    dy_hbm,
    lens_ref,
    tab_ref,
    g1_ref,
    b1_ref,
    g2_ref,
    b2_ref,
    wq_in,
    bq_ref,
    wsh_in,
    bsh_ref,
    wout_in,
    bout_ref,
    wup_in,
    bup_ref,
    wdown_in,
    bdown_ref,
    out_hbm,
    gx_hbm,
    wf,
    grads,
    early,
    late,
    wsh,
    wq,
    wb,
    won,
    wv,
    ball,
    bcol,
    x_ref,
    dym,
    h1,
    h2,
    qt,
    att,
    da,
    tmp,
    acc,
    dh2,
    lse_ref,
    kvt,
    kvo,
    kc,
    vc,
    kt,
    vte,
    bias_o,
    bias_s,
    dkv,
    dkvs,
    dkvr,
    dkvn,
    gring,
    gb,
    gq,
    gkv,
    sums,
    early_in,
    late_in,
    rc,
    r2a,
    r2b,
    r3,
    r4,
    gsend,
    gsem,
    rsend,
    rsem,
    lsem,
    wsem,
    ysem,
    esem,
    asem,
):
    S, HT, NH, NF, T = dims["S"], dims["HT"], dims["NH"], dims["NF"], dims["T"]
    D = x_ref.shape[1]
    R = wq_in.shape[0]
    NB = S // 256
    p = Place()
    bar, npeers = p.greet()
    x_copy = pltpu.make_async_copy(x_hbm, x_ref, lsem.at[1])
    x_copy.start()
    dy_copy = pltpu.make_async_copy(dy_hbm, dym, lsem.at[0])
    dy_copy.start()

    def parts_of(ref, widths, orders):
        at = [sum(widths[:i]) for i in range(len(widths))]
        return [(ref.at[:, pl.ds(o, w)], o, w, order) for o, w, order in zip(at, widths, orders)]

    wide = [w for _, w in split_cols(HT)]
    pieces = [
        ([(wsh_in, 0, 128, "zx")], wsh),
        (parts_of(wq_in, wide, ("zxy", "zyx")), wq),
        (parts_of(wout_in, wide, ("zxy", "zyx")), wb),
    ]
    for f in range(NF):
        cols = pl.ds(256 * f, 256)
        parts = [(wup_in.at[:, cols], 0, 256, "zxy"), (wdown_in.at[:, cols], 256, 256, "zyx")]
        pieces.append((parts, wf.at[f]))
    g = Gather(p, pieces, gsend, gsem)
    pl.semaphore_wait(bar, npeers)
    g.run(HEAD_OPS[0])
    locals_ = [
        pltpu.make_async_copy(wsh_in, wsh.at[p.z, p.x, p.core], lsem.at[2]),
        pltpu.make_async_copy(wq_in, wq.at[p.t, p.z, p.x, p.core], lsem.at[3]),
        pltpu.make_async_copy(wout_in, wb.at[p.t, p.z, p.x, p.core], lsem.at[4]),
    ]
    for cp in locals_:
        cp.start()
    for c in range(3, len(pieces)):
        for h in (0, 1):
            pltpu.make_async_copy(pieces[c][0][h][0], g.own(c, h), lsem.at[5]).start()
    held = wf.at[:, 0, 0, 0, 0]
    locals_.append(pltpu.make_async_copy(held, held, lsem.at[5]))
    first = HT // 128
    rows_b = ball.shape[1]
    ball[p.t, 0:first, :] = bq_ref[...].reshape(first, 128)
    ball[p.t, first : first + 2 * NF, :] = bup_ref[...].reshape(2 * NF, 128)
    ball[p.t, first + 2 * NF :, :] = jnp.zeros((rows_b - first - 2 * NF, 128), F32)
    bias_copy = remote(ball.at[p.t], ball.at[p.t], ysem.at[0], ysem.at[1], p.y_peer())
    bias_copy.start()

    gain1, shift1, gain2, shift2 = (
        ref[...].reshape(1, D) for ref in (g1_ref, b1_ref, g2_ref, b2_ref)
    )

    def norm_block(i):
        rows = pl.ds(pl.multiple_of(i * 128, 128), 128)
        z, _ = normal_rows(x_ref[rows, :].astype(F32))
        h1[rows, :] = (z * gain1 + shift1).astype(BF)
        h2[rows, :] = (z * gain2 + shift2).astype(BF)

    half = T // 256
    x_copy.wait()
    pl.loop(0, half)(norm_block)
    for cp in locals_:
        cp.wait()
    g.run(HEAD_OPS[1])
    pl.loop(half, 2 * half)(norm_block)
    g.run(HEAD_OPS[2])
    fill_bias(p, lens_ref, bias_o, bias_s, S)
    bias_copy.wait()
    nq = HT // 128
    for t in range(2):
        for j in range(nq):
            row = jnp.broadcast_to(ball[t, j : j + 1, :], (128, 128))
            bcol[(t * nq + j) * 128 : (t * nq + j + 1) * 128, :] = row.T
    bcol[2 * HT : 2 * HT + 128, :] = jnp.broadcast_to(bsh_ref[...].reshape(1, 128), (128, 128)).T
    g.run(HEAD_OPS[3])

    id256 = eye(256)
    cosine, sine = tab_ref[p.t, 0:8, :], tab_ref[p.t, 8:16, :]
    wsh_t = nt(eye(128), flat(wsh[...])).astype(BF)
    kv_copies = [
        remote(kvt.at[m], kvo.at[m], ysem.at[2 + 2 * m], ysem.at[3 + 2 * m], p.y_peer())
        for m in range(MB)
    ]
    for m in range(MB):
        kv = nt(wsh_t, h1[m * S : m * S + S, :]) + bcol[2 * HT : 2 * HT + 128, 0:1]
        kvt[m, 0:HEAD_DIM, :] = rotate_t(kv[0:HEAD_DIM], cosine, sine).astype(BF)
        kvt[m, HEAD_DIM:, :] = kv[HEAD_DIM:].astype(BF)
        kv_copies[m].start()
    g.run(HEAD_OPS[4])
    dy_copy.wait()
    sums[...] = jnp.zeros_like(sums)
    for b in range(T // 256):
        rows = slice(b * 256, b * 256 + 256)
        dy = masked_rows(p.t, lens_ref, dym[rows, :], b * 256, S)
        dym[rows, :] = dy.astype(BF)
        sums[6:7, :] += jnp.sum(dy, axis=0, keepdims=True)
    g.run(HEAD_OPS[5])

    for t in range(2):
        wq_t = nt(eye(HT), flat(wq[t])).astype(BF)
        for m in range(MB):
            cols = slice(m * S, m * S + S)
            q = nt(wq_t, h1[cols, :])
            for h in range(HT // HEAD_DIM):
                base = t * HT + h * HEAD_DIM
                qh = q[h * HEAD_DIM : (h + 1) * HEAD_DIM] + bcol[base : base + HEAD_DIM, 0:1]
                qh = rotate_t(qh, cosine, sine) * (0.125 * LOG2E)
                qt[base : base + HEAD_DIM, cols] = qh.astype(BF)

    def both_halves(m):
        kv_copies[m].wait()
        for part, src in ((0, kvo), (1, kvt)):
            keys = slice(part * S, part * S + S)
            kt[m, :, keys] = src[m, 0:HEAD_DIM, :]
            vte[m, 0:HEAD_DIM, keys] = src[m, HEAD_DIM:, :]
        vte[m, HEAD_DIM:, :] = (
            lax.broadcasted_iota(jnp.int32, (16, 2 * S), 0) == 0
        ).astype(BF)
        for b in range(2 * NB):
            blk = slice(b * 256, b * 256 + 256)
            kc[m, blk, :] = nt(id256, kt[m, :, blk]).astype(BF)
            vc[m, blk, :] = nt(id256, vte[m, 0:HEAD_DIM, blk]).astype(BF)

    both_halves(0)

    def spots(i, group, by_thirds=False):
        res = []
        for u in range(group):
            j = i * group + u
            m, h = lax.div(j, NH), lax.rem(j, NH)
            if by_thirds:
                k = lax.div(h, 2)
                h = lax.rem(k, 2) * (NH // 2) + lax.div(k, 2) * 2 + u
                j = m * NH + h
            head = pl.ds(pl.multiple_of(h * HEAD_DIM, HEAD_DIM), HEAD_DIM)
            for r in range(NB):
                cols = pl.ds(pl.multiple_of(m * S + r * 256, 256), 256)
                res.append((j, m, head, cols, S + 256 * (r + 1), r))
        return res

    def scores(m, q, nk, r):
        s = nn(kc[m, 0:nk, :], q)
        wide = slice(r * 256, r * 256 + 256)
        other = bias_o[m]
        other = jnp.concatenate([other, other], axis=1)
        return jnp.concatenate([s[0:S] + other, s[S:nk] + bias_s[m, 0 : nk - S, wide]], axis=0)

    group = 3

    @pl.loop(0, MB * NH // group)
    def _(i):
        for m in range(1, MB):
            pl.when(i == m * NH // group)(partial(both_halves, m))
        for at, ops in ATTENTION_OPS.items():
            pl.when(i == at)(partial(g.run, ops))
        todo = spots(i, group)
        sc = [scores(m, qt[head, cols], nk, r) for _, m, head, cols, nk, r in todo]
        tops = [jnp.max(s, axis=0, keepdims=True) for s in sc]
        ex = [jnp.exp2(s - top).astype(BF) for s, top in zip(sc, tops)]
        for (j, m, head, cols, nk, r), e, top in zip(todo, ex, tops):
            o = nn(vte[m, :, 0:nk], e)
            total = o[HEAD_DIM : HEAD_DIM + 1]
            att[head, cols] = (o[0:HEAD_DIM] * (1.0 / total)).astype(BF)
            lse_ref[j, :, r * 256 : r * 256 + 256] = top + jnp.log2(total)

    g.run(MIDDLE_OPS)
    for t in range(2):
        won[t * HT : (t + 1) * HT, :] = nt(eye(HT), flat(wb[t])).astype(BF)

    def load(f, slot):
        return pltpu.make_async_copy(wf.at[f], wv.at[slot], wsem.at[slot])

    load(0, 0).start()
    for b in range(T // 256):
        rows = slice(b * 256, b * 256 + 256)
        tmp[rows, :] = nt(id256, att[:, rows]).astype(BF)
    tail_bias = (bout_ref[...] + bdown_ref[...]).reshape(1, D)
    acc[...] = x_ref[...].astype(F32) + tail_bias + nn(tmp[...], won[...])
    for t in range(2):
        cols = slice(t * HT, (t + 1) * HT)
        gb[t] = tn(dym[...], tmp[:, cols]).astype(BF).reshape(ZC, XC, CC, R, HT)

    def put(*firsts):
        def store(parts):
            for o, v in zip(firsts, parts):
                grads[:, o : o + v.shape[1]] = v

        return store

    at_out, at_up, at_down = HT + 128, 2 * HT + 128, 2 * HT + 128 + 256 * NF
    thirds = HT // 128

    def by_cols(*widths):
        at = [sum(widths[:i]) for i in range(len(widths))]
        return [(0, R, o, w) for o, w in zip(at, widths)]

    def put_rows(first):
        def store(parts):
            r = 0
            for v in parts:
                grads[r : r + v.shape[0], first : first + 128] = v
                r += v.shape[0]

        return store

    by_rows = [(0, 32, 0, 128), (32, R - 32, 0, 128)]
    sums_of = [(gb, by_cols(*wide), put(at_out, at_out + wide[0]), (0, 0, 0, 0))]
    for f in range(NF):
        store = put(at_up + 256 * f, at_down + 256 * f)
        sums_of.append((gring.at[f % 3], by_cols(256, 256), store, (1 + f, 0, 1 + f, 0)))
    for k in range(thirds + 1):
        store = put_rows(128 * k)
        slot = (NF + 1, 128 * k, NF + 1 + k // 2, 128 * (k % 2))
        sums_of.append((gq.at[k] if k < thirds else gkv, by_rows, store, slot))
    red = Reduce(p, sums_of, rc, r2a, r2b, r3, r4, rsend, rsem)
    last = NF + 1
    red.run([(0, 0)])
    dh2[...] = jnp.zeros_like(dh2)

    @pl.loop(0, NF)
    def _(f):
        slot = lax.rem(f, 2)
        load(f, slot).wait()
        for k in range(NF - 1):

            @pl.when(f == k)
            def _():
                g.run(FFN_OPS.get(k, ()))
                load(k + 1, (k + 1) % 2).start()

        for k, ops in FFN_SUMS.items():
            pl.when(f == k)(partial(red.run, ops))
        wu = [flat(wv[slot, t, :, :, :, :, 0:256]) for t in range(2)]
        wd = [flat(wv[slot, t, :, :, :, :, 256:512]) for t in range(2)]
        gslot = lax.rem(f, 3)
        hid = [nn(h2[...], wu[t]) for t in range(2)]
        dact = [nn(dym[...], wd[t]) for t in range(2)]
        act, dhid = [], []
        for t in range(2):
            row = jnp.concatenate(
                [ball[t, pl.ds(first + 2 * f, 1), :], ball[t, pl.ds(first + 2 * f + 1, 1), :]],
                axis=1,
            )
            u = hid[t] + row
            cdf = 0.5 + 0.5 * lax.erf(u * 0.7071067811865476)
            dens = jnp.exp(-0.5 * u * u) * 0.3989422804014327
            act.append((u * cdf).astype(BF))
            d = (dact[t] * (cdf + u * dens)).astype(BF)
            dhid.append(d)
            total = jnp.sum(d.astype(F32), axis=0, keepdims=True)
            for j in (0, 1):
                at = D // 128 + 4 * f + 2 * t + j
                early[pl.ds(at, 1), :] = total[:, 128 * j : 128 * j + 128]
        acc[...] += nt(act[0], wd[0]) + nt(act[1], wd[1])
        dh2[...] += nt(dhid[0], wu[0]) + nt(dhid[1], wu[1])
        for t in range(2):
            gd = tn(dym[...], act[t]).astype(BF)
            gring[gslot, t, :, :, :, :, 256:512] = gd.reshape(ZC, XC, CC, R, 256)
            gu = tn(h2[...], dhid[t]).astype(BF)
            gring[gslot, t, :, :, :, :, 0:256] = gu.reshape(ZC, XC, CC, R, 256)
        for k in range(NF):
            pl.when(f == k)(partial(red.run, [(1 + k, 0)]))

    h2[...] = acc[...].astype(BF)
    out_copy = pltpu.make_async_copy(h2, out_hbm, lsem.at[6])
    out_copy.start()

    n = D // 128
    early[0:n, :] = sums[6:7, :].reshape(n, 128)
    early[n + 4 * NF :, :] = jnp.zeros((early.shape[0] - n - 4 * NF, 128), F32)
    early_sum = AllSum(p, early, early_in, esem)
    early_sum.start(0)

    da[...] = nt(won[...], dym[...]).astype(BF)
    dkv[...] = jnp.zeros_like(dkv)
    back = 2
    dkv_copies = [
        remote(dkvs.at[m], dkvr.at[m], ysem.at[6 + 2 * m], ysem.at[7 + 2 * m], p.y_peer())
        for m in range(MB)
    ]

    def send_dkv(m):
        dkvs[m] = dkv[m, 0:S, :].astype(BF)
        dkv_copies[m].start()

    def query_third(k):
        for t in range(2):
            at = t * HT + 128 * k
            for b in range(T // 256):
                rows = slice(b * 256, b * 256 + 256)
                tmp[rows, at : at + 128] = nt(id256, qt[at : at + 128, rows]).astype(BF)
            v = tn(h1[...], tmp[:, at : at + 128]).astype(BF)
            gq[k, t] = v.reshape(ZC, XC, CC, R, 128)
        red.run([(last + k, 0)])

    def early_next():
        early_sum.end(0)
        early_sum.start(1)

    @pl.loop(0, MB * NH // back)
    def _(i):
        for m in range(1, MB):
            pl.when(i == m * NH // back)(partial(send_dkv, m - 1))
        pl.when(i == 2)(early_next)
        for at, ops in BACK_SUMS.items():
            pl.when(i == at)(partial(red.run, ops))
        for k in range(thirds - 1):
            at = MB * NH // back - 2 * (thirds - 1 - k)
            pl.when(i == at)(partial(query_third, k))
        todo = spots(i, back, True)
        qs = [qt[head, cols] for _, m, head, cols, nk, r in todo]
        das = [da[head, cols] for _, m, head, cols, nk, r in todo]
        sc = [scores(m, q, nk, r) for (_, m, head, cols, nk, r), q in zip(todo, qs)]
        dp = [nn(vc[m, 0:nk, :], d) for (_, m, head, cols, nk, r), d in zip(todo, das)]
        pr, ds = [], []
        for (j, m, head, cols, nk, r), d, s, dpj in zip(todo, das, sc, dp):
            delta = jnp.sum(d.astype(F32) * att[head, cols].astype(F32), axis=0, keepdims=True)
            w = jnp.exp2(s - lse_ref[j, :, r * 256 : r * 256 + 256])
            pr.append(w.astype(BF))
            ds.append((w * (dpj - delta)).astype(BF))
        for (j, m, head, cols, nk, r), d in zip(todo, ds):
            wide = slice(r * 256, r * 256 + 256)
            dq = nn(kt[m, :, 0:nk], d)
            dq = unrotate_t(dq, tab_ref[p.t, 0:8, wide], tab_ref[p.t, 8:16, wide])
            qt[head, cols] = (dq * 0.125).astype(BF)
        m = todo[0][1]
        for blk in range(NB):
            lo = 0 if blk == 0 else S + 256 * blk
            hi = S + 256 * (blk + 1)
            left, right = [], []
            for u, (_, _, _, _, nk, r) in enumerate(todo):
                if nk >= hi:
                    zero = jnp.zeros_like(qs[u])
                    left += [ds[u][lo:hi], pr[u][lo:hi]]
                    right += [
                        jnp.concatenate([qs[u], zero], axis=0),
                        jnp.concatenate([zero, das[u]], axis=0),
                    ]
            dkv[m, lo:hi, :] += nt(
                jnp.concatenate(left, axis=1), jnp.concatenate(right, axis=1)
            )

    send_dkv(MB - 1)
    query_third(thirds - 1)
    red.run(LAST_SUMS[0])

    def own_dkv(m):
        dkv_copies[m].wait()
        both = (dkv[m, S : 2 * S, :] + dkvr[m].astype(F32)).T
        dk = unrotate_t(both[0:HEAD_DIM], cosine, sine) * LN2
        both = jnp.concatenate([dk, both[HEAD_DIM:]], axis=0).astype(BF)
        for b in range(NB):
            rows = slice(m * S + b * 256, m * S + b * 256 + 256)
            dkvn[rows, :] = nt(id256, both[:, b * 256 : b * 256 + 256]).astype(BF)

    wqf = [flat(wq[t]) for t in range(2)]
    wshf = flat(wsh[...])

    def input_grad(b):
        rows = slice(b * 256, b * 256 + 256)
        dq, dkvb = tmp[rows, :], dkvn[rows, :]
        dh1 = nt(dq[:, 0:HT], wqf[0]) + nt(dq[:, HT:], wqf[1]) + nt(dkvb, wshf)
        dh2b = dh2[rows, :]
        z, scale = normal_rows(x_ref[rows, :].astype(F32))
        dy = dym[rows, :].astype(F32)
        e = dh1 * gain1 + dh2b * gain2
        back_in = scale * (
            e - jnp.mean(e, axis=-1, keepdims=True) - z * jnp.mean(e * z, axis=-1, keepdims=True)
        )
        tmp[rows, :] = (dy + back_in).astype(BF)
        for k, v in enumerate((dh1 * z, dh1, dh2b * z, dh2b, dq.astype(F32))):
            sums[k : k + 1, :] += jnp.sum(v, axis=0, keepdims=True)
        sums[5:6, 0:128] += jnp.sum(dkvb.astype(F32), axis=0, keepdims=True)

    own_dkv(0)
    input_grad(0)
    red.run(LAST_SUMS[1])
    input_grad(1)
    own_dkv(1)
    gkvs = tn(h1[...], dkvn[...]).astype(BF).reshape(ZC, XC, CC, R, 128)
    for t in range(2):
        gkv[t] = gkvs
    red.run([(last + thirds, 0)])
    red.run(LAST_SUMS[2])
    input_grad(2)
    red.run(LAST_SUMS[3])
    input_grad(3)
    gx_copy = pltpu.make_async_copy(tmp, gx_hbm, lsem.at[7])
    gx_copy.start()
    for k in range(5):
        late[k * n : k * n + n, :] = sums[k : k + 1, :].reshape(n, 128)
    late[5 * n : 5 * n + 1, :] = sums[5:6, 0:128]
    late[5 * n + 1 :, :] = jnp.zeros((late.shape[0] - 5 * n - 1, 128), F32)
    late_sum = AllSum(p, late, late_in, asem)
    late_sum.start(0)
    early_sum.end(1)
    red.run(LAST_SUMS[4])
    late_sum.end(0)
    late_sum.start(1)
    red.run(LAST_SUMS[5])
    late_sum.end(1)
    out_copy.wait()
    gx_copy.wait()


def finish_kernel(dims, out_in, gx_in, grads, early, late, *refs):
    (out, gx, g1, b1, g2, b2, gq, bq, gkv, bkv, go, bo, gup, bup, gdn, bd, held, sem) = refs
    HT, NF = dims["HT"], dims["NF"]
    there, back = [], []
    for k, (src, dst) in enumerate(((out_in, out), (gx_in, gx))):
        there.append(pltpu.make_async_copy(src, held.at[k], sem.at[2 * k]))
        back.append(pltpu.make_async_copy(held.at[k], dst, sem.at[2 * k + 1]))
    for cp in there:
        cp.start()
    t = lax.axis_index("tensor")
    n = g1.shape[0] // 128
    for cp, then in zip(there, back):
        cp.wait()
        then.start()
    for k, ref in enumerate((g1, b1, g2, b2)):
        ref[...] = late[k * n : k * n + n, :].reshape(n * 128)
    half = HT // 128
    bq[...] = late[pl.ds(4 * n + half * t, half), :].reshape(HT)
    bkv[...] = late[5 * n : 5 * n + 1, :].reshape(128)
    total = early[0:n, :].reshape(n * 128)
    bo[...] = total
    bd[...] = total
    for f in range(NF):
        for j in (0, 1):
            at = 256 * f + 128 * j
            bup[at : at + 128] = early[pl.ds(n + 4 * f + 2 * t + j, 1), :].reshape(128)
    at = 0
    for ref in (gq, gkv, go, gup, gdn):
        width = ref.shape[1]
        ref[...] = grads[:, at : at + width]
        at += width
    for cp in back:
        cp.wait()


def angle_table(S):
    places = np.arange(2 * S, dtype=np.float64)
    freqs = 10000.0 ** (-np.arange(ROT // 2) * 2.0 / ROT)
    angles = (places[:, None] * freqs[None, :]).astype(np.float32).astype(np.float64)
    tab = np.concatenate([np.cos(angles).T, np.sin(angles).T], axis=0).astype(np.float32)
    return tab.reshape(ROT, 2, S).transpose(1, 0, 2)


def token_plan(
    block_input,
    cotangent,
    lengths,
    ln1_gain,
    ln1_bias,
    ln2_gain,
    ln2_bias,
    w_query,
    b_query,
    w_shared,
    b_shared,
    w_out,
    b_out,
    w_up,
    b_up,
    w_down,
    b_down,
):
    S, D = block_input.shape[2:]
    R, HT = w_query.shape
    FT = w_up.shape[1]
    NF, T, NH = FT // 256, MB * S, 2 * HT // HEAD_DIM
    dims = dict(S=S, HT=HT, NF=NF, T=T, NH=NH)
    plane = (ZC, XC, CC, R)
    full = (2,) + plane
    t = lax.axis_index("tensor")

    def s(shape, dtype):
        return jax.ShapeDtypeStruct(shape, dtype)

    vm = pl.BlockSpec(memory_space=VMEM)
    hbm = pl.BlockSpec(memory_space=pl.ANY)
    smem = pl.BlockSpec(memory_space=pltpu.SMEM)

    nb = HT // 128 + 2 * NF + 1
    n_gather, n_reduce = NF + 3, NF + 2 + HT // 128
    n_early, n_late = 8 * ((D // 128 + 4 * NF + 7) // 8), 8 * ((5 * (D // 128) + 8) // 8)
    n_grads = 2 * HT + 128 + 2 * FT

    outs = pl.pallas_call(
        partial(block_kernel, dims),
        out_shape=[
            s((T, D), BF),
            s((T, D), BF),
            s((NF,) + full + (512,), BF),
            s((R, n_grads), F32),
            s((n_early, 128), F32),
            s((n_late, 128), F32),
        ],
        in_specs=[hbm, hbm, smem] + [vm] * 15,
        out_specs=[hbm] * 3 + [vm] * 3,
        scratch_shapes=[
            VMEM(plane + (128,), BF),
            VMEM(full + (HT,), BF),
            VMEM(full + (HT,), BF),
            VMEM((2 * HT, D), BF),
            VMEM((2,) + full + (512,), BF),
            VMEM((2, nb, 128), F32),
            VMEM((2 * HT + 128, 128), F32),
            VMEM((T, D), BF),
            VMEM((T, D), BF),
            VMEM((T, D), BF),
            VMEM((T, D), BF),
            VMEM((D, T), BF),
            VMEM((D, T), BF),
            VMEM((D, T), BF),
            VMEM((T, D), BF),
            VMEM((T, D), F32),
            VMEM((T, D), F32),
            VMEM((MB * NH, 1, S), F32),
            VMEM((MB, 128, S), BF),
            VMEM((MB, 128, S), BF),
            VMEM((MB, 2 * S, HEAD_DIM), BF),
            VMEM((MB, 2 * S, HEAD_DIM), BF),
            VMEM((MB, HEAD_DIM, 2 * S), BF),
            VMEM((MB, HEAD_DIM + 16, 2 * S), BF),
            VMEM((MB, S, 128), F32),
            VMEM((MB, S, S), F32),
            VMEM((MB, 2 * S, 128), F32),
            VMEM((MB, S, 128), BF),
            VMEM((MB, S, 128), BF),
            VMEM((T, 128), BF),
            VMEM((3,) + full + (512,), BF),
            VMEM(full + (HT,), BF),
            VMEM((HT // 128,) + full + (128,), BF),
            VMEM(full + (128,), BF),
            VMEM((8, D), F32),
            VMEM((10, n_early, 128), F32),
            VMEM((10, n_late, 128), F32),
            VMEM((NF + 2, 2, ZC, XC, R, 512), BF),
            VMEM((NF + 3, ZC, XC, R, 256), BF),
            VMEM((NF + 3, 2, ZC, R, 256), BF),
            VMEM((NF + 3, 2, ZC, R, 256), BF),
            VMEM((NF + 3, 2, 3, R, 256), BF),
            DMA((Gather.SLOTS, 4)),
            DMA((n_gather, 4)),
            DMA((Reduce.SLOTS, 4)),
            DMA((n_reduce, 4)),
            DMA((8,)),
            DMA((2,)),
            DMA((6 + 2 * MB,)),
            DMA((4,)),
            DMA((4,)),
        ],
        compiler_params=pltpu.CompilerParams(
            vmem_limit_bytes=VMEM_LIMIT, collective_id=0, has_side_effects=True
        ),
        name="block",
    )(
        block_input.reshape(T, D),
        cotangent.reshape(T, D),
        lengths.reshape(MB),
        jnp.asarray(angle_table(S)),
        ln1_gain,
        ln1_bias,
        ln2_gain,
        ln2_bias,
        w_query,
        b_query,
        w_shared,
        b_shared,
        w_out.T,
        b_out,
        w_up,
        b_up,
        w_down.T,
        b_down,
    )
    out, gx, _, grads, early, late = outs
    vec = s((D,), F32)
    shapes = [s((T, D), BF), s((T, D), BF), vec, vec, vec, vec, s((R, HT), F32), s((HT,), F32)]
    shapes += [s((R, 128), F32), s((128,), F32), s((R, HT), F32), vec, s((R, FT), F32)]
    shapes += [s((FT,), F32), s((R, FT), F32), vec]
    outs = pl.pallas_call(
        partial(finish_kernel, dims),
        out_shape=shapes,
        in_specs=[hbm, hbm, vm, vm, vm],
        out_specs=[hbm, hbm] + [vm] * 14,
        scratch_shapes=[VMEM((2, T, D), BF), DMA((4,))],
        compiler_params=pltpu.CompilerParams(vmem_limit_bytes=VMEM_LIMIT),
        name="finish",
    )(out, gx, grads, early, late)
    res = list(outs)
    res[0] = res[0].reshape(block_input.shape)
    res[1] = res[1].reshape(block_input.shape)
    res[10] = res[10].T
    res[14] = res[14].T
    return tuple(res)


def fits_token_plan(mesh):
    return dict(mesh.shape) == {"dp": ZC * XC * CC, "tensor": 2}


def solution(mesh):
    in_specs = (
        P(None, "dp", "tensor", None),
        P(None, "dp", "tensor", None),
        P(None, "dp"),
        P(),
        P(),
        P(),
        P(),
        P("dp", "tensor"),
        P("tensor"),
        P("dp", None),
        P(),
        P("tensor", "dp"),
        P(),
        P("dp", "tensor"),
        P("tensor"),
        P("tensor", "dp"),
        P(),
    )
    out_specs = (
        P(None, "dp", "tensor", None),
        P(None, "dp", "tensor", None),
        P(),
        P(),
        P(),
        P(),
        P("dp", "tensor"),
        P("tensor"),
        P("dp", None),
        P(),
        P("tensor", "dp"),
        P(),
        P("dp", "tensor"),
        P("tensor"),
        P("tensor", "dp"),
        P(),
    )
    step = token_plan if fits_token_plan(mesh) else per_device
    return jax.shard_map(
        step, mesh=mesh, in_specs=in_specs, out_specs=out_specs, check_vma=False
    )
```

```python
from functools import partial

import jax
import jax.numpy as jnp
import numpy as np
from jax import lax
from jax.experimental import pallas as pl
from jax.experimental.pallas import tpu as pltpu
from jax.sharding import PartitionSpec as P

HEAD_DIM = 64
ROT = 16
MB = 2
QBLK = 512


EPS = 1e-05


def tables(count):
    places = jnp.arange(count).astype(jnp.float32)
    freqs = jnp.power(10000.0, -jnp.arange(ROT // 2).astype(jnp.float32) * 2.0 / ROT)
    angles = places[:, None] * freqs[None, :]
    return (jnp.cos(angles)[:, None, :], jnp.sin(angles)[:, None, :])


def rotate(vector, cosine, sine):
    first = vector[..., : ROT // 2]
    second = vector[..., ROT // 2 : ROT]
    return jnp.concatenate(
        [first * cosine - second * sine, second * cosine + first * sine, vector[..., ROT:]], axis=-1
    )


def unrotate(grad, cosine, sine):
    first = grad[..., : ROT // 2]
    second = grad[..., ROT // 2 : ROT]
    return jnp.concatenate(
        [first * cosine + second * sine, second * cosine - first * sine, grad[..., ROT:]], axis=-1
    )


def normalize(vector):
    centre = vector - jnp.mean(vector, axis=-1, keepdims=True)
    spread = jnp.mean(centre * centre, axis=-1, keepdims=True)
    scale = lax.rsqrt(spread + EPS)
    return (centre * scale, scale)


def norm_back(grad, normed, scale, gain):
    weighted = grad * gain
    return scale * (
        weighted
        - jnp.mean(weighted, axis=-1, keepdims=True)
        - normed * jnp.mean(weighted * normed, axis=-1, keepdims=True)
    )


def block_scores(rows, keys, start, limit, count):
    scores = jnp.einsum("qhd,kd->hqk", rows, keys, preferred_element_type=jnp.float32)
    row_pos = start + jnp.arange(QBLK)
    key_pos = jnp.arange(count)
    allowed = (key_pos[None, :] <= row_pos[:, None]) & (key_pos[None, :] < limit)
    return (scores, allowed[None])


def attend(queries, keys, values, limit):
    count = queries.shape[0]

    def block(start):
        rows = lax.dynamic_slice_in_dim(queries, start, QBLK, 0)
        scores, allowed = block_scores(rows, keys, start, limit, count)
        scores = jnp.where(allowed, scores, jnp.float32(-1e30))
        top = jnp.max(scores, axis=-1, keepdims=True)
        expo = jnp.exp(scores - top)
        total = jnp.sum(expo, axis=-1, keepdims=True)
        weights = (expo / total).astype(jnp.bfloat16)
        result = jnp.einsum("hqk,kd->qhd", weights, values, preferred_element_type=jnp.float32)
        return (result, (top + jnp.log(total))[..., 0])

    starts = jnp.arange(count // QBLK) * QBLK
    results, logsum = lax.map(block, starts)
    return (results.reshape(count, -1, HEAD_DIM), logsum)


def attend_back(queries, keys, values, limit, logsum, grad_out):
    count = queries.shape[0]

    def block(carry, item):
        start, block_logsum = item
        rows = lax.dynamic_slice_in_dim(queries, start, QBLK, 0)
        grads = lax.dynamic_slice_in_dim(grad_out, start, QBLK, 0)
        scores, allowed = block_scores(rows, keys, start, limit, count)
        probs = jnp.where(allowed, jnp.exp(scores - block_logsum[:, :, None]), 0.0)
        weights = probs.astype(jnp.bfloat16)
        dprobs = jnp.einsum("qhd,kd->hqk", grads, values, preferred_element_type=jnp.float32)
        delta = jnp.sum(probs * dprobs, axis=-1, keepdims=True)
        dscores = (probs * (dprobs - delta)).astype(jnp.bfloat16)
        drows = jnp.einsum("hqk,kd->qhd", dscores, keys, preferred_element_type=jnp.float32)
        dkeys = carry[0] + jnp.einsum(
            "hqk,qhd->kd", dscores, rows, preferred_element_type=jnp.float32
        )
        dvalues = carry[1] + jnp.einsum(
            "hqk,qhd->kd", weights, grads, preferred_element_type=jnp.float32
        )
        return ((dkeys, dvalues), drows)

    starts = jnp.arange(count // QBLK) * QBLK
    empty = jnp.zeros((count, HEAD_DIM), jnp.float32)
    (dkeys, dvalues), drows = lax.scan(block, (empty, empty), (starts, logsum))
    return (drows.reshape(count, -1, HEAD_DIM), dkeys, dvalues)


def fetch_each(w_query, w_shared, w_out, w_up, w_down):
    return (
        lax.all_gather(w_query, "dp", axis=0, tiled=True),
        lax.all_gather(w_shared, "dp", axis=0, tiled=True),
        lax.all_gather(w_out, "dp", axis=1, tiled=True),
        lax.all_gather(w_up, "dp", axis=0, tiled=True),
        lax.all_gather(w_down, "dp", axis=1, tiled=True),
    )


def reduce_each(step_grads):
    return (
        lax.psum_scatter(step_grads[0], "dp", scatter_dimension=0, tiled=True),
        lax.psum_scatter(step_grads[1], "dp", scatter_dimension=0, tiled=True),
        lax.psum_scatter(step_grads[2], "dp", scatter_dimension=1, tiled=True),
        lax.psum_scatter(step_grads[3], "dp", scatter_dimension=0, tiled=True),
        lax.psum_scatter(step_grads[4], "dp", scatter_dimension=1, tiled=True),
    )


def per_device(
    block_input,
    cotangent,
    lengths,
    ln1_gain,
    ln1_bias,
    ln2_gain,
    ln2_bias,
    w_query,
    b_query,
    w_shared,
    b_shared,
    w_out,
    b_out,
    w_up,
    b_up,
    w_down,
    b_down,
):
    shard_rows = block_input.shape[2]
    groups = lax.axis_size("tensor")
    rank = lax.axis_index("tensor")
    seq_len = shard_rows * groups
    tail_bias = b_out + b_down
    weight_sums = None
    cos_all, sin_all = tables(seq_len)
    own_pos = rank * shard_rows + jnp.arange(shard_rows)
    outputs = []
    input_grads = []
    sum_bq = jnp.zeros(b_query.shape, jnp.float32)
    sum_bkv = jnp.zeros(b_shared.shape, jnp.float32)
    sum_bup = jnp.zeros(b_up.shape, jnp.float32)
    sum_gain1 = jnp.zeros(ln1_gain.shape, jnp.float32)
    sum_shift1 = jnp.zeros(ln1_gain.shape, jnp.float32)
    sum_gain2 = jnp.zeros(ln1_gain.shape, jnp.float32)
    sum_shift2 = jnp.zeros(ln1_gain.shape, jnp.float32)
    sum_out = jnp.zeros(ln1_gain.shape, jnp.float32)
    for micro in range(MB):
        fetched = fetch_each(w_query, w_shared, w_out, w_up, w_down)
        wq_all, wkv_all, wo_all, wup_all, wdown_all = fetched
        limit = lengths[micro, 0]
        inputs = block_input[micro, 0].astype(jnp.float32)
        normed_one, scale_one = normalize(inputs)
        normed_two, scale_two = normalize(inputs)
        low_one = (normed_one * ln1_gain + ln1_bias).astype(jnp.bfloat16)
        low_two = (normed_two * ln2_gain + ln2_bias).astype(jnp.bfloat16)
        whole_one, whole_two = (
            lax.all_gather(low_one, "tensor", axis=0, tiled=True),
            lax.all_gather(low_two, "tensor", axis=0, tiled=True),
        )
        query_lin = jnp.dot(whole_one, wq_all, preferred_element_type=jnp.float32) + b_query
        query_lin = query_lin.reshape(seq_len, -1, HEAD_DIM)
        queries = (rotate(query_lin, cos_all, sin_all) * 0.125).astype(jnp.bfloat16)
        shared = jnp.dot(whole_one, wkv_all, preferred_element_type=jnp.float32) + b_shared
        keys = rotate(shared[:, None, :HEAD_DIM], cos_all, sin_all)[:, 0].astype(jnp.bfloat16)
        values = shared[:, HEAD_DIM:].astype(jnp.bfloat16)
        attended, logsum = attend(queries, keys, values, limit)
        attended_low = attended.reshape(seq_len, -1).astype(jnp.bfloat16)
        hidden = jnp.dot(whole_two, wup_all, preferred_element_type=jnp.float32) + b_up
        active = jax.nn.gelu(hidden, approximate=False).astype(jnp.bfloat16)
        partial_out = jnp.dot(attended_low, wo_all, preferred_element_type=jnp.float32) + jnp.dot(
            active, wdown_all, preferred_element_type=jnp.float32
        )
        branch = lax.psum_scatter(partial_out, "tensor", scatter_dimension=0, tiled=True)
        outputs.append((inputs + branch + tail_bias).astype(jnp.bfloat16))
        valid = (own_pos < limit).astype(jnp.float32)[:, None]
        upstream = cotangent[micro, 0].astype(jnp.float32) * valid
        whole_up = lax.all_gather(upstream.astype(jnp.bfloat16), "tensor", axis=0, tiled=True)
        sum_out = sum_out + jnp.sum(upstream, axis=0)
        grad_down = jnp.einsum("lf,ld->fd", active, whole_up, preferred_element_type=jnp.float32)
        dactive = jnp.einsum("ld,fd->lf", whole_up, wdown_all, preferred_element_type=jnp.float32)
        gelu_pull = jax.vjp(partial(jax.nn.gelu, approximate=False), hidden)[1]
        dhidden = gelu_pull(dactive)[0].astype(jnp.bfloat16)
        sum_bup = sum_bup + jnp.sum(dhidden.astype(jnp.float32), axis=0)
        grad_up = jnp.einsum("ld,lf->df", whole_two, dhidden, preferred_element_type=jnp.float32)
        dnormed_two = jnp.einsum("lf,df->ld", dhidden, wup_all, preferred_element_type=jnp.float32)
        dattended = jnp.einsum("ld,ed->le", whole_up, wo_all, preferred_element_type=jnp.float32)
        dattended = dattended.astype(jnp.bfloat16).reshape(seq_len, -1, HEAD_DIM)
        grad_out = jnp.einsum(
            "le,ld->ed", attended_low, whole_up, preferred_element_type=jnp.float32
        )
        dqueries, dkeys, dvalues = attend_back(queries, keys, values, limit, logsum, dattended)
        dquery_lin = (
            unrotate(dqueries * 0.125, cos_all, sin_all).reshape(seq_len, -1).astype(jnp.bfloat16)
        )
        dkey_lin = unrotate(dkeys[:, None, :], cos_all, sin_all)[:, 0]
        dshared = lax.psum(jnp.concatenate([dkey_lin, dvalues], axis=1), "tensor")
        dshared = dshared.astype(jnp.bfloat16)
        sum_bq = sum_bq + jnp.sum(dquery_lin.astype(jnp.float32), axis=0)
        sum_bkv = sum_bkv + jnp.sum(dshared.astype(jnp.float32), axis=0)
        grad_q = jnp.einsum("ld,le->de", whole_one, dquery_lin, preferred_element_type=jnp.float32)
        grad_kv = jnp.einsum("ld,lc->dc", whole_one, dshared, preferred_element_type=jnp.float32)
        dnormed_one = jnp.einsum(
            "le,de->ld", dquery_lin, wq_all, preferred_element_type=jnp.float32
        )
        dnormed_one, dnormed_two = (
            lax.psum_scatter(dnormed_one, "tensor", scatter_dimension=0, tiled=True),
            lax.psum_scatter(dnormed_two, "tensor", scatter_dimension=0, tiled=True),
        )
        own_shared = lax.dynamic_slice_in_dim(dshared, rank * shard_rows, shard_rows, 0)
        dnormed_one = dnormed_one + jnp.einsum(
            "lc,dc->ld", own_shared, wkv_all, preferred_element_type=jnp.float32
        )
        sum_gain1 = sum_gain1 + jnp.sum(dnormed_one * normed_one, axis=0)
        sum_shift1 = sum_shift1 + jnp.sum(dnormed_one, axis=0)
        sum_gain2 = sum_gain2 + jnp.sum(dnormed_two * normed_two, axis=0)
        sum_shift2 = sum_shift2 + jnp.sum(dnormed_two, axis=0)
        dinputs = (
            upstream
            + norm_back(dnormed_one, normed_one, scale_one, ln1_gain)
            + norm_back(dnormed_two, normed_two, scale_two, ln2_gain)
        )
        input_grads.append(dinputs.astype(jnp.bfloat16))
        step_grads = (grad_q, grad_kv, grad_out, grad_up, grad_down)
        step_grads = reduce_each(step_grads)
        if weight_sums is None:
            weight_sums = step_grads
        else:
            weight_sums = jax.tree.map(jnp.add, weight_sums, step_grads)
    output = jnp.stack(outputs, axis=0)[:, None]
    grad_input = jnp.stack(input_grads, axis=0)[:, None]
    sum_bq, sum_bkv, sum_bup = lax.psum((sum_bq, sum_bkv, sum_bup), "dp")
    sum_gain1, sum_shift1, sum_gain2, sum_shift2, sum_out = lax.psum(
        (sum_gain1, sum_shift1, sum_gain2, sum_shift2, sum_out), ("dp", "tensor")
    )
    grad_q, grad_kv, grad_o, grad_up, grad_down = weight_sums
    return (
        output,
        grad_input,
        sum_gain1,
        sum_shift1,
        sum_gain2,
        sum_shift2,
        grad_q,
        sum_bq,
        grad_kv,
        sum_bkv,
        grad_o,
        sum_out,
        grad_up,
        sum_bup,
        grad_down,
        sum_out,
    )


MESH = pl.DeviceIdType.MESH
BF = jnp.bfloat16
F32 = jnp.float32
LOG2E = 1.4426950408889634
LN2 = 0.6931471805599453
NEG = -1e30
ZC, XC, CC = 4, 2, 2
DMA = pltpu.SemaphoreType.DMA
VMEM = pltpu.VMEM
VMEM_LIMIT = (64 << 20) - 65536


def nn(a, b):
    return lax.dot_general(a, b, (((1,), (0,)), ((), ())), preferred_element_type=F32)


def nt(a, b):
    return lax.dot_general(a, b, (((1,), (1,)), ((), ())), preferred_element_type=F32)


def tn(a, b):
    return lax.dot_general(a, b, (((0,), (0,)), ((), ())), preferred_element_type=F32)


def eye(n):
    return (
        lax.broadcasted_iota(jnp.int32, (n, n), 0) == lax.broadcasted_iota(jnp.int32, (n, n), 1)
    ).astype(BF)


def flat(block):
    return block.reshape(-1, block.shape[-1])


class Place:
    def __init__(self):
        self.dp = lax.axis_index("dp")
        self.t = lax.axis_index("tensor")
        self.core = lax.rem(self.dp, CC)
        self.x = lax.rem(lax.div(self.dp, CC), XC)
        self.z = lax.div(self.dp, CC * XC)

    def at(self, z, x, core):
        return (z * XC + x) * CC + core

    def z_peer(self, d):
        return {"dp": self.at(lax.rem(self.z + d, ZC), self.x, self.core)}

    def x_peer(self):
        return {"dp": self.at(self.z, 1 - self.x, self.core)}

    def core_peer(self):
        return {"dp": self.at(self.z, self.x, 1 - self.core)}

    def y_peer(self):
        return {"tensor": 1 - self.t}

    def layer_peers(self):
        res = []
        for k in range(1, 8):
            x = 1 - self.x if k & 1 else self.x
            t = 1 - self.t if k & 2 else self.t
            core = 1 - self.core if k & 4 else self.core
            res.append({"dp": self.at(self.z, x, core), "tensor": t})
        return res

    def greet(self):
        bar = pltpu.get_barrier_semaphore()
        peers = [self.z_peer(d) for d in (1, 2, 3)] + self.layer_peers()
        for p in peers:
            pl.semaphore_signal(bar, inc=1, device_id=p, device_id_type=MESH)
        return bar, len(peers)


def remote(src, dst, ss, rs, peer):
    return pltpu.make_async_remote_copy(
        src_ref=src, dst_ref=dst, send_sem=ss, recv_sem=rs, device_id=peer, device_id_type=MESH
    )


def split_cols(width):
    a = (width // 128 + 1) // 2 * 128
    return ((0, a), (a, width - a))


class Gather:
    SLOTS = 3

    def __init__(self, place, pieces, sends, gots):
        self.p = place
        self.pieces = pieces
        self.sends, self.gots = sends, gots

    def own(self, c, h):
        p = self.p
        _, o, w, order = self.pieces[c][0][h]
        index = (p.z, p.x, p.core, slice(None), pl.ds(o, w))
        return self.pieces[c][1].at[(p.t,) + index if "y" in order else index]

    def copies(self, c, k):
        p = self.p
        every = slice(None)
        res = []
        for h, (src, o, w, order) in enumerate(self.pieces[c][0]):
            if k == 0:
                pairs = [(src, self.own(c, h), p.z_peer(d)) for d in (1, 2, 3)]
            elif k <= len(order):
                done = order[:k]
                index = (every, every if "x" in done else p.x, p.core, every, pl.ds(o, w))
                if "y" in order:
                    index = (every if "y" in done else p.t,) + index
                view = self.pieces[c][1].at[index]
                axis = order[k] if k < len(order) else "core"
                peers = {"x": p.x_peer(), "y": p.y_peer(), "core": p.core_peer()}
                pairs = [(view, view, peers[axis])]
            else:
                pairs = []
            for a, b, peer in pairs:
                res.append(remote(a, b, self.sends.at[c % self.SLOTS, k], self.gots.at[c, k], peer))
        return res

    def total(self, c, k):
        parts, out = self.pieces[c]
        z = pl.ds(0, 3) if k == 0 else slice(None)
        x = slice(None) if k > 1 else 0
        index = (z, x, 0)
        if "y" in parts[0][3]:
            index = (slice(None) if k > 2 else 0,) + index
        view = out.at[index]
        return remote(
            view, view, self.sends.at[c % self.SLOTS, k], self.gots.at[c, k], self.p.core_peer()
        )

    def run(self, ops):
        for op in ops:
            c, k = (op, -1) if isinstance(op, int) else op
            if k >= 0:
                self.total(c, k).wait()
            for cp in self.copies(c, k + 1):
                cp.start()


class AllSum:
    def __init__(self, place, buf, got, sems):
        self.p = place
        self.buf, self.got, self.sems = buf, got, sems

    def part(self, k):
        return (7, 3) if k else (0, 7)

    def start(self, k):
        peers = [self.p.z_peer(d) for d in (1, 2, 3)] if k else self.p.layer_peers()
        at, _ = self.part(k)
        for i, peer in enumerate(peers):
            got = self.got.at[at + i]
            remote(self.buf, got, self.sems.at[2 * k], self.sems.at[2 * k + 1], peer).start()

    def end(self, k):
        at, n = self.part(k)
        view = self.got.at[pl.ds(at, n)]
        whole = remote(
            view, view, self.sems.at[2 * k], self.sems.at[2 * k + 1], self.p.core_peer()
        )
        whole.wait()
        total = self.buf[...]
        for i in range(at, at + n):
            total = total + self.got[i]
        self.buf[...] = total


def normal_rows(rows):
    mean = jnp.mean(rows, axis=-1, keepdims=True)
    centre = rows - mean
    var = jnp.mean(centre * centre, axis=-1, keepdims=True)
    scale = lax.rsqrt(var + EPS)
    return centre * scale, scale


def rotate_t(v, cosine, sine):
    a, b = v[0:8], v[8:16]
    return jnp.concatenate([a * cosine - b * sine, b * cosine + a * sine, v[16:]], axis=0)


def unrotate_t(v, cosine, sine):
    a, b = v[0:8], v[8:16]
    return jnp.concatenate([a * cosine + b * sine, b * cosine - a * sine, v[16:]], axis=0)


def fill_bias(place, lens_ref, other_ref, own_ref, S):
    t = place.t
    for m in range(MB):
        limit = lens_ref[m]
        key = lax.broadcasted_iota(jnp.int32, (S, 128), 0)
        limit_other = jnp.where(t == 1, limit, 0)
        other_ref[m] = jnp.where(key < limit_other, 0.0, NEG).astype(F32)
        key = lax.broadcasted_iota(jnp.int32, (S, S), 0)
        row = lax.broadcasted_iota(jnp.int32, (S, S), 1)
        own = (key <= row) & (key + t * S < limit)
        own_ref[m] = jnp.where(own, 0.0, NEG).astype(F32)


def masked_rows(place_t, lens_ref, dy, start, S):
    m, off = divmod(start, S)
    pos = place_t * S + off + lax.broadcasted_iota(jnp.int32, (dy.shape[0], 1), 0)
    return jnp.where(pos < lens_ref[m], dy.astype(F32), 0.0)


class Reduce:
    SLOTS = 3

    def __init__(self, place, pieces, rc, r2a, r2b, r3, r4, sends, gots):
        self.p = place
        self.pieces = pieces
        self.rc, self.r2a, self.r2b, self.r3, self.r4 = rc, r2a, r2b, r3, r4
        self.sends, self.gots = sends, gots

    def part(self, c, h):
        r, n, o, w = self.pieces[c][1][h]
        _, first, _, second = self.pieces[c][3]
        o += first
        return (slice(r, r + n), slice(o, o + w)), (slice(0, n), slice(second, second + w))

    def wide(self, c):
        first = self.pieces[c][3][1]
        return slice(first, first + self.pieces[c][0].shape[-1])

    def sems(self, c, k):
        return self.sends.at[c % self.SLOTS, k], self.gots.at[c, k]

    def copies(self, c, k):
        p = self.p
        if k == 0:
            src = self.pieces[c][0].at[:, :, :, 1 - p.core]
            dst = self.rc.at[self.pieces[c][3][0], :, :, :, :, self.wide(c)]
            return [remote(src, dst, *self.sems(c, k), p.core_peer())]
        res = []
        a, _, b, _ = self.pieces[c][3]
        for h in (0, 1):
            here, there = self.part(c, h)
            if k == 1 and h == 0:
                src, dst = self.rc.at[(a, 1 - p.t, slice(None), slice(None)) + here], self.r2a
                todo = [(src, dst.at[(b, slice(None), slice(None)) + there], p.y_peer())]
            elif k == 1:
                src, dst = self.rc.at[(a, slice(None), slice(None), 1 - p.x) + here], self.r2b
                todo = [(src, dst.at[(b, slice(None), slice(None)) + there], p.x_peer())]
            elif k == 2:
                if h == 0:
                    src, peer = self.r2a.at[(b, slice(None), 1 - p.x) + there], p.x_peer()
                else:
                    src, peer = self.r2b.at[(b, 1 - p.t, slice(None)) + there], p.y_peer()
                todo = [(src, self.r3.at[(b, h, slice(None)) + there], peer)]
            else:
                todo = [
                    (
                        self.r3.at[(b, h, lax.rem(p.z + d, ZC)) + there],
                        self.r4.at[(b, h, d - 1) + there],
                        p.z_peer(d),
                    )
                    for d in (1, 2, 3)
                ]
            res += [remote(src, dst, *self.sems(c, k), peer) for src, dst, peer in todo]
        return res

    def total(self, c, k):
        cols = self.wide(c)
        every = slice(None)
        index = {
            0: (every, every, every, every, cols),
            1: (0, every, every, every, cols),
            2: (0, every, 0, every, cols),
            3: (0, pl.ds(0, 3), 0, every, cols),
        }[k]
        view = self.rc.at[(self.pieces[c][3][0],) + index]
        return remote(view, view, *self.sems(c, k), self.p.core_peer())

    def start(self, c, k):
        for cp in self.copies(c, k):
            cp.start()

    def add(self, c, k):
        p = self.p
        a, _, b, _ = self.pieces[c][3]
        if k == 1:
            cols = self.wide(c)
            mine = self.pieces[c][0][:, :, :, p.core].astype(F32)
            mine = mine + self.rc[a, :, :, :, :, cols].astype(F32)
            self.rc[a, :, :, :, :, cols] = mine.astype(BF)
            return
        sums = []
        for h in (0, 1):
            here, there = self.part(c, h)
            every = slice(None)
            if k == 2:
                if h == 0:
                    ref, mine = self.r2a, self.rc[(a, p.t, every, every) + here]
                else:
                    ref, mine = self.r2b, self.rc[(a, every, every, p.x) + here]
                at = (b, every, every) + there
                ref[at] = (mine.astype(F32) + ref[at].astype(F32)).astype(BF)
            elif k == 3:
                if h == 0:
                    mine = self.r2a[(b, every, p.x) + there]
                else:
                    mine = self.r2b[(b, p.t, every) + there]
                at = (b, h, every) + there
                self.r3[at] = (mine.astype(F32) + self.r3[at].astype(F32)).astype(BF)
            else:
                total = self.r3[(b, h, p.z) + there].astype(F32)
                for d in range(3):
                    total = total + self.r4[(b, h, d) + there].astype(F32)
                sums.append(total)
        if k == 4:
            self.pieces[c][2](sums)

    def run(self, ops):
        for c, k in ops:
            if k:
                self.total(c, k - 1).wait()
                self.add(c, k)
            if k < 4:
                self.start(c, k)


HEAD_OPS = (
    (0, 1),
    ((0, 0), (1, 0), 2),
    ((0, 1), (1, 1), 3),
    ((0, 2),),
    ((1, 2), 4),
    ((1, 3), (2, 0), (3, 0), 5),
)
ATTENTION_OPS = {
    0: ((2, 1), 6),
    2: ((4, 0),),
    4: ((3, 1), (5, 0), 7),
    5: ((2, 2),),
    7: ((3, 2), (2, 3), (4, 1), (6, 0), 8),
}
BACK_OPS = {
    0: ((3, 3), (4, 2), (5, 1), (7, 0)),
    3: ((4, 3), (5, 2), (6, 1), (8, 0)),
    5: ((5, 3), (6, 2), (7, 1)),
}
FFN_OPS = {
    0: (),
    1: ((6, 3), (7, 2), (8, 1)),
    2: ((7, 3), (8, 2)),
    3: ((8, 3),),
}


FFN_SUMS = {
    0: ((0, 1),),
    2: ((0, 2), (1, 1)),
    3: ((0, 3), (2, 1)),
    4: ((0, 4), (1, 2), (3, 1)),
    5: ((1, 3), (2, 2), (4, 1)),
}
BACK_SUMS = {
    6: ((1, 4), (2, 3), (3, 2), (5, 1)),
    8: ((2, 4), (3, 3), (4, 2), (6, 1)),
    9: ((7, 1),),
    10: ((3, 4), (4, 3), (5, 2)),
    11: ((7, 2), (8, 1), (6, 2)),
}
LAST_SUMS = (
    ((4, 4), (5, 3), (7, 3), (8, 2)),
    ((9, 1), (6, 3)),
    ((10, 1), (9, 2), (5, 4), (8, 3)),
    ((10, 2), (6, 4), (9, 3), (7, 4)),
    ((10, 3), (8, 4)),
    ((9, 4), (10, 4)),
)


def block_kernel(
    dims,
    x_hbm,
    dy_hbm,
    lens_ref,
    tab_ref,
    g1_ref,
    b1_ref,
    g2_ref,
    b2_ref,
    wq_in,
    bq_ref,
    wsh_in,
    bsh_ref,
    wout_in,
    bout_ref,
    wup_in,
    bup_ref,
    wdown_in,
    bdown_ref,
    out_hbm,
    gx_hbm,
    wf,
    grads,
    early,
    late,
    wsh,
    wq,
    wb,
    won,
    wv,
    ball,
    bcol,
    x_ref,
    dym,
    h1,
    h2,
    qt,
    att,
    da,
    tmp,
    acc,
    dh2,
    lse_ref,
    kvt,
    kvo,
    kc,
    vc,
    kt,
    vte,
    bias_o,
    bias_s,
    dkv,
    dkvs,
    dkvr,
    dkvn,
    gring,
    gb,
    gq,
    gkv,
    sums,
    early_in,
    late_in,
    rc,
    r2a,
    r2b,
    r3,
    r4,
    gsend,
    gsem,
    rsend,
    rsem,
    lsem,
    wsem,
    ysem,
    esem,
    asem,
):
    S, HT, NH, NF, T = dims["S"], dims["HT"], dims["NH"], dims["NF"], dims["T"]
    D = x_ref.shape[1]
    R = wq_in.shape[0]
    NB = S // 256
    p = Place()
    bar, npeers = p.greet()
    x_copy = pltpu.make_async_copy(x_hbm, x_ref, lsem.at[1])
    x_copy.start()
    dy_copy = pltpu.make_async_copy(dy_hbm, dym, lsem.at[0])
    dy_copy.start()

    def parts_of(ref, widths, orders):
        at = [sum(widths[:i]) for i in range(len(widths))]
        return [(ref.at[:, pl.ds(o, w)], o, w, order) for o, w, order in zip(at, widths, orders)]

    wide = [w for _, w in split_cols(HT)]
    pieces = [
        ([(wsh_in, 0, 128, "zx")], wsh),
        (parts_of(wq_in, wide, ("zxy", "zyx")), wq),
        (parts_of(wout_in, wide, ("zxy", "zyx")), wb),
    ]
    for f in range(NF):
        cols = pl.ds(256 * f, 256)
        parts = [(wup_in.at[:, cols], 0, 256, "zxy"), (wdown_in.at[:, cols], 256, 256, "zyx")]
        pieces.append((parts, wf.at[f]))
    g = Gather(p, pieces, gsend, gsem)
    pl.semaphore_wait(bar, npeers)
    g.run(HEAD_OPS[0])
    locals_ = [
        pltpu.make_async_copy(wsh_in, wsh.at[p.z, p.x, p.core], lsem.at[2]),
        pltpu.make_async_copy(wq_in, wq.at[p.t, p.z, p.x, p.core], lsem.at[3]),
        pltpu.make_async_copy(wout_in, wb.at[p.t, p.z, p.x, p.core], lsem.at[4]),
    ]
    for cp in locals_:
        cp.start()
    for c in range(3, len(pieces)):
        for h in (0, 1):
            pltpu.make_async_copy(pieces[c][0][h][0], g.own(c, h), lsem.at[5]).start()
    held = wf.at[:, 0, 0, 0, 0]
    locals_.append(pltpu.make_async_copy(held, held, lsem.at[5]))
    first = HT // 128
    rows_b = ball.shape[1]
    ball[p.t, 0:first, :] = bq_ref[...].reshape(first, 128)
    ball[p.t, first : first + 2 * NF, :] = bup_ref[...].reshape(2 * NF, 128)
    ball[p.t, first + 2 * NF :, :] = jnp.zeros((rows_b - first - 2 * NF, 128), F32)
    bias_copy = remote(ball.at[p.t], ball.at[p.t], ysem.at[0], ysem.at[1], p.y_peer())
    bias_copy.start()

    gain1, shift1, gain2, shift2 = (
        ref[...].reshape(1, D) for ref in (g1_ref, b1_ref, g2_ref, b2_ref)
    )

    def norm_block(i):
        rows = pl.ds(pl.multiple_of(i * 128, 128), 128)
        z, _ = normal_rows(x_ref[rows, :].astype(F32))
        h1[rows, :] = (z * gain1 + shift1).astype(BF)
        h2[rows, :] = (z * gain2 + shift2).astype(BF)

    half = T // 256
    x_copy.wait()
    pl.loop(0, half)(norm_block)
    for cp in locals_:
        cp.wait()
    g.run(HEAD_OPS[1])
    pl.loop(half, 2 * half)(norm_block)
    g.run(HEAD_OPS[2])
    fill_bias(p, lens_ref, bias_o, bias_s, S)
    for ref in (dkv, dh2, sums):
        ref[...] = jnp.zeros_like(ref)
    bias_copy.wait()
    nq = HT // 128
    for t in range(2):
        for j in range(nq):
            row = jnp.broadcast_to(ball[t, j : j + 1, :], (128, 128))
            bcol[(t * nq + j) * 128 : (t * nq + j + 1) * 128, :] = row.T
    bcol[2 * HT : 2 * HT + 128, :] = jnp.broadcast_to(bsh_ref[...].reshape(1, 128), (128, 128)).T
    g.run(HEAD_OPS[3])

    id256 = eye(256)
    cosine, sine = tab_ref[p.t, 0:8, :], tab_ref[p.t, 8:16, :]
    wsh_t = nt(eye(128), flat(wsh[...])).astype(BF)
    kv_copies = [
        remote(kvt.at[m], kvo.at[m], ysem.at[2 + 2 * m], ysem.at[3 + 2 * m], p.y_peer())
        for m in range(MB)
    ]
    for m in range(MB):
        kv = nt(wsh_t, h1[m * S : m * S + S, :]) + bcol[2 * HT : 2 * HT + 128, 0:1]
        kvt[m, 0:HEAD_DIM, :] = rotate_t(kv[0:HEAD_DIM], cosine, sine).astype(BF)
        kvt[m, HEAD_DIM:, :] = kv[HEAD_DIM:].astype(BF)
    g.run(HEAD_OPS[4])
    kv_copies[0].start()
    dy_copy.wait()
    for b in range(T // 256):
        rows = slice(b * 256, b * 256 + 256)
        dy = masked_rows(p.t, lens_ref, dym[rows, :], b * 256, S)
        dym[rows, :] = dy.astype(BF)
        sums[6:7, :] += jnp.sum(dy, axis=0, keepdims=True)
    g.run(HEAD_OPS[5])

    for t in range(2):
        wq_t = nt(eye(HT), flat(wq[t])).astype(BF)
        for m in range(MB):
            cols = slice(m * S, m * S + S)
            q = nt(wq_t, h1[cols, :])
            for h in range(HT // HEAD_DIM):
                base = t * HT + h * HEAD_DIM
                qh = q[h * HEAD_DIM : (h + 1) * HEAD_DIM] + bcol[base : base + HEAD_DIM, 0:1]
                qh = rotate_t(qh, cosine, sine) * (0.125 * LOG2E)
                qt[base : base + HEAD_DIM, cols] = qh.astype(BF)

    def both_halves(m):
        kv_copies[m].wait()
        for part, src in ((0, kvo), (1, kvt)):
            keys = slice(part * S, part * S + S)
            kt[m, :, keys] = src[m, 0:HEAD_DIM, :]
            vte[m, 0:HEAD_DIM, keys] = src[m, HEAD_DIM:, :]
        vte[m, HEAD_DIM:, :] = (
            lax.broadcasted_iota(jnp.int32, (16, 2 * S), 0) == 0
        ).astype(BF)
        for b in range(2 * NB):
            blk = slice(b * 256, b * 256 + 256)
            kc[m, blk, :] = nt(id256, kt[m, :, blk]).astype(BF)
            vc[m, blk, :] = nt(id256, vte[m, 0:HEAD_DIM, blk]).astype(BF)

    both_halves(0)

    def spots(i, group, by_thirds=False):
        res = []
        for u in range(group):
            j = i * group + u
            m, h = lax.div(j, NH), lax.rem(j, NH)
            if by_thirds:
                k = lax.div(h, 2)
                h = lax.rem(k, 2) * (NH // 2) + lax.div(k, 2) * 2 + u
                j = m * NH + h
            head = pl.ds(pl.multiple_of(h * HEAD_DIM, HEAD_DIM), HEAD_DIM)
            for r in range(NB):
                cols = pl.ds(pl.multiple_of(m * S + r * 256, 256), 256)
                res.append((j, m, head, cols, S + 256 * (r + 1), r))
        return res

    def scores(m, q, nk, r):
        s = nn(kc[m, 0:nk, :], q)
        wide = slice(r * 256, r * 256 + 256)
        other = bias_o[m]
        other = jnp.concatenate([other, other], axis=1)
        return jnp.concatenate([s[0:S] + other, s[S:nk] + bias_s[m, 0 : nk - S, wide]], axis=0)

    group = 3

    @pl.loop(0, MB * NH // group)
    def _(i):
        for m in range(1, MB):
            pl.when(i == (m - 1) * NH // group)(kv_copies[m].start)
            pl.when(i == m * NH // group)(partial(both_halves, m))
        for at, ops in ATTENTION_OPS.items():
            pl.when(i == at)(partial(g.run, ops))
        todo = spots(i, group)
        sc = [scores(m, qt[head, cols], nk, r) for _, m, head, cols, nk, r in todo]
        tops = [jnp.max(s, axis=0, keepdims=True) for s in sc]
        ex = [jnp.exp2(s - top).astype(BF) for s, top in zip(sc, tops)]
        for (j, m, head, cols, nk, r), e, top in zip(todo, ex, tops):
            o = nn(vte[m, :, 0:nk], e)
            total = o[HEAD_DIM : HEAD_DIM + 1]
            att[head, cols] = (o[0:HEAD_DIM] * (1.0 / total)).astype(BF)
            lse_ref[j, :, r * 256 : r * 256 + 256] = top + jnp.log2(total)

    for t in range(2):
        won[t * HT : (t + 1) * HT, :] = nt(eye(HT), flat(wb[t])).astype(BF)

    def load(f, slot):
        return pltpu.make_async_copy(wf.at[f], wv.at[slot], wsem.at[slot])

    for b in range(T // 256):
        rows = slice(b * 256, b * 256 + 256)
        tmp[rows, :] = nt(id256, att[:, rows]).astype(BF)
    tail_bias = (bout_ref[...] + bdown_ref[...]).reshape(1, D)
    acc[...] = x_ref[...].astype(F32) + tail_bias + nn(tmp[...], won[...])
    for t in range(2):
        cols = slice(t * HT, (t + 1) * HT)
        gb[t] = tn(dym[...], tmp[:, cols]).astype(BF).reshape(ZC, XC, CC, R, HT)

    def put(*firsts):
        def store(parts):
            for o, v in zip(firsts, parts):
                grads[:, o : o + v.shape[1]] = v

        return store

    at_out, at_up, at_down = HT + 128, 2 * HT + 128, 2 * HT + 128 + 256 * NF
    thirds = HT // 128

    def by_cols(*widths):
        at = [sum(widths[:i]) for i in range(len(widths))]
        return [(0, R, o, w) for o, w in zip(at, widths)]

    def put_rows(first):
        def store(parts):
            r = 0
            for v in parts:
                grads[r : r + v.shape[0], first : first + 128] = v
                r += v.shape[0]

        return store

    by_rows = [(0, 32, 0, 128), (32, R - 32, 0, 128)]
    sums_of = [(gb, by_cols(*wide), put(at_out, at_out + wide[0]), (0, 0, 0, 0))]
    for f in range(NF):
        store = put(at_up + 256 * f, at_down + 256 * f)
        sums_of.append((gring.at[f % 3], by_cols(256, 256), store, (1 + f, 0, 1 + f, 0)))
    for k in range(thirds + 1):
        store = put_rows(128 * k)
        slot = (NF + 1, 128 * k, NF + 1 + k // 2, 128 * (k % 2))
        sums_of.append((gq.at[k] if k < thirds else gkv, by_rows, store, slot))
    red = Reduce(p, sums_of, rc, r2a, r2b, r3, r4, rsend, rsem)
    last = NF + 1
    red.run([(0, 0)])

    n = D // 128
    early_sum = AllSum(p, early, early_in, esem)
    da[...] = nt(won[...], dym[...]).astype(BF)
    back = 2
    dkv_copies = [
        remote(dkvs.at[m], dkvr.at[m], ysem.at[6 + 2 * m], ysem.at[7 + 2 * m], p.y_peer())
        for m in range(MB)
    ]

    def send_dkv(m):
        dkvs[m] = dkv[m, 0:S, :].astype(BF)
        dkv_copies[m].start()

    def query_third(k):
        for t in range(2):
            at = t * HT + 128 * k
            for b in range(T // 256):
                rows = slice(b * 256, b * 256 + 256)
                tmp[rows, at : at + 128] = nt(id256, qt[at : at + 128, rows]).astype(BF)
            v = tn(h1[...], tmp[:, at : at + 128]).astype(BF)
            gq[k, t] = v.reshape(ZC, XC, CC, R, 128)
        red.run([(last + k, 0)])

    def own_dkv(m):
        dkv_copies[m].wait()
        both = (dkv[m, S : 2 * S, :] + dkvr[m].astype(F32)).T
        dk = unrotate_t(both[0:HEAD_DIM], cosine, sine) * LN2
        both = jnp.concatenate([dk, both[HEAD_DIM:]], axis=0).astype(BF)
        for b in range(NB):
            rows = slice(m * S + b * 256, m * S + b * 256 + 256)
            dkvn[rows, :] = nt(id256, both[:, b * 256 : b * 256 + 256]).astype(BF)

    def early_next():
        early_sum.end(0)
        early_sum.start(1)

    def back_step(i):
        for at, ops in BACK_OPS.items():
            pl.when(i == at)(partial(g.run, ops))
        pl.when(i == NH // back + 2)(early_next)
        pl.when(i == NH // back + 3)(partial(own_dkv, 0))
        for at, ops in BACK_SUMS.items():
            pl.when(i == at)(partial(red.run, ops))
        for k in range(thirds - 1):
            at = MB * NH // back - 2 * (thirds - 1 - k)
            pl.when(i == at)(partial(query_third, k))
        todo = spots(i, back, True)
        qs = [qt[head, cols] for _, m, head, cols, nk, r in todo]
        das = [da[head, cols] for _, m, head, cols, nk, r in todo]
        sc = [scores(m, q, nk, r) for (_, m, head, cols, nk, r), q in zip(todo, qs)]
        dp = [nn(vc[m, 0:nk, :], d) for (_, m, head, cols, nk, r), d in zip(todo, das)]
        pr, ds = [], []
        for (j, m, head, cols, nk, r), d, s, dpj in zip(todo, das, sc, dp):
            delta = jnp.sum(d.astype(F32) * att[head, cols].astype(F32), axis=0, keepdims=True)
            w = jnp.exp2(s - lse_ref[j, :, r * 256 : r * 256 + 256])
            pr.append(w.astype(BF))
            ds.append((w * (dpj - delta)).astype(BF))
        for (j, m, head, cols, nk, r), d in zip(todo, ds):
            wide = slice(r * 256, r * 256 + 256)
            dq = nn(kt[m, :, 0:nk], d)
            dq = unrotate_t(dq, tab_ref[p.t, 0:8, wide], tab_ref[p.t, 8:16, wide])
            qt[head, cols] = (dq * 0.125).astype(BF)
        m = todo[0][1]
        for blk in range(NB):
            lo = 0 if blk == 0 else S + 256 * blk
            hi = S + 256 * (blk + 1)
            left, right = [], []
            for u, (_, _, _, _, nk, r) in enumerate(todo):
                if nk >= hi:
                    zero = jnp.zeros_like(qs[u])
                    left += [ds[u][lo:hi], pr[u][lo:hi]]
                    right += [
                        jnp.concatenate([qs[u], zero], axis=0),
                        jnp.concatenate([zero, das[u]], axis=0),
                    ]
            dkv[m, lo:hi, :] += nt(
                jnp.concatenate(left, axis=1), jnp.concatenate(right, axis=1)
            )

    per = NH // back
    pl.loop(0, per * (MB - 1))(back_step)
    for m in range(MB - 1):
        send_dkv(m)
    load(0, 0).start()

    @pl.loop(0, NF)
    def _(f):
        slot = lax.rem(f, 2)
        load(f, slot).wait()
        for k in range(NF - 1):

            @pl.when(f == k)
            def _():
                g.run(FFN_OPS.get(k, ()))
                load(k + 1, (k + 1) % 2).start()

        for k, ops in FFN_SUMS.items():
            pl.when(f == k)(partial(red.run, ops))
        wu = [flat(wv[slot, t, :, :, :, :, 0:256]) for t in range(2)]
        wd = [flat(wv[slot, t, :, :, :, :, 256:512]) for t in range(2)]
        gslot = lax.rem(f, 3)
        hid = [nn(h2[...], wu[t]) for t in range(2)]
        dact = [nn(dym[...], wd[t]) for t in range(2)]
        act, dhid = [], []
        for t in range(2):
            row = jnp.concatenate(
                [ball[t, pl.ds(first + 2 * f, 1), :], ball[t, pl.ds(first + 2 * f + 1, 1), :]],
                axis=1,
            )
            u = hid[t] + row
            cdf = 0.5 + 0.5 * lax.erf(u * 0.7071067811865476)
            dens = jnp.exp(-0.5 * u * u) * 0.3989422804014327
            act.append((u * cdf).astype(BF))
            d = (dact[t] * (cdf + u * dens)).astype(BF)
            dhid.append(d)
            total = jnp.sum(d.astype(F32), axis=0, keepdims=True)
            for j in (0, 1):
                at = D // 128 + 4 * f + 2 * t + j
                early[pl.ds(at, 1), :] = total[:, 128 * j : 128 * j + 128]
        acc[...] += nt(act[0], wd[0]) + nt(act[1], wd[1])
        dh2[...] += nt(dhid[0], wu[0]) + nt(dhid[1], wu[1])
        for t in range(2):
            gd = tn(dym[...], act[t]).astype(BF)
            gring[gslot, t, :, :, :, :, 256:512] = gd.reshape(ZC, XC, CC, R, 256)
            gu = tn(h2[...], dhid[t]).astype(BF)
            gring[gslot, t, :, :, :, :, 0:256] = gu.reshape(ZC, XC, CC, R, 256)
        for k in range(NF):
            pl.when(f == k)(partial(red.run, [(1 + k, 0)]))

    h2[...] = acc[...].astype(BF)
    out_copy = pltpu.make_async_copy(h2, out_hbm, lsem.at[6])
    out_copy.start()

    early[0:n, :] = sums[6:7, :].reshape(n, 128)
    early[n + 4 * NF :, :] = jnp.zeros((early.shape[0] - n - 4 * NF, 128), F32)
    early_sum.start(0)

    pl.loop(per * (MB - 1), per * MB)(back_step)
    send_dkv(MB - 1)
    query_third(thirds - 1)
    red.run(LAST_SUMS[0])

    wqf = [flat(wq[t]) for t in range(2)]
    wshf = flat(wsh[...])

    def input_grad(b):
        rows = slice(b * 256, b * 256 + 256)
        dq, dkvb = tmp[rows, :], dkvn[rows, :]
        dh1 = nt(dq[:, 0:HT], wqf[0]) + nt(dq[:, HT:], wqf[1]) + nt(dkvb, wshf)
        dh2b = dh2[rows, :]
        z, scale = normal_rows(x_ref[rows, :].astype(F32))
        dy = dym[rows, :].astype(F32)
        e = dh1 * gain1 + dh2b * gain2
        back_in = scale * (
            e - jnp.mean(e, axis=-1, keepdims=True) - z * jnp.mean(e * z, axis=-1, keepdims=True)
        )
        tmp[rows, :] = (dy + back_in).astype(BF)
        for k, v in enumerate((dh1 * z, dh1, dh2b * z, dh2b, dq.astype(F32))):
            sums[k : k + 1, :] += jnp.sum(v, axis=0, keepdims=True)
        sums[5:6, 0:128] += jnp.sum(dkvb.astype(F32), axis=0, keepdims=True)

    input_grad(0)
    own_dkv(1)
    red.run(LAST_SUMS[1])
    gkvs = tn(h1[...], dkvn[...]).astype(BF).reshape(ZC, XC, CC, R, 128)
    for t in range(2):
        gkv[t] = gkvs
    red.run([(last + thirds, 0)])
    input_grad(1)
    input_grad(2)
    red.run(LAST_SUMS[2])
    input_grad(3)
    for k in range(5):
        late[k * n : k * n + n, :] = sums[k : k + 1, :].reshape(n, 128)
    late[5 * n : 5 * n + 1, :] = sums[5:6, 0:128]
    late[5 * n + 1 :, :] = jnp.zeros((late.shape[0] - 5 * n - 1, 128), F32)
    late_sum = AllSum(p, late, late_in, asem)
    late_sum.start(0)
    gx_copy = pltpu.make_async_copy(tmp, gx_hbm, lsem.at[7])
    gx_copy.start()
    red.run(LAST_SUMS[3])
    late_sum.end(0)
    late_sum.start(1)
    early_sum.end(1)
    red.run(LAST_SUMS[4])
    red.run(LAST_SUMS[5])
    late_sum.end(1)
    out_copy.wait()
    gx_copy.wait()


def finish_kernel(dims, out_in, gx_in, grads, early, late, *refs):
    (out, gx, g1, b1, g2, b2, gq, bq, gkv, bkv, go, bo, gup, bup, gdn, bd, held, sem) = refs
    HT, NF = dims["HT"], dims["NF"]
    there, back = [], []
    for k, (src, dst) in enumerate(((out_in, out), (gx_in, gx))):
        there.append(pltpu.make_async_copy(src, held.at[k], sem.at[2 * k]))
        back.append(pltpu.make_async_copy(held.at[k], dst, sem.at[2 * k + 1]))
    for cp in there:
        cp.start()
    t = lax.axis_index("tensor")
    n = g1.shape[0] // 128
    for cp, then in zip(there, back):
        cp.wait()
        then.start()
    for k, ref in enumerate((g1, b1, g2, b2)):
        ref[...] = late[k * n : k * n + n, :].reshape(n * 128)
    half = HT // 128
    bq[...] = late[pl.ds(4 * n + half * t, half), :].reshape(HT)
    bkv[...] = late[5 * n : 5 * n + 1, :].reshape(128)
    total = early[0:n, :].reshape(n * 128)
    bo[...] = total
    bd[...] = total
    for f in range(NF):
        for j in (0, 1):
            at = 256 * f + 128 * j
            bup[at : at + 128] = early[pl.ds(n + 4 * f + 2 * t + j, 1), :].reshape(128)
    at = 0
    for ref in (gq, gkv, go, gup, gdn):
        width = ref.shape[1]
        ref[...] = grads[:, at : at + width]
        at += width
    for cp in back:
        cp.wait()


def angle_table(S):
    places = np.arange(2 * S, dtype=np.float64)
    freqs = 10000.0 ** (-np.arange(ROT // 2) * 2.0 / ROT)
    angles = (places[:, None] * freqs[None, :]).astype(np.float32).astype(np.float64)
    tab = np.concatenate([np.cos(angles).T, np.sin(angles).T], axis=0).astype(np.float32)
    return tab.reshape(ROT, 2, S).transpose(1, 0, 2)


def token_plan(
    block_input,
    cotangent,
    lengths,
    ln1_gain,
    ln1_bias,
    ln2_gain,
    ln2_bias,
    w_query,
    b_query,
    w_shared,
    b_shared,
    w_out,
    b_out,
    w_up,
    b_up,
    w_down,
    b_down,
):
    S, D = block_input.shape[2:]
    R, HT = w_query.shape
    FT = w_up.shape[1]
    NF, T, NH = FT // 256, MB * S, 2 * HT // HEAD_DIM
    dims = dict(S=S, HT=HT, NF=NF, T=T, NH=NH)
    plane = (ZC, XC, CC, R)
    full = (2,) + plane
    t = lax.axis_index("tensor")

    def s(shape, dtype):
        return jax.ShapeDtypeStruct(shape, dtype)

    vm = pl.BlockSpec(memory_space=VMEM)
    hbm = pl.BlockSpec(memory_space=pl.ANY)
    smem = pl.BlockSpec(memory_space=pltpu.SMEM)

    nb = HT // 128 + 2 * NF + 1
    n_gather, n_reduce = NF + 3, NF + 2 + HT // 128
    n_early, n_late = 8 * ((D // 128 + 4 * NF + 7) // 8), 8 * ((5 * (D // 128) + 8) // 8)
    n_grads = 2 * HT + 128 + 2 * FT

    outs = pl.pallas_call(
        partial(block_kernel, dims),
        out_shape=[
            s((T, D), BF),
            s((T, D), BF),
            s((NF,) + full + (512,), BF),
            s((R, n_grads), F32),
            s((n_early, 128), F32),
            s((n_late, 128), F32),
        ],
        in_specs=[hbm, hbm, smem] + [vm] * 15,
        out_specs=[hbm] * 3 + [vm] * 3,
        scratch_shapes=[
            VMEM(plane + (128,), BF),
            VMEM(full + (HT,), BF),
            VMEM(full + (HT,), BF),
            VMEM((2 * HT, D), BF),
            VMEM((2,) + full + (512,), BF),
            VMEM((2, nb, 128), F32),
            VMEM((2 * HT + 128, 128), F32),
            VMEM((T, D), BF),
            VMEM((T, D), BF),
            VMEM((T, D), BF),
            VMEM((T, D), BF),
            VMEM((D, T), BF),
            VMEM((D, T), BF),
            VMEM((D, T), BF),
            VMEM((T, D), BF),
            VMEM((T, D), F32),
            VMEM((T, D), F32),
            VMEM((MB * NH, 1, S), F32),
            VMEM((MB, 128, S), BF),
            VMEM((MB, 128, S), BF),
            VMEM((MB, 2 * S, HEAD_DIM), BF),
            VMEM((MB, 2 * S, HEAD_DIM), BF),
            VMEM((MB, HEAD_DIM, 2 * S), BF),
            VMEM((MB, HEAD_DIM + 16, 2 * S), BF),
            VMEM((MB, S, 128), F32),
            VMEM((MB, S, S), F32),
            VMEM((MB, 2 * S, 128), F32),
            VMEM((MB, S, 128), BF),
            VMEM((MB, S, 128), BF),
            VMEM((T, 128), BF),
            VMEM((3,) + full + (512,), BF),
            VMEM(full + (HT,), BF),
            VMEM((HT // 128,) + full + (128,), BF),
            VMEM(full + (128,), BF),
            VMEM((8, D), F32),
            VMEM((10, n_early, 128), F32),
            VMEM((10, n_late, 128), F32),
            VMEM((NF + 2, 2, ZC, XC, R, 512), BF),
            VMEM((NF + 3, ZC, XC, R, 256), BF),
            VMEM((NF + 3, 2, ZC, R, 256), BF),
            VMEM((NF + 3, 2, ZC, R, 256), BF),
            VMEM((NF + 3, 2, 3, R, 256), BF),
            DMA((Gather.SLOTS, 4)),
            DMA((n_gather, 4)),
            DMA((Reduce.SLOTS, 4)),
            DMA((n_reduce, 4)),
            DMA((8,)),
            DMA((2,)),
            DMA((6 + 2 * MB,)),
            DMA((4,)),
            DMA((4,)),
        ],
        compiler_params=pltpu.CompilerParams(
            vmem_limit_bytes=VMEM_LIMIT, collective_id=0, has_side_effects=True
        ),
        name="block",
    )(
        block_input.reshape(T, D),
        cotangent.reshape(T, D),
        lengths.reshape(MB),
        jnp.asarray(angle_table(S)),
        ln1_gain,
        ln1_bias,
        ln2_gain,
        ln2_bias,
        w_query,
        b_query,
        w_shared,
        b_shared,
        w_out.T,
        b_out,
        w_up,
        b_up,
        w_down.T,
        b_down,
    )
    out, gx, _, grads, early, late = outs
    vec = s((D,), F32)
    shapes = [s((T, D), BF), s((T, D), BF), vec, vec, vec, vec, s((R, HT), F32), s((HT,), F32)]
    shapes += [s((R, 128), F32), s((128,), F32), s((R, HT), F32), vec, s((R, FT), F32)]
    shapes += [s((FT,), F32), s((R, FT), F32), vec]
    outs = pl.pallas_call(
        partial(finish_kernel, dims),
        out_shape=shapes,
        in_specs=[hbm, hbm, vm, vm, vm],
        out_specs=[hbm, hbm] + [vm] * 14,
        scratch_shapes=[VMEM((2, T, D), BF), DMA((4,))],
        compiler_params=pltpu.CompilerParams(vmem_limit_bytes=VMEM_LIMIT),
        name="finish",
    )(out, gx, grads, early, late)
    res = list(outs)
    res[0] = res[0].reshape(block_input.shape)
    res[1] = res[1].reshape(block_input.shape)
    res[10] = res[10].T
    res[14] = res[14].T
    return tuple(res)


def fits_token_plan(mesh):
    return dict(mesh.shape) == {"dp": ZC * XC * CC, "tensor": 2}


def solution(mesh):
    in_specs = (
        P(None, "dp", "tensor", None),
        P(None, "dp", "tensor", None),
        P(None, "dp"),
        P(),
        P(),
        P(),
        P(),
        P("dp", "tensor"),
        P("tensor"),
        P("dp", None),
        P(),
        P("tensor", "dp"),
        P(),
        P("dp", "tensor"),
        P("tensor"),
        P("tensor", "dp"),
        P(),
    )
    out_specs = (
        P(None, "dp", "tensor", None),
        P(None, "dp", "tensor", None),
        P(),
        P(),
        P(),
        P(),
        P("dp", "tensor"),
        P("tensor"),
        P("dp", None),
        P(),
        P("tensor", "dp"),
        P(),
        P("dp", "tensor"),
        P("tensor"),
        P("tensor", "dp"),
        P(),
    )
    step = token_plan if fits_token_plan(mesh) else per_device
    return jax.shard_map(
        step, mesh=mesh, in_specs=in_specs, out_specs=out_specs, check_vma=False
    )
```

```python
from functools import partial

import jax
import jax.numpy as jnp
import numpy as np
from jax import lax
from jax.experimental import pallas as pl
from jax.experimental.pallas import tpu as pltpu
from jax.sharding import PartitionSpec as P

HEAD_DIM = 64
ROT = 16
MB = 2
QBLK = 512


EPS = 1e-05


def tables(count):
    places = jnp.arange(count).astype(jnp.float32)
    freqs = jnp.power(10000.0, -jnp.arange(ROT // 2).astype(jnp.float32) * 2.0 / ROT)
    angles = places[:, None] * freqs[None, :]
    return (jnp.cos(angles)[:, None, :], jnp.sin(angles)[:, None, :])


def rotate(vector, cosine, sine):
    first = vector[..., : ROT // 2]
    second = vector[..., ROT // 2 : ROT]
    return jnp.concatenate(
        [first * cosine - second * sine, second * cosine + first * sine, vector[..., ROT:]], axis=-1
    )


def unrotate(grad, cosine, sine):
    first = grad[..., : ROT // 2]
    second = grad[..., ROT // 2 : ROT]
    return jnp.concatenate(
        [first * cosine + second * sine, second * cosine - first * sine, grad[..., ROT:]], axis=-1
    )


def normalize(vector):
    centre = vector - jnp.mean(vector, axis=-1, keepdims=True)
    spread = jnp.mean(centre * centre, axis=-1, keepdims=True)
    scale = lax.rsqrt(spread + EPS)
    return (centre * scale, scale)


def norm_back(grad, normed, scale, gain):
    weighted = grad * gain
    return scale * (
        weighted
        - jnp.mean(weighted, axis=-1, keepdims=True)
        - normed * jnp.mean(weighted * normed, axis=-1, keepdims=True)
    )


def block_scores(rows, keys, start, limit, count):
    scores = jnp.einsum("qhd,kd->hqk", rows, keys, preferred_element_type=jnp.float32)
    row_pos = start + jnp.arange(QBLK)
    key_pos = jnp.arange(count)
    allowed = (key_pos[None, :] <= row_pos[:, None]) & (key_pos[None, :] < limit)
    return (scores, allowed[None])


def attend(queries, keys, values, limit):
    count = queries.shape[0]

    def block(start):
        rows = lax.dynamic_slice_in_dim(queries, start, QBLK, 0)
        scores, allowed = block_scores(rows, keys, start, limit, count)
        scores = jnp.where(allowed, scores, jnp.float32(-1e30))
        top = jnp.max(scores, axis=-1, keepdims=True)
        expo = jnp.exp(scores - top)
        total = jnp.sum(expo, axis=-1, keepdims=True)
        weights = (expo / total).astype(jnp.bfloat16)
        result = jnp.einsum("hqk,kd->qhd", weights, values, preferred_element_type=jnp.float32)
        return (result, (top + jnp.log(total))[..., 0])

    starts = jnp.arange(count // QBLK) * QBLK
    results, logsum = lax.map(block, starts)
    return (results.reshape(count, -1, HEAD_DIM), logsum)


def attend_back(queries, keys, values, limit, logsum, grad_out):
    count = queries.shape[0]

    def block(carry, item):
        start, block_logsum = item
        rows = lax.dynamic_slice_in_dim(queries, start, QBLK, 0)
        grads = lax.dynamic_slice_in_dim(grad_out, start, QBLK, 0)
        scores, allowed = block_scores(rows, keys, start, limit, count)
        probs = jnp.where(allowed, jnp.exp(scores - block_logsum[:, :, None]), 0.0)
        weights = probs.astype(jnp.bfloat16)
        dprobs = jnp.einsum("qhd,kd->hqk", grads, values, preferred_element_type=jnp.float32)
        delta = jnp.sum(probs * dprobs, axis=-1, keepdims=True)
        dscores = (probs * (dprobs - delta)).astype(jnp.bfloat16)
        drows = jnp.einsum("hqk,kd->qhd", dscores, keys, preferred_element_type=jnp.float32)
        dkeys = carry[0] + jnp.einsum(
            "hqk,qhd->kd", dscores, rows, preferred_element_type=jnp.float32
        )
        dvalues = carry[1] + jnp.einsum(
            "hqk,qhd->kd", weights, grads, preferred_element_type=jnp.float32
        )
        return ((dkeys, dvalues), drows)

    starts = jnp.arange(count // QBLK) * QBLK
    empty = jnp.zeros((count, HEAD_DIM), jnp.float32)
    (dkeys, dvalues), drows = lax.scan(block, (empty, empty), (starts, logsum))
    return (drows.reshape(count, -1, HEAD_DIM), dkeys, dvalues)


def fetch_each(w_query, w_shared, w_out, w_up, w_down):
    return (
        lax.all_gather(w_query, "dp", axis=0, tiled=True),
        lax.all_gather(w_shared, "dp", axis=0, tiled=True),
        lax.all_gather(w_out, "dp", axis=1, tiled=True),
        lax.all_gather(w_up, "dp", axis=0, tiled=True),
        lax.all_gather(w_down, "dp", axis=1, tiled=True),
    )


def reduce_each(step_grads):
    return (
        lax.psum_scatter(step_grads[0], "dp", scatter_dimension=0, tiled=True),
        lax.psum_scatter(step_grads[1], "dp", scatter_dimension=0, tiled=True),
        lax.psum_scatter(step_grads[2], "dp", scatter_dimension=1, tiled=True),
        lax.psum_scatter(step_grads[3], "dp", scatter_dimension=0, tiled=True),
        lax.psum_scatter(step_grads[4], "dp", scatter_dimension=1, tiled=True),
    )


def per_device(
    block_input,
    cotangent,
    lengths,
    ln1_gain,
    ln1_bias,
    ln2_gain,
    ln2_bias,
    w_query,
    b_query,
    w_shared,
    b_shared,
    w_out,
    b_out,
    w_up,
    b_up,
    w_down,
    b_down,
):
    shard_rows = block_input.shape[2]
    groups = lax.axis_size("tensor")
    rank = lax.axis_index("tensor")
    seq_len = shard_rows * groups
    tail_bias = b_out + b_down
    weight_sums = None
    cos_all, sin_all = tables(seq_len)
    own_pos = rank * shard_rows + jnp.arange(shard_rows)
    outputs = []
    input_grads = []
    sum_bq = jnp.zeros(b_query.shape, jnp.float32)
    sum_bkv = jnp.zeros(b_shared.shape, jnp.float32)
    sum_bup = jnp.zeros(b_up.shape, jnp.float32)
    sum_gain1 = jnp.zeros(ln1_gain.shape, jnp.float32)
    sum_shift1 = jnp.zeros(ln1_gain.shape, jnp.float32)
    sum_gain2 = jnp.zeros(ln1_gain.shape, jnp.float32)
    sum_shift2 = jnp.zeros(ln1_gain.shape, jnp.float32)
    sum_out = jnp.zeros(ln1_gain.shape, jnp.float32)
    for micro in range(MB):
        fetched = fetch_each(w_query, w_shared, w_out, w_up, w_down)
        wq_all, wkv_all, wo_all, wup_all, wdown_all = fetched
        limit = lengths[micro, 0]
        inputs = block_input[micro, 0].astype(jnp.float32)
        normed_one, scale_one = normalize(inputs)
        normed_two, scale_two = normalize(inputs)
        low_one = (normed_one * ln1_gain + ln1_bias).astype(jnp.bfloat16)
        low_two = (normed_two * ln2_gain + ln2_bias).astype(jnp.bfloat16)
        whole_one, whole_two = (
            lax.all_gather(low_one, "tensor", axis=0, tiled=True),
            lax.all_gather(low_two, "tensor", axis=0, tiled=True),
        )
        query_lin = jnp.dot(whole_one, wq_all, preferred_element_type=jnp.float32) + b_query
        query_lin = query_lin.reshape(seq_len, -1, HEAD_DIM)
        queries = (rotate(query_lin, cos_all, sin_all) * 0.125).astype(jnp.bfloat16)
        shared = jnp.dot(whole_one, wkv_all, preferred_element_type=jnp.float32) + b_shared
        keys = rotate(shared[:, None, :HEAD_DIM], cos_all, sin_all)[:, 0].astype(jnp.bfloat16)
        values = shared[:, HEAD_DIM:].astype(jnp.bfloat16)
        attended, logsum = attend(queries, keys, values, limit)
        attended_low = attended.reshape(seq_len, -1).astype(jnp.bfloat16)
        hidden = jnp.dot(whole_two, wup_all, preferred_element_type=jnp.float32) + b_up
        active = jax.nn.gelu(hidden, approximate=False).astype(jnp.bfloat16)
        partial_out = jnp.dot(attended_low, wo_all, preferred_element_type=jnp.float32) + jnp.dot(
            active, wdown_all, preferred_element_type=jnp.float32
        )
        branch = lax.psum_scatter(partial_out, "tensor", scatter_dimension=0, tiled=True)
        outputs.append((inputs + branch + tail_bias).astype(jnp.bfloat16))
        valid = (own_pos < limit).astype(jnp.float32)[:, None]
        upstream = cotangent[micro, 0].astype(jnp.float32) * valid
        whole_up = lax.all_gather(upstream.astype(jnp.bfloat16), "tensor", axis=0, tiled=True)
        sum_out = sum_out + jnp.sum(upstream, axis=0)
        grad_down = jnp.einsum("lf,ld->fd", active, whole_up, preferred_element_type=jnp.float32)
        dactive = jnp.einsum("ld,fd->lf", whole_up, wdown_all, preferred_element_type=jnp.float32)
        gelu_pull = jax.vjp(partial(jax.nn.gelu, approximate=False), hidden)[1]
        dhidden = gelu_pull(dactive)[0].astype(jnp.bfloat16)
        sum_bup = sum_bup + jnp.sum(dhidden.astype(jnp.float32), axis=0)
        grad_up = jnp.einsum("ld,lf->df", whole_two, dhidden, preferred_element_type=jnp.float32)
        dnormed_two = jnp.einsum("lf,df->ld", dhidden, wup_all, preferred_element_type=jnp.float32)
        dattended = jnp.einsum("ld,ed->le", whole_up, wo_all, preferred_element_type=jnp.float32)
        dattended = dattended.astype(jnp.bfloat16).reshape(seq_len, -1, HEAD_DIM)
        grad_out = jnp.einsum(
            "le,ld->ed", attended_low, whole_up, preferred_element_type=jnp.float32
        )
        dqueries, dkeys, dvalues = attend_back(queries, keys, values, limit, logsum, dattended)
        dquery_lin = (
            unrotate(dqueries * 0.125, cos_all, sin_all).reshape(seq_len, -1).astype(jnp.bfloat16)
        )
        dkey_lin = unrotate(dkeys[:, None, :], cos_all, sin_all)[:, 0]
        dshared = lax.psum(jnp.concatenate([dkey_lin, dvalues], axis=1), "tensor")
        dshared = dshared.astype(jnp.bfloat16)
        sum_bq = sum_bq + jnp.sum(dquery_lin.astype(jnp.float32), axis=0)
        sum_bkv = sum_bkv + jnp.sum(dshared.astype(jnp.float32), axis=0)
        grad_q = jnp.einsum("ld,le->de", whole_one, dquery_lin, preferred_element_type=jnp.float32)
        grad_kv = jnp.einsum("ld,lc->dc", whole_one, dshared, preferred_element_type=jnp.float32)
        dnormed_one = jnp.einsum(
            "le,de->ld", dquery_lin, wq_all, preferred_element_type=jnp.float32
        )
        dnormed_one, dnormed_two = (
            lax.psum_scatter(dnormed_one, "tensor", scatter_dimension=0, tiled=True),
            lax.psum_scatter(dnormed_two, "tensor", scatter_dimension=0, tiled=True),
        )
        own_shared = lax.dynamic_slice_in_dim(dshared, rank * shard_rows, shard_rows, 0)
        dnormed_one = dnormed_one + jnp.einsum(
            "lc,dc->ld", own_shared, wkv_all, preferred_element_type=jnp.float32
        )
        sum_gain1 = sum_gain1 + jnp.sum(dnormed_one * normed_one, axis=0)
        sum_shift1 = sum_shift1 + jnp.sum(dnormed_one, axis=0)
        sum_gain2 = sum_gain2 + jnp.sum(dnormed_two * normed_two, axis=0)
        sum_shift2 = sum_shift2 + jnp.sum(dnormed_two, axis=0)
        dinputs = (
            upstream
            + norm_back(dnormed_one, normed_one, scale_one, ln1_gain)
            + norm_back(dnormed_two, normed_two, scale_two, ln2_gain)
        )
        input_grads.append(dinputs.astype(jnp.bfloat16))
        step_grads = (grad_q, grad_kv, grad_out, grad_up, grad_down)
        step_grads = reduce_each(step_grads)
        if weight_sums is None:
            weight_sums = step_grads
        else:
            weight_sums = jax.tree.map(jnp.add, weight_sums, step_grads)
    output = jnp.stack(outputs, axis=0)[:, None]
    grad_input = jnp.stack(input_grads, axis=0)[:, None]
    sum_bq, sum_bkv, sum_bup = lax.psum((sum_bq, sum_bkv, sum_bup), "dp")
    sum_gain1, sum_shift1, sum_gain2, sum_shift2, sum_out = lax.psum(
        (sum_gain1, sum_shift1, sum_gain2, sum_shift2, sum_out), ("dp", "tensor")
    )
    grad_q, grad_kv, grad_o, grad_up, grad_down = weight_sums
    return (
        output,
        grad_input,
        sum_gain1,
        sum_shift1,
        sum_gain2,
        sum_shift2,
        grad_q,
        sum_bq,
        grad_kv,
        sum_bkv,
        grad_o,
        sum_out,
        grad_up,
        sum_bup,
        grad_down,
        sum_out,
    )


MESH = pl.DeviceIdType.MESH
BF = jnp.bfloat16
F32 = jnp.float32
LOG2E = 1.4426950408889634
LN2 = 0.6931471805599453
NEG = -1e30
ZC, XC, CC = 4, 2, 2
DMA = pltpu.SemaphoreType.DMA
VMEM = pltpu.VMEM
VMEM_LIMIT = (64 << 20) - 65536


def nn(a, b):
    return lax.dot_general(a, b, (((1,), (0,)), ((), ())), preferred_element_type=F32)


def nt(a, b):
    return lax.dot_general(a, b, (((1,), (1,)), ((), ())), preferred_element_type=F32)


def tn(a, b):
    return lax.dot_general(a, b, (((0,), (0,)), ((), ())), preferred_element_type=F32)


def eye(n):
    return (
        lax.broadcasted_iota(jnp.int32, (n, n), 0) == lax.broadcasted_iota(jnp.int32, (n, n), 1)
    ).astype(BF)


def flat(block):
    return block.reshape(-1, block.shape[-1])


class Place:
    def __init__(self):
        self.dp = lax.axis_index("dp")
        self.t = lax.axis_index("tensor")
        self.core = lax.rem(self.dp, CC)
        self.x = lax.rem(lax.div(self.dp, CC), XC)
        self.z = lax.div(self.dp, CC * XC)

    def at(self, z, x, core):
        return (z * XC + x) * CC + core

    def z_peer(self, d):
        return {"dp": self.at(lax.rem(self.z + d, ZC), self.x, self.core)}

    def x_peer(self):
        return {"dp": self.at(self.z, 1 - self.x, self.core)}

    def core_peer(self):
        return {"dp": self.at(self.z, self.x, 1 - self.core)}

    def y_peer(self):
        return {"tensor": 1 - self.t}

    def layer_peers(self):
        res = []
        for k in range(1, 8):
            x = 1 - self.x if k & 1 else self.x
            t = 1 - self.t if k & 2 else self.t
            core = 1 - self.core if k & 4 else self.core
            res.append({"dp": self.at(self.z, x, core), "tensor": t})
        return res

    def greet(self):
        bar = pltpu.get_barrier_semaphore()
        peers = [self.z_peer(d) for d in (1, 2, 3)] + self.layer_peers()
        for p in peers:
            pl.semaphore_signal(bar, inc=1, device_id=p, device_id_type=MESH)
        return bar, len(peers)


def remote(src, dst, ss, rs, peer):
    return pltpu.make_async_remote_copy(
        src_ref=src, dst_ref=dst, send_sem=ss, recv_sem=rs, device_id=peer, device_id_type=MESH
    )


def split_cols(width):
    a = (width // 128 + 1) // 2 * 128
    return ((0, a), (a, width - a))


class Gather:
    SLOTS = 3

    def __init__(self, place, pieces, sends, gots):
        self.p = place
        self.pieces = pieces
        self.sends, self.gots = sends, gots

    def own(self, c, h):
        p = self.p
        _, o, w, order = self.pieces[c][0][h]
        index = (p.z, p.x, p.core, slice(None), pl.ds(o, w))
        return self.pieces[c][1].at[(p.t,) + index if "y" in order else index]

    def copies(self, c, k):
        p = self.p
        every = slice(None)
        res = []
        for h, (src, o, w, order) in enumerate(self.pieces[c][0]):
            if k == 0:
                pairs = [(src, self.own(c, h), p.z_peer(d)) for d in (1, 2, 3)]
            elif k <= len(order):
                done = order[:k]
                index = (every, every if "x" in done else p.x, p.core, every, pl.ds(o, w))
                if "y" in order:
                    index = (every if "y" in done else p.t,) + index
                view = self.pieces[c][1].at[index]
                axis = order[k] if k < len(order) else "core"
                peers = {"x": p.x_peer(), "y": p.y_peer(), "core": p.core_peer()}
                pairs = [(view, view, peers[axis])]
            else:
                pairs = []
            for a, b, peer in pairs:
                res.append(remote(a, b, self.sends.at[c % self.SLOTS, k], self.gots.at[c, k], peer))
        return res

    def total(self, c, k):
        parts, out = self.pieces[c]
        z = pl.ds(0, 3) if k == 0 else slice(None)
        x = slice(None) if k > 1 else 0
        index = (z, x, 0)
        if "y" in parts[0][3]:
            index = (slice(None) if k > 2 else 0,) + index
        view = out.at[index]
        return remote(
            view, view, self.sends.at[c % self.SLOTS, k], self.gots.at[c, k], self.p.core_peer()
        )

    def run(self, ops):
        for op in ops:
            c, k = (op, -1) if isinstance(op, int) else op
            if k >= 0:
                self.total(c, k).wait()
            for cp in self.copies(c, k + 1):
                cp.start()


class AllSum:
    def __init__(self, place, buf, got, sems):
        self.p = place
        self.buf, self.got, self.sems = buf, got, sems

    def part(self, k):
        return (7, 3) if k else (0, 7)

    def start(self, k):
        peers = [self.p.z_peer(d) for d in (1, 2, 3)] if k else self.p.layer_peers()
        at, _ = self.part(k)
        for i, peer in enumerate(peers):
            got = self.got.at[at + i]
            remote(self.buf, got, self.sems.at[2 * k], self.sems.at[2 * k + 1], peer).start()

    def end(self, k):
        at, n = self.part(k)
        view = self.got.at[pl.ds(at, n)]
        whole = remote(
            view, view, self.sems.at[2 * k], self.sems.at[2 * k + 1], self.p.core_peer()
        )
        whole.wait()
        total = self.buf[...]
        for i in range(at, at + n):
            total = total + self.got[i]
        self.buf[...] = total


def normal_rows(rows):
    mean = jnp.mean(rows, axis=-1, keepdims=True)
    centre = rows - mean
    var = jnp.mean(centre * centre, axis=-1, keepdims=True)
    scale = lax.rsqrt(var + EPS)
    return centre * scale, scale


def rotate_t(v, cosine, sine):
    a, b = v[0:8], v[8:16]
    return jnp.concatenate([a * cosine - b * sine, b * cosine + a * sine, v[16:]], axis=0)


def unrotate_t(v, cosine, sine):
    a, b = v[0:8], v[8:16]
    return jnp.concatenate([a * cosine + b * sine, b * cosine - a * sine, v[16:]], axis=0)


def fill_bias(place, lens_ref, other_ref, own_ref, S):
    t = place.t
    for m in range(MB):
        limit = lens_ref[m]
        key = lax.broadcasted_iota(jnp.int32, (S, 128), 0)
        limit_other = jnp.where(t == 1, limit, 0)
        other_ref[m] = jnp.where(key < limit_other, 0.0, NEG).astype(F32)
        key = lax.broadcasted_iota(jnp.int32, (S, S), 0)
        row = lax.broadcasted_iota(jnp.int32, (S, S), 1)
        own = (key <= row) & (key + t * S < limit)
        own_ref[m] = jnp.where(own, 0.0, NEG).astype(F32)


def masked_rows(place_t, lens_ref, dy, start, S):
    m, off = divmod(start, S)
    pos = place_t * S + off + lax.broadcasted_iota(jnp.int32, (dy.shape[0], 1), 0)
    return jnp.where(pos < lens_ref[m], dy.astype(F32), 0.0)


class Reduce:
    SLOTS = 3

    def __init__(self, place, pieces, rc, r2a, r2b, r3, r4, sends, gots):
        self.p = place
        self.pieces = pieces
        self.rc, self.r2a, self.r2b, self.r3, self.r4 = rc, r2a, r2b, r3, r4
        self.sends, self.gots = sends, gots

    def part(self, c, h):
        r, n, o, w = self.pieces[c][1][h]
        _, first, _, second = self.pieces[c][3]
        o += first
        return (slice(r, r + n), slice(o, o + w)), (slice(0, n), slice(second, second + w))

    def wide(self, c):
        first = self.pieces[c][3][1]
        return slice(first, first + self.pieces[c][0].shape[-1])

    def sems(self, c, k):
        return self.sends.at[c % self.SLOTS, k], self.gots.at[c, k]

    def copies(self, c, k):
        p = self.p
        if k == 0:
            src = self.pieces[c][0].at[:, :, :, 1 - p.core]
            dst = self.rc.at[self.pieces[c][3][0], :, :, :, :, self.wide(c)]
            return [remote(src, dst, *self.sems(c, k), p.core_peer())]
        res = []
        a, _, b, _ = self.pieces[c][3]
        for h in (0, 1):
            here, there = self.part(c, h)
            if k == 1 and h == 0:
                src, dst = self.rc.at[(a, 1 - p.t, slice(None), slice(None)) + here], self.r2a
                todo = [(src, dst.at[(b, slice(None), slice(None)) + there], p.y_peer())]
            elif k == 1:
                src, dst = self.rc.at[(a, slice(None), slice(None), 1 - p.x) + here], self.r2b
                todo = [(src, dst.at[(b, slice(None), slice(None)) + there], p.x_peer())]
            elif k == 2:
                if h == 0:
                    src, peer = self.r2a.at[(b, slice(None), 1 - p.x) + there], p.x_peer()
                else:
                    src, peer = self.r2b.at[(b, 1 - p.t, slice(None)) + there], p.y_peer()
                todo = [(src, self.r3.at[(b, h, slice(None)) + there], peer)]
            else:
                todo = [
                    (
                        self.r3.at[(b, h, lax.rem(p.z + d, ZC)) + there],
                        self.r4.at[(b, h, d - 1) + there],
                        p.z_peer(d),
                    )
                    for d in (1, 2, 3)
                ]
            res += [remote(src, dst, *self.sems(c, k), peer) for src, dst, peer in todo]
        return res

    def total(self, c, k):
        cols = self.wide(c)
        every = slice(None)
        index = {
            0: (every, every, every, every, cols),
            1: (0, every, every, every, cols),
            2: (0, every, 0, every, cols),
            3: (0, pl.ds(0, 3), 0, every, cols),
        }[k]
        view = self.rc.at[(self.pieces[c][3][0],) + index]
        return remote(view, view, *self.sems(c, k), self.p.core_peer())

    def start(self, c, k):
        for cp in self.copies(c, k):
            cp.start()

    def add(self, c, k):
        p = self.p
        a, _, b, _ = self.pieces[c][3]
        if k == 1:
            cols = self.wide(c)
            mine = self.pieces[c][0][:, :, :, p.core].astype(F32)
            mine = mine + self.rc[a, :, :, :, :, cols].astype(F32)
            self.rc[a, :, :, :, :, cols] = mine.astype(BF)
            return
        sums = []
        for h in (0, 1):
            here, there = self.part(c, h)
            every = slice(None)
            if k == 2:
                if h == 0:
                    ref, mine = self.r2a, self.rc[(a, p.t, every, every) + here]
                else:
                    ref, mine = self.r2b, self.rc[(a, every, every, p.x) + here]
                at = (b, every, every) + there
                ref[at] = (mine.astype(F32) + ref[at].astype(F32)).astype(BF)
            elif k == 3:
                if h == 0:
                    mine = self.r2a[(b, every, p.x) + there]
                else:
                    mine = self.r2b[(b, p.t, every) + there]
                at = (b, h, every) + there
                self.r3[at] = (mine.astype(F32) + self.r3[at].astype(F32)).astype(BF)
            else:
                total = self.r3[(b, h, p.z) + there].astype(F32)
                for d in range(3):
                    total = total + self.r4[(b, h, d) + there].astype(F32)
                sums.append(total)
        if k == 4:
            self.pieces[c][2](sums)

    def run(self, ops):
        for c, k in ops:
            if k:
                self.total(c, k - 1).wait()
                self.add(c, k)
            if k < 4:
                self.start(c, k)


HEAD_OPS = (
    (0, 1),
    ((0, 0), (1, 0), 2),
    ((0, 1), (1, 1), 3),
    ((0, 2),),
    ((1, 2), 4),
    ((1, 3), (2, 0), (3, 0), 5),
)
ATTENTION_OPS = {
    0: ((2, 1), 6),
    2: ((4, 0),),
    4: ((3, 1), (5, 0), 7),
    5: ((2, 2),),
    7: ((3, 2), (2, 3), (4, 1), (6, 0), 8),
}
BACK_OPS = {
    0: ((3, 3), (4, 2), (5, 1), (7, 0)),
    3: ((4, 3), (5, 2), (6, 1), (8, 0)),
    5: ((5, 3), (6, 2), (7, 1)),
}
FFN_OPS = {
    0: (),
    1: ((6, 3), (7, 2), (8, 1)),
    2: ((7, 3), (8, 2)),
    3: ((8, 3),),
}


FFN_SUMS = {
    0: ((0, 1),),
    2: ((0, 2), (1, 1)),
    3: ((0, 3), (2, 1)),
    4: ((0, 4), (1, 2), (3, 1)),
    5: ((1, 3), (2, 2), (4, 1)),
}
BACK_SUMS = {
    6: ((1, 4), (2, 3), (3, 2), (5, 1)),
    8: ((2, 4), (3, 3), (4, 2), (6, 1)),
    9: ((7, 1),),
    10: ((3, 4), (4, 3), (5, 2)),
    11: ((7, 2), (8, 1), (6, 2)),
}
LAST_SUMS = (
    ((4, 4), (5, 3), (7, 3), (8, 2)),
    ((9, 1), (6, 3)),
    ((10, 1), (9, 2), (5, 4), (8, 3)),
    ((10, 2), (6, 4), (9, 3), (7, 4)),
    ((10, 3), (8, 4)),
    ((9, 4), (10, 4)),
)


def block_kernel(
    dims,
    x_hbm,
    dy_hbm,
    lens_ref,
    tab_ref,
    g1_ref,
    b1_ref,
    g2_ref,
    b2_ref,
    wq_in,
    bq_ref,
    wsh_in,
    bsh_ref,
    wout_in,
    bout_ref,
    wup_in,
    bup_ref,
    wdown_in,
    bdown_ref,
    out_hbm,
    gx_hbm,
    wf,
    grads,
    early,
    late,
    wsh,
    wq,
    wb,
    won,
    wv,
    ball,
    bcol,
    x_ref,
    dym,
    h1,
    h2,
    qt,
    att,
    da,
    tmp,
    acc,
    dh2,
    lse_ref,
    kvt,
    kvo,
    kc,
    vc,
    kt,
    vte,
    bias_o,
    bias_s,
    dkv,
    dkvs,
    dkvr,
    dkvn,
    gring,
    gb,
    gq,
    gkv,
    sums,
    early_in,
    late_in,
    rc,
    r2a,
    r2b,
    r3,
    r4,
    gsend,
    gsem,
    rsend,
    rsem,
    lsem,
    wsem,
    ysem,
    esem,
    asem,
):
    S, HT, NH, NF, T = dims["S"], dims["HT"], dims["NH"], dims["NF"], dims["T"]
    D = x_ref.shape[1]
    R = wq_in.shape[0]
    NB = S // 256
    p = Place()
    bar, npeers = p.greet()
    x_copy = pltpu.make_async_copy(x_hbm, x_ref, lsem.at[1])
    x_copy.start()
    dy_copy = pltpu.make_async_copy(dy_hbm, dym, lsem.at[0])
    dy_copy.start()

    def parts_of(ref, widths, orders):
        at = [sum(widths[:i]) for i in range(len(widths))]
        return [(ref.at[:, pl.ds(o, w)], o, w, order) for o, w, order in zip(at, widths, orders)]

    wide = [w for _, w in split_cols(HT)]
    pieces = [
        ([(wsh_in, 0, 128, "zx")], wsh),
        (parts_of(wq_in, wide, ("zxy", "zyx")), wq),
        (parts_of(wout_in, wide, ("zxy", "zyx")), wb),
    ]
    for f in range(NF):
        cols = pl.ds(256 * f, 256)
        parts = [(wup_in.at[:, cols], 0, 256, "zxy"), (wdown_in.at[:, cols], 256, 256, "zyx")]
        pieces.append((parts, wf.at[f]))
    g = Gather(p, pieces, gsend, gsem)
    pl.semaphore_wait(bar, npeers)
    g.run(HEAD_OPS[0])
    locals_ = [
        pltpu.make_async_copy(wsh_in, wsh.at[p.z, p.x, p.core], lsem.at[2]),
        pltpu.make_async_copy(wq_in, wq.at[p.t, p.z, p.x, p.core], lsem.at[3]),
        pltpu.make_async_copy(wout_in, wb.at[p.t, p.z, p.x, p.core], lsem.at[4]),
    ]
    for cp in locals_:
        cp.start()
    for c in range(3, len(pieces)):
        for h in (0, 1):
            pltpu.make_async_copy(pieces[c][0][h][0], g.own(c, h), lsem.at[5]).start()
    held = wf.at[:, 0, 0, 0, 0]
    locals_.append(pltpu.make_async_copy(held, held, lsem.at[5]))
    first = HT // 128
    rows_b = ball.shape[1]
    ball[p.t, 0:first, :] = bq_ref[...].reshape(first, 128)
    ball[p.t, first : first + 2 * NF, :] = bup_ref[...].reshape(2 * NF, 128)
    ball[p.t, first + 2 * NF :, :] = jnp.zeros((rows_b - first - 2 * NF, 128), F32)
    bias_copy = remote(ball.at[p.t], ball.at[p.t], ysem.at[0], ysem.at[1], p.y_peer())
    bias_copy.start()

    gain1, shift1, gain2, shift2 = (
        ref[...].reshape(1, D) for ref in (g1_ref, b1_ref, g2_ref, b2_ref)
    )

    def norm_block(i):
        rows = pl.ds(pl.multiple_of(i * 128, 128), 128)
        z, _ = normal_rows(x_ref[rows, :].astype(F32))
        h1[rows, :] = (z * gain1 + shift1).astype(BF)
        h2[rows, :] = (z * gain2 + shift2).astype(BF)

    half = T // 256
    x_copy.wait()
    pl.loop(0, half)(norm_block)
    for cp in locals_:
        cp.wait()
    g.run(HEAD_OPS[1])
    pl.loop(half, 2 * half)(norm_block)
    g.run(HEAD_OPS[2])
    fill_bias(p, lens_ref, bias_o, bias_s, S)
    for ref in (dkv, dh2, sums):
        ref[...] = jnp.zeros_like(ref)
    bias_copy.wait()
    nq = HT // 128
    for t in range(2):
        for j in range(nq):
            row = jnp.broadcast_to(ball[t, j : j + 1, :], (128, 128))
            bcol[(t * nq + j) * 128 : (t * nq + j + 1) * 128, :] = row.T
    bcol[2 * HT : 2 * HT + 128, :] = jnp.broadcast_to(bsh_ref[...].reshape(1, 128), (128, 128)).T
    g.run(HEAD_OPS[3])

    id256 = eye(256)
    cosine, sine = tab_ref[p.t, 0:8, :], tab_ref[p.t, 8:16, :]
    wsh_t = nt(eye(128), flat(wsh[...])).astype(BF)
    kv_copies = [
        remote(kvt.at[m], kvo.at[m], ysem.at[2 + 2 * m], ysem.at[3 + 2 * m], p.y_peer())
        for m in range(MB)
    ]
    for m in range(MB):
        kv = nt(wsh_t, h1[m * S : m * S + S, :]) + bcol[2 * HT : 2 * HT + 128, 0:1]
        kvt[m, 0:HEAD_DIM, :] = rotate_t(kv[0:HEAD_DIM], cosine, sine).astype(BF)
        kvt[m, HEAD_DIM:, :] = kv[HEAD_DIM:].astype(BF)
    g.run(HEAD_OPS[4])
    kv_copies[0].start()
    dy_copy.wait()
    for b in range(T // 256):
        rows = slice(b * 256, b * 256 + 256)
        dy = masked_rows(p.t, lens_ref, dym[rows, :], b * 256, S)
        dym[rows, :] = dy.astype(BF)
        sums[6:7, :] += jnp.sum(dy, axis=0, keepdims=True)
    g.run(HEAD_OPS[5])

    for t in range(2):
        wq_t = nt(eye(HT), flat(wq[t])).astype(BF)
        for m in range(MB):
            cols = slice(m * S, m * S + S)
            q = nt(wq_t, h1[cols, :])
            for h in range(HT // HEAD_DIM):
                base = t * HT + h * HEAD_DIM
                qh = q[h * HEAD_DIM : (h + 1) * HEAD_DIM] + bcol[base : base + HEAD_DIM, 0:1]
                qh = rotate_t(qh, cosine, sine) * (0.125 * LOG2E)
                qt[base : base + HEAD_DIM, cols] = qh.astype(BF)

    def both_halves(m):
        kv_copies[m].wait()
        for part, src in ((0, kvo), (1, kvt)):
            keys = slice(part * S, part * S + S)
            kt[m, :, keys] = src[m, 0:HEAD_DIM, :]
            vte[m, 0:HEAD_DIM, keys] = src[m, HEAD_DIM:, :]
        vte[m, HEAD_DIM:, :] = (
            lax.broadcasted_iota(jnp.int32, (16, 2 * S), 0) == 0
        ).astype(BF)
        for b in range(2 * NB):
            blk = slice(b * 256, b * 256 + 256)
            kc[m, blk, :] = nt(id256, kt[m, :, blk]).astype(BF)
            vc[m, blk, :] = nt(id256, vte[m, 0:HEAD_DIM, blk]).astype(BF)

    both_halves(0)

    def spots(i, group, by_thirds=False):
        res = []
        for u in range(group):
            j = i * group + u
            m, h = lax.div(j, NH), lax.rem(j, NH)
            if by_thirds:
                k = lax.div(h, 2)
                h = lax.rem(k, 2) * (NH // 2) + lax.div(k, 2) * 2 + u
                j = m * NH + h
            head = pl.ds(pl.multiple_of(h * HEAD_DIM, HEAD_DIM), HEAD_DIM)
            for r in range(NB):
                cols = pl.ds(pl.multiple_of(m * S + r * 256, 256), 256)
                res.append((j, m, head, cols, S + 256 * (r + 1), r))
        return res

    def scores(m, q, nk, r):
        s = nn(kc[m, 0:nk, :], q)
        wide = slice(r * 256, r * 256 + 256)
        other = bias_o[m]
        other = jnp.concatenate([other, other], axis=1)
        return jnp.concatenate([s[0:S] + other, s[S:nk] + bias_s[m, 0 : nk - S, wide]], axis=0)

    group = 3

    @pl.loop(0, MB * NH // group)
    def _(i):
        for m in range(1, MB):
            pl.when(i == (m - 1) * NH // group)(kv_copies[m].start)
            pl.when(i == m * NH // group)(partial(both_halves, m))
        for at, ops in ATTENTION_OPS.items():
            pl.when(i == at)(partial(g.run, ops))
        todo = spots(i, group)
        sc = [scores(m, qt[head, cols], nk, r) for _, m, head, cols, nk, r in todo]
        tops = [jnp.max(s, axis=0, keepdims=True) for s in sc]
        ex = [jnp.exp2(s - top).astype(BF) for s, top in zip(sc, tops)]
        for (j, m, head, cols, nk, r), e, top in zip(todo, ex, tops):
            o = nn(vte[m, :, 0:nk], e)
            total = o[HEAD_DIM : HEAD_DIM + 1]
            att[head, cols] = (o[0:HEAD_DIM] * (1.0 / total)).astype(BF)
            lse_ref[j, :, r * 256 : r * 256 + 256] = top + jnp.log2(total)

    for t in range(2):
        won[t * HT : (t + 1) * HT, :] = nt(eye(HT), flat(wb[t])).astype(BF)

    def load(f, slot):
        return pltpu.make_async_copy(wf.at[f], wv.at[slot], wsem.at[slot])

    for b in range(T // 256):
        rows = slice(b * 256, b * 256 + 256)
        tmp[rows, :] = nt(id256, att[:, rows]).astype(BF)
    tail_bias = (bout_ref[...] + bdown_ref[...]).reshape(1, D)
    acc[...] = x_ref[...].astype(F32) + tail_bias + nn(tmp[...], won[...])
    for t in range(2):
        cols = slice(t * HT, (t + 1) * HT)
        gb[t] = tn(dym[...], tmp[:, cols]).astype(BF).reshape(ZC, XC, CC, R, HT)

    def put(*firsts):
        def store(parts):
            for o, v in zip(firsts, parts):
                grads[:, o : o + v.shape[1]] = v

        return store

    at_out, at_up, at_down = HT + 128, 2 * HT + 128, 2 * HT + 128 + 256 * NF
    thirds = HT // 128

    def by_cols(*widths):
        at = [sum(widths[:i]) for i in range(len(widths))]
        return [(0, R, o, w) for o, w in zip(at, widths)]

    def put_rows(first):
        def store(parts):
            r = 0
            for v in parts:
                grads[r : r + v.shape[0], first : first + 128] = v
                r += v.shape[0]

        return store

    by_rows = [(0, 32, 0, 128), (32, R - 32, 0, 128)]
    sums_of = [(gb, by_cols(*wide), put(at_out, at_out + wide[0]), (0, 0, 0, 0))]
    for f in range(NF):
        store = put(at_up + 256 * f, at_down + 256 * f)
        sums_of.append((gring.at[f % 3], by_cols(256, 256), store, (1 + f, 0, 1 + f, 0)))
    for k in range(thirds + 1):
        store = put_rows(128 * k)
        slot = (NF + 1, 128 * k, NF + 1 + k // 2, 128 * (k % 2))
        sums_of.append((gq.at[k] if k < thirds else gkv, by_rows, store, slot))
    red = Reduce(p, sums_of, rc, r2a, r2b, r3, r4, rsend, rsem)
    last = NF + 1
    red.run([(0, 0)])

    n = D // 128
    early_sum = AllSum(p, early, early_in, esem)
    da[...] = nt(won[...], dym[...]).astype(BF)
    back = 2
    dkv_copies = [
        remote(dkvs.at[m], dkvr.at[m], ysem.at[6 + 2 * m], ysem.at[7 + 2 * m], p.y_peer())
        for m in range(MB)
    ]

    def send_dkv(m):
        dkvs[m] = dkv[m, 0:S, :].astype(BF)
        dkv_copies[m].start()

    def query_third(k):
        for t in range(2):
            at = t * HT + 128 * k
            for b in range(T // 256):
                rows = slice(b * 256, b * 256 + 256)
                tmp[rows, at : at + 128] = nt(id256, qt[at : at + 128, rows]).astype(BF)
            v = tn(h1[...], tmp[:, at : at + 128]).astype(BF)
            gq[k, t] = v.reshape(ZC, XC, CC, R, 128)
        red.run([(last + k, 0)])

    def own_dkv(m):
        dkv_copies[m].wait()
        both = (dkv[m, S : 2 * S, :] + dkvr[m].astype(F32)).T
        dk = unrotate_t(both[0:HEAD_DIM], cosine, sine) * LN2
        both = jnp.concatenate([dk, both[HEAD_DIM:]], axis=0).astype(BF)
        for b in range(NB):
            rows = slice(m * S + b * 256, m * S + b * 256 + 256)
            dkvn[rows, :] = nt(id256, both[:, b * 256 : b * 256 + 256]).astype(BF)

    def early_next():
        early_sum.end(0)
        early_sum.start(1)

    def back_step(i):
        for at, ops in BACK_OPS.items():
            pl.when(i == at)(partial(g.run, ops))
        pl.when(i == NH // back + 2)(early_next)
        pl.when(i == NH // back + 3)(partial(own_dkv, 0))
        for at, ops in BACK_SUMS.items():
            pl.when(i == at)(partial(red.run, ops))
        for k in range(thirds - 1):
            at = MB * NH // back - 2 * (thirds - 1 - k)
            pl.when(i == at)(partial(query_third, k))
        todo = spots(i, back, True)
        qs = [qt[head, cols] for _, m, head, cols, nk, r in todo]
        das = [da[head, cols] for _, m, head, cols, nk, r in todo]
        sc = [scores(m, q, nk, r) for (_, m, head, cols, nk, r), q in zip(todo, qs)]
        dp = [nn(vc[m, 0:nk, :], d) for (_, m, head, cols, nk, r), d in zip(todo, das)]
        pr, ds = [], []
        for (j, m, head, cols, nk, r), d, s, dpj in zip(todo, das, sc, dp):
            delta = jnp.sum(d.astype(F32) * att[head, cols].astype(F32), axis=0, keepdims=True)
            w = jnp.exp2(s - lse_ref[j, :, r * 256 : r * 256 + 256])
            pr.append(w.astype(BF))
            ds.append((w * (dpj - delta)).astype(BF))
        for (j, m, head, cols, nk, r), d in zip(todo, ds):
            wide = slice(r * 256, r * 256 + 256)
            dq = nn(kt[m, :, 0:nk], d)
            dq = unrotate_t(dq, tab_ref[p.t, 0:8, wide], tab_ref[p.t, 8:16, wide])
            qt[head, cols] = (dq * 0.125).astype(BF)
        m = todo[0][1]
        for blk in range(NB):
            lo = 0 if blk == 0 else S + 256 * blk
            hi = S + 256 * (blk + 1)
            left, right = [], []
            for u, (_, _, _, _, nk, r) in enumerate(todo):
                if nk >= hi:
                    zero = jnp.zeros_like(qs[u])
                    left += [ds[u][lo:hi], pr[u][lo:hi]]
                    right += [
                        jnp.concatenate([qs[u], zero], axis=0),
                        jnp.concatenate([zero, das[u]], axis=0),
                    ]
            dkv[m, lo:hi, :] += nt(
                jnp.concatenate(left, axis=1), jnp.concatenate(right, axis=1)
            )

    per = NH // back
    lead = per * (MB - 1)
    def ffn_step(f):
        slot = lax.rem(f, 2)
        load(f, slot).wait()
        for k in range(NF - 1):

            @pl.when(f == k)
            def _():
                g.run(FFN_OPS.get(k, ()))
                load(k + 1, (k + 1) % 2).start()

        for k, ops in FFN_SUMS.items():
            pl.when(f == k)(partial(red.run, ops))
        wu = [flat(wv[slot, t, :, :, :, :, 0:256]) for t in range(2)]
        wd = [flat(wv[slot, t, :, :, :, :, 256:512]) for t in range(2)]
        gslot = lax.rem(f, 3)
        hid = [nn(h2[...], wu[t]) for t in range(2)]
        dact = [nn(dym[...], wd[t]) for t in range(2)]
        act, dhid = [], []
        for t in range(2):
            row = jnp.concatenate(
                [ball[t, pl.ds(first + 2 * f, 1), :], ball[t, pl.ds(first + 2 * f + 1, 1), :]],
                axis=1,
            )
            u = hid[t] + row
            cdf = 0.5 + 0.5 * lax.erf(u * 0.7071067811865476)
            dens = jnp.exp(-0.5 * u * u) * 0.3989422804014327
            act.append((u * cdf).astype(BF))
            d = (dact[t] * (cdf + u * dens)).astype(BF)
            dhid.append(d)
            total = jnp.sum(d.astype(F32), axis=0, keepdims=True)
            for j in (0, 1):
                at = D // 128 + 4 * f + 2 * t + j
                early[pl.ds(at, 1), :] = total[:, 128 * j : 128 * j + 128]
        acc[...] += nt(act[0], wd[0]) + nt(act[1], wd[1])
        dh2[...] += nt(dhid[0], wu[0]) + nt(dhid[1], wu[1])
        for t in range(2):
            gd = tn(dym[...], act[t]).astype(BF)
            gring[gslot, t, :, :, :, :, 256:512] = gd.reshape(ZC, XC, CC, R, 256)
            gu = tn(h2[...], dhid[t]).astype(BF)
            gring[gslot, t, :, :, :, :, 0:256] = gu.reshape(ZC, XC, CC, R, 256)
        for k in range(NF):
            pl.when(f == k)(partial(red.run, [(1 + k, 0)]))

    out_copy = pltpu.make_async_copy(h2, out_hbm, lsem.at[6])

    def after_lead():
        for m in range(MB - 1):
            send_dkv(m)
        load(0, 0).start()

    def after_ffn():
        h2[...] = acc[...].astype(BF)
        out_copy.start()
        early[0:n, :] = sums[6:7, :].reshape(n, 128)
        early[n + 4 * NF :, :] = jnp.zeros((early.shape[0] - n - 4 * NF, 128), F32)
        early_sum.start(0)

    @pl.loop(0, per * MB + NF)
    def _(i):
        pl.when(i == lead)(after_lead)
        pl.when(i == lead + NF)(after_ffn)
        in_ffn = (i >= lead) & (i < lead + NF)
        pl.when(in_ffn)(lambda: ffn_step(i - lead))
        pl.when(jnp.logical_not(in_ffn))(lambda: back_step(jnp.where(i < lead, i, i - NF)))

    send_dkv(MB - 1)
    query_third(thirds - 1)
    red.run(LAST_SUMS[0])

    wqf = [flat(wq[t]) for t in range(2)]
    wshf = flat(wsh[...])

    def input_grad(b):
        rows = slice(b * 256, b * 256 + 256)
        dq, dkvb = tmp[rows, :], dkvn[rows, :]
        dh1 = nt(dq[:, 0:HT], wqf[0]) + nt(dq[:, HT:], wqf[1]) + nt(dkvb, wshf)
        dh2b = dh2[rows, :]
        z, scale = normal_rows(x_ref[rows, :].astype(F32))
        dy = dym[rows, :].astype(F32)
        e = dh1 * gain1 + dh2b * gain2
        back_in = scale * (
            e - jnp.mean(e, axis=-1, keepdims=True) - z * jnp.mean(e * z, axis=-1, keepdims=True)
        )
        tmp[rows, :] = (dy + back_in).astype(BF)
        for k, v in enumerate((dh1 * z, dh1, dh2b * z, dh2b, dq.astype(F32))):
            sums[k : k + 1, :] += jnp.sum(v, axis=0, keepdims=True)
        sums[5:6, 0:128] += jnp.sum(dkvb.astype(F32), axis=0, keepdims=True)

    input_grad(0)
    own_dkv(1)
    red.run(LAST_SUMS[1])
    gkvs = tn(h1[...], dkvn[...]).astype(BF).reshape(ZC, XC, CC, R, 128)
    for t in range(2):
        gkv[t] = gkvs
    red.run([(last + thirds, 0)])
    input_grad(1)
    input_grad(2)
    red.run(LAST_SUMS[2])
    input_grad(3)
    for k in range(5):
        late[k * n : k * n + n, :] = sums[k : k + 1, :].reshape(n, 128)
    late[5 * n : 5 * n + 1, :] = sums[5:6, 0:128]
    late[5 * n + 1 :, :] = jnp.zeros((late.shape[0] - 5 * n - 1, 128), F32)
    late_sum = AllSum(p, late, late_in, asem)
    late_sum.start(0)
    gx_copy = pltpu.make_async_copy(tmp, gx_hbm, lsem.at[7])
    gx_copy.start()
    red.run(LAST_SUMS[3])
    late_sum.end(0)
    late_sum.start(1)
    early_sum.end(1)
    red.run(LAST_SUMS[4])
    red.run(LAST_SUMS[5])
    late_sum.end(1)
    out_copy.wait()
    gx_copy.wait()


def finish_kernel(dims, out_in, gx_in, grads_in, early, late, *refs):
    (out, gx, g1, b1, g2, b2, gq, bq, gkv, bkv, go, bo, gup, bup, gdn, bd) = refs[:16]
    held, grads, sem = refs[16:]
    HT, NF = dims["HT"], dims["NF"]
    there = [
        pltpu.make_async_copy(grads_in, grads, sem.at[0]),
        pltpu.make_async_copy(out_in, held.at[0], sem.at[1]),
        pltpu.make_async_copy(gx_in, held.at[1], sem.at[2]),
    ]
    for cp in there:
        cp.start()
    parts, at = [], 0
    for k, ref in enumerate((gq, gkv, go, gup, gdn)):
        cols = pl.ds(at, ref.shape[1])
        parts.append(pltpu.make_async_copy(grads.at[:, cols], ref, sem.at[3 + k]))
        at += ref.shape[1]
    back = [
        parts,
        [pltpu.make_async_copy(held.at[0], out, sem.at[8])],
        [pltpu.make_async_copy(held.at[1], gx, sem.at[9])],
    ]
    t = lax.axis_index("tensor")
    n = g1.shape[0] // 128
    for k, ref in enumerate((g1, b1, g2, b2)):
        ref[...] = late[k * n : k * n + n, :].reshape(n * 128)
    half = HT // 128
    bq[...] = late[pl.ds(4 * n + half * t, half), :].reshape(HT)
    bkv[...] = late[5 * n : 5 * n + 1, :].reshape(128)
    total = early[0:n, :].reshape(n * 128)
    bo[...] = total
    bd[...] = total
    for cp, then in zip(there, back):
        cp.wait()
        for after in then:
            after.start()
    for f in range(NF):
        for j in (0, 1):
            at = 256 * f + 128 * j
            bup[at : at + 128] = early[pl.ds(n + 4 * f + 2 * t + j, 1), :].reshape(128)
    for then in back:
        for cp in then:
            cp.wait()


def angle_table(S):
    places = np.arange(2 * S, dtype=np.float64)
    freqs = 10000.0 ** (-np.arange(ROT // 2) * 2.0 / ROT)
    angles = (places[:, None] * freqs[None, :]).astype(np.float32).astype(np.float64)
    tab = np.concatenate([np.cos(angles).T, np.sin(angles).T], axis=0).astype(np.float32)
    return tab.reshape(ROT, 2, S).transpose(1, 0, 2)


def token_plan(
    block_input,
    cotangent,
    lengths,
    ln1_gain,
    ln1_bias,
    ln2_gain,
    ln2_bias,
    w_query,
    b_query,
    w_shared,
    b_shared,
    w_out,
    b_out,
    w_up,
    b_up,
    w_down,
    b_down,
):
    S, D = block_input.shape[2:]
    R, HT = w_query.shape
    FT = w_up.shape[1]
    NF, T, NH = FT // 256, MB * S, 2 * HT // HEAD_DIM
    dims = dict(S=S, HT=HT, NF=NF, T=T, NH=NH)
    plane = (ZC, XC, CC, R)
    full = (2,) + plane
    t = lax.axis_index("tensor")

    def s(shape, dtype):
        return jax.ShapeDtypeStruct(shape, dtype)

    vm = pl.BlockSpec(memory_space=VMEM)
    hbm = pl.BlockSpec(memory_space=pl.ANY)
    smem = pl.BlockSpec(memory_space=pltpu.SMEM)

    nb = HT // 128 + 2 * NF + 1
    n_gather, n_reduce = NF + 3, NF + 2 + HT // 128
    n_early, n_late = 8 * ((D // 128 + 4 * NF + 7) // 8), 8 * ((5 * (D // 128) + 8) // 8)
    n_grads = 2 * HT + 128 + 2 * FT

    outs = pl.pallas_call(
        partial(block_kernel, dims),
        out_shape=[
            s((T, D), BF),
            s((T, D), BF),
            s((NF,) + full + (512,), BF),
            s((R, n_grads), F32),
            s((n_early, 128), F32),
            s((n_late, 128), F32),
        ],
        in_specs=[hbm, hbm, smem] + [vm] * 15,
        out_specs=[hbm] * 3 + [vm] * 3,
        scratch_shapes=[
            VMEM(plane + (128,), BF),
            VMEM(full + (HT,), BF),
            VMEM(full + (HT,), BF),
            VMEM((2 * HT, D), BF),
            VMEM((2,) + full + (512,), BF),
            VMEM((2, nb, 128), F32),
            VMEM((2 * HT + 128, 128), F32),
            VMEM((T, D), BF),
            VMEM((T, D), BF),
            VMEM((T, D), BF),
            VMEM((T, D), BF),
            VMEM((D, T), BF),
            VMEM((D, T), BF),
            VMEM((D, T), BF),
            VMEM((T, D), BF),
            VMEM((T, D), F32),
            VMEM((T, D), F32),
            VMEM((MB * NH, 1, S), F32),
            VMEM((MB, 128, S), BF),
            VMEM((MB, 128, S), BF),
            VMEM((MB, 2 * S, HEAD_DIM), BF),
            VMEM((MB, 2 * S, HEAD_DIM), BF),
            VMEM((MB, HEAD_DIM, 2 * S), BF),
            VMEM((MB, HEAD_DIM + 16, 2 * S), BF),
            VMEM((MB, S, 128), F32),
            VMEM((MB, S, S), F32),
            VMEM((MB, 2 * S, 128), F32),
            VMEM((MB, S, 128), BF),
            VMEM((MB, S, 128), BF),
            VMEM((T, 128), BF),
            VMEM((3,) + full + (512,), BF),
            VMEM(full + (HT,), BF),
            VMEM((HT // 128,) + full + (128,), BF),
            VMEM(full + (128,), BF),
            VMEM((8, D), F32),
            VMEM((10, n_early, 128), F32),
            VMEM((10, n_late, 128), F32),
            VMEM((NF + 2, 2, ZC, XC, R, 512), BF),
            VMEM((NF + 3, ZC, XC, R, 256), BF),
            VMEM((NF + 3, 2, ZC, R, 256), BF),
            VMEM((NF + 3, 2, ZC, R, 256), BF),
            VMEM((NF + 3, 2, 3, R, 256), BF),
            DMA((Gather.SLOTS, 4)),
            DMA((n_gather, 4)),
            DMA((Reduce.SLOTS, 4)),
            DMA((n_reduce, 4)),
            DMA((8,)),
            DMA((2,)),
            DMA((6 + 2 * MB,)),
            DMA((4,)),
            DMA((4,)),
        ],
        compiler_params=pltpu.CompilerParams(
            vmem_limit_bytes=VMEM_LIMIT, collective_id=0, has_side_effects=True
        ),
        name="block",
    )(
        block_input.reshape(T, D),
        cotangent.reshape(T, D),
        lengths.reshape(MB),
        jnp.asarray(angle_table(S)),
        ln1_gain,
        ln1_bias,
        ln2_gain,
        ln2_bias,
        w_query,
        b_query,
        w_shared,
        b_shared,
        w_out.T,
        b_out,
        w_up,
        b_up,
        w_down.T,
        b_down,
    )
    out, gx, _, grads, early, late = outs
    vec = s((D,), F32)
    shapes = [s((T, D), BF), s((T, D), BF), vec, vec, vec, vec, s((R, HT), F32), s((HT,), F32)]
    shapes += [s((R, 128), F32), s((128,), F32), s((R, HT), F32), vec, s((R, FT), F32)]
    shapes += [s((FT,), F32), s((R, FT), F32), vec]
    outs = pl.pallas_call(
        partial(finish_kernel, dims),
        out_shape=shapes,
        in_specs=[hbm, hbm, hbm, vm, vm],
        out_specs=[hbm if len(shape.shape) > 1 else vm for shape in shapes],
        scratch_shapes=[VMEM((2, T, D), BF), VMEM((R, n_grads), F32), DMA((10,))],
        compiler_params=pltpu.CompilerParams(vmem_limit_bytes=VMEM_LIMIT),
        name="finish",
    )(out, gx, grads, early, late)
    res = list(outs)
    res[0] = res[0].reshape(block_input.shape)
    res[1] = res[1].reshape(block_input.shape)
    res[10] = res[10].T
    res[14] = res[14].T
    return tuple(res)


def fits_token_plan(mesh):
    return dict(mesh.shape) == {"dp": ZC * XC * CC, "tensor": 2}


def solution(mesh):
    in_specs = (
        P(None, "dp", "tensor", None),
        P(None, "dp", "tensor", None),
        P(None, "dp"),
        P(),
        P(),
        P(),
        P(),
        P("dp", "tensor"),
        P("tensor"),
        P("dp", None),
        P(),
        P("tensor", "dp"),
        P(),
        P("dp", "tensor"),
        P("tensor"),
        P("tensor", "dp"),
        P(),
    )
    out_specs = (
        P(None, "dp", "tensor", None),
        P(None, "dp", "tensor", None),
        P(),
        P(),
        P(),
        P(),
        P("dp", "tensor"),
        P("tensor"),
        P("dp", None),
        P(),
        P("tensor", "dp"),
        P(),
        P("dp", "tensor"),
        P("tensor"),
        P("tensor", "dp"),
        P(),
    )
    step = token_plan if fits_token_plan(mesh) else per_device
    return jax.shard_map(
        step, mesh=mesh, in_specs=in_specs, out_specs=out_specs, check_vma=False
    )
```

```python
from functools import partial

import jax
import jax.numpy as jnp
import numpy as np
from jax import lax
from jax.experimental import pallas as pl
from jax.experimental.pallas import tpu as pltpu
from jax.sharding import PartitionSpec as P

HEAD_DIM = 64
ROT = 16
MB = 2
QBLK = 512


EPS = 1e-05


def tables(count):
    places = jnp.arange(count).astype(jnp.float32)
    freqs = jnp.power(10000.0, -jnp.arange(ROT // 2).astype(jnp.float32) * 2.0 / ROT)
    angles = places[:, None] * freqs[None, :]
    return (jnp.cos(angles)[:, None, :], jnp.sin(angles)[:, None, :])


def rotate(vector, cosine, sine):
    first = vector[..., : ROT // 2]
    second = vector[..., ROT // 2 : ROT]
    return jnp.concatenate(
        [first * cosine - second * sine, second * cosine + first * sine, vector[..., ROT:]], axis=-1
    )


def unrotate(grad, cosine, sine):
    first = grad[..., : ROT // 2]
    second = grad[..., ROT // 2 : ROT]
    return jnp.concatenate(
        [first * cosine + second * sine, second * cosine - first * sine, grad[..., ROT:]], axis=-1
    )


def normalize(vector):
    centre = vector - jnp.mean(vector, axis=-1, keepdims=True)
    spread = jnp.mean(centre * centre, axis=-1, keepdims=True)
    scale = lax.rsqrt(spread + EPS)
    return (centre * scale, scale)


def norm_back(grad, normed, scale, gain):
    weighted = grad * gain
    return scale * (
        weighted
        - jnp.mean(weighted, axis=-1, keepdims=True)
        - normed * jnp.mean(weighted * normed, axis=-1, keepdims=True)
    )


def block_scores(rows, keys, start, limit, count):
    scores = jnp.einsum("qhd,kd->hqk", rows, keys, preferred_element_type=jnp.float32)
    row_pos = start + jnp.arange(QBLK)
    key_pos = jnp.arange(count)
    allowed = (key_pos[None, :] <= row_pos[:, None]) & (key_pos[None, :] < limit)
    return (scores, allowed[None])


def attend(queries, keys, values, limit):
    count = queries.shape[0]

    def block(start):
        rows = lax.dynamic_slice_in_dim(queries, start, QBLK, 0)
        scores, allowed = block_scores(rows, keys, start, limit, count)
        scores = jnp.where(allowed, scores, jnp.float32(-1e30))
        top = jnp.max(scores, axis=-1, keepdims=True)
        expo = jnp.exp(scores - top)
        total = jnp.sum(expo, axis=-1, keepdims=True)
        weights = (expo / total).astype(jnp.bfloat16)
        result = jnp.einsum("hqk,kd->qhd", weights, values, preferred_element_type=jnp.float32)
        return (result, (top + jnp.log(total))[..., 0])

    starts = jnp.arange(count // QBLK) * QBLK
    results, logsum = lax.map(block, starts)
    return (results.reshape(count, -1, HEAD_DIM), logsum)


def attend_back(queries, keys, values, limit, logsum, grad_out):
    count = queries.shape[0]

    def block(carry, item):
        start, block_logsum = item
        rows = lax.dynamic_slice_in_dim(queries, start, QBLK, 0)
        grads = lax.dynamic_slice_in_dim(grad_out, start, QBLK, 0)
        scores, allowed = block_scores(rows, keys, start, limit, count)
        probs = jnp.where(allowed, jnp.exp(scores - block_logsum[:, :, None]), 0.0)
        weights = probs.astype(jnp.bfloat16)
        dprobs = jnp.einsum("qhd,kd->hqk", grads, values, preferred_element_type=jnp.float32)
        delta = jnp.sum(probs * dprobs, axis=-1, keepdims=True)
        dscores = (probs * (dprobs - delta)).astype(jnp.bfloat16)
        drows = jnp.einsum("hqk,kd->qhd", dscores, keys, preferred_element_type=jnp.float32)
        dkeys = carry[0] + jnp.einsum(
            "hqk,qhd->kd", dscores, rows, preferred_element_type=jnp.float32
        )
        dvalues = carry[1] + jnp.einsum(
            "hqk,qhd->kd", weights, grads, preferred_element_type=jnp.float32
        )
        return ((dkeys, dvalues), drows)

    starts = jnp.arange(count // QBLK) * QBLK
    empty = jnp.zeros((count, HEAD_DIM), jnp.float32)
    (dkeys, dvalues), drows = lax.scan(block, (empty, empty), (starts, logsum))
    return (drows.reshape(count, -1, HEAD_DIM), dkeys, dvalues)


def fetch_each(w_query, w_shared, w_out, w_up, w_down):
    return (
        lax.all_gather(w_query, "dp", axis=0, tiled=True),
        lax.all_gather(w_shared, "dp", axis=0, tiled=True),
        lax.all_gather(w_out, "dp", axis=1, tiled=True),
        lax.all_gather(w_up, "dp", axis=0, tiled=True),
        lax.all_gather(w_down, "dp", axis=1, tiled=True),
    )


def reduce_each(step_grads):
    return (
        lax.psum_scatter(step_grads[0], "dp", scatter_dimension=0, tiled=True),
        lax.psum_scatter(step_grads[1], "dp", scatter_dimension=0, tiled=True),
        lax.psum_scatter(step_grads[2], "dp", scatter_dimension=1, tiled=True),
        lax.psum_scatter(step_grads[3], "dp", scatter_dimension=0, tiled=True),
        lax.psum_scatter(step_grads[4], "dp", scatter_dimension=1, tiled=True),
    )


def per_device(
    block_input,
    cotangent,
    lengths,
    ln1_gain,
    ln1_bias,
    ln2_gain,
    ln2_bias,
    w_query,
    b_query,
    w_shared,
    b_shared,
    w_out,
    b_out,
    w_up,
    b_up,
    w_down,
    b_down,
):
    shard_rows = block_input.shape[2]
    groups = lax.axis_size("tensor")
    rank = lax.axis_index("tensor")
    seq_len = shard_rows * groups
    tail_bias = b_out + b_down
    weight_sums = None
    cos_all, sin_all = tables(seq_len)
    own_pos = rank * shard_rows + jnp.arange(shard_rows)
    outputs = []
    input_grads = []
    sum_bq = jnp.zeros(b_query.shape, jnp.float32)
    sum_bkv = jnp.zeros(b_shared.shape, jnp.float32)
    sum_bup = jnp.zeros(b_up.shape, jnp.float32)
    sum_gain1 = jnp.zeros(ln1_gain.shape, jnp.float32)
    sum_shift1 = jnp.zeros(ln1_gain.shape, jnp.float32)
    sum_gain2 = jnp.zeros(ln1_gain.shape, jnp.float32)
    sum_shift2 = jnp.zeros(ln1_gain.shape, jnp.float32)
    sum_out = jnp.zeros(ln1_gain.shape, jnp.float32)
    for micro in range(MB):
        fetched = fetch_each(w_query, w_shared, w_out, w_up, w_down)
        wq_all, wkv_all, wo_all, wup_all, wdown_all = fetched
        limit = lengths[micro, 0]
        inputs = block_input[micro, 0].astype(jnp.float32)
        normed_one, scale_one = normalize(inputs)
        normed_two, scale_two = normalize(inputs)
        low_one = (normed_one * ln1_gain + ln1_bias).astype(jnp.bfloat16)
        low_two = (normed_two * ln2_gain + ln2_bias).astype(jnp.bfloat16)
        whole_one, whole_two = (
            lax.all_gather(low_one, "tensor", axis=0, tiled=True),
            lax.all_gather(low_two, "tensor", axis=0, tiled=True),
        )
        query_lin = jnp.dot(whole_one, wq_all, preferred_element_type=jnp.float32) + b_query
        query_lin = query_lin.reshape(seq_len, -1, HEAD_DIM)
        queries = (rotate(query_lin, cos_all, sin_all) * 0.125).astype(jnp.bfloat16)
        shared = jnp.dot(whole_one, wkv_all, preferred_element_type=jnp.float32) + b_shared
        keys = rotate(shared[:, None, :HEAD_DIM], cos_all, sin_all)[:, 0].astype(jnp.bfloat16)
        values = shared[:, HEAD_DIM:].astype(jnp.bfloat16)
        attended, logsum = attend(queries, keys, values, limit)
        attended_low = attended.reshape(seq_len, -1).astype(jnp.bfloat16)
        hidden = jnp.dot(whole_two, wup_all, preferred_element_type=jnp.float32) + b_up
        active = jax.nn.gelu(hidden, approximate=False).astype(jnp.bfloat16)
        partial_out = jnp.dot(attended_low, wo_all, preferred_element_type=jnp.float32) + jnp.dot(
            active, wdown_all, preferred_element_type=jnp.float32
        )
        branch = lax.psum_scatter(partial_out, "tensor", scatter_dimension=0, tiled=True)
        outputs.append((inputs + branch + tail_bias).astype(jnp.bfloat16))
        valid = (own_pos < limit).astype(jnp.float32)[:, None]
        upstream = cotangent[micro, 0].astype(jnp.float32) * valid
        whole_up = lax.all_gather(upstream.astype(jnp.bfloat16), "tensor", axis=0, tiled=True)
        sum_out = sum_out + jnp.sum(upstream, axis=0)
        grad_down = jnp.einsum("lf,ld->fd", active, whole_up, preferred_element_type=jnp.float32)
        dactive = jnp.einsum("ld,fd->lf", whole_up, wdown_all, preferred_element_type=jnp.float32)
        gelu_pull = jax.vjp(partial(jax.nn.gelu, approximate=False), hidden)[1]
        dhidden = gelu_pull(dactive)[0].astype(jnp.bfloat16)
        sum_bup = sum_bup + jnp.sum(dhidden.astype(jnp.float32), axis=0)
        grad_up = jnp.einsum("ld,lf->df", whole_two, dhidden, preferred_element_type=jnp.float32)
        dnormed_two = jnp.einsum("lf,df->ld", dhidden, wup_all, preferred_element_type=jnp.float32)
        dattended = jnp.einsum("ld,ed->le", whole_up, wo_all, preferred_element_type=jnp.float32)
        dattended = dattended.astype(jnp.bfloat16).reshape(seq_len, -1, HEAD_DIM)
        grad_out = jnp.einsum(
            "le,ld->ed", attended_low, whole_up, preferred_element_type=jnp.float32
        )
        dqueries, dkeys, dvalues = attend_back(queries, keys, values, limit, logsum, dattended)
        dquery_lin = (
            unrotate(dqueries * 0.125, cos_all, sin_all).reshape(seq_len, -1).astype(jnp.bfloat16)
        )
        dkey_lin = unrotate(dkeys[:, None, :], cos_all, sin_all)[:, 0]
        dshared = lax.psum(jnp.concatenate([dkey_lin, dvalues], axis=1), "tensor")
        dshared = dshared.astype(jnp.bfloat16)
        sum_bq = sum_bq + jnp.sum(dquery_lin.astype(jnp.float32), axis=0)
        sum_bkv = sum_bkv + jnp.sum(dshared.astype(jnp.float32), axis=0)
        grad_q = jnp.einsum("ld,le->de", whole_one, dquery_lin, preferred_element_type=jnp.float32)
        grad_kv = jnp.einsum("ld,lc->dc", whole_one, dshared, preferred_element_type=jnp.float32)
        dnormed_one = jnp.einsum(
            "le,de->ld", dquery_lin, wq_all, preferred_element_type=jnp.float32
        )
        dnormed_one, dnormed_two = (
            lax.psum_scatter(dnormed_one, "tensor", scatter_dimension=0, tiled=True),
            lax.psum_scatter(dnormed_two, "tensor", scatter_dimension=0, tiled=True),
        )
        own_shared = lax.dynamic_slice_in_dim(dshared, rank * shard_rows, shard_rows, 0)
        dnormed_one = dnormed_one + jnp.einsum(
            "lc,dc->ld", own_shared, wkv_all, preferred_element_type=jnp.float32
        )
        sum_gain1 = sum_gain1 + jnp.sum(dnormed_one * normed_one, axis=0)
        sum_shift1 = sum_shift1 + jnp.sum(dnormed_one, axis=0)
        sum_gain2 = sum_gain2 + jnp.sum(dnormed_two * normed_two, axis=0)
        sum_shift2 = sum_shift2 + jnp.sum(dnormed_two, axis=0)
        dinputs = (
            upstream
            + norm_back(dnormed_one, normed_one, scale_one, ln1_gain)
            + norm_back(dnormed_two, normed_two, scale_two, ln2_gain)
        )
        input_grads.append(dinputs.astype(jnp.bfloat16))
        step_grads = (grad_q, grad_kv, grad_out, grad_up, grad_down)
        step_grads = reduce_each(step_grads)
        if weight_sums is None:
            weight_sums = step_grads
        else:
            weight_sums = jax.tree.map(jnp.add, weight_sums, step_grads)
    output = jnp.stack(outputs, axis=0)[:, None]
    grad_input = jnp.stack(input_grads, axis=0)[:, None]
    sum_bq, sum_bkv, sum_bup = lax.psum((sum_bq, sum_bkv, sum_bup), "dp")
    sum_gain1, sum_shift1, sum_gain2, sum_shift2, sum_out = lax.psum(
        (sum_gain1, sum_shift1, sum_gain2, sum_shift2, sum_out), ("dp", "tensor")
    )
    grad_q, grad_kv, grad_o, grad_up, grad_down = weight_sums
    return (
        output,
        grad_input,
        sum_gain1,
        sum_shift1,
        sum_gain2,
        sum_shift2,
        grad_q,
        sum_bq,
        grad_kv,
        sum_bkv,
        grad_o,
        sum_out,
        grad_up,
        sum_bup,
        grad_down,
        sum_out,
    )


MESH = pl.DeviceIdType.MESH
BF = jnp.bfloat16
F32 = jnp.float32
LOG2E = 1.4426950408889634
LN2 = 0.6931471805599453
NEG = -1e30
ZC, XC, CC = 4, 2, 2
DMA = pltpu.SemaphoreType.DMA
VMEM = pltpu.VMEM
VMEM_LIMIT = (64 << 20) - 65536


def nn(a, b):
    return lax.dot_general(a, b, (((1,), (0,)), ((), ())), preferred_element_type=F32)


def nt(a, b):
    return lax.dot_general(a, b, (((1,), (1,)), ((), ())), preferred_element_type=F32)


def tn(a, b):
    return lax.dot_general(a, b, (((0,), (0,)), ((), ())), preferred_element_type=F32)


def eye(n):
    return (
        lax.broadcasted_iota(jnp.int32, (n, n), 0) == lax.broadcasted_iota(jnp.int32, (n, n), 1)
    ).astype(BF)


def flat(block):
    return block.reshape(-1, block.shape[-1])


class Place:
    def __init__(self):
        self.dp = lax.axis_index("dp")
        self.t = lax.axis_index("tensor")
        self.core = lax.rem(self.dp, CC)
        self.x = lax.rem(lax.div(self.dp, CC), XC)
        self.z = lax.div(self.dp, CC * XC)

    def at(self, z, x, core):
        return (z * XC + x) * CC + core

    def z_peer(self, d):
        return {"dp": self.at(lax.rem(self.z + d, ZC), self.x, self.core)}

    def x_peer(self):
        return {"dp": self.at(self.z, 1 - self.x, self.core)}

    def core_peer(self):
        return {"dp": self.at(self.z, self.x, 1 - self.core)}

    def y_peer(self):
        return {"tensor": 1 - self.t}

    def layer_peers(self):
        res = []
        for k in range(1, 8):
            x = 1 - self.x if k & 1 else self.x
            t = 1 - self.t if k & 2 else self.t
            core = 1 - self.core if k & 4 else self.core
            res.append({"dp": self.at(self.z, x, core), "tensor": t})
        return res

    def greet(self):
        bar = pltpu.get_barrier_semaphore()
        peers = [self.z_peer(d) for d in (1, 2, 3)] + self.layer_peers()
        for p in peers:
            pl.semaphore_signal(bar, inc=1, device_id=p, device_id_type=MESH)
        return bar, len(peers)


def remote(src, dst, ss, rs, peer):
    return pltpu.make_async_remote_copy(
        src_ref=src, dst_ref=dst, send_sem=ss, recv_sem=rs, device_id=peer, device_id_type=MESH
    )


def split_cols(width):
    a = (width // 128 + 1) // 2 * 128
    return ((0, a), (a, width - a))


class Gather:
    SLOTS = 3

    def __init__(self, place, pieces, sends, gots):
        self.p = place
        self.pieces = pieces
        self.sends, self.gots = sends, gots

    def own(self, c, h):
        p = self.p
        _, o, w, order = self.pieces[c][0][h]
        index = (p.z, p.x, p.core, slice(None), pl.ds(o, w))
        return self.pieces[c][1].at[(p.t,) + index if "y" in order else index]

    def copies(self, c, k):
        p = self.p
        every = slice(None)
        res = []
        for h, (src, o, w, order) in enumerate(self.pieces[c][0]):
            if k == 0:
                pairs = [(src, self.own(c, h), p.z_peer(d)) for d in (1, 2, 3)]
            elif k <= len(order):
                done = order[:k]
                index = (every, every if "x" in done else p.x, p.core, every, pl.ds(o, w))
                if "y" in order:
                    index = (every if "y" in done else p.t,) + index
                view = self.pieces[c][1].at[index]
                axis = order[k] if k < len(order) else "core"
                peers = {"x": p.x_peer(), "y": p.y_peer(), "core": p.core_peer()}
                pairs = [(view, view, peers[axis])]
            else:
                pairs = []
            for a, b, peer in pairs:
                res.append(remote(a, b, self.sends.at[c % self.SLOTS, k], self.gots.at[c, k], peer))
        return res

    def total(self, c, k):
        parts, out = self.pieces[c]
        z = pl.ds(0, 3) if k == 0 else slice(None)
        x = slice(None) if k > 1 else 0
        index = (z, x, 0)
        if "y" in parts[0][3]:
            index = (slice(None) if k > 2 else 0,) + index
        view = out.at[index]
        return remote(
            view, view, self.sends.at[c % self.SLOTS, k], self.gots.at[c, k], self.p.core_peer()
        )

    def run(self, ops):
        for op in ops:
            c, k = (op, -1) if isinstance(op, int) else op
            if k >= 0:
                self.total(c, k).wait()
            for cp in self.copies(c, k + 1):
                cp.start()


class AllSum:
    def __init__(self, place, buf, got, sems):
        self.p = place
        self.buf, self.got, self.sems = buf, got, sems

    def part(self, k):
        return (7, 3) if k else (0, 7)

    def start(self, k):
        peers = [self.p.z_peer(d) for d in (1, 2, 3)] if k else self.p.layer_peers()
        at, _ = self.part(k)
        for i, peer in enumerate(peers):
            got = self.got.at[at + i]
            remote(self.buf, got, self.sems.at[2 * k], self.sems.at[2 * k + 1], peer).start()

    def end(self, k):
        at, n = self.part(k)
        view = self.got.at[pl.ds(at, n)]
        whole = remote(
            view, view, self.sems.at[2 * k], self.sems.at[2 * k + 1], self.p.core_peer()
        )
        whole.wait()
        total = self.buf[...]
        for i in range(at, at + n):
            total = total + self.got[i]
        self.buf[...] = total


def normal_rows(rows):
    mean = jnp.mean(rows, axis=-1, keepdims=True)
    centre = rows - mean
    var = jnp.mean(centre * centre, axis=-1, keepdims=True)
    scale = lax.rsqrt(var + EPS)
    return centre * scale, scale


def rotate_t(v, cosine, sine):
    a, b = v[0:8], v[8:16]
    return jnp.concatenate([a * cosine - b * sine, b * cosine + a * sine, v[16:]], axis=0)


def unrotate_t(v, cosine, sine):
    a, b = v[0:8], v[8:16]
    return jnp.concatenate([a * cosine + b * sine, b * cosine - a * sine, v[16:]], axis=0)


def fill_bias(place, lens_ref, other_ref, own_ref, S):
    t = place.t
    for m in range(MB):
        limit = lens_ref[m]
        key = lax.broadcasted_iota(jnp.int32, (S, 128), 0)
        limit_other = jnp.where(t == 1, limit, 0)
        other_ref[m] = jnp.where(key < limit_other, 0.0, NEG).astype(F32)
        key = lax.broadcasted_iota(jnp.int32, (S, S), 0)
        row = lax.broadcasted_iota(jnp.int32, (S, S), 1)
        own = (key <= row) & (key + t * S < limit)
        own_ref[m] = jnp.where(own, 0.0, NEG).astype(F32)


def masked_rows(place_t, lens_ref, dy, start, S):
    m, off = divmod(start, S)
    pos = place_t * S + off + lax.broadcasted_iota(jnp.int32, (dy.shape[0], 1), 0)
    return jnp.where(pos < lens_ref[m], dy.astype(F32), 0.0)


class Reduce:
    SLOTS = 3

    def __init__(self, place, pieces, rc, r2a, r2b, r3, r4, sends, gots):
        self.p = place
        self.pieces = pieces
        self.rc, self.r2a, self.r2b, self.r3, self.r4 = rc, r2a, r2b, r3, r4
        self.sends, self.gots = sends, gots

    def part(self, c, h):
        r, n, o, w = self.pieces[c][1][h]
        _, first, _, second = self.pieces[c][3]
        o += first
        return (slice(r, r + n), slice(o, o + w)), (slice(0, n), slice(second, second + w))

    def wide(self, c):
        first = self.pieces[c][3][1]
        return slice(first, first + self.pieces[c][0].shape[-1])

    def sems(self, c, k):
        return self.sends.at[c % self.SLOTS, k], self.gots.at[c, k]

    def copies(self, c, k):
        p = self.p
        if k == 0:
            src = self.pieces[c][0].at[:, :, :, 1 - p.core]
            dst = self.rc.at[self.pieces[c][3][0], :, :, :, :, self.wide(c)]
            return [remote(src, dst, *self.sems(c, k), p.core_peer())]
        res = []
        a, _, b, _ = self.pieces[c][3]
        for h in (0, 1):
            here, there = self.part(c, h)
            if k == 1 and h == 0:
                src, dst = self.rc.at[(a, 1 - p.t, slice(None), slice(None)) + here], self.r2a
                todo = [(src, dst.at[(b, slice(None), slice(None)) + there], p.y_peer())]
            elif k == 1:
                src, dst = self.rc.at[(a, slice(None), slice(None), 1 - p.x) + here], self.r2b
                todo = [(src, dst.at[(b, slice(None), slice(None)) + there], p.x_peer())]
            elif k == 2:
                if h == 0:
                    src, peer = self.r2a.at[(b, slice(None), 1 - p.x) + there], p.x_peer()
                else:
                    src, peer = self.r2b.at[(b, 1 - p.t, slice(None)) + there], p.y_peer()
                todo = [(src, self.r3.at[(b, h, slice(None)) + there], peer)]
            else:
                todo = [
                    (
                        self.r3.at[(b, h, lax.rem(p.z + d, ZC)) + there],
                        self.r4.at[(b, h, d - 1) + there],
                        p.z_peer(d),
                    )
                    for d in (1, 2, 3)
                ]
            res += [remote(src, dst, *self.sems(c, k), peer) for src, dst, peer in todo]
        return res

    def total(self, c, k):
        cols = self.wide(c)
        every = slice(None)
        index = {
            0: (every, every, every, every, cols),
            1: (0, every, every, every, cols),
            2: (0, every, 0, every, cols),
            3: (0, pl.ds(0, 3), 0, every, cols),
        }[k]
        view = self.rc.at[(self.pieces[c][3][0],) + index]
        return remote(view, view, *self.sems(c, k), self.p.core_peer())

    def start(self, c, k):
        for cp in self.copies(c, k):
            cp.start()

    def add(self, c, k):
        p = self.p
        a, _, b, _ = self.pieces[c][3]
        if k == 1:
            cols = self.wide(c)
            mine = self.pieces[c][0][:, :, :, p.core].astype(F32)
            mine = mine + self.rc[a, :, :, :, :, cols].astype(F32)
            self.rc[a, :, :, :, :, cols] = mine.astype(BF)
            return
        sums = []
        for h in (0, 1):
            here, there = self.part(c, h)
            every = slice(None)
            if k == 2:
                if h == 0:
                    ref, mine = self.r2a, self.rc[(a, p.t, every, every) + here]
                else:
                    ref, mine = self.r2b, self.rc[(a, every, every, p.x) + here]
                at = (b, every, every) + there
                ref[at] = (mine.astype(F32) + ref[at].astype(F32)).astype(BF)
            elif k == 3:
                if h == 0:
                    mine = self.r2a[(b, every, p.x) + there]
                else:
                    mine = self.r2b[(b, p.t, every) + there]
                at = (b, h, every) + there
                self.r3[at] = (mine.astype(F32) + self.r3[at].astype(F32)).astype(BF)
            else:
                total = self.r3[(b, h, p.z) + there].astype(F32)
                for d in range(3):
                    total = total + self.r4[(b, h, d) + there].astype(F32)
                sums.append(total)
        if k == 4:
            self.pieces[c][2](sums)

    def run(self, ops):
        for c, k in ops:
            if k:
                self.total(c, k - 1).wait()
                self.add(c, k)
            if k < 4:
                self.start(c, k)


HEAD_OPS = (
    (0, 1),
    ((0, 0), (1, 0), 2),
    ((0, 1), (1, 1), 3),
    ((0, 2),),
    ((1, 2), 4),
    ((1, 3), (2, 0), (3, 0), 5),
)
ATTENTION_OPS = {
    0: (6,),
    1: ((2, 1),),
    2: ((4, 0),),
    4: ((3, 1), (5, 0), 7),
    5: ((2, 2),),
    7: ((2, 3), (4, 1), (6, 0), 8),
}
BACK_OPS = {
    0: ((3, 2), (4, 2), (5, 1), (7, 0)),
    3: ((3, 3), (4, 3), (5, 2), (6, 1), (8, 0)),
    5: ((5, 3), (7, 1)),
}
FFN_OPS = {
    0: ((6, 2),),
    1: ((6, 3), (7, 2), (8, 1)),
    2: ((7, 3),),
    3: ((8, 2),),
    4: ((8, 3),),
}


FFN_SUMS = {
    0: ((0, 1),),
    2: ((0, 2), (1, 1)),
    3: ((0, 3), (2, 1)),
    4: ((0, 4), (1, 2), (3, 1)),
    5: ((1, 3), (2, 2), (4, 1)),
}
BACK_SUMS = {
    6: ((1, 4), (2, 3), (3, 2), (5, 1)),
    8: ((2, 4), (3, 3), (4, 2), (6, 1)),
    9: ((7, 1),),
    10: ((3, 4), (4, 3), (5, 2)),
    11: ((7, 2), (8, 1), (6, 2)),
}
LAST_SUMS = (
    ((4, 4), (5, 3), (7, 3), (8, 2)),
    ((9, 1), (6, 3)),
    ((10, 1), (9, 2), (5, 4), (8, 3)),
    ((10, 2), (6, 4), (9, 3), (7, 4)),
    ((10, 3), (8, 4)),
    ((9, 4), (10, 4)),
)


def block_kernel(
    dims,
    x_hbm,
    dy_hbm,
    lens_ref,
    tab_ref,
    g1_ref,
    b1_ref,
    g2_ref,
    b2_ref,
    wq_in,
    bq_ref,
    wsh_in,
    bsh_ref,
    wout_in,
    bout_ref,
    wup_in,
    bup_ref,
    wdown_in,
    bdown_ref,
    out_hbm,
    gx_hbm,
    wf,
    grads,
    early,
    late,
    wsh,
    wq,
    wb,
    won,
    wv,
    ball,
    bcol,
    x_ref,
    dym,
    h1,
    h2,
    qt,
    att,
    da,
    tmp,
    acc,
    dh2,
    lse_ref,
    kvt,
    kvo,
    kc,
    vc,
    kt,
    vte,
    bias_o,
    bias_s,
    dkv,
    dkvs,
    dkvr,
    dkvn,
    gring,
    gb,
    gq,
    gkv,
    sums,
    early_in,
    late_in,
    rc,
    r2a,
    r2b,
    r3,
    r4,
    gsend,
    gsem,
    rsend,
    rsem,
    lsem,
    wsem,
    ysem,
    esem,
    asem,
):
    S, HT, NH, NF, T = dims["S"], dims["HT"], dims["NH"], dims["NF"], dims["T"]
    D = x_ref.shape[1]
    R = wq_in.shape[0]
    NB = S // 256
    p = Place()
    bar, npeers = p.greet()
    x_copy = pltpu.make_async_copy(x_hbm, x_ref, lsem.at[1])
    x_copy.start()
    dy_copy = pltpu.make_async_copy(dy_hbm, dym, lsem.at[0])
    dy_copy.start()

    def parts_of(ref, widths, orders):
        at = [sum(widths[:i]) for i in range(len(widths))]
        return [(ref.at[:, pl.ds(o, w)], o, w, order) for o, w, order in zip(at, widths, orders)]

    wide = [w for _, w in split_cols(HT)]
    pieces = [
        ([(wsh_in, 0, 128, "zx")], wsh),
        (parts_of(wq_in, wide, ("zxy", "zyx")), wq),
        (parts_of(wout_in, wide, ("zxy", "zyx")), wb),
    ]
    for f in range(NF):
        cols = pl.ds(256 * f, 256)
        parts = [(wup_in.at[:, cols], 0, 256, "zxy"), (wdown_in.at[:, cols], 256, 256, "zyx")]
        pieces.append((parts, wf.at[f]))
    g = Gather(p, pieces, gsend, gsem)
    pl.semaphore_wait(bar, npeers)
    g.run(HEAD_OPS[0])
    locals_ = [
        pltpu.make_async_copy(wsh_in, wsh.at[p.z, p.x, p.core], lsem.at[2]),
        pltpu.make_async_copy(wq_in, wq.at[p.t, p.z, p.x, p.core], lsem.at[3]),
        pltpu.make_async_copy(wout_in, wb.at[p.t, p.z, p.x, p.core], lsem.at[4]),
    ]
    for cp in locals_:
        cp.start()
    for c in range(3, len(pieces)):
        for h in (0, 1):
            pltpu.make_async_copy(pieces[c][0][h][0], g.own(c, h), lsem.at[5]).start()
    held = wf.at[:, 0, 0, 0, 0]
    locals_.append(pltpu.make_async_copy(held, held, lsem.at[5]))
    first = HT // 128
    rows_b = ball.shape[1]
    ball[p.t, 0:first, :] = bq_ref[...].reshape(first, 128)
    ball[p.t, first : first + 2 * NF, :] = bup_ref[...].reshape(2 * NF, 128)
    ball[p.t, first + 2 * NF :, :] = jnp.zeros((rows_b - first - 2 * NF, 128), F32)
    bias_copy = remote(ball.at[p.t], ball.at[p.t], ysem.at[0], ysem.at[1], p.y_peer())
    bias_copy.start()

    gain1, shift1, gain2, shift2 = (
        ref[...].reshape(1, D) for ref in (g1_ref, b1_ref, g2_ref, b2_ref)
    )

    def norm_block(i):
        rows = pl.ds(pl.multiple_of(i * 128, 128), 128)
        z, _ = normal_rows(x_ref[rows, :].astype(F32))
        h1[rows, :] = (z * gain1 + shift1).astype(BF)
        h2[rows, :] = (z * gain2 + shift2).astype(BF)

    half = T // 256
    x_copy.wait()
    pl.loop(0, half)(norm_block)
    for cp in locals_:
        cp.wait()
    g.run(HEAD_OPS[1])
    pl.loop(half, 2 * half)(norm_block)
    g.run(HEAD_OPS[2])
    fill_bias(p, lens_ref, bias_o, bias_s, S)
    for ref in (dkv, dh2, sums):
        ref[...] = jnp.zeros_like(ref)
    bias_copy.wait()
    nq = HT // 128
    for t in range(2):
        for j in range(nq):
            row = jnp.broadcast_to(ball[t, j : j + 1, :], (128, 128))
            bcol[(t * nq + j) * 128 : (t * nq + j + 1) * 128, :] = row.T
    bcol[2 * HT : 2 * HT + 128, :] = jnp.broadcast_to(bsh_ref[...].reshape(1, 128), (128, 128)).T
    g.run(HEAD_OPS[3])

    id256 = eye(256)
    cosine, sine = tab_ref[p.t, 0:8, :], tab_ref[p.t, 8:16, :]
    wsh_t = nt(eye(128), flat(wsh[...])).astype(BF)
    kv_copies = [
        remote(kvt.at[m], kvo.at[m], ysem.at[2 + 2 * m], ysem.at[3 + 2 * m], p.y_peer())
        for m in range(MB)
    ]
    for m in range(MB):
        kv = nt(wsh_t, h1[m * S : m * S + S, :]) + bcol[2 * HT : 2 * HT + 128, 0:1]
        kvt[m, 0:HEAD_DIM, :] = rotate_t(kv[0:HEAD_DIM], cosine, sine).astype(BF)
        kvt[m, HEAD_DIM:, :] = kv[HEAD_DIM:].astype(BF)
    g.run(HEAD_OPS[4])
    kv_copies[0].start()
    dy_copy.wait()
    for b in range(T // 256):
        rows = slice(b * 256, b * 256 + 256)
        dy = masked_rows(p.t, lens_ref, dym[rows, :], b * 256, S)
        dym[rows, :] = dy.astype(BF)
        sums[6:7, :] += jnp.sum(dy, axis=0, keepdims=True)
    g.run(HEAD_OPS[5])

    for t in range(2):
        wq_t = nt(eye(HT), flat(wq[t])).astype(BF)
        for m in range(MB):
            cols = slice(m * S, m * S + S)
            q = nt(wq_t, h1[cols, :])
            for h in range(HT // HEAD_DIM):
                base = t * HT + h * HEAD_DIM
                qh = q[h * HEAD_DIM : (h + 1) * HEAD_DIM] + bcol[base : base + HEAD_DIM, 0:1]
                qh = rotate_t(qh, cosine, sine) * (0.125 * LOG2E)
                qt[base : base + HEAD_DIM, cols] = qh.astype(BF)

    def both_halves(m):
        kv_copies[m].wait()
        for part, src in ((0, kvo), (1, kvt)):
            keys = slice(part * S, part * S + S)
            kt[m, :, keys] = src[m, 0:HEAD_DIM, :]
            vte[m, 0:HEAD_DIM, keys] = src[m, HEAD_DIM:, :]
        vte[m, HEAD_DIM:, :] = (
            lax.broadcasted_iota(jnp.int32, (16, 2 * S), 0) == 0
        ).astype(BF)
        for b in range(2 * NB):
            blk = slice(b * 256, b * 256 + 256)
            kc[m, blk, :] = nt(id256, kt[m, :, blk]).astype(BF)
            vc[m, blk, :] = nt(id256, vte[m, 0:HEAD_DIM, blk]).astype(BF)

    both_halves(0)

    def spots(i, group, by_thirds=False):
        res = []
        for u in range(group):
            j = i * group + u
            m, h = lax.div(j, NH), lax.rem(j, NH)
            if by_thirds:
                k = lax.div(h, 2)
                h = lax.rem(k, 2) * (NH // 2) + lax.div(k, 2) * 2 + u
                j = m * NH + h
            head = pl.ds(pl.multiple_of(h * HEAD_DIM, HEAD_DIM), HEAD_DIM)
            for r in range(NB):
                cols = pl.ds(pl.multiple_of(m * S + r * 256, 256), 256)
                res.append((j, m, head, cols, S + 256 * (r + 1), r))
        return res

    def scores(m, q, nk, r):
        s = nn(kc[m, 0:nk, :], q)
        wide = slice(r * 256, r * 256 + 256)
        other = bias_o[m]
        other = jnp.concatenate([other, other], axis=1)
        return jnp.concatenate([s[0:S] + other, s[S:nk] + bias_s[m, 0 : nk - S, wide]], axis=0)

    group = 3

    @pl.loop(0, MB * NH // group)
    def _(i):
        for m in range(1, MB):
            pl.when(i == (m - 1) * NH // group)(kv_copies[m].start)
            pl.when(i == m * NH // group)(partial(both_halves, m))
        for at, ops in ATTENTION_OPS.items():
            pl.when(i == at)(partial(g.run, ops))
        todo = spots(i, group)
        sc = [scores(m, qt[head, cols], nk, r) for _, m, head, cols, nk, r in todo]
        tops = [jnp.max(s, axis=0, keepdims=True) for s in sc]
        ex = [jnp.exp2(s - top).astype(BF) for s, top in zip(sc, tops)]
        for (j, m, head, cols, nk, r), e, top in zip(todo, ex, tops):
            o = nn(vte[m, :, 0:nk], e)
            total = o[HEAD_DIM : HEAD_DIM + 1]
            att[head, cols] = (o[0:HEAD_DIM] * (1.0 / total)).astype(BF)
            lse_ref[j, :, r * 256 : r * 256 + 256] = top + jnp.log2(total)

    for t in range(2):
        won[t * HT : (t + 1) * HT, :] = nt(eye(HT), flat(wb[t])).astype(BF)

    def load(f, slot):
        return pltpu.make_async_copy(wf.at[f], wv.at[slot], wsem.at[slot])

    for b in range(T // 256):
        rows = slice(b * 256, b * 256 + 256)
        tmp[rows, :] = nt(id256, att[:, rows]).astype(BF)
    tail_bias = (bout_ref[...] + bdown_ref[...]).reshape(1, D)
    acc[...] = x_ref[...].astype(F32) + tail_bias + nn(tmp[...], won[...])
    for t in range(2):
        cols = slice(t * HT, (t + 1) * HT)
        gb[t] = tn(dym[...], tmp[:, cols]).astype(BF).reshape(ZC, XC, CC, R, HT)

    def put(*firsts):
        def store(parts):
            for o, v in zip(firsts, parts):
                grads[:, o : o + v.shape[1]] = v

        return store

    at_out, at_up, at_down = HT + 128, 2 * HT + 128, 2 * HT + 128 + 256 * NF
    thirds = HT // 128

    def by_cols(*widths):
        at = [sum(widths[:i]) for i in range(len(widths))]
        return [(0, R, o, w) for o, w in zip(at, widths)]

    def put_rows(first):
        def store(parts):
            r = 0
            for v in parts:
                grads[r : r + v.shape[0], first : first + 128] = v
                r += v.shape[0]

        return store

    by_rows = [(0, 32, 0, 128), (32, R - 32, 0, 128)]
    sums_of = [(gb, by_cols(*wide), put(at_out, at_out + wide[0]), (0, 0, 0, 0))]
    for f in range(NF):
        store = put(at_up + 256 * f, at_down + 256 * f)
        sums_of.append((gring.at[f % 3], by_cols(256, 256), store, (1 + f, 0, 1 + f, 0)))
    for k in range(thirds + 1):
        store = put_rows(128 * k)
        slot = (NF + 1, 128 * k, NF + 1 + k // 2, 128 * (k % 2))
        sums_of.append((gq.at[k] if k < thirds else gkv, by_rows, store, slot))
    red = Reduce(p, sums_of, rc, r2a, r2b, r3, r4, rsend, rsem)
    last = NF + 1
    red.run([(0, 0)])

    n = D // 128
    early_sum = AllSum(p, early, early_in, esem)
    da[...] = nt(won[...], dym[...]).astype(BF)
    back = 2
    dkv_copies = [
        remote(dkvs.at[m], dkvr.at[m], ysem.at[6 + 2 * m], ysem.at[7 + 2 * m], p.y_peer())
        for m in range(MB)
    ]

    def send_dkv(m):
        dkvs[m] = dkv[m, 0:S, :].astype(BF)
        dkv_copies[m].start()

    def query_third(k):
        for t in range(2):
            at = t * HT + 128 * k
            for b in range(T // 256):
                rows = slice(b * 256, b * 256 + 256)
                tmp[rows, at : at + 128] = nt(id256, qt[at : at + 128, rows]).astype(BF)
            v = tn(h1[...], tmp[:, at : at + 128]).astype(BF)
            gq[k, t] = v.reshape(ZC, XC, CC, R, 128)
        red.run([(last + k, 0)])

    def own_dkv(m):
        dkv_copies[m].wait()
        both = (dkv[m, S : 2 * S, :] + dkvr[m].astype(F32)).T
        dk = unrotate_t(both[0:HEAD_DIM], cosine, sine) * LN2
        both = jnp.concatenate([dk, both[HEAD_DIM:]], axis=0).astype(BF)
        for b in range(NB):
            rows = slice(m * S + b * 256, m * S + b * 256 + 256)
            dkvn[rows, :] = nt(id256, both[:, b * 256 : b * 256 + 256]).astype(BF)

    def early_next():
        early_sum.end(0)
        early_sum.start(1)

    def back_step(i):
        for at, ops in BACK_OPS.items():
            pl.when(i == at)(partial(g.run, ops))
        pl.when(i == NH // back + 2)(early_next)
        pl.when(i == NH // back + 3)(partial(own_dkv, 0))
        for at, ops in BACK_SUMS.items():
            pl.when(i == at)(partial(red.run, ops))
        for k in range(thirds - 1):
            at = MB * NH // back - 2 * (thirds - 1 - k)
            pl.when(i == at)(partial(query_third, k))
        todo = spots(i, back, True)
        qs = [qt[head, cols] for _, m, head, cols, nk, r in todo]
        das = [da[head, cols] for _, m, head, cols, nk, r in todo]
        sc = [scores(m, q, nk, r) for (_, m, head, cols, nk, r), q in zip(todo, qs)]
        dp = [nn(vc[m, 0:nk, :], d) for (_, m, head, cols, nk, r), d in zip(todo, das)]
        pr, ds = [], []
        for (j, m, head, cols, nk, r), d, s, dpj in zip(todo, das, sc, dp):
            delta = jnp.sum(d.astype(F32) * att[head, cols].astype(F32), axis=0, keepdims=True)
            w = jnp.exp2(s - lse_ref[j, :, r * 256 : r * 256 + 256])
            pr.append(w.astype(BF))
            ds.append((w * (dpj - delta)).astype(BF))
        for (j, m, head, cols, nk, r), d in zip(todo, ds):
            wide = slice(r * 256, r * 256 + 256)
            dq = nn(kt[m, :, 0:nk], d)
            dq = unrotate_t(dq, tab_ref[p.t, 0:8, wide], tab_ref[p.t, 8:16, wide])
            qt[head, cols] = (dq * 0.125).astype(BF)
        m = todo[0][1]
        for blk in range(NB):
            lo = 0 if blk == 0 else S + 256 * blk
            hi = S + 256 * (blk + 1)
            left, right = [], []
            for u, (_, _, _, _, nk, r) in enumerate(todo):
                if nk >= hi:
                    zero = jnp.zeros_like(qs[u])
                    left += [ds[u][lo:hi], pr[u][lo:hi]]
                    right += [
                        jnp.concatenate([qs[u], zero], axis=0),
                        jnp.concatenate([zero, das[u]], axis=0),
                    ]
            dkv[m, lo:hi, :] += nt(
                jnp.concatenate(left, axis=1), jnp.concatenate(right, axis=1)
            )

    per = NH // back
    lead = per * (MB - 1)
    def ffn_step(f):
        slot = lax.rem(f, 2)
        load(f, slot).wait()
        for k in range(NF - 1):

            @pl.when(f == k)
            def _():
                g.run(FFN_OPS.get(k, ()))
                load(k + 1, (k + 1) % 2).start()

        for k, ops in FFN_SUMS.items():
            pl.when(f == k)(partial(red.run, ops))
        wu = [flat(wv[slot, t, :, :, :, :, 0:256]) for t in range(2)]
        wd = [flat(wv[slot, t, :, :, :, :, 256:512]) for t in range(2)]
        gslot = lax.rem(f, 3)
        hid = [nn(h2[...], wu[t]) for t in range(2)]
        dact = [nn(dym[...], wd[t]) for t in range(2)]
        act, dhid = [], []
        for t in range(2):
            row = jnp.concatenate(
                [ball[t, pl.ds(first + 2 * f, 1), :], ball[t, pl.ds(first + 2 * f + 1, 1), :]],
                axis=1,
            )
            u = hid[t] + row
            cdf = 0.5 + 0.5 * lax.erf(u * 0.7071067811865476)
            dens = jnp.exp(-0.5 * u * u) * 0.3989422804014327
            act.append((u * cdf).astype(BF))
            d = (dact[t] * (cdf + u * dens)).astype(BF)
            dhid.append(d)
            total = jnp.sum(d.astype(F32), axis=0, keepdims=True)
            for j in (0, 1):
                at = D // 128 + 4 * f + 2 * t + j
                early[pl.ds(at, 1), :] = total[:, 128 * j : 128 * j + 128]
        acc[...] += nt(act[0], wd[0]) + nt(act[1], wd[1])
        dh2[...] += nt(dhid[0], wu[0]) + nt(dhid[1], wu[1])
        for t in range(2):
            gd = tn(dym[...], act[t]).astype(BF)
            gring[gslot, t, :, :, :, :, 256:512] = gd.reshape(ZC, XC, CC, R, 256)
            gu = tn(h2[...], dhid[t]).astype(BF)
            gring[gslot, t, :, :, :, :, 0:256] = gu.reshape(ZC, XC, CC, R, 256)
        for k in range(NF):
            pl.when(f == k)(partial(red.run, [(1 + k, 0)]))

    out_copy = pltpu.make_async_copy(h2, out_hbm, lsem.at[6])

    def after_lead():
        for m in range(MB - 1):
            send_dkv(m)
        load(0, 0).start()

    def after_ffn():
        h2[...] = acc[...].astype(BF)
        out_copy.start()
        early[0:n, :] = sums[6:7, :].reshape(n, 128)
        early[n + 4 * NF :, :] = jnp.zeros((early.shape[0] - n - 4 * NF, 128), F32)
        early_sum.start(0)

    @pl.loop(0, per * MB + NF)
    def _(i):
        pl.when(i == lead)(after_lead)
        pl.when(i == lead + NF)(after_ffn)
        in_ffn = (i >= lead) & (i < lead + NF)
        pl.when(in_ffn)(lambda: ffn_step(i - lead))
        pl.when(jnp.logical_not(in_ffn))(lambda: back_step(jnp.where(i < lead, i, i - NF)))

    send_dkv(MB - 1)
    query_third(thirds - 1)
    red.run(LAST_SUMS[0])

    wqf = [flat(wq[t]) for t in range(2)]
    wshf = flat(wsh[...])

    def input_grad(b):
        rows = slice(b * 256, b * 256 + 256)
        dq, dkvb = tmp[rows, :], dkvn[rows, :]
        dh1 = nt(dq[:, 0:HT], wqf[0]) + nt(dq[:, HT:], wqf[1]) + nt(dkvb, wshf)
        dh2b = dh2[rows, :]
        z, scale = normal_rows(x_ref[rows, :].astype(F32))
        dy = dym[rows, :].astype(F32)
        e = dh1 * gain1 + dh2b * gain2
        back_in = scale * (
            e - jnp.mean(e, axis=-1, keepdims=True) - z * jnp.mean(e * z, axis=-1, keepdims=True)
        )
        tmp[rows, :] = (dy + back_in).astype(BF)
        for k, v in enumerate((dh1 * z, dh1, dh2b * z, dh2b, dq.astype(F32))):
            sums[k : k + 1, :] += jnp.sum(v, axis=0, keepdims=True)
        sums[5:6, 0:128] += jnp.sum(dkvb.astype(F32), axis=0, keepdims=True)

    input_grad(0)
    own_dkv(1)
    red.run(LAST_SUMS[1])
    gkvs = tn(h1[...], dkvn[...]).astype(BF).reshape(ZC, XC, CC, R, 128)
    for t in range(2):
        gkv[t] = gkvs
    red.run([(last + thirds, 0)])
    input_grad(1)
    input_grad(2)
    red.run(LAST_SUMS[2])
    input_grad(3)
    for k in range(5):
        late[k * n : k * n + n, :] = sums[k : k + 1, :].reshape(n, 128)
    late[5 * n : 5 * n + 1, :] = sums[5:6, 0:128]
    late[5 * n + 1 :, :] = jnp.zeros((late.shape[0] - 5 * n - 1, 128), F32)
    late_sum = AllSum(p, late, late_in, asem)
    late_sum.start(0)
    gx_copy = pltpu.make_async_copy(tmp, gx_hbm, lsem.at[7])
    gx_copy.start()
    red.run(LAST_SUMS[3])
    late_sum.end(0)
    late_sum.start(1)
    early_sum.end(1)
    red.run(LAST_SUMS[4])
    red.run(LAST_SUMS[5])
    late_sum.end(1)
    out_copy.wait()
    gx_copy.wait()


def finish_kernel(dims, out_in, gx_in, grads_in, early, late, *refs):
    (out, gx, g1, b1, g2, b2, gq, bq, gkv, bkv, go, bo, gup, bup, gdn, bd) = refs[:16]
    held, grads, sem = refs[16:]
    HT, NF = dims["HT"], dims["NF"]
    there = [pltpu.make_async_copy(grads_in, grads, sem.at[0])]
    parts, at = [], 0
    for k, ref in enumerate((gq, gkv, go, gup, gdn)):
        cols = pl.ds(at, ref.shape[1])
        parts.append(pltpu.make_async_copy(grads.at[:, cols], ref, sem.at[1 + k]))
        at += ref.shape[1]
    back = [parts]
    for k, (src, dst) in enumerate(((out_in, out), (gx_in, gx))):
        rows = src.shape[0] // 4
        for j in range(4):
            part, at = pl.ds(j * rows, rows), 6 + 2 * (4 * k + j)
            there.append(pltpu.make_async_copy(src.at[part], held.at[k, part], sem.at[at]))
            back.append([pltpu.make_async_copy(held.at[k, part], dst.at[part], sem.at[at + 1])])
    for cp in there:
        cp.start()
    t = lax.axis_index("tensor")
    n = g1.shape[0] // 128
    for k, ref in enumerate((g1, b1, g2, b2)):
        ref[...] = late[k * n : k * n + n, :].reshape(n * 128)
    half = HT // 128
    bq[...] = late[pl.ds(4 * n + half * t, half), :].reshape(HT)
    bkv[...] = late[5 * n : 5 * n + 1, :].reshape(128)
    total = early[0:n, :].reshape(n * 128)
    bo[...] = total
    bd[...] = total
    for cp, then in zip(there, back):
        cp.wait()
        for after in then:
            after.start()
    for f in range(NF):
        for j in (0, 1):
            at = 256 * f + 128 * j
            bup[at : at + 128] = early[pl.ds(n + 4 * f + 2 * t + j, 1), :].reshape(128)
    for then in back:
        for cp in then:
            cp.wait()


def angle_table(S):
    places = np.arange(2 * S, dtype=np.float64)
    freqs = 10000.0 ** (-np.arange(ROT // 2) * 2.0 / ROT)
    angles = (places[:, None] * freqs[None, :]).astype(np.float32).astype(np.float64)
    tab = np.concatenate([np.cos(angles).T, np.sin(angles).T], axis=0).astype(np.float32)
    return tab.reshape(ROT, 2, S).transpose(1, 0, 2)


def token_plan(
    block_input,
    cotangent,
    lengths,
    ln1_gain,
    ln1_bias,
    ln2_gain,
    ln2_bias,
    w_query,
    b_query,
    w_shared,
    b_shared,
    w_out,
    b_out,
    w_up,
    b_up,
    w_down,
    b_down,
):
    S, D = block_input.shape[2:]
    R, HT = w_query.shape
    FT = w_up.shape[1]
    NF, T, NH = FT // 256, MB * S, 2 * HT // HEAD_DIM
    dims = dict(S=S, HT=HT, NF=NF, T=T, NH=NH)
    plane = (ZC, XC, CC, R)
    full = (2,) + plane
    t = lax.axis_index("tensor")

    def s(shape, dtype):
        return jax.ShapeDtypeStruct(shape, dtype)

    vm = pl.BlockSpec(memory_space=VMEM)
    hbm = pl.BlockSpec(memory_space=pl.ANY)
    smem = pl.BlockSpec(memory_space=pltpu.SMEM)

    nb = HT // 128 + 2 * NF + 1
    n_gather, n_reduce = NF + 3, NF + 2 + HT // 128
    n_early, n_late = 8 * ((D // 128 + 4 * NF + 7) // 8), 8 * ((5 * (D // 128) + 8) // 8)
    n_grads = 2 * HT + 128 + 2 * FT

    outs = pl.pallas_call(
        partial(block_kernel, dims),
        out_shape=[
            s((T, D), BF),
            s((T, D), BF),
            s((NF,) + full + (512,), BF),
            s((R, n_grads), F32),
            s((n_early, 128), F32),
            s((n_late, 128), F32),
        ],
        in_specs=[hbm, hbm, smem] + [vm] * 15,
        out_specs=[hbm] * 3 + [vm] * 3,
        scratch_shapes=[
            VMEM(plane + (128,), BF),
            VMEM(full + (HT,), BF),
            VMEM(full + (HT,), BF),
            VMEM((2 * HT, D), BF),
            VMEM((2,) + full + (512,), BF),
            VMEM((2, nb, 128), F32),
            VMEM((2 * HT + 128, 128), F32),
            VMEM((T, D), BF),
            VMEM((T, D), BF),
            VMEM((T, D), BF),
            VMEM((T, D), BF),
            VMEM((D, T), BF),
            VMEM((D, T), BF),
            VMEM((D, T), BF),
            VMEM((T, D), BF),
            VMEM((T, D), F32),
            VMEM((T, D), F32),
            VMEM((MB * NH, 1, S), F32),
            VMEM((MB, 128, S), BF),
            VMEM((MB, 128, S), BF),
            VMEM((MB, 2 * S, HEAD_DIM), BF),
            VMEM((MB, 2 * S, HEAD_DIM), BF),
            VMEM((MB, HEAD_DIM, 2 * S), BF),
            VMEM((MB, HEAD_DIM + 16, 2 * S), BF),
            VMEM((MB, S, 128), F32),
            VMEM((MB, S, S), F32),
            VMEM((MB, 2 * S, 128), F32),
            VMEM((MB, S, 128), BF),
            VMEM((MB, S, 128), BF),
            VMEM((T, 128), BF),
            VMEM((3,) + full + (512,), BF),
            VMEM(full + (HT,), BF),
            VMEM((HT // 128,) + full + (128,), BF),
            VMEM(full + (128,), BF),
            VMEM((8, D), F32),
            VMEM((10, n_early, 128), F32),
            VMEM((10, n_late, 128), F32),
            VMEM((NF + 2, 2, ZC, XC, R, 512), BF),
            VMEM((NF + 3, ZC, XC, R, 256), BF),
            VMEM((NF + 3, 2, ZC, R, 256), BF),
            VMEM((NF + 3, 2, ZC, R, 256), BF),
            VMEM((NF + 3, 2, 3, R, 256), BF),
            DMA((Gather.SLOTS, 4)),
            DMA((n_gather, 4)),
            DMA((Reduce.SLOTS, 4)),
            DMA((n_reduce, 4)),
            DMA((8,)),
            DMA((2,)),
            DMA((6 + 2 * MB,)),
            DMA((4,)),
            DMA((4,)),
        ],
        compiler_params=pltpu.CompilerParams(
            vmem_limit_bytes=VMEM_LIMIT, collective_id=0, has_side_effects=True
        ),
        name="block",
    )(
        block_input.reshape(T, D),
        cotangent.reshape(T, D),
        lengths.reshape(MB),
        jnp.asarray(angle_table(S)),
        ln1_gain,
        ln1_bias,
        ln2_gain,
        ln2_bias,
        w_query,
        b_query,
        w_shared,
        b_shared,
        w_out.T,
        b_out,
        w_up,
        b_up,
        w_down.T,
        b_down,
    )
    out, gx, _, grads, early, late = outs
    vec = s((D,), F32)
    shapes = [s((T, D), BF), s((T, D), BF), vec, vec, vec, vec, s((R, HT), F32), s((HT,), F32)]
    shapes += [s((R, 128), F32), s((128,), F32), s((R, HT), F32), vec, s((R, FT), F32)]
    shapes += [s((FT,), F32), s((R, FT), F32), vec]
    outs = pl.pallas_call(
        partial(finish_kernel, dims),
        out_shape=shapes,
        in_specs=[hbm, hbm, hbm, vm, vm],
        out_specs=[hbm if len(shape.shape) > 1 else vm for shape in shapes],
        scratch_shapes=[VMEM((2, T, D), BF), VMEM((R, n_grads), F32), DMA((22,))],
        compiler_params=pltpu.CompilerParams(vmem_limit_bytes=VMEM_LIMIT),
        name="finish",
    )(out, gx, grads, early, late)
    res = list(outs)
    res[0] = res[0].reshape(block_input.shape)
    res[1] = res[1].reshape(block_input.shape)
    res[10] = res[10].T
    res[14] = res[14].T
    return tuple(res)


def fits_token_plan(mesh):
    return dict(mesh.shape) == {"dp": ZC * XC * CC, "tensor": 2}


def solution(mesh):
    in_specs = (
        P(None, "dp", "tensor", None),
        P(None, "dp", "tensor", None),
        P(None, "dp"),
        P(),
        P(),
        P(),
        P(),
        P("dp", "tensor"),
        P("tensor"),
        P("dp", None),
        P(),
        P("tensor", "dp"),
        P(),
        P("dp", "tensor"),
        P("tensor"),
        P("tensor", "dp"),
        P(),
    )
    out_specs = (
        P(None, "dp", "tensor", None),
        P(None, "dp", "tensor", None),
        P(),
        P(),
        P(),
        P(),
        P("dp", "tensor"),
        P("tensor"),
        P("dp", None),
        P(),
        P("tensor", "dp"),
        P(),
        P("dp", "tensor"),
        P("tensor"),
        P("tensor", "dp"),
        P(),
    )
    step = token_plan if fits_token_plan(mesh) else per_device
    return jax.shard_map(
        step, mesh=mesh, in_specs=in_specs, out_specs=out_specs, check_vma=False
    )
```

```python
from functools import partial

import jax
import jax.numpy as jnp
import numpy as np
from jax import lax
from jax.experimental import pallas as pl
from jax.experimental.pallas import tpu as pltpu
from jax.sharding import PartitionSpec as P

HEAD_DIM = 64
ROT = 16
MB = 2
QBLK = 512


EPS = 1e-05


def tables(count):
    places = jnp.arange(count).astype(jnp.float32)
    freqs = jnp.power(10000.0, -jnp.arange(ROT // 2).astype(jnp.float32) * 2.0 / ROT)
    angles = places[:, None] * freqs[None, :]
    return (jnp.cos(angles)[:, None, :], jnp.sin(angles)[:, None, :])


def rotate(vector, cosine, sine):
    first = vector[..., : ROT // 2]
    second = vector[..., ROT // 2 : ROT]
    return jnp.concatenate(
        [first * cosine - second * sine, second * cosine + first * sine, vector[..., ROT:]], axis=-1
    )


def unrotate(grad, cosine, sine):
    first = grad[..., : ROT // 2]
    second = grad[..., ROT // 2 : ROT]
    return jnp.concatenate(
        [first * cosine + second * sine, second * cosine - first * sine, grad[..., ROT:]], axis=-1
    )


def normalize(vector):
    centre = vector - jnp.mean(vector, axis=-1, keepdims=True)
    spread = jnp.mean(centre * centre, axis=-1, keepdims=True)
    scale = lax.rsqrt(spread + EPS)
    return (centre * scale, scale)


def norm_back(grad, normed, scale, gain):
    weighted = grad * gain
    return scale * (
        weighted
        - jnp.mean(weighted, axis=-1, keepdims=True)
        - normed * jnp.mean(weighted * normed, axis=-1, keepdims=True)
    )


def block_scores(rows, keys, start, limit, count):
    scores = jnp.einsum("qhd,kd->hqk", rows, keys, preferred_element_type=jnp.float32)
    row_pos = start + jnp.arange(QBLK)
    key_pos = jnp.arange(count)
    allowed = (key_pos[None, :] <= row_pos[:, None]) & (key_pos[None, :] < limit)
    return (scores, allowed[None])


def attend(queries, keys, values, limit):
    count = queries.shape[0]

    def block(start):
        rows = lax.dynamic_slice_in_dim(queries, start, QBLK, 0)
        scores, allowed = block_scores(rows, keys, start, limit, count)
        scores = jnp.where(allowed, scores, jnp.float32(-1e30))
        top = jnp.max(scores, axis=-1, keepdims=True)
        expo = jnp.exp(scores - top)
        total = jnp.sum(expo, axis=-1, keepdims=True)
        weights = (expo / total).astype(jnp.bfloat16)
        result = jnp.einsum("hqk,kd->qhd", weights, values, preferred_element_type=jnp.float32)
        return (result, (top + jnp.log(total))[..., 0])

    starts = jnp.arange(count // QBLK) * QBLK
    results, logsum = lax.map(block, starts)
    return (results.reshape(count, -1, HEAD_DIM), logsum)


def attend_back(queries, keys, values, limit, logsum, grad_out):
    count = queries.shape[0]

    def block(carry, item):
        start, block_logsum = item
        rows = lax.dynamic_slice_in_dim(queries, start, QBLK, 0)
        grads = lax.dynamic_slice_in_dim(grad_out, start, QBLK, 0)
        scores, allowed = block_scores(rows, keys, start, limit, count)
        probs = jnp.where(allowed, jnp.exp(scores - block_logsum[:, :, None]), 0.0)
        weights = probs.astype(jnp.bfloat16)
        dprobs = jnp.einsum("qhd,kd->hqk", grads, values, preferred_element_type=jnp.float32)
        delta = jnp.sum(probs * dprobs, axis=-1, keepdims=True)
        dscores = (probs * (dprobs - delta)).astype(jnp.bfloat16)
        drows = jnp.einsum("hqk,kd->qhd", dscores, keys, preferred_element_type=jnp.float32)
        dkeys = carry[0] + jnp.einsum(
            "hqk,qhd->kd", dscores, rows, preferred_element_type=jnp.float32
        )
        dvalues = carry[1] + jnp.einsum(
            "hqk,qhd->kd", weights, grads, preferred_element_type=jnp.float32
        )
        return ((dkeys, dvalues), drows)

    starts = jnp.arange(count // QBLK) * QBLK
    empty = jnp.zeros((count, HEAD_DIM), jnp.float32)
    (dkeys, dvalues), drows = lax.scan(block, (empty, empty), (starts, logsum))
    return (drows.reshape(count, -1, HEAD_DIM), dkeys, dvalues)


def fetch_each(w_query, w_shared, w_out, w_up, w_down):
    return (
        lax.all_gather(w_query, "dp", axis=0, tiled=True),
        lax.all_gather(w_shared, "dp", axis=0, tiled=True),
        lax.all_gather(w_out, "dp", axis=1, tiled=True),
        lax.all_gather(w_up, "dp", axis=0, tiled=True),
        lax.all_gather(w_down, "dp", axis=1, tiled=True),
    )


def reduce_each(step_grads):
    return (
        lax.psum_scatter(step_grads[0], "dp", scatter_dimension=0, tiled=True),
        lax.psum_scatter(step_grads[1], "dp", scatter_dimension=0, tiled=True),
        lax.psum_scatter(step_grads[2], "dp", scatter_dimension=1, tiled=True),
        lax.psum_scatter(step_grads[3], "dp", scatter_dimension=0, tiled=True),
        lax.psum_scatter(step_grads[4], "dp", scatter_dimension=1, tiled=True),
    )


def per_device(
    block_input,
    cotangent,
    lengths,
    ln1_gain,
    ln1_bias,
    ln2_gain,
    ln2_bias,
    w_query,
    b_query,
    w_shared,
    b_shared,
    w_out,
    b_out,
    w_up,
    b_up,
    w_down,
    b_down,
):
    shard_rows = block_input.shape[2]
    groups = lax.axis_size("tensor")
    rank = lax.axis_index("tensor")
    seq_len = shard_rows * groups
    tail_bias = b_out + b_down
    weight_sums = None
    cos_all, sin_all = tables(seq_len)
    own_pos = rank * shard_rows + jnp.arange(shard_rows)
    outputs = []
    input_grads = []
    sum_bq = jnp.zeros(b_query.shape, jnp.float32)
    sum_bkv = jnp.zeros(b_shared.shape, jnp.float32)
    sum_bup = jnp.zeros(b_up.shape, jnp.float32)
    sum_gain1 = jnp.zeros(ln1_gain.shape, jnp.float32)
    sum_shift1 = jnp.zeros(ln1_gain.shape, jnp.float32)
    sum_gain2 = jnp.zeros(ln1_gain.shape, jnp.float32)
    sum_shift2 = jnp.zeros(ln1_gain.shape, jnp.float32)
    sum_out = jnp.zeros(ln1_gain.shape, jnp.float32)
    for micro in range(MB):
        fetched = fetch_each(w_query, w_shared, w_out, w_up, w_down)
        wq_all, wkv_all, wo_all, wup_all, wdown_all = fetched
        limit = lengths[micro, 0]
        inputs = block_input[micro, 0].astype(jnp.float32)
        normed_one, scale_one = normalize(inputs)
        normed_two, scale_two = normalize(inputs)
        low_one = (normed_one * ln1_gain + ln1_bias).astype(jnp.bfloat16)
        low_two = (normed_two * ln2_gain + ln2_bias).astype(jnp.bfloat16)
        whole_one, whole_two = (
            lax.all_gather(low_one, "tensor", axis=0, tiled=True),
            lax.all_gather(low_two, "tensor", axis=0, tiled=True),
        )
        query_lin = jnp.dot(whole_one, wq_all, preferred_element_type=jnp.float32) + b_query
        query_lin = query_lin.reshape(seq_len, -1, HEAD_DIM)
        queries = (rotate(query_lin, cos_all, sin_all) * 0.125).astype(jnp.bfloat16)
        shared = jnp.dot(whole_one, wkv_all, preferred_element_type=jnp.float32) + b_shared
        keys = rotate(shared[:, None, :HEAD_DIM], cos_all, sin_all)[:, 0].astype(jnp.bfloat16)
        values = shared[:, HEAD_DIM:].astype(jnp.bfloat16)
        attended, logsum = attend(queries, keys, values, limit)
        attended_low = attended.reshape(seq_len, -1).astype(jnp.bfloat16)
        hidden = jnp.dot(whole_two, wup_all, preferred_element_type=jnp.float32) + b_up
        active = jax.nn.gelu(hidden, approximate=False).astype(jnp.bfloat16)
        partial_out = jnp.dot(attended_low, wo_all, preferred_element_type=jnp.float32) + jnp.dot(
            active, wdown_all, preferred_element_type=jnp.float32
        )
        branch = lax.psum_scatter(partial_out, "tensor", scatter_dimension=0, tiled=True)
        outputs.append((inputs + branch + tail_bias).astype(jnp.bfloat16))
        valid = (own_pos < limit).astype(jnp.float32)[:, None]
        upstream = cotangent[micro, 0].astype(jnp.float32) * valid
        whole_up = lax.all_gather(upstream.astype(jnp.bfloat16), "tensor", axis=0, tiled=True)
        sum_out = sum_out + jnp.sum(upstream, axis=0)
        grad_down = jnp.einsum("lf,ld->fd", active, whole_up, preferred_element_type=jnp.float32)
        dactive = jnp.einsum("ld,fd->lf", whole_up, wdown_all, preferred_element_type=jnp.float32)
        gelu_pull = jax.vjp(partial(jax.nn.gelu, approximate=False), hidden)[1]
        dhidden = gelu_pull(dactive)[0].astype(jnp.bfloat16)
        sum_bup = sum_bup + jnp.sum(dhidden.astype(jnp.float32), axis=0)
        grad_up = jnp.einsum("ld,lf->df", whole_two, dhidden, preferred_element_type=jnp.float32)
        dnormed_two = jnp.einsum("lf,df->ld", dhidden, wup_all, preferred_element_type=jnp.float32)
        dattended = jnp.einsum("ld,ed->le", whole_up, wo_all, preferred_element_type=jnp.float32)
        dattended = dattended.astype(jnp.bfloat16).reshape(seq_len, -1, HEAD_DIM)
        grad_out = jnp.einsum(
            "le,ld->ed", attended_low, whole_up, preferred_element_type=jnp.float32
        )
        dqueries, dkeys, dvalues = attend_back(queries, keys, values, limit, logsum, dattended)
        dquery_lin = (
            unrotate(dqueries * 0.125, cos_all, sin_all).reshape(seq_len, -1).astype(jnp.bfloat16)
        )
        dkey_lin = unrotate(dkeys[:, None, :], cos_all, sin_all)[:, 0]
        dshared = lax.psum(jnp.concatenate([dkey_lin, dvalues], axis=1), "tensor")
        dshared = dshared.astype(jnp.bfloat16)
        sum_bq = sum_bq + jnp.sum(dquery_lin.astype(jnp.float32), axis=0)
        sum_bkv = sum_bkv + jnp.sum(dshared.astype(jnp.float32), axis=0)
        grad_q = jnp.einsum("ld,le->de", whole_one, dquery_lin, preferred_element_type=jnp.float32)
        grad_kv = jnp.einsum("ld,lc->dc", whole_one, dshared, preferred_element_type=jnp.float32)
        dnormed_one = jnp.einsum(
            "le,de->ld", dquery_lin, wq_all, preferred_element_type=jnp.float32
        )
        dnormed_one, dnormed_two = (
            lax.psum_scatter(dnormed_one, "tensor", scatter_dimension=0, tiled=True),
            lax.psum_scatter(dnormed_two, "tensor", scatter_dimension=0, tiled=True),
        )
        own_shared = lax.dynamic_slice_in_dim(dshared, rank * shard_rows, shard_rows, 0)
        dnormed_one = dnormed_one + jnp.einsum(
            "lc,dc->ld", own_shared, wkv_all, preferred_element_type=jnp.float32
        )
        sum_gain1 = sum_gain1 + jnp.sum(dnormed_one * normed_one, axis=0)
        sum_shift1 = sum_shift1 + jnp.sum(dnormed_one, axis=0)
        sum_gain2 = sum_gain2 + jnp.sum(dnormed_two * normed_two, axis=0)
        sum_shift2 = sum_shift2 + jnp.sum(dnormed_two, axis=0)
        dinputs = (
            upstream
            + norm_back(dnormed_one, normed_one, scale_one, ln1_gain)
            + norm_back(dnormed_two, normed_two, scale_two, ln2_gain)
        )
        input_grads.append(dinputs.astype(jnp.bfloat16))
        step_grads = (grad_q, grad_kv, grad_out, grad_up, grad_down)
        step_grads = reduce_each(step_grads)
        if weight_sums is None:
            weight_sums = step_grads
        else:
            weight_sums = jax.tree.map(jnp.add, weight_sums, step_grads)
    output = jnp.stack(outputs, axis=0)[:, None]
    grad_input = jnp.stack(input_grads, axis=0)[:, None]
    sum_bq, sum_bkv, sum_bup = lax.psum((sum_bq, sum_bkv, sum_bup), "dp")
    sum_gain1, sum_shift1, sum_gain2, sum_shift2, sum_out = lax.psum(
        (sum_gain1, sum_shift1, sum_gain2, sum_shift2, sum_out), ("dp", "tensor")
    )
    grad_q, grad_kv, grad_o, grad_up, grad_down = weight_sums
    return (
        output,
        grad_input,
        sum_gain1,
        sum_shift1,
        sum_gain2,
        sum_shift2,
        grad_q,
        sum_bq,
        grad_kv,
        sum_bkv,
        grad_o,
        sum_out,
        grad_up,
        sum_bup,
        grad_down,
        sum_out,
    )


MESH = pl.DeviceIdType.MESH
BF = jnp.bfloat16
F32 = jnp.float32
LOG2E = 1.4426950408889634
LN2 = 0.6931471805599453
NEG = -1e30
ZC, XC, CC = 4, 2, 2
DMA = pltpu.SemaphoreType.DMA
VMEM = pltpu.VMEM
VMEM_LIMIT = (64 << 20) - 65536


def nn(a, b):
    return lax.dot_general(a, b, (((1,), (0,)), ((), ())), preferred_element_type=F32)


def nt(a, b):
    return lax.dot_general(a, b, (((1,), (1,)), ((), ())), preferred_element_type=F32)


def tn(a, b):
    return lax.dot_general(a, b, (((0,), (0,)), ((), ())), preferred_element_type=F32)


def eye(n):
    return (
        lax.broadcasted_iota(jnp.int32, (n, n), 0) == lax.broadcasted_iota(jnp.int32, (n, n), 1)
    ).astype(BF)


def flat(block):
    return block.reshape(-1, block.shape[-1])


class Place:
    def __init__(self):
        self.dp = lax.axis_index("dp")
        self.t = lax.axis_index("tensor")
        self.core = lax.rem(self.dp, CC)
        self.x = lax.rem(lax.div(self.dp, CC), XC)
        self.z = lax.div(self.dp, CC * XC)

    def at(self, z, x, core):
        return (z * XC + x) * CC + core

    def z_peer(self, d):
        return {"dp": self.at(lax.rem(self.z + d, ZC), self.x, self.core)}

    def x_peer(self):
        return {"dp": self.at(self.z, 1 - self.x, self.core)}

    def core_peer(self):
        return {"dp": self.at(self.z, self.x, 1 - self.core)}

    def y_peer(self):
        return {"tensor": 1 - self.t}

    def layer_peers(self):
        res = []
        for k in range(1, 8):
            x = 1 - self.x if k & 1 else self.x
            t = 1 - self.t if k & 2 else self.t
            core = 1 - self.core if k & 4 else self.core
            res.append({"dp": self.at(self.z, x, core), "tensor": t})
        return res

    def greet(self):
        bar = pltpu.get_barrier_semaphore()
        peers = [self.z_peer(d) for d in (1, 2, 3)] + self.layer_peers()
        for p in peers:
            pl.semaphore_signal(bar, inc=1, device_id=p, device_id_type=MESH)
        return bar, len(peers)


def remote(src, dst, ss, rs, peer):
    return pltpu.make_async_remote_copy(
        src_ref=src, dst_ref=dst, send_sem=ss, recv_sem=rs, device_id=peer, device_id_type=MESH
    )


def split_cols(width):
    a = (width // 128 + 1) // 2 * 128
    return ((0, a), (a, width - a))


class Gather:
    SLOTS = 3

    def __init__(self, place, pieces, sends, gots):
        self.p = place
        self.pieces = pieces
        self.sends, self.gots = sends, gots

    def own(self, c, h):
        p = self.p
        _, o, w, order = self.pieces[c][0][h]
        index = (p.z, p.x, p.core, slice(None), pl.ds(o, w))
        return self.pieces[c][1].at[(p.t,) + index if "y" in order else index]

    def copies(self, c, k):
        p = self.p
        every = slice(None)
        res = []
        for h, (src, o, w, order) in enumerate(self.pieces[c][0]):
            if k == 0:
                pairs = [(src, self.own(c, h), p.z_peer(d)) for d in (1, 2, 3)]
            elif k <= len(order):
                done = order[:k]
                index = (every, every if "x" in done else p.x, p.core, every, pl.ds(o, w))
                if "y" in order:
                    index = (every if "y" in done else p.t,) + index
                view = self.pieces[c][1].at[index]
                axis = order[k] if k < len(order) else "core"
                peers = {"x": p.x_peer(), "y": p.y_peer(), "core": p.core_peer()}
                pairs = [(view, view, peers[axis])]
            else:
                pairs = []
            for a, b, peer in pairs:
                res.append(remote(a, b, self.sends.at[c % self.SLOTS, k], self.gots.at[c, k], peer))
        return res

    def total(self, c, k):
        parts, out = self.pieces[c]
        z = pl.ds(0, 3) if k == 0 else slice(None)
        x = slice(None) if k > 1 else 0
        index = (z, x, 0)
        if "y" in parts[0][3]:
            index = (slice(None) if k > 2 else 0,) + index
        view = out.at[index]
        return remote(
            view, view, self.sends.at[c % self.SLOTS, k], self.gots.at[c, k], self.p.core_peer()
        )

    def run(self, ops):
        for op in ops:
            c, k = (op, -1) if isinstance(op, int) else op
            if k >= 0:
                self.total(c, k).wait()
            for cp in self.copies(c, k + 1):
                cp.start()


class AllSum:
    def __init__(self, place, buf, got, sems):
        self.p = place
        self.buf, self.got, self.sems = buf, got, sems

    def part(self, k):
        return (7, 3) if k else (0, 7)

    def start(self, k):
        peers = [self.p.z_peer(d) for d in (1, 2, 3)] if k else self.p.layer_peers()
        at, _ = self.part(k)
        for i, peer in enumerate(peers):
            got = self.got.at[at + i]
            remote(self.buf, got, self.sems.at[2 * k], self.sems.at[2 * k + 1], peer).start()

    def end(self, k):
        at, n = self.part(k)
        view = self.got.at[pl.ds(at, n)]
        whole = remote(
            view, view, self.sems.at[2 * k], self.sems.at[2 * k + 1], self.p.core_peer()
        )
        whole.wait()
        total = self.buf[...]
        for i in range(at, at + n):
            total = total + self.got[i]
        self.buf[...] = total


def normal_rows(rows):
    mean = jnp.mean(rows, axis=-1, keepdims=True)
    centre = rows - mean
    var = jnp.mean(centre * centre, axis=-1, keepdims=True)
    scale = lax.rsqrt(var + EPS)
    return centre * scale, scale


def rotate_t(v, cosine, sine):
    a, b = v[0:8], v[8:16]
    return jnp.concatenate([a * cosine - b * sine, b * cosine + a * sine, v[16:]], axis=0)


def unrotate_t(v, cosine, sine):
    a, b = v[0:8], v[8:16]
    return jnp.concatenate([a * cosine + b * sine, b * cosine - a * sine, v[16:]], axis=0)


def fill_bias(place, lens_ref, other_ref, own_ref, S):
    t = place.t
    for m in range(MB):
        limit = lens_ref[m]
        key = lax.broadcasted_iota(jnp.int32, (S, 128), 0)
        limit_other = jnp.where(t == 1, limit, 0)
        other_ref[m] = jnp.where(key < limit_other, 0.0, NEG).astype(F32)
        key = lax.broadcasted_iota(jnp.int32, (S, S), 0)
        row = lax.broadcasted_iota(jnp.int32, (S, S), 1)
        own = (key <= row) & (key + t * S < limit)
        own_ref[m] = jnp.where(own, 0.0, NEG).astype(F32)


def masked_rows(place_t, lens_ref, dy, start, S):
    m, off = divmod(start, S)
    pos = place_t * S + off + lax.broadcasted_iota(jnp.int32, (dy.shape[0], 1), 0)
    return jnp.where(pos < lens_ref[m], dy.astype(F32), 0.0)


class Reduce:
    SLOTS = 3

    def __init__(self, place, pieces, rc, r2a, r2b, r3, r4, sends, gots):
        self.p = place
        self.pieces = pieces
        self.rc, self.r2a, self.r2b, self.r3, self.r4 = rc, r2a, r2b, r3, r4
        self.sends, self.gots = sends, gots

    def part(self, c, h):
        r, n, o, w = self.pieces[c][1][h]
        _, first, _, second = self.pieces[c][3]
        o += first
        return (slice(r, r + n), slice(o, o + w)), (slice(0, n), slice(second, second + w))

    def wide(self, c):
        first = self.pieces[c][3][1]
        return slice(first, first + self.pieces[c][0].shape[-1])

    def sems(self, c, k):
        return self.sends.at[c % self.SLOTS, k], self.gots.at[c, k]

    def copies(self, c, k):
        p = self.p
        if k == 0:
            src = self.pieces[c][0].at[:, :, :, 1 - p.core]
            dst = self.rc.at[self.pieces[c][3][0], :, :, :, :, self.wide(c)]
            return [remote(src, dst, *self.sems(c, k), p.core_peer())]
        res = []
        a, _, b, _ = self.pieces[c][3]
        for h in (0, 1):
            here, there = self.part(c, h)
            if k == 1 and h == 0:
                src, dst = self.rc.at[(a, 1 - p.t, slice(None), slice(None)) + here], self.r2a
                todo = [(src, dst.at[(b, slice(None), slice(None)) + there], p.y_peer())]
            elif k == 1:
                src, dst = self.rc.at[(a, slice(None), slice(None), 1 - p.x) + here], self.r2b
                todo = [(src, dst.at[(b, slice(None), slice(None)) + there], p.x_peer())]
            elif k == 2:
                if h == 0:
                    src, peer = self.r2a.at[(b, slice(None), 1 - p.x) + there], p.x_peer()
                else:
                    src, peer = self.r2b.at[(b, 1 - p.t, slice(None)) + there], p.y_peer()
                todo = [(src, self.r3.at[(b, h, slice(None)) + there], peer)]
            else:
                todo = [
                    (
                        self.r3.at[(b, h, lax.rem(p.z + d, ZC)) + there],
                        self.r4.at[(b, h, d - 1) + there],
                        p.z_peer(d),
                    )
                    for d in (1, 2, 3)
                ]
            res += [remote(src, dst, *self.sems(c, k), peer) for src, dst, peer in todo]
        return res

    def total(self, c, k):
        cols = self.wide(c)
        every = slice(None)
        index = {
            0: (every, every, every, every, cols),
            1: (0, every, every, every, cols),
            2: (0, every, 0, every, cols),
            3: (0, pl.ds(0, 3), 0, every, cols),
        }[k]
        view = self.rc.at[(self.pieces[c][3][0],) + index]
        return remote(view, view, *self.sems(c, k), self.p.core_peer())

    def start(self, c, k):
        for cp in self.copies(c, k):
            cp.start()

    def add(self, c, k):
        p = self.p
        a, _, b, _ = self.pieces[c][3]
        if k == 1:
            cols = self.wide(c)
            mine = self.pieces[c][0][:, :, :, p.core].astype(F32)
            mine = mine + self.rc[a, :, :, :, :, cols].astype(F32)
            self.rc[a, :, :, :, :, cols] = mine.astype(BF)
            return
        sums = []
        for h in (0, 1):
            here, there = self.part(c, h)
            every = slice(None)
            if k == 2:
                if h == 0:
                    ref, mine = self.r2a, self.rc[(a, p.t, every, every) + here]
                else:
                    ref, mine = self.r2b, self.rc[(a, every, every, p.x) + here]
                at = (b, every, every) + there
                ref[at] = (mine.astype(F32) + ref[at].astype(F32)).astype(BF)
            elif k == 3:
                if h == 0:
                    mine = self.r2a[(b, every, p.x) + there]
                else:
                    mine = self.r2b[(b, p.t, every) + there]
                at = (b, h, every) + there
                self.r3[at] = (mine.astype(F32) + self.r3[at].astype(F32)).astype(BF)
            else:
                total = self.r3[(b, h, p.z) + there].astype(F32)
                for d in range(3):
                    total = total + self.r4[(b, h, d) + there].astype(F32)
                sums.append(total)
        if k == 4:
            self.pieces[c][2](sums)

    def run(self, ops):
        for c, k in ops:
            if k:
                self.total(c, k - 1).wait()
                self.add(c, k)
            if k < 4:
                self.start(c, k)


HEAD_OPS = (
    (0, 1),
    ((0, 0), (1, 0), 2),
    ((0, 1), (1, 1), 3),
    ((0, 2),),
    ((1, 2), 4),
    ((1, 3), (2, 0), (3, 0), 5),
)
ATTENTION_OPS = {
    0: (6,),
    1: ((2, 1),),
    2: ((4, 0),),
    4: ((3, 1), (5, 0), 7),
    5: ((2, 2),),
    7: ((2, 3), (4, 1), (6, 0), 8),
}
BACK_OPS = {
    0: ((3, 2), (4, 2), (5, 1), (7, 0)),
    3: ((3, 3), (4, 3), (5, 2), (6, 1), (8, 0)),
    5: ((5, 3), (7, 1)),
}
FFN_OPS = {
    0: ((6, 2),),
    1: ((6, 3), (7, 2), (8, 1)),
    2: ((7, 3),),
    3: ((8, 2),),
    4: ((8, 3),),
}


FFN_SUMS = {
    0: ((0, 1),),
    2: ((0, 2), (1, 1)),
    3: ((0, 3), (2, 1)),
    4: ((0, 4), (1, 2), (3, 1)),
    5: ((1, 3), (2, 2), (4, 1)),
}
BACK_SUMS = {
    6: ((1, 4), (2, 3), (3, 2), (5, 1)),
    8: ((2, 4), (3, 3), (4, 2), (6, 1)),
    9: ((7, 1),),
    10: ((3, 4), (4, 3), (5, 2)),
    11: ((7, 2), (8, 1), (6, 2)),
}
LAST_SUMS = (
    ((4, 4), (5, 3), (7, 3), (8, 2)),
    ((9, 1), (6, 3)),
    ((10, 1), (9, 2), (5, 4), (8, 3)),
    ((10, 2), (6, 4), (9, 3), (7, 4)),
    ((10, 3), (8, 4)),
    ((9, 4), (10, 4)),
)


def block_kernel(
    dims,
    x_hbm,
    dy_hbm,
    lens_ref,
    tab_ref,
    g1_ref,
    b1_ref,
    g2_ref,
    b2_ref,
    wq_in,
    bq_ref,
    wsh_in,
    bsh_ref,
    wout_in,
    bout_ref,
    wup_in,
    bup_ref,
    wdown_in,
    bdown_ref,
    out_hbm,
    gx_hbm,
    wf,
    grads,
    early,
    late,
    wsh,
    wq,
    wb,
    won,
    wv,
    ball,
    bcol,
    x_ref,
    dym,
    h1,
    h2,
    qt,
    att,
    da,
    tmp,
    acc,
    dh2,
    lse_ref,
    kvt,
    kvo,
    kc,
    vc,
    kt,
    vte,
    bias_o,
    bias_s,
    dkv,
    dkvs,
    dkvr,
    dkvn,
    gring,
    gb,
    gq,
    gkv,
    sums,
    early_in,
    late_in,
    rc,
    r2a,
    r2b,
    r3,
    r4,
    gsend,
    gsem,
    rsend,
    rsem,
    lsem,
    wsem,
    ysem,
    esem,
    asem,
):
    S, HT, NH, NF, T = dims["S"], dims["HT"], dims["NH"], dims["NF"], dims["T"]
    D = x_ref.shape[1]
    R = wq_in.shape[0]
    NB = S // 256
    p = Place()
    bar, npeers = p.greet()
    x_copy = pltpu.make_async_copy(x_hbm, x_ref, lsem.at[1])
    x_copy.start()
    dy_copy = pltpu.make_async_copy(dy_hbm, dym, lsem.at[0])
    dy_copy.start()

    def parts_of(ref, widths, orders):
        at = [sum(widths[:i]) for i in range(len(widths))]
        return [(ref.at[:, pl.ds(o, w)], o, w, order) for o, w, order in zip(at, widths, orders)]

    wide = [w for _, w in split_cols(HT)]
    pieces = [
        ([(wsh_in, 0, 128, "zx")], wsh),
        (parts_of(wq_in, wide, ("zxy", "zyx")), wq),
        (parts_of(wout_in, wide, ("zxy", "zyx")), wb),
    ]
    for f in range(NF):
        cols = pl.ds(256 * f, 256)
        parts = [(wup_in.at[:, cols], 0, 256, "zxy"), (wdown_in.at[:, cols], 256, 256, "zyx")]
        pieces.append((parts, wf.at[f]))
    g = Gather(p, pieces, gsend, gsem)
    pl.semaphore_wait(bar, npeers)
    g.run(HEAD_OPS[0])
    locals_ = [
        pltpu.make_async_copy(wsh_in, wsh.at[p.z, p.x, p.core], lsem.at[2]),
        pltpu.make_async_copy(wq_in, wq.at[p.t, p.z, p.x, p.core], lsem.at[3]),
        pltpu.make_async_copy(wout_in, wb.at[p.t, p.z, p.x, p.core], lsem.at[4]),
    ]
    for cp in locals_:
        cp.start()
    for c in range(3, len(pieces)):
        for h in (0, 1):
            pltpu.make_async_copy(pieces[c][0][h][0], g.own(c, h), lsem.at[5]).start()
    held = wf.at[:, 0, 0, 0, 0]
    locals_.append(pltpu.make_async_copy(held, held, lsem.at[5]))
    first = HT // 128
    rows_b = ball.shape[1]
    ball[p.t, 0:first, :] = bq_ref[...].reshape(first, 128)
    ball[p.t, first : first + 2 * NF, :] = bup_ref[...].reshape(2 * NF, 128)
    ball[p.t, first + 2 * NF :, :] = jnp.zeros((rows_b - first - 2 * NF, 128), F32)
    bias_copy = remote(ball.at[p.t], ball.at[p.t], ysem.at[0], ysem.at[1], p.y_peer())
    bias_copy.start()

    gain1, shift1, gain2, shift2 = (
        ref[...].reshape(1, D) for ref in (g1_ref, b1_ref, g2_ref, b2_ref)
    )

    def norm_block(i):
        rows = pl.ds(pl.multiple_of(i * 128, 128), 128)
        z, _ = normal_rows(x_ref[rows, :].astype(F32))
        h1[rows, :] = (z * gain1 + shift1).astype(BF)
        h2[rows, :] = (z * gain2 + shift2).astype(BF)

    half = T // 256
    x_copy.wait()
    pl.loop(0, half)(norm_block)
    for cp in locals_:
        cp.wait()
    g.run(HEAD_OPS[1])
    pl.loop(half, 2 * half)(norm_block)
    g.run(HEAD_OPS[2])
    fill_bias(p, lens_ref, bias_o, bias_s, S)
    for ref in (dkv, dh2, sums):
        ref[...] = jnp.zeros_like(ref)
    bias_copy.wait()
    nq = HT // 128
    for t in range(2):
        for j in range(nq):
            row = jnp.broadcast_to(ball[t, j : j + 1, :], (128, 128))
            bcol[(t * nq + j) * 128 : (t * nq + j + 1) * 128, :] = row.T
    bcol[2 * HT : 2 * HT + 128, :] = jnp.broadcast_to(bsh_ref[...].reshape(1, 128), (128, 128)).T
    g.run(HEAD_OPS[3])

    id256 = eye(256)
    cosine, sine = tab_ref[p.t, 0:8, :], tab_ref[p.t, 8:16, :]
    wsh_t = nt(eye(128), flat(wsh[...])).astype(BF)
    kv_copies = [
        remote(kvt.at[m], kvo.at[m], ysem.at[2 + 2 * m], ysem.at[3 + 2 * m], p.y_peer())
        for m in range(MB)
    ]
    for m in range(MB):
        kv = nt(wsh_t, h1[m * S : m * S + S, :]) + bcol[2 * HT : 2 * HT + 128, 0:1]
        kvt[m, 0:HEAD_DIM, :] = rotate_t(kv[0:HEAD_DIM], cosine, sine).astype(BF)
        kvt[m, HEAD_DIM:, :] = kv[HEAD_DIM:].astype(BF)
    g.run(HEAD_OPS[4])
    kv_copies[0].start()
    dy_copy.wait()
    for b in range(T // 256):
        rows = slice(b * 256, b * 256 + 256)
        dy = masked_rows(p.t, lens_ref, dym[rows, :], b * 256, S)
        dym[rows, :] = dy.astype(BF)
        sums[6:7, :] += jnp.sum(dy, axis=0, keepdims=True)
    g.run(HEAD_OPS[5])

    for t in range(2):
        wq_t = nt(eye(HT), flat(wq[t])).astype(BF)
        for m in range(MB):
            cols = slice(m * S, m * S + S)
            q = nt(wq_t, h1[cols, :])
            for h in range(HT // HEAD_DIM):
                base = t * HT + h * HEAD_DIM
                qh = q[h * HEAD_DIM : (h + 1) * HEAD_DIM] + bcol[base : base + HEAD_DIM, 0:1]
                qh = rotate_t(qh, cosine, sine) * (0.125 * LOG2E)
                qt[base : base + HEAD_DIM, cols] = qh.astype(BF)

    def both_halves(m):
        kv_copies[m].wait()
        for part, src in ((0, kvo), (1, kvt)):
            keys = slice(part * S, part * S + S)
            kt[m, :, keys] = src[m, 0:HEAD_DIM, :]
            vte[m, 0:HEAD_DIM, keys] = src[m, HEAD_DIM:, :]
        vte[m, HEAD_DIM:, :] = (
            lax.broadcasted_iota(jnp.int32, (16, 2 * S), 0) == 0
        ).astype(BF)
        for b in range(2 * NB):
            blk = slice(b * 256, b * 256 + 256)
            kc[m, blk, :] = nt(id256, kt[m, :, blk]).astype(BF)
            vc[m, blk, :] = nt(id256, vte[m, 0:HEAD_DIM, blk]).astype(BF)

    both_halves(0)

    def spots(i, group, by_thirds=False):
        res = []
        for u in range(group):
            j = i * group + u
            m, h = lax.div(j, NH), lax.rem(j, NH)
            if by_thirds:
                k = lax.div(h, 2)
                h = lax.rem(k, 2) * (NH // 2) + lax.div(k, 2) * 2 + u
                j = m * NH + h
            head = pl.ds(pl.multiple_of(h * HEAD_DIM, HEAD_DIM), HEAD_DIM)
            for r in range(NB):
                cols = pl.ds(pl.multiple_of(m * S + r * 256, 256), 256)
                res.append((j, m, head, cols, S + 256 * (r + 1), r))
        return res

    def scores(m, q, nk, r):
        s = nn(kc[m, 0:nk, :], q)
        wide = slice(r * 256, r * 256 + 256)
        other = bias_o[m]
        other = jnp.concatenate([other, other], axis=1)
        return jnp.concatenate([s[0:S] + other, s[S:nk] + bias_s[m, 0 : nk - S, wide]], axis=0)

    group = 3

    @pl.loop(0, MB * NH // group)
    def _(i):
        for m in range(1, MB):
            pl.when(i == (m - 1) * NH // group)(kv_copies[m].start)
            pl.when(i == m * NH // group)(partial(both_halves, m))
        for at, ops in ATTENTION_OPS.items():
            pl.when(i == at)(partial(g.run, ops))
        todo = spots(i, group)
        sc = [scores(m, qt[head, cols], nk, r) for _, m, head, cols, nk, r in todo]
        tops = [jnp.max(s, axis=0, keepdims=True) for s in sc]
        ex = [jnp.exp2(s - top).astype(BF) for s, top in zip(sc, tops)]
        for (j, m, head, cols, nk, r), e, top in zip(todo, ex, tops):
            o = nn(vte[m, :, 0:nk], e)
            total = o[HEAD_DIM : HEAD_DIM + 1]
            att[head, cols] = (o[0:HEAD_DIM] * (1.0 / total)).astype(BF)
            lse_ref[j, :, r * 256 : r * 256 + 256] = top + jnp.log2(total)

    for t in range(2):
        won[t * HT : (t + 1) * HT, :] = nt(eye(HT), flat(wb[t])).astype(BF)

    def load(f, slot):
        return pltpu.make_async_copy(wf.at[f], wv.at[slot], wsem.at[slot])

    for b in range(T // 256):
        rows = slice(b * 256, b * 256 + 256)
        tmp[rows, :] = nt(id256, att[:, rows]).astype(BF)
    tail_bias = (bout_ref[...] + bdown_ref[...]).reshape(1, D)
    acc[...] = x_ref[...].astype(F32) + tail_bias + nn(tmp[...], won[...])
    for t in range(2):
        cols = slice(t * HT, (t + 1) * HT)
        gb[t] = tn(dym[...], tmp[:, cols]).astype(BF).reshape(ZC, XC, CC, R, HT)

    def put(*firsts):
        def store(parts):
            for o, v in zip(firsts, parts):
                grads[:, o : o + v.shape[1]] = v

        return store

    at_out, at_up, at_down = HT + 128, 2 * HT + 128, 2 * HT + 128 + 256 * NF
    thirds = HT // 128

    def by_cols(*widths):
        at = [sum(widths[:i]) for i in range(len(widths))]
        return [(0, R, o, w) for o, w in zip(at, widths)]

    def put_rows(first):
        def store(parts):
            r = 0
            for v in parts:
                grads[r : r + v.shape[0], first : first + 128] = v
                r += v.shape[0]

        return store

    by_rows = [(0, 32, 0, 128), (32, R - 32, 0, 128)]
    sums_of = [(gb, by_cols(*wide), put(at_out, at_out + wide[0]), (0, 0, 0, 0))]
    for f in range(NF):
        store = put(at_up + 256 * f, at_down + 256 * f)
        sums_of.append((gring.at[f % 3], by_cols(256, 256), store, (1 + f, 0, 1 + f, 0)))
    for k in range(thirds + 1):
        store = put_rows(128 * k)
        slot = (NF + 1, 128 * k, NF + 1 + k // 2, 128 * (k % 2))
        sums_of.append((gq.at[k] if k < thirds else gkv, by_rows, store, slot))
    red = Reduce(p, sums_of, rc, r2a, r2b, r3, r4, rsend, rsem)
    last = NF + 1
    red.run([(0, 0)])

    n = D // 128
    early_sum = AllSum(p, early, early_in, esem)
    da[...] = nt(won[...], dym[...]).astype(BF)
    back = 2
    dkv_copies = [
        remote(dkvs.at[m], dkvr.at[m], ysem.at[6 + 2 * m], ysem.at[7 + 2 * m], p.y_peer())
        for m in range(MB)
    ]

    def send_dkv(m):
        dkvs[m] = dkv[m, 0:S, :].astype(BF)
        dkv_copies[m].start()

    def query_third(k):
        for t in range(2):
            at = t * HT + 128 * k
            for b in range(T // 256):
                rows = slice(b * 256, b * 256 + 256)
                tmp[rows, at : at + 128] = nt(id256, qt[at : at + 128, rows]).astype(BF)
            v = tn(h1[...], tmp[:, at : at + 128]).astype(BF)
            gq[k, t] = v.reshape(ZC, XC, CC, R, 128)
        red.run([(last + k, 0)])

    def own_dkv(m):
        dkv_copies[m].wait()
        both = (dkv[m, S : 2 * S, :] + dkvr[m].astype(F32)).T
        dk = unrotate_t(both[0:HEAD_DIM], cosine, sine) * LN2
        both = jnp.concatenate([dk, both[HEAD_DIM:]], axis=0).astype(BF)
        for b in range(NB):
            rows = slice(m * S + b * 256, m * S + b * 256 + 256)
            dkvn[rows, :] = nt(id256, both[:, b * 256 : b * 256 + 256]).astype(BF)

    def early_next():
        early_sum.end(0)
        early_sum.start(1)

    def back_step(i):
        for at, ops in BACK_OPS.items():
            pl.when(i == at)(partial(g.run, ops))
        pl.when(i == NH // back + 2)(early_next)
        pl.when(i == NH // back + 3)(partial(own_dkv, 0))
        for at, ops in BACK_SUMS.items():
            pl.when(i == at)(partial(red.run, ops))
        for k in range(thirds - 1):
            at = MB * NH // back - 2 * (thirds - 1 - k)
            pl.when(i == at)(partial(query_third, k))
        todo = spots(i, back, True)
        qs = [qt[head, cols] for _, m, head, cols, nk, r in todo]
        das = [da[head, cols] for _, m, head, cols, nk, r in todo]
        sc = [scores(m, q, nk, r) for (_, m, head, cols, nk, r), q in zip(todo, qs)]
        dp = [nn(vc[m, 0:nk, :], d) for (_, m, head, cols, nk, r), d in zip(todo, das)]
        pr, ds = [], []
        for (j, m, head, cols, nk, r), d, s, dpj in zip(todo, das, sc, dp):
            delta = jnp.sum(d.astype(F32) * att[head, cols].astype(F32), axis=0, keepdims=True)
            w = jnp.exp2(s - lse_ref[j, :, r * 256 : r * 256 + 256])
            pr.append(w.astype(BF))
            ds.append((w * (dpj - delta)).astype(BF))
        for (j, m, head, cols, nk, r), d in zip(todo, ds):
            wide = slice(r * 256, r * 256 + 256)
            dq = nn(kt[m, :, 0:nk], d)
            dq = unrotate_t(dq, tab_ref[p.t, 0:8, wide], tab_ref[p.t, 8:16, wide])
            qt[head, cols] = (dq * 0.125).astype(BF)
        m = todo[0][1]
        for blk in range(NB):
            lo = 0 if blk == 0 else S + 256 * blk
            hi = S + 256 * (blk + 1)
            left, right = [], []
            for u, (_, _, _, _, nk, r) in enumerate(todo):
                if nk >= hi:
                    zero = jnp.zeros_like(qs[u])
                    left += [ds[u][lo:hi], pr[u][lo:hi]]
                    right += [
                        jnp.concatenate([qs[u], zero], axis=0),
                        jnp.concatenate([zero, das[u]], axis=0),
                    ]
            dkv[m, lo:hi, :] += nt(
                jnp.concatenate(left, axis=1), jnp.concatenate(right, axis=1)
            )

    per = NH // back
    lead = per * (MB - 1)
    def ffn_step(f):
        slot = lax.rem(f, 2)
        load(f, slot).wait()
        for k in range(NF - 1):

            @pl.when(f == k)
            def _():
                g.run(FFN_OPS.get(k, ()))
                load(k + 1, (k + 1) % 2).start()

        for k, ops in FFN_SUMS.items():
            pl.when(f == k)(partial(red.run, ops))
        wu = [flat(wv[slot, t, :, :, :, :, 0:256]) for t in range(2)]
        wd = [flat(wv[slot, t, :, :, :, :, 256:512]) for t in range(2)]
        gslot = lax.rem(f, 3)
        hid = [nn(h2[...], wu[t]) for t in range(2)]
        dact = [nn(dym[...], wd[t]) for t in range(2)]
        act, dhid = [], []
        for t in range(2):
            row = jnp.concatenate(
                [ball[t, pl.ds(first + 2 * f, 1), :], ball[t, pl.ds(first + 2 * f + 1, 1), :]],
                axis=1,
            )
            u = hid[t] + row
            cdf = 0.5 + 0.5 * lax.erf(u * 0.7071067811865476)
            dens = jnp.exp(-0.5 * u * u) * 0.3989422804014327
            act.append((u * cdf).astype(BF))
            d = (dact[t] * (cdf + u * dens)).astype(BF)
            dhid.append(d)
            total = jnp.sum(d.astype(F32), axis=0, keepdims=True)
            for j in (0, 1):
                at = D // 128 + 4 * f + 2 * t + j
                early[pl.ds(at, 1), :] = total[:, 128 * j : 128 * j + 128]
        acc[...] += nt(act[0], wd[0]) + nt(act[1], wd[1])
        dh2[...] += nt(dhid[0], wu[0]) + nt(dhid[1], wu[1])
        for t in range(2):
            gd = tn(dym[...], act[t]).astype(BF)
            gring[gslot, t, :, :, :, :, 256:512] = gd.reshape(ZC, XC, CC, R, 256)
            gu = tn(h2[...], dhid[t]).astype(BF)
            gring[gslot, t, :, :, :, :, 0:256] = gu.reshape(ZC, XC, CC, R, 256)
        for k in range(NF):
            pl.when(f == k)(partial(red.run, [(1 + k, 0)]))

    out_copy = pltpu.make_async_copy(h2, out_hbm, lsem.at[6])

    def after_lead():
        for m in range(MB - 1):
            send_dkv(m)
        load(0, 0).start()

    def after_ffn():
        h2[...] = acc[...].astype(BF)
        out_copy.start()
        early[0:n, :] = sums[6:7, :].reshape(n, 128)
        early[n + 4 * NF :, :] = jnp.zeros((early.shape[0] - n - 4 * NF, 128), F32)
        early_sum.start(0)

    @pl.loop(0, per * MB + NF)
    def _(i):
        pl.when(i == lead)(after_lead)
        pl.when(i == lead + NF)(after_ffn)
        in_ffn = (i >= lead) & (i < lead + NF)
        pl.when(in_ffn)(lambda: ffn_step(i - lead))
        pl.when(jnp.logical_not(in_ffn))(lambda: back_step(jnp.where(i < lead, i, i - NF)))

    send_dkv(MB - 1)
    query_third(thirds - 1)
    red.run(LAST_SUMS[0])

    wqf = [flat(wq[t]) for t in range(2)]
    wshf = flat(wsh[...])

    def input_grad(b):
        rows = slice(b * 256, b * 256 + 256)
        dq, dkvb = tmp[rows, :], dkvn[rows, :]
        dh1 = nt(dq[:, 0:HT], wqf[0]) + nt(dq[:, HT:], wqf[1]) + nt(dkvb, wshf)
        dh2b = dh2[rows, :]
        z, scale = normal_rows(x_ref[rows, :].astype(F32))
        dy = dym[rows, :].astype(F32)
        e = dh1 * gain1 + dh2b * gain2
        back_in = scale * (
            e - jnp.mean(e, axis=-1, keepdims=True) - z * jnp.mean(e * z, axis=-1, keepdims=True)
        )
        tmp[rows, :] = (dy + back_in).astype(BF)
        for k, v in enumerate((dh1 * z, dh1, dh2b * z, dh2b, dq.astype(F32))):
            sums[k : k + 1, :] += jnp.sum(v, axis=0, keepdims=True)
        sums[5:6, 0:128] += jnp.sum(dkvb.astype(F32), axis=0, keepdims=True)

    input_grad(0)
    red.run(LAST_SUMS[1])
    input_grad(1)
    own_dkv(1)
    gkvs = tn(h1[...], dkvn[...]).astype(BF).reshape(ZC, XC, CC, R, 128)
    for t in range(2):
        gkv[t] = gkvs
    red.run([(last + thirds, 0)])
    input_grad(2)
    red.run(LAST_SUMS[2])
    input_grad(3)
    for k in range(5):
        late[k * n : k * n + n, :] = sums[k : k + 1, :].reshape(n, 128)
    late[5 * n : 5 * n + 1, :] = sums[5:6, 0:128]
    late[5 * n + 1 :, :] = jnp.zeros((late.shape[0] - 5 * n - 1, 128), F32)
    late_sum = AllSum(p, late, late_in, asem)
    late_sum.start(0)
    gx_copy = pltpu.make_async_copy(tmp, gx_hbm, lsem.at[7])
    gx_copy.start()
    red.run(LAST_SUMS[3])
    late_sum.end(0)
    late_sum.start(1)
    early_sum.end(1)
    red.run(LAST_SUMS[4])
    red.run(LAST_SUMS[5])
    late_sum.end(1)
    out_copy.wait()
    gx_copy.wait()


def finish_kernel(dims, out_in, gx_in, grads_in, early, late, *refs):
    (out, gx, g1, b1, g2, b2, gq, bq, gkv, bkv, go, bo, gup, bup, gdn, bd) = refs[:16]
    held, grads, sem = refs[16:]
    HT, NF = dims["HT"], dims["NF"]
    there = [pltpu.make_async_copy(grads_in, grads, sem.at[0])]
    parts, at = [], 0
    for k, ref in enumerate((gq, gkv, go, gup, gdn)):
        cols = pl.ds(at, ref.shape[1])
        parts.append(pltpu.make_async_copy(grads.at[:, cols], ref, sem.at[1 + k]))
        at += ref.shape[1]
    back = [parts]
    for k, (src, dst) in enumerate(((out_in, out), (gx_in, gx))):
        rows = src.shape[0] // 4
        for j in range(4):
            part, at = pl.ds(j * rows, rows), 6 + 2 * (4 * k + j)
            there.append(pltpu.make_async_copy(src.at[part], held.at[k, part], sem.at[at]))
            back.append([pltpu.make_async_copy(held.at[k, part], dst.at[part], sem.at[at + 1])])
    for cp in there:
        cp.start()
    t = lax.axis_index("tensor")
    n = g1.shape[0] // 128
    for k, ref in enumerate((g1, b1, g2, b2)):
        ref[...] = late[k * n : k * n + n, :].reshape(n * 128)
    half = HT // 128
    bq[...] = late[pl.ds(4 * n + half * t, half), :].reshape(HT)
    bkv[...] = late[5 * n : 5 * n + 1, :].reshape(128)
    total = early[0:n, :].reshape(n * 128)
    bo[...] = total
    bd[...] = total
    for cp, then in zip(there, back):
        cp.wait()
        for after in then:
            after.start()
    for f in range(NF):
        for j in (0, 1):
            at = 256 * f + 128 * j
            bup[at : at + 128] = early[pl.ds(n + 4 * f + 2 * t + j, 1), :].reshape(128)
    for then in back:
        for cp in then:
            cp.wait()


def angle_table(S):
    places = np.arange(2 * S, dtype=np.float64)
    freqs = 10000.0 ** (-np.arange(ROT // 2) * 2.0 / ROT)
    angles = (places[:, None] * freqs[None, :]).astype(np.float32).astype(np.float64)
    tab = np.concatenate([np.cos(angles).T, np.sin(angles).T], axis=0).astype(np.float32)
    return tab.reshape(ROT, 2, S).transpose(1, 0, 2)


def token_plan(
    block_input,
    cotangent,
    lengths,
    ln1_gain,
    ln1_bias,
    ln2_gain,
    ln2_bias,
    w_query,
    b_query,
    w_shared,
    b_shared,
    w_out,
    b_out,
    w_up,
    b_up,
    w_down,
    b_down,
):
    S, D = block_input.shape[2:]
    R, HT = w_query.shape
    FT = w_up.shape[1]
    NF, T, NH = FT // 256, MB * S, 2 * HT // HEAD_DIM
    dims = dict(S=S, HT=HT, NF=NF, T=T, NH=NH)
    plane = (ZC, XC, CC, R)
    full = (2,) + plane
    t = lax.axis_index("tensor")

    def s(shape, dtype):
        return jax.ShapeDtypeStruct(shape, dtype)

    vm = pl.BlockSpec(memory_space=VMEM)
    hbm = pl.BlockSpec(memory_space=pl.ANY)
    smem = pl.BlockSpec(memory_space=pltpu.SMEM)

    nb = HT // 128 + 2 * NF + 1
    n_gather, n_reduce = NF + 3, NF + 2 + HT // 128
    n_early, n_late = 8 * ((D // 128 + 4 * NF + 7) // 8), 8 * ((5 * (D // 128) + 8) // 8)
    n_grads = 2 * HT + 128 + 2 * FT

    outs = pl.pallas_call(
        partial(block_kernel, dims),
        out_shape=[
            s((T, D), BF),
            s((T, D), BF),
            s((NF,) + full + (512,), BF),
            s((R, n_grads), F32),
            s((n_early, 128), F32),
            s((n_late, 128), F32),
        ],
        in_specs=[hbm, hbm, smem] + [vm] * 15,
        out_specs=[hbm] * 3 + [vm] * 3,
        scratch_shapes=[
            VMEM(plane + (128,), BF),
            VMEM(full + (HT,), BF),
            VMEM(full + (HT,), BF),
            VMEM((2 * HT, D), BF),
            VMEM((2,) + full + (512,), BF),
            VMEM((2, nb, 128), F32),
            VMEM((2 * HT + 128, 128), F32),
            VMEM((T, D), BF),
            VMEM((T, D), BF),
            VMEM((T, D), BF),
            VMEM((T, D), BF),
            VMEM((D, T), BF),
            VMEM((D, T), BF),
            VMEM((D, T), BF),
            VMEM((T, D), BF),
            VMEM((T, D), F32),
            VMEM((T, D), F32),
            VMEM((MB * NH, 1, S), F32),
            VMEM((MB, 128, S), BF),
            VMEM((MB, 128, S), BF),
            VMEM((MB, 2 * S, HEAD_DIM), BF),
            VMEM((MB, 2 * S, HEAD_DIM), BF),
            VMEM((MB, HEAD_DIM, 2 * S), BF),
            VMEM((MB, HEAD_DIM + 16, 2 * S), BF),
            VMEM((MB, S, 128), F32),
            VMEM((MB, S, S), F32),
            VMEM((MB, 2 * S, 128), F32),
            VMEM((MB, S, 128), BF),
            VMEM((MB, S, 128), BF),
            VMEM((T, 128), BF),
            VMEM((3,) + full + (512,), BF),
            VMEM(full + (HT,), BF),
            VMEM((HT // 128,) + full + (128,), BF),
            VMEM(full + (128,), BF),
            VMEM((8, D), F32),
            VMEM((10, n_early, 128), F32),
            VMEM((10, n_late, 128), F32),
            VMEM((NF + 2, 2, ZC, XC, R, 512), BF),
            VMEM((NF + 3, ZC, XC, R, 256), BF),
            VMEM((NF + 3, 2, ZC, R, 256), BF),
            VMEM((NF + 3, 2, ZC, R, 256), BF),
            VMEM((NF + 3, 2, 3, R, 256), BF),
            DMA((Gather.SLOTS, 4)),
            DMA((n_gather, 4)),
            DMA((Reduce.SLOTS, 4)),
            DMA((n_reduce, 4)),
            DMA((8,)),
            DMA((2,)),
            DMA((6 + 2 * MB,)),
            DMA((4,)),
            DMA((4,)),
        ],
        compiler_params=pltpu.CompilerParams(
            vmem_limit_bytes=VMEM_LIMIT, collective_id=0, has_side_effects=True
        ),
        name="block",
    )(
        block_input.reshape(T, D),
        cotangent.reshape(T, D),
        lengths.reshape(MB),
        jnp.asarray(angle_table(S)),
        ln1_gain,
        ln1_bias,
        ln2_gain,
        ln2_bias,
        w_query,
        b_query,
        w_shared,
        b_shared,
        w_out.T,
        b_out,
        w_up,
        b_up,
        w_down.T,
        b_down,
    )
    out, gx, _, grads, early, late = outs
    vec = s((D,), F32)
    shapes = [s((T, D), BF), s((T, D), BF), vec, vec, vec, vec, s((R, HT), F32), s((HT,), F32)]
    shapes += [s((R, 128), F32), s((128,), F32), s((R, HT), F32), vec, s((R, FT), F32)]
    shapes += [s((FT,), F32), s((R, FT), F32), vec]
    outs = pl.pallas_call(
        partial(finish_kernel, dims),
        out_shape=shapes,
        in_specs=[hbm, hbm, hbm, vm, vm],
        out_specs=[hbm if len(shape.shape) > 1 else vm for shape in shapes],
        scratch_shapes=[VMEM((2, T, D), BF), VMEM((R, n_grads), F32), DMA((22,))],
        compiler_params=pltpu.CompilerParams(vmem_limit_bytes=VMEM_LIMIT),
        name="finish",
    )(out, gx, grads, early, late)
    res = list(outs)
    res[0] = res[0].reshape(block_input.shape)
    res[1] = res[1].reshape(block_input.shape)
    res[10] = res[10].T
    res[14] = res[14].T
    return tuple(res)


def fits_token_plan(mesh):
    return dict(mesh.shape) == {"dp": ZC * XC * CC, "tensor": 2}


def solution(mesh):
    in_specs = (
        P(None, "dp", "tensor", None),
        P(None, "dp", "tensor", None),
        P(None, "dp"),
        P(),
        P(),
        P(),
        P(),
        P("dp", "tensor"),
        P("tensor"),
        P("dp", None),
        P(),
        P("tensor", "dp"),
        P(),
        P("dp", "tensor"),
        P("tensor"),
        P("tensor", "dp"),
        P(),
    )
    out_specs = (
        P(None, "dp", "tensor", None),
        P(None, "dp", "tensor", None),
        P(),
        P(),
        P(),
        P(),
        P("dp", "tensor"),
        P("tensor"),
        P("dp", None),
        P(),
        P("tensor", "dp"),
        P(),
        P("dp", "tensor"),
        P("tensor"),
        P("tensor", "dp"),
        P(),
    )
    step = token_plan if fits_token_plan(mesh) else per_device
    return jax.shard_map(
        step, mesh=mesh, in_specs=in_specs, out_specs=out_specs, check_vma=False
    )
```
